32 devices in a mesh: section: 4 (over y, x), dp: 8 (over z, core).
Axes of the slice: x: 2, y: 2, z: 4, core: 2. Of those that a mesh axis runs over, the one named last changes fastest.
Arguments:
- bottom_tier_source: bfloat16 [2, 1024, 1024], P(None, 'dp'), may hold values from -6 to 6
- topmost_emitted_cotangent: bfloat16 [2, 1024, 1024], P(None, 'dp'), may hold values from -6 to 6
- packed_span_sizes: int32 [2, 5], replicated, may hold values from 1 to 1020, as said below
- attention_standardize_scale: float32 [4, 1024], P('section'), may hold values from 0.5 to 1.5
- attention_standardize_offset: float32 [4, 1024], P('section'), may hold values from -1 to 1
- lagged_lookup_mix: float32 [4, 1024], P('section'), may hold values from 0.05 to 0.95
- lagged_payload_mix: float32 [4, 1024], P('section'), may hold values from 0.05 to 0.95
- lagged_sigmoid_mix: float32 [4, 1024], P('section'), may hold values from 0.05 to 0.95
- fading_rate_logarithm: float32 [4, 1024], P('section'), may hold values from -9 to -3.5
- present_element_extra: float32 [4, 1024], P('section'), may hold values from -1 to 1
- lookup_projection: bfloat16 [4, 1024, 1024], P('section'), may hold values from -0.1875 to 0.1875
- payload_projection: bfloat16 [4, 1024, 1024], P('section'), may hold values from -0.1875 to 0.1875
- sigmoid_projection: bfloat16 [4, 1024, 1024], P('section'), may hold values from -0.1875 to 0.1875
- attention_emit_projection: bfloat16 [4, 1024, 1024], P('section'), may hold values from -0.75 to 0.75
- feedforward_standardize_scale: float32 [4, 1024], P('section'), may hold values from 0.5 to 1.5
- feedforward_standardize_offset: float32 [4, 1024], P('section'), may hold values from -1 to 1
- lagged_feedforward_lookup_mix: float32 [4, 1024], P('section'), may hold values from 0.05 to 0.95
- lagged_feedforward_sigmoid_mix: float32 [4, 1024], P('section'), may hold values from 0.05 to 0.95
- feedforward_lookup_projection: bfloat16 [4, 1024, 4096], P('section'), may hold values from -0.1875 to 0.1875
- feedforward_payload_projection: bfloat16 [4, 4096, 1024], P('section'), may hold values from -0.09375 to 0.09375
- feedforward_sigmoid_projection: bfloat16 [4, 1024, 1024], P('section'), may hold values from -0.1875 to 0.1875
Outputs:
- layer_output: bfloat16 [4, 2, 1024, 1024], P('section', None, 'dp')
- input_grad: bfloat16 [4, 2, 1024, 1024], P('section', None, 'dp')
- norm_gain_grad: float32 [4, 1024], P('section', 'dp')
- norm_bias_grad: float32 [4, 1024], P('section', 'dp')
- shift_key_grad: float32 [4, 1024], P('section', 'dp')
- shift_value_grad: float32 [4, 1024], P('section', 'dp')
- shift_gate_grad: float32 [4, 1024], P('section', 'dp')
- decay_rate_grad: float32 [4, 1024], P('section', 'dp')
- first_bonus_grad: float32 [4, 1024], P('section', 'dp')
- key_weight_grad: float32 [4, 1024, 1024], P('section', 'dp')
- value_weight_grad: float32 [4, 1024, 1024], P('section', 'dp')
- gate_weight_grad: float32 [4, 1024, 1024], P('section', 'dp')
- output_weight_grad: float32 [4, 1024, 1024], P('section', 'dp')
- second_gain_grad: float32 [4, 1024], P('section', 'dp')
- second_bias_grad: float32 [4, 1024], P('section', 'dp')
- shift_hidden_grad: float32 [4, 1024], P('section', 'dp')
- shift_filter_grad: float32 [4, 1024], P('section', 'dp')
- hidden_weight_grad: float32 [4, 1024, 4096], P('section', 'dp')
- project_weight_grad: float32 [4, 4096, 1024], P('section', 'dp')
- filter_weight_grad: float32 [4, 1024, 1024], P('section', 'dp')
The draws below stay inside these ranges and needn't reach their ends.
Inputs may be any that keep to these rules, and one draw needn't show every extreme that they name: `packed_span_sizes`: in each micro-batch the lengths sum to 1024; the second sequence begins within the first 128 tokens and ends within the last 128 tokens; the first micro-batch's lengths are 1, 1020, 1, 1, 1.
All inputs are finite; a program needn't handle non-finite values.
Results may differ from the reference program's by a relative error of at most 0.02.
Values may be sent and summed in bfloat16 or wider, within the bound.
A program may use at most 320 MiB of HBM per device.

```python
import jax
import jax.numpy as jnp
from jax import lax

EMBED_DIMENSION = 1024
FF = 4096
TOK_DEV = 128
MICRO = 2
SEQS = 5
DEPTH_TOTAL = 4
TOKENS = 1024


def draw_packed_span_sizes(key, part):
    key = jax.random.fold_in(key, 7)
    head_key, tail_key = jax.random.split(key)
    head_lengths = jax.random.randint(head_key, (MICRO, 1), 1, TOK_DEV)
    tail_lengths = jax.random.randint(tail_key, (MICRO, SEQS - 2), 1, TOK_DEV // 4 + 1)
    first_row = (jnp.arange(MICRO) == 0)[:, None]
    head_lengths = jnp.where(first_row, 1, head_lengths)
    tail_lengths = jnp.where(first_row, 1, tail_lengths)
    longest = TOKENS - head_lengths - jnp.sum(tail_lengths, axis=1, keepdims=True)
    return jnp.concatenate([head_lengths, longest, tail_lengths], axis=1).astype(jnp.int32)


def levels(key, dims, cuts, least, largest):
    def one(dim, shards_of):
        heights = jax.random.uniform(jax.random.fold_in(jax.random.fold_in(key, 6), dim), (shards_of,), jnp.float32, least / len(cuts), largest / len(cuts))
        return jnp.repeat(jnp.exp(heights), dims[dim] // shards_of).reshape((-1,) + (1,) * (len(dims) - dim - 1))

    level = one(*cuts[0])
    for cut in cuts[1:]:
        level = level * one(*cut)
    return level


def scatter_about(rng, extent, deviation, limit, cuts=(), kind=jnp.bfloat16):
    drawn = jax.random.normal(rng, extent, jnp.float32) * deviation
    if len(cuts) > 0:
        drawn = levels(rng, extent, cuts, -0.22, 0.18) * drawn
    return jnp.clip(drawn, min=-limit, max=limit).astype(kind)


def setup_inputs(seed: int = 0) -> dict:
    splits = jax.random.split(jax.random.key(seed), 22)
    return {
        "bottom_tier_source": scatter_about(splits[0], (MICRO, TOKENS, EMBED_DIMENSION), 1.0, 6.0, ((1, 8),)),
        "topmost_emitted_cotangent": scatter_about(splits[1], (MICRO, TOKENS, EMBED_DIMENSION), 1.0, 6.0, ((1, 8),)),
        "packed_span_sizes": draw_packed_span_sizes(jax.random.fold_in(splits[21], 71), 0),
        "attention_standardize_scale": jnp.clip(1.0 + 0.1 * jax.random.normal(splits[3], (DEPTH_TOTAL, EMBED_DIMENSION), jnp.float32), 0.5, 1.5),
        "attention_standardize_offset": scatter_about(splits[4], (DEPTH_TOTAL, EMBED_DIMENSION), 0.2, 1.0, ((0, 4),), jnp.float32),
        "lagged_lookup_mix": jnp.clip(0.05 + 0.9 * jax.random.uniform(splits[5], (DEPTH_TOTAL, EMBED_DIMENSION), jnp.float32) ** levels(splits[5], (DEPTH_TOTAL, EMBED_DIMENSION), ((0, 4),), -0.2, 0.2), 0.05, 0.95),
        "lagged_payload_mix": jnp.clip(0.05 + 0.9 * jax.random.uniform(splits[6], (DEPTH_TOTAL, EMBED_DIMENSION), jnp.float32) ** levels(splits[6], (DEPTH_TOTAL, EMBED_DIMENSION), ((0, 4),), -0.2, 0.2), 0.05, 0.95),
        "lagged_sigmoid_mix": jnp.clip(0.05 + 0.9 * jax.random.uniform(splits[7], (DEPTH_TOTAL, EMBED_DIMENSION), jnp.float32) ** levels(splits[7], (DEPTH_TOTAL, EMBED_DIMENSION), ((0, 4),), -0.2, 0.2), 0.05, 0.95),
        "fading_rate_logarithm": jnp.clip(-9.0 + 5.5 * jax.random.uniform(splits[8], (DEPTH_TOTAL, EMBED_DIMENSION), jnp.float32) ** levels(splits[8], (DEPTH_TOTAL, EMBED_DIMENSION), ((0, 4),), -0.2, 0.2), -9.0, -3.5),
        "present_element_extra": jnp.clip(jax.random.uniform(splits[9], (DEPTH_TOTAL, EMBED_DIMENSION), jnp.float32, -1.0, 1.0) * levels(splits[9], (DEPTH_TOTAL, EMBED_DIMENSION), ((0, 4),), -0.4, 0.0), -1.0, 1.0),
        "lookup_projection": scatter_about(splits[10], (DEPTH_TOTAL, EMBED_DIMENSION, EMBED_DIMENSION), EMBED_DIMENSION ** -0.5, 0.1875, ((0, 4),)),
        "payload_projection": scatter_about(splits[11], (DEPTH_TOTAL, EMBED_DIMENSION, EMBED_DIMENSION), EMBED_DIMENSION ** -0.5, 0.1875, ((0, 4),)),
        "sigmoid_projection": scatter_about(splits[12], (DEPTH_TOTAL, EMBED_DIMENSION, EMBED_DIMENSION), EMBED_DIMENSION ** -0.5, 0.1875, ((0, 4),)),
        "attention_emit_projection": scatter_about(splits[13], (DEPTH_TOTAL, EMBED_DIMENSION, EMBED_DIMENSION), (EMBED_DIMENSION // 16) ** -0.5, 0.75, ((0, 4),)),
        "feedforward_standardize_scale": jnp.clip(1.0 + 0.1 * jax.random.normal(splits[14], (DEPTH_TOTAL, EMBED_DIMENSION), jnp.float32), 0.5, 1.5),
        "feedforward_standardize_offset": scatter_about(splits[15], (DEPTH_TOTAL, EMBED_DIMENSION), 0.2, 1.0, ((0, 4),), jnp.float32),
        "lagged_feedforward_lookup_mix": jnp.clip(0.05 + 0.9 * jax.random.uniform(splits[16], (DEPTH_TOTAL, EMBED_DIMENSION), jnp.float32) ** levels(splits[16], (DEPTH_TOTAL, EMBED_DIMENSION), ((0, 4),), -0.2, 0.2), 0.05, 0.95),
        "lagged_feedforward_sigmoid_mix": jnp.clip(0.05 + 0.9 * jax.random.uniform(splits[17], (DEPTH_TOTAL, EMBED_DIMENSION), jnp.float32) ** levels(splits[17], (DEPTH_TOTAL, EMBED_DIMENSION), ((0, 4),), -0.2, 0.2), 0.05, 0.95),
        "feedforward_lookup_projection": scatter_about(splits[18], (DEPTH_TOTAL, EMBED_DIMENSION, FF), EMBED_DIMENSION ** -0.5, 0.1875, ((0, 4),)),
        "feedforward_payload_projection": scatter_about(splits[19], (DEPTH_TOTAL, FF, EMBED_DIMENSION), FF ** -0.5, 0.09375, ((0, 4),)),
        "feedforward_sigmoid_projection": scatter_about(splits[20], (DEPTH_TOTAL, EMBED_DIMENSION, EMBED_DIMENSION), EMBED_DIMENSION ** -0.5, 0.1875, ((0, 4),)),
    }


EPS = 1e-05

@jax.custom_vjp
def low(v):
    return lax.optimization_barrier(v.astype(jnp.bfloat16)).astype(jnp.float32)

@jax.custom_vjp
def low_back(v):
    return v

def low_keep(v):
    return (low(v), None)

def low_pass(kept, grad):
    return (grad,)

def back_keep(v):
    return (v, None)

def back_low(kept, grad):
    return (low(grad),)
low.defvjp(low_keep, low_pass)
low_back.defvjp(back_keep, back_low)

def layer_norm(source, attention_standardize_scale, attention_standardize_offset):
    average = lax.optimization_barrier(jnp.mean(source, axis=-1, keepdims=True))
    centred = source - average
    variance = lax.optimization_barrier(jnp.mean(centred * centred, axis=-1, keepdims=True))
    return centred * lax.rsqrt(variance + EPS) * attention_standardize_scale + attention_standardize_offset

def combine_pairs(earlier, later_part):
    return (earlier[0] * later_part[0], later_part[0] * earlier[1] + later_part[1], later_part[0] * earlier[2] + later_part[2])

def product_high(left_rows, right_rows):
    return jnp.dot(left_rows, right_rows, preferred_element_type=jnp.float32, precision=lax.Precision.HIGHEST)

def blend_rows(normed, earlier, coefficient):
    return normed * coefficient + earlier * (1.0 - coefficient)

def shift_rows(source, retain_mask):
    earlier = jnp.concatenate([jnp.zeros_like(source[:1]), source[:-1]], axis=0)
    return earlier * retain_mask[:, None]

def keep_rows(lengths, offset, row_count):
    starts = (jnp.cumsum(lengths) - lengths).astype(jnp.int32)
    position = (offset + jnp.arange(row_count, dtype=jnp.int32)).astype(jnp.int32)
    hits = jnp.any(position[:, None] == starts[None, :], axis=1)
    return jnp.where(hits, 0.0, 1.0).astype(jnp.float32)

def rwkv_layer(current, retain_mask, tier_coefficients):
    attention_standardize_scale, attention_standardize_offset, lagged_lookup_mix, lagged_payload_mix, lagged_sigmoid_mix, fading_rate_logarithm, present_element_extra, lookup_projection, payload_projection, sigmoid_projection, attention_emit_projection, feedforward_standardize_scale, feedforward_standardize_offset, lagged_feedforward_lookup_mix, lagged_feedforward_sigmoid_mix, feedforward_lookup_projection, feedforward_payload_projection, feedforward_sigmoid_projection = tier_coefficients
    normed = layer_norm(current, attention_standardize_scale, attention_standardize_offset)
    earlier = shift_rows(normed, retain_mask)
    lookup_projected_vectors = low_back(product_high(low(blend_rows(normed, earlier, lagged_lookup_mix)), lookup_projection))
    payload_vectors = low_back(product_high(low(blend_rows(normed, earlier, lagged_payload_mix)), payload_projection))
    gate_pre = low_back(product_high(low(blend_rows(normed, earlier, lagged_sigmoid_mix)), sigmoid_projection))
    factor = retain_mask[:, None] * jnp.exp(-jnp.exp(fading_rate_logarithm))[None, :]
    weight = jnp.exp(lookup_projected_vectors)
    totals, acc_a, acc_b = lax.associative_scan(combine_pairs, (factor, weight * payload_vectors, weight), axis=0)
    prior_primary_carry = shift_rows(acc_a, retain_mask)
    prior_auxiliary_carry = shift_rows(acc_b, retain_mask)
    present_extra_term = jnp.exp(present_element_extra[None, :] + lookup_projected_vectors)
    interpolated_vectors = (prior_primary_carry + present_extra_term * payload_vectors) / (prior_auxiliary_carry + present_extra_term)
    gated_rows = jax.nn.sigmoid(gate_pre) * interpolated_vectors
    middle = current + low_back(product_high(low(gated_rows), attention_emit_projection))
    second = layer_norm(middle, feedforward_standardize_scale, feedforward_standardize_offset)
    earlier_two = shift_rows(second, retain_mask)
    hidden_pre = low_back(product_high(low(blend_rows(second, earlier_two, lagged_feedforward_lookup_mix)), feedforward_lookup_projection))
    active = jnp.maximum(hidden_pre, 0.0)
    projected = low_back(product_high(low(active * active), feedforward_payload_projection))
    sieve_rows = jax.nn.sigmoid(low_back(product_high(low(blend_rows(second, earlier_two, lagged_feedforward_sigmoid_mix)), feedforward_sigmoid_projection)))
    return middle + sieve_rows * projected

def reference(bottom_tier_source, topmost_emitted_cotangent, packed_span_sizes, attention_standardize_scale, attention_standardize_offset, lagged_lookup_mix, lagged_payload_mix, lagged_sigmoid_mix, fading_rate_logarithm, present_element_extra, lookup_projection, payload_projection, sigmoid_projection, attention_emit_projection, feedforward_standardize_scale, feedforward_standardize_offset, lagged_feedforward_lookup_mix, lagged_feedforward_sigmoid_mix, feedforward_lookup_projection, feedforward_payload_projection, feedforward_sigmoid_projection):
    coefficient_bundle = tuple((peer_device_rank.astype(jnp.float32) for peer_device_rank in (attention_standardize_scale, attention_standardize_offset, lagged_lookup_mix, lagged_payload_mix, lagged_sigmoid_mix, fading_rate_logarithm, present_element_extra, lookup_projection, payload_projection, sigmoid_projection, attention_emit_projection, feedforward_standardize_scale, feedforward_standardize_offset, lagged_feedforward_lookup_mix, lagged_feedforward_sigmoid_mix, feedforward_lookup_projection, feedforward_payload_projection, feedforward_sigmoid_projection)))
    tokens = bottom_tier_source.astype(jnp.float32)
    keep_masks = [keep_rows(packed_span_sizes[batch_index], 0, TOKENS) for batch_index in range(MICRO)]
    layer_step = jax.checkpoint(rwkv_layer)

    def forward(weights, probes):
        stacked_layers = []
        for batch_index in range(MICRO):
            current = low_back(tokens[batch_index] + probes[0, batch_index])
            results = []
            for layer_index in range(DEPTH_TOTAL):
                rounded = low(layer_step(current, keep_masks[batch_index], tuple((peer_device_rank[layer_index] for peer_device_rank in weights))))
                results.append(rounded)
                if layer_index + 1 < DEPTH_TOTAL:
                    current = low_back(rounded + probes[layer_index + 1, batch_index])
            stacked_layers.append(jnp.stack(results))
        return jnp.stack(stacked_layers, axis=1)
    probes = jnp.zeros((DEPTH_TOTAL, MICRO, TOKENS, EMBED_DIMENSION), jnp.float32)
    stacked, back_fn = jax.vjp(forward, coefficient_bundle, probes)
    cotangent = jnp.concatenate([jnp.zeros((DEPTH_TOTAL - 1, MICRO, TOKENS, EMBED_DIMENSION), jnp.float32), topmost_emitted_cotangent.astype(jnp.float32)[None]], axis=0)
    param_grads, probe_grads = back_fn(cotangent)
    return (stacked.astype(jnp.bfloat16), probe_grads.astype(jnp.bfloat16), param_grads[0], param_grads[1], param_grads[2], param_grads[3], param_grads[4], param_grads[5], param_grads[6], param_grads[7], param_grads[8], param_grads[9], param_grads[10], param_grads[11], param_grads[12], param_grads[13], param_grads[14], param_grads[15], param_grads[16], param_grads[17])
```

```python
from functools import partial

import jax
import jax.numpy as jnp
from jax import lax
from jax.experimental import pallas as pl
from jax.experimental.pallas import tpu as pltpu
from jax.sharding import PartitionSpec as P

EPS = 1e-05
MESH = pl.DeviceIdType.MESH
RB = 32
VECTORS = 16
F32 = jnp.float32
BF16 = jnp.bfloat16


def dot_nn(left, right):
    return jnp.dot(left, right, preferred_element_type=F32)


def dot_nt(left, right):
    return lax.dot_general(left, right, (((1,), (1,)), ((), ())), preferred_element_type=F32)


def dot_tn(left, right):
    return lax.dot_general(left, right, (((0,), (0,)), ((), ())), preferred_element_type=F32)


def sigmoid(v):
    return 1.0 / (1.0 + jnp.exp(-v))


def normalise(source):
    centred = source - jnp.mean(source, axis=-1, keepdims=True)
    spread = lax.rsqrt(jnp.mean(centred * centred, axis=-1, keepdims=True) + EPS)
    return centred * spread, spread


def moved_down(rows, first):
    place = lax.broadcasted_iota(jnp.int32, rows.shape, 0)
    return jnp.where(place == 0, first, pltpu.roll(rows, 1, 0))


def moved_up(rows, last):
    count = rows.shape[0]
    place = lax.broadcasted_iota(jnp.int32, rows.shape, 0)
    return jnp.where(place == count - 1, last, pltpu.roll(rows, count - 1, 0))


def fold(rows):
    total = rows[0:8]
    for at in range(8, rows.shape[0], 8):
        total = total + rows[at : at + 8]
    return total


def relay_kernel(sections, peers, split_vectors, *refs):
    (
        spans, x_in, top_in,
        gain1, bias1, mix_k, mix_v, mix_g, log_rate, extra, gain2, bias2, mix_h, mix_f,
        wk_in, wv_in, wg_in, wo_in, wh_in, wp_in, wf_in,
        out, back, vec_out, lk, lv, lg, lgt, lh, lf, sq, dk, dv, dg, datt, dproj, dsv, dh,
        wk, wv, wg, wo, wh, wp, wf,
        xs, hx, dys, kk, vv, sg, sa, sb, mid, hmid, proj, sv, act, halo1, halo2,
        e0, e1, low_mask, up_mask, split, acc, t1, t2, t3,
        states, back_states, de2, de1, sum_row, sum_back, send_de2, send_de1, vg, vgs, vgr,
        w_sem, x_sem, top_sem, s_h0, s_x, s_hx, s_st, s_mid, s_dy, s_de2, s_bst, s_de1, s_vg,
        r_x, r_hx, r_st, r_mid, r_dy, r_de2, r_bst, r_de1, r_vg,
    ) = refs
    me_s = lax.axis_index("section")
    me = lax.axis_index("dp")
    batches, row_count, width = x_in.shape
    hidden = wh.shape[1]
    chunks = row_count // RB
    base = me * row_count

    def at(section, index):
        return (section, index)

    barrier = pltpu.get_barrier_semaphore()

    def greet(section, index):
        pl.semaphore_signal(barrier, inc=1, device_id=at(section, index), device_id_type=MESH)

    def greet_peer(k, carry):
        @pl.when(k != me)
        def _():
            greet(me_s, k)

        return carry

    lax.fori_loop(0, peers, greet_peer, 0)
    has_next = me_s + 1 < sections
    has_prior = me_s > 0
    has_right = me + 1 < peers
    has_left = me > 0

    @pl.when(has_next)
    def _():
        greet(me_s + 1, me)

    @pl.when(has_prior)
    def _():
        greet(me_s - 1, me)

    @pl.when(has_next & has_right)
    def _():
        greet(me_s + 1, me + 1)

    @pl.when(has_prior & has_left)
    def _():
        greet(me_s - 1, me - 1)

    weight_copies = [
        pltpu.make_async_copy(source, target, w_sem.at[index])
        for index, (source, target) in enumerate(
            ((wk_in, wk), (wv_in, wv), (wg_in, wg), (wo_in, wo), (wf_in, wf), (wh_in, wh), (wp_in, wp))
        )
    ]

    @pl.when(me_s == 0)
    def _():
        pltpu.make_async_copy(x_in, xs, x_sem).start()

    for copy in weight_copies:
        copy.start()

    @pl.when(me_s == sections - 1)
    def _():
        pltpu.make_async_copy(top_in, dys, top_sem).start()

    rate = jnp.exp(log_rate[...])
    decay_block = jnp.exp(-rate * row_count)
    grow_block = jnp.exp(rate * row_count)

    def starts_of(m):
        found = []
        total = jnp.int32(0)
        for j in range(spans.shape[1]):
            found.append(total)
            total = total + spans[m, j]
        return found

    def segment(position, starts):
        total = jnp.where(position >= starts[0], 1, 0)
        for start in starts[1:]:
            total = total + jnp.where(position >= start, 1, 0)
        return total

    def column(i):
        return base + i * RB + lax.broadcasted_iota(jnp.int32, (RB, 1), 0)

    def keep_of(position, starts):
        return jnp.where(segment(position, starts) == segment(position - 1, starts), 1.0, 0.0)

    def fill_powers(i, carry):
        place = (i * RB + lax.broadcasted_iota(jnp.int32, (RB, width), 0)).astype(F32)
        e0[pl.ds(pl.multiple_of(i * RB, RB), RB), :] = jnp.exp(-place * rate)
        e1[pl.ds(pl.multiple_of(i * RB, RB), RB), :] = jnp.exp((place - (row_count - 1.0)) * rate)
        return carry

    lax.fori_loop(0, chunks, fill_powers, 0)
    for m in range(batches):
        starts = starts_of(m)
        row_at = lax.broadcasted_iota(jnp.int32, (row_count, row_count), 0)
        column_at = lax.broadcasted_iota(jnp.int32, (row_count, row_count), 1)
        same = segment(base + row_at, starts) == segment(base + column_at, starts)
        lower = jnp.where(same & (column_at < row_at), 1.0, 0.0).astype(BF16)
        upper = jnp.where(same & (column_at > row_at), 1.0, 0.0).astype(BF16)
        low_mask[m, :, 0:row_count] = lower
        low_mask[m, :, row_count:] = lower
        up_mask[m, :, 0:row_count] = upper
        up_mask[m, :, row_count:] = upper
    vg[...] = jnp.zeros_like(vg)

    @pl.when(me == 0)
    def _():
        hx[...] = jnp.zeros_like(hx)
        hmid[...] = jnp.zeros_like(hmid)

    @pl.when(me == peers - 1)
    def _():
        de1[...] = jnp.zeros_like(de1)
        de2[...] = jnp.zeros_like(de2)

    greeted = (
        peers - 1
        + jnp.where(has_next, 1, 0)
        + jnp.where(has_prior, 1, 0)
        + jnp.where(has_next & has_right, 1, 0)
        + jnp.where(has_prior & has_left, 1, 0)
    )
    pl.semaphore_wait(barrier, greeted)

    def remote(source, target, send, receive, section, index):
        return pltpu.make_async_remote_copy(
            src_ref=source, dst_ref=target, send_sem=send, recv_sem=receive,
            device_id=at(section, index), device_id_type=MESH,
        )

    right = jnp.minimum(me + 1, peers - 1)
    left = jnp.maximum(me - 1, 0)
    above = jnp.minimum(me_s + 1, sections - 1)
    below = jnp.maximum(me_s - 1, 0)
    tail = pl.ds(row_count - 16, 16)
    tail8 = pl.ds(row_count - 8, 8)

    def start_halo(m):
        return remote(x_in.at[m, tail], hx.at[m], s_h0.at[m], r_hx.at[m], me_s, right)

    def result_copy(m):
        return remote(out.at[m], xs.at[m], s_x.at[m], r_x.at[m], above, me)

    def result_halo(m):
        return remote(out.at[m, tail], hx.at[m], s_hx.at[m], r_hx.at[m], above, right)

    def middle_halo(m):
        return remote(mid.at[m, tail8], hmid.at[m], s_mid.at[m], r_mid.at[m], me_s, right)

    def state_copy(m, k, slot):
        return remote(sum_row.at[m], states.at[m, slot], s_st.at[m, k], r_st.at[m, slot], me_s, k)

    def back_copy(m):
        return remote(back.at[m], dys.at[m], s_dy.at[m], r_dy.at[m], below, me)

    def second_copy(m):
        return remote(send_de2.at[m], de2.at[m], s_de2.at[m], r_de2.at[m], me_s, left)

    def first_copy(m):
        return remote(send_de1.at[m], de1.at[m], s_de1.at[m], r_de1.at[m], me_s, left)

    def back_state_copy(m, k, slot):
        return remote(
            sum_back.at[m], back_states.at[m, slot], s_bst.at[m, k], r_bst.at[m, slot], me_s, k
        )

    @pl.when((me_s == 0) & has_right)
    def _():
        for m in range(batches):
            start_halo(m).start()

    @pl.when(me_s == 0)
    def _():
        pltpu.make_async_copy(x_in, xs, x_sem).wait()

    def span_of(i):
        return pl.ds(pl.multiple_of(i * RB, RB), RB)

    def forward(m, carry):
        starts = starts_of(m)

        @pl.when(has_prior)
        def _():
            result_copy(m).wait_recv()

        @pl.when(has_left)
        def _():
            start_halo(m).wait_recv()

        halo_rows, _ = normalise(hx[m].astype(F32))
        halo_rows = halo_rows * gain1[...] + bias1[...]
        halo1[m] = halo_rows[8:16]

        def mix_in(i, last):
            rows = span_of(i)
            normed, _ = normalise(xs[m, rows, :].astype(F32))
            normed = normed * gain1[...] + bias1[...]
            earlier = moved_down(normed, last) * keep_of(column(i), starts)
            gap = normed - earlier
            lk[m, rows, :] = (earlier + gap * mix_k[...]).astype(BF16)
            lv[m, rows, :] = (earlier + gap * mix_v[...]).astype(BF16)
            lg[m, rows, :] = (earlier + gap * mix_g[...]).astype(BF16)
            return normed[RB - 1 : RB]

        lax.fori_loop(0, chunks, mix_in, halo_rows[15:16])

        @pl.when(m == 0)
        def _():
            for copy in weight_copies[0:2]:
                copy.wait()

        kk[m] = dot_nn(lk[m], wk[...])
        vv[m] = dot_nn(lv[m], wv[...])
        end_segment = segment(base + row_count - 1, starts)

        def spread_in(i, totals):
            rows = span_of(i)
            weight = jnp.exp(kk[m, rows, :]) * e1[rows, :]
            weighted = weight * vv[m, rows, :]
            high_a = weighted.astype(BF16)
            high_b = weight.astype(BF16)
            split[rows, 0:width] = high_a
            split[rows, width:] = high_b
            low = pl.ds(pl.multiple_of(row_count + i * RB, RB), RB)
            split[low, 0:width] = (weighted - high_a.astype(F32)).astype(BF16)
            split[low, width:] = (weight - high_b.astype(F32)).astype(BF16)
            chosen = segment(column(i), starts) == end_segment
            return (
                totals[0] + fold(jnp.where(chosen, weighted, 0.0)),
                totals[1] + fold(jnp.where(chosen, weight, 0.0)),
            )

        nothing = jnp.zeros((8, width), F32)
        total_a, total_b = lax.fori_loop(0, chunks, spread_in, (nothing, nothing))
        sum_row[m, 0:1] = jnp.sum(total_a, axis=0, keepdims=True)
        sum_row[m, 1:2] = jnp.sum(total_b, axis=0, keepdims=True)

        def send_state(k, carry):
            state_copy(m, k, me).start()
            return carry

        lax.fori_loop(me + 1, peers, send_state, 0)

        @pl.when(m == 0)
        def _():
            weight_copies[2].wait()

        sg[m] = dot_nn(lg[m], wg[...])
        acc[...] = dot_nn(low_mask[m], split[...])

        def receive_state(k, held):
            state_copy(m, k, k).wait_recv()
            unbroken = segment(k * row_count - 1, starts) == segment(
                (k + 1) * row_count - 1, starts
            )
            passing = jnp.where(unbroken, 1.0, 0.0) * decay_block
            return (
                passing * held[0] + states[m, k, 0:1],
                passing * held[1] + states[m, k, 1:2],
            )

        none = jnp.zeros((1, width), F32)
        enter_a, enter_b = lax.fori_loop(0, me, receive_state, (none, none))
        prior_segment = segment(base - 1, starts)

        def mix_states(i, carry):
            rows = span_of(i)
            falling = e0[rows, :]
            chosen = jnp.where(segment(column(i), starts) == prior_segment, 1.0, 0.0)
            grown = falling * grow_block
            held = falling * chosen
            state_a = grown * acc[rows, 0:width] + held * enter_a
            state_b = grown * acc[rows, width:] + held * enter_b
            sa[m, rows, :] = state_a
            sb[m, rows, :] = state_b
            present = jnp.exp(extra[...] + kk[m, rows, :])
            gate = sigmoid(sg[m, rows, :])
            sg[m, rows, :] = gate
            found = (state_a + present * vv[m, rows, :]) / (state_b + present)
            lgt[m, rows, :] = (gate * found).astype(BF16)
            return carry

        lax.fori_loop(0, chunks, mix_states, 0)

        @pl.when(m == 0)
        def _():
            weight_copies[3].wait()

        mid[m] = xs[m].astype(F32) + dot_nn(lgt[m], wo[...])

        @pl.when(has_right)
        def _():
            middle_halo(m).start()

        def mix_second(i, last):
            rows = span_of(i)
            normed, _ = normalise(mid[m, rows, :])
            normed = normed * gain2[...] + bias2[...]
            earlier = moved_down(normed, last) * keep_of(column(i), starts)
            gap = normed - earlier
            lh[m, rows, :] = (earlier + gap * mix_h[...]).astype(BF16)
            lf[m, rows, :] = (earlier + gap * mix_f[...]).astype(BF16)
            return normed[RB - 1 : RB]

        lax.fori_loop(0, chunks, mix_second, none)

        @pl.when(has_left)
        def _():
            middle_halo(m).wait_recv()

        halo_rows, _ = normalise(hmid[m])
        halo_rows = halo_rows * gain2[...] + bias2[...]
        halo2[m] = halo_rows
        mix_second(0, halo_rows[7:8])

        @pl.when(m == 0)
        def _():
            for copy in weight_copies[4:7]:
                copy.wait()

        sv[m] = dot_nn(lf[m], wf[...])

        def widen(j, carry):
            columns = pl.ds(pl.multiple_of(j * width, width), width)
            active = jnp.maximum(dot_nn(lh[m], wh[:, columns]), 0.0)
            act[m, :, columns] = active.astype(BF16)
            sq[m, :, columns] = (active * active).astype(BF16)
            return carry

        lax.fori_loop(0, hidden // width, widen, 0)
        proj[m] = dot_nn(sq[m], wp[...])

        def finish(i, carry):
            rows = span_of(i)
            sieve = sigmoid(sv[m, rows, :])
            sv[m, rows, :] = sieve
            out[m, rows, :] = (mid[m, rows, :] + sieve * proj[m, rows, :]).astype(BF16)
            return carry

        lax.fori_loop(0, chunks, finish, 0)

        @pl.when(has_next)
        def _():
            result_copy(m).start()

        @pl.when(has_next & has_right)
        def _():
            result_halo(m).start()

        return carry

    lax.fori_loop(0, batches, forward, 0)

    def add_vector(index, value):
        vg[index] += fold(value)

    @pl.when(me_s == sections - 1)
    def _():
        pltpu.make_async_copy(top_in, dys, top_sem).wait()

    def backward(m, carry):
        starts = starts_of(m)
        none = jnp.zeros((1, width), F32)

        @pl.when(has_next)
        def _():
            back_copy(m).wait_recv()

        def open_back(i, carry):
            rows = span_of(i)
            incoming = dys[m, rows, :].astype(F32)
            sieve = sv[m, rows, :]
            gained = incoming * sieve
            dproj[m, rows, :] = gained.astype(BF16)
            dsv[m, rows, :] = (gained * proj[m, rows, :] * (1.0 - sieve)).astype(BF16)
            return carry

        lax.fori_loop(0, chunks, open_back, 0)
        t1[...] = jnp.zeros_like(t1)

        def narrow(j, carry):
            columns = pl.ds(pl.multiple_of(j * width, width), width)
            grown = dot_nt(dproj[m], wp[columns, :])
            dh[m, :, columns] = (grown * 2.0 * act[m, :, columns].astype(F32)).astype(BF16)
            t1[...] += dot_nt(dh[m, :, columns], wh[:, columns])
            return carry

        lax.fori_loop(0, hidden // width, narrow, 0)
        t2[...] = dot_nt(dsv[m], wf[...])

        def second_earlier(rows, position):
            whole = t1[rows, :] * (1.0 - mix_h[...]) + t2[rows, :] * (1.0 - mix_f[...])
            return whole * keep_of(position, starts)

        eight = lax.broadcasted_iota(jnp.int32, (8, 1), 0)
        send_de2[m] = second_earlier(pl.ds(0, 8), base + eight)

        @pl.when(has_left)
        def _():
            second_copy(m).start()

        def back_second(i, last, following):
            rows = span_of(i)
            spare, spread = normalise(mid[m, rows, :])
            normed = spare * gain2[...] + bias2[...]
            kept = keep_of(column(i), starts)
            gap = normed - moved_down(normed, last) * kept
            from_h = t1[rows, :]
            from_f = t2[rows, :]
            add_vector(9, from_h * gap)
            add_vector(10, from_f * gap)
            straight = from_h * mix_h[...] + from_f * mix_f[...]
            earlier = (from_h + from_f - straight) * kept
            d_normed = straight + moved_up(earlier, following)
            add_vector(7, d_normed * spare)
            add_vector(8, d_normed)
            scaled = d_normed * gain2[...]
            mean_one = jnp.mean(scaled, axis=-1, keepdims=True)
            mean_two = jnp.mean(scaled * spare, axis=-1, keepdims=True)
            d_mid = dys[m, rows, :].astype(F32) + spread * (scaled - mean_one - spare * mean_two)
            t3[rows, :] = d_mid
            datt[m, rows, :] = d_mid.astype(BF16)
            return normed[RB - 1 : RB]

        def following_second(i):
            start = pl.multiple_of((i + 1) * RB, RB)
            return second_earlier(pl.ds(start, 8), base + start + eight)[0:1]

        last = lax.fori_loop(
            0, chunks - 1,
            lambda i, last: back_second(i, last, following_second(i)),
            halo2[m, 7:8],
        )

        @pl.when(has_right)
        def _():
            second_copy(m).wait_recv()

        back_second(chunks - 1, last, de2[m, 0:1])
        t1[...] = dot_nt(datt[m], wo[...])
        open_segment = segment(base, starts)

        def back_states_in(i, totals):
            rows = span_of(i)
            d_gated = t1[rows, :]
            gate = sg[m, rows, :]
            keys = kk[m, rows, :]
            values = vv[m, rows, :]
            present = jnp.exp(extra[...] + keys)
            inverse = 1.0 / (sb[m, rows, :] + present)
            found = (sa[m, rows, :] + present * values) * inverse
            d_found = d_gated * gate
            dg[m, rows, :] = (d_found * found * (1.0 - gate)).astype(BF16)
            d_a = d_found * inverse
            d_b = -d_a * found
            d_key = (d_a * values + d_b) * present
            add_vector(6, d_key)
            t1[rows, :] = d_key
            t2[rows, :] = d_a * present
            falling = e0[rows, :]
            scaled_a = d_a * falling
            scaled_b = d_b * falling
            high_a = scaled_a.astype(BF16)
            high_b = scaled_b.astype(BF16)
            split[rows, 0:width] = high_a
            split[rows, width:] = high_b
            low = pl.ds(pl.multiple_of(row_count + i * RB, RB), RB)
            split[low, 0:width] = (scaled_a - high_a.astype(F32)).astype(BF16)
            split[low, width:] = (scaled_b - high_b.astype(F32)).astype(BF16)
            chosen = segment(column(i), starts) == open_segment
            return (
                totals[0] + fold(jnp.where(chosen, scaled_a, 0.0)),
                totals[1] + fold(jnp.where(chosen, scaled_b, 0.0)),
            )

        nothing = jnp.zeros((8, width), F32)
        total_a, total_b = lax.fori_loop(0, chunks, back_states_in, (nothing, nothing))
        sum_back[m, 0:1] = jnp.sum(total_a, axis=0, keepdims=True)
        sum_back[m, 1:2] = jnp.sum(total_b, axis=0, keepdims=True)

        def send_state(k, carry):
            back_state_copy(m, k, me).start()
            return carry

        lax.fori_loop(0, me, send_state, 0)
        acc[...] = dot_nn(up_mask[m], split[...])

        def receive_state(turn, held):
            k = peers - 1 - turn
            back_state_copy(m, k, k).wait_recv()
            first = segment(k * row_count, starts)
            unbroken = first == segment((k + 1) * row_count - 1, starts)
            joined = jnp.where(first == segment(k * row_count - 1, starts), 1.0, 0.0)
            passing = jnp.where(unbroken, 1.0, 0.0) * decay_block
            return (
                joined * (passing * held[0] + back_states[m, k, 0:1]),
                joined * (passing * held[1] + back_states[m, k, 1:2]),
            )

        enter_a, enter_b = lax.fori_loop(0, peers - 1 - me, receive_state, (none, none))
        end_segment = segment(base + row_count - 1, starts)

        def back_keys(i, carry):
            rows = span_of(i)
            rising = e1[rows, :]
            chosen = jnp.where(segment(column(i), starts) == end_segment, 1.0, 0.0)
            grown = rising * grow_block
            held = rising * chosen
            d_a = grown * acc[rows, 0:width] + held * enter_a
            d_b = grown * acc[rows, width:] + held * enter_b
            add_vector(5, d_a * sa[m, rows, :] + d_b * sb[m, rows, :])
            weight = jnp.exp(kk[m, rows, :])
            dv[m, rows, :] = (t2[rows, :] + d_a * weight).astype(BF16)
            dk[m, rows, :] = (t1[rows, :] + (d_a * vv[m, rows, :] + d_b) * weight).astype(BF16)
            return carry

        lax.fori_loop(0, chunks, back_keys, 0)
        t1[...] = dot_nt(dk[m], wk[...])
        t2[...] = dot_nt(dv[m], wv[...])
        acc[:, 0:width] = dot_nt(dg[m], wg[...])

        def first_earlier(rows, position):
            whole = (
                t1[rows, :] * (1.0 - mix_k[...])
                + t2[rows, :] * (1.0 - mix_v[...])
                + acc[rows, 0:width] * (1.0 - mix_g[...])
            )
            return whole * keep_of(position, starts)

        send_de1[m] = first_earlier(pl.ds(0, 8), base + eight)

        @pl.when(has_left)
        def _():
            first_copy(m).start()

        def back_first(i, last, following):
            rows = span_of(i)
            spare, spread = normalise(xs[m, rows, :].astype(F32))
            normed = spare * gain1[...] + bias1[...]
            kept = keep_of(column(i), starts)
            gap = normed - moved_down(normed, last) * kept
            from_k = t1[rows, :]
            from_v = t2[rows, :]
            from_g = acc[rows, 0:width]
            add_vector(2, from_k * gap)
            add_vector(3, from_v * gap)
            add_vector(4, from_g * gap)
            straight = from_k * mix_k[...] + from_v * mix_v[...] + from_g * mix_g[...]
            earlier = (from_k + from_v + from_g - straight) * kept
            d_normed = straight + moved_up(earlier, following)
            add_vector(0, d_normed * spare)
            add_vector(1, d_normed)
            scaled = d_normed * gain1[...]
            mean_one = jnp.mean(scaled, axis=-1, keepdims=True)
            mean_two = jnp.mean(scaled * spare, axis=-1, keepdims=True)
            found = t3[rows, :] + spread * (scaled - mean_one - spare * mean_two)
            back[m, rows, :] = found.astype(BF16)
            return normed[RB - 1 : RB]

        def following_first(i):
            start = pl.multiple_of((i + 1) * RB, RB)
            return first_earlier(pl.ds(start, 8), base + start + eight)[0:1]

        last = lax.fori_loop(
            0, chunks - 1,
            lambda i, last: back_first(i, last, following_first(i)),
            halo1[m, 7:8],
        )

        @pl.when(has_right)
        def _():
            first_copy(m).wait_recv()

        back_first(chunks - 1, last, de1[m, 0:1])

        @pl.when(has_prior)
        def _():
            back_copy(m).start()

        return carry

    lax.fori_loop(0, batches, backward, 0)

    vgs[...] = jnp.sum(vg[...], axis=1)
    vgs[5:6] = vgs[5:6] * (-rate * jnp.exp(-rate))
    share = vgr.shape[2]

    def part(k):
        if split_vectors:
            return vgs.at[:, pl.ds(pl.multiple_of(k * share, share), share)]
        return vgs

    def vector_copy(k, slot):
        return remote(part(k), vgr.at[slot], s_vg.at[k], r_vg.at[slot], me_s, k)

    def each_peer(action):
        def turn(k, carry):
            @pl.when(k != me)
            def _():
                action(k)

            return carry

        lax.fori_loop(0, peers, turn, 0)

    each_peer(lambda k: vector_copy(k, me).start())
    if split_vectors:
        vec_out[...] = vgs[:, pl.ds(pl.multiple_of(me * share, share), share)]
    else:
        vec_out[...] = vgs[...]

    def collect(k):
        vector_copy(k, k).wait_recv()
        vec_out[...] += vgr[k]

    each_peer(collect)

    each_peer(lambda k: vector_copy(k, me).wait_send())

    def close(m, carry):
        @pl.when((me_s == 0) & has_right)
        def _():
            start_halo(m).wait_send()

        @pl.when(has_next)
        def _():
            result_copy(m).wait_send()

        @pl.when(has_next & has_right)
        def _():
            result_halo(m).wait_send()

        @pl.when(has_right)
        def _():
            middle_halo(m).wait_send()

        @pl.when(has_left)
        def _():
            second_copy(m).wait_send()
            first_copy(m).wait_send()

        @pl.when(has_prior)
        def _():
            back_copy(m).wait_send()

        def ended(k, carry):
            state_copy(m, k, me).wait_send()
            return carry

        lax.fori_loop(me + 1, peers, ended, 0)

        def ended_back(k, carry):
            back_state_copy(m, k, me).wait_send()
            return carry

        lax.fori_loop(0, me, ended_back, 0)
        return carry

    lax.fori_loop(0, batches, close, 0)


def relay(sections, peers, x, top, spans, vectors, matrices):
    batches, rows, width = x.shape
    hidden = matrices[4].shape[1]
    share = width // peers
    split_vectors = share % 128 == 0
    if not split_vectors:
        share = width
    shape = jax.ShapeDtypeStruct
    low = shape((batches, rows, width), BF16)
    low_wide = shape((batches, rows, hidden), BF16)
    vmem = pl.BlockSpec(memory_space=pltpu.VMEM)
    anywhere = pl.BlockSpec(memory_space=pl.ANY)
    dma = pltpu.SemaphoreType.DMA

    def narrow(kind):
        return pltpu.VMEM((batches, rows, width), kind)

    return pl.pallas_call(
        partial(relay_kernel, sections, peers, split_vectors),
        out_shape=(
            low, low, shape((VECTORS, share), F32),
            low, low, low, low, low, low, low_wide,
            low, low, low, low, low, low, low_wide,
        ),
        in_specs=[pl.BlockSpec(memory_space=pltpu.SMEM), anywhere, anywhere]
        + [vmem] * 11
        + [anywhere] * 7,
        out_specs=[vmem] * 17,
        scratch_shapes=[pltpu.VMEM(matrix.shape, BF16) for matrix in matrices_order(matrices)]
        + [
            narrow(BF16), pltpu.VMEM((batches, 16, width), BF16), narrow(BF16),
            narrow(F32), narrow(F32), narrow(F32), narrow(F32), narrow(F32), narrow(F32),
            pltpu.VMEM((batches, 8, width), F32), narrow(F32), narrow(F32),
            pltpu.VMEM((batches, rows, hidden), BF16),
            pltpu.VMEM((batches, 8, width), F32), pltpu.VMEM((batches, 8, width), F32),
            pltpu.VMEM((rows, width), F32), pltpu.VMEM((rows, width), F32),
            pltpu.VMEM((batches, rows, 2 * rows), BF16), pltpu.VMEM((batches, rows, 2 * rows), BF16),
            pltpu.VMEM((2 * rows, 2 * width), BF16), pltpu.VMEM((rows, 2 * width), F32),
            pltpu.VMEM((rows, width), F32), pltpu.VMEM((rows, width), F32), pltpu.VMEM((rows, width), F32),
            pltpu.VMEM((batches, peers, 2, width), F32), pltpu.VMEM((batches, peers, 2, width), F32),
            pltpu.VMEM((batches, 8, width), F32), pltpu.VMEM((batches, 8, width), F32),
            pltpu.VMEM((batches, 2, width), F32), pltpu.VMEM((batches, 2, width), F32),
            pltpu.VMEM((batches, 8, width), F32), pltpu.VMEM((batches, 8, width), F32),
            pltpu.VMEM((VECTORS, 8, width), F32), pltpu.VMEM((VECTORS, width), F32),
            pltpu.VMEM((peers, VECTORS, share), F32),
            dma((7,)), dma, dma,
            dma((batches,)), dma((batches,)), dma((batches,)), dma((batches, peers)), dma((batches,)),
            dma((batches,)), dma((batches,)), dma((batches, peers)), dma((batches,)), dma((peers,)),
            dma((batches,)), dma((batches,)), dma((batches, peers)), dma((batches,)),
            dma((batches,)), dma((batches,)), dma((batches, peers)), dma((batches,)), dma((peers,)),
        ],
        compiler_params=pltpu.CompilerParams(
            collective_id=0, has_side_effects=True, vmem_limit_bytes=63 * 2**20
        ),
        name="relay",
    )(spans, x, top, *vectors, *matrices_order(matrices))


def matrices_order(matrices):
    wk, wv, wg, wo, wh, wp, wf = matrices
    return (wk, wv, wg, wo, wh, wp, wf)


def per_device(x, top, spans, *parameters):
    sections = lax.axis_size("section")
    peers = lax.axis_size("dp")
    gain1, bias1, mix_k, mix_v, mix_g, log_rate, extra = parameters[0:7]
    wk, wv, wg, wo = parameters[7:11]
    gain2, bias2, mix_h, mix_f = parameters[11:15]
    wh, wp, wf = parameters[15:18]
    vectors = (gain1, bias1, mix_k, mix_v, mix_g, log_rate, extra, gain2, bias2, mix_h, mix_f)
    matrices = tuple(w[0] for w in (wk, wv, wg, wo, wh, wp, wf))
    found = relay(sections, peers, x, top, spans, vectors, matrices)
    out, back, vec = found[0:3]
    lk, lv, lg, lgt, lh, lf, sq = found[3:10]
    dk, dv, dg, datt, dproj, dsv, dh = found[10:17]
    share = x.shape[2] // peers
    if vec.shape[1] != share:
        vec = lax.dynamic_slice_in_dim(vec, lax.axis_index("dp") * share, share, 1)

    def weight_grad(left, right):
        local = lax.dot_general(
            left, right, (((0, 1), (0, 1)), ((), ())), preferred_element_type=F32
        )
        whole = lax.psum_scatter(local.astype(BF16), "dp", scatter_dimension=0, tiled=True)
        return whole.astype(F32)[None]

    def row(index):
        return vec[index : index + 1]

    return (
        out[None], back[None],
        row(0), row(1), row(2), row(3), row(4), row(5), row(6),
        weight_grad(lk, dk), weight_grad(lv, dv), weight_grad(lg, dg), weight_grad(lgt, datt),
        row(7), row(8), row(9), row(10),
        weight_grad(lh, dh), weight_grad(sq, dproj), weight_grad(lf, dsv),
    )


def solution(mesh):
    tokens = P(None, "dp", None)
    vector = P("section", None)
    matrix = P("section", None, None)
    result = P("section", None, "dp", None)
    vector_grad = P("section", "dp")
    matrix_grad = P("section", "dp", None)
    return jax.shard_map(
        per_device,
        mesh=mesh,
        in_specs=(tokens, tokens, P())
        + (vector,) * 7 + (matrix,) * 4 + (vector,) * 4 + (matrix,) * 3,
        out_specs=(result, result)
        + (vector_grad,) * 7 + (matrix_grad,) * 4 + (vector_grad,) * 4 + (matrix_grad,) * 3,
        check_vma=False,
    )
```

```python
from functools import partial

import jax
import jax.numpy as jnp
from jax import lax
from jax.experimental import pallas as pl
from jax.experimental.pallas import tpu as pltpu
from jax.sharding import PartitionSpec as P

EPS = 1e-05
MESH = pl.DeviceIdType.MESH
RB = 32
VECTORS = 16
F32 = jnp.float32
BF16 = jnp.bfloat16


def dot_nn(left, right):
    return jnp.dot(left, right, preferred_element_type=F32)


def dot_nt(left, right):
    return lax.dot_general(left, right, (((1,), (1,)), ((), ())), preferred_element_type=F32)


def dot_tn(left, right):
    return lax.dot_general(left, right, (((0,), (0,)), ((), ())), preferred_element_type=F32)


def sigmoid(v):
    return 1.0 / (1.0 + jnp.exp(-v))


def normalise(source):
    centred = source - jnp.mean(source, axis=-1, keepdims=True)
    spread = lax.rsqrt(jnp.mean(centred * centred, axis=-1, keepdims=True) + EPS)
    return centred * spread, spread


def moved_down(rows, first):
    place = lax.broadcasted_iota(jnp.int32, rows.shape, 0)
    return jnp.where(place == 0, first, pltpu.roll(rows, 1, 0))


def moved_up(rows, last):
    count = rows.shape[0]
    place = lax.broadcasted_iota(jnp.int32, rows.shape, 0)
    return jnp.where(place == count - 1, last, pltpu.roll(rows, count - 1, 0))


def fold(rows):
    total = rows[0:8]
    for at in range(8, rows.shape[0], 8):
        total = total + rows[at : at + 8]
    return total


def relay_kernel(sections, peers, split_vectors, *refs):
    (
        spans, x_in, top_in,
        gain1, bias1, mix_k, mix_v, mix_g, log_rate, extra, gain2, bias2, mix_h, mix_f,
        wk_in, wv_in, wg_in, wo_in, wh_in, wp_in, wf_in,
        out, back, vec_out, lk, lv, lg, lgt, lf, dk, dv, dg, datt, dsv, lh_all, dproj_all,
        lh, sq, dproj, dh,
        wk, wv, wg, wo, wh, wp, wf,
        xs, hx, dys, kk, vv, sg, sa, sb, mid, hmid, proj, sv, act, halo1, halo2,
        e0, e1, low_mask, up_mask, split, acc, t1, t2, t3,
        states, back_states, de2, de1, sum_row, sum_back, send_de2, send_de1, vg, vgs, vgr,
        w_sem, x_sem, top_sem, s_h0, s_x, s_hx, s_st, s_mid, s_dy, s_de2, s_bst, s_de1, s_vg,
        r_x, r_hx, r_st, r_mid, r_dy, r_de2, r_bst, r_de1, r_vg,
        s_lh, r_lh, s_dp, r_dp, own_sem,
    ) = refs
    me_s = lax.axis_index("section")
    me = lax.axis_index("dp")
    batches, row_count, width = x_in.shape
    hidden = wh.shape[1]
    chunks = row_count // RB
    base = me * row_count

    def at(section, index):
        return (section, index)

    barrier = pltpu.get_barrier_semaphore()

    def greet(section, index):
        pl.semaphore_signal(barrier, inc=1, device_id=at(section, index), device_id_type=MESH)

    def greet_peer(k, carry):
        @pl.when(k != me)
        def _():
            greet(me_s, k)

        return carry

    lax.fori_loop(0, peers, greet_peer, 0)
    has_next = me_s + 1 < sections
    has_prior = me_s > 0
    has_right = me + 1 < peers
    has_left = me > 0

    @pl.when(has_next)
    def _():
        greet(me_s + 1, me)

    @pl.when(has_prior)
    def _():
        greet(me_s - 1, me)

    @pl.when(has_next & has_right)
    def _():
        greet(me_s + 1, me + 1)

    @pl.when(has_prior & has_left)
    def _():
        greet(me_s - 1, me - 1)

    weight_copies = [
        pltpu.make_async_copy(source, target, w_sem.at[index])
        for index, (source, target) in enumerate(
            ((wk_in, wk), (wv_in, wv), (wg_in, wg), (wo_in, wo), (wf_in, wf), (wh_in, wh), (wp_in, wp))
        )
    ]

    @pl.when(me_s == 0)
    def _():
        pltpu.make_async_copy(x_in, xs, x_sem).start()

    for copy in weight_copies:
        copy.start()

    @pl.when(me_s == sections - 1)
    def _():
        pltpu.make_async_copy(top_in, dys, top_sem).start()

    rate = jnp.exp(log_rate[...])
    decay_block = jnp.exp(-rate * row_count)
    grow_block = jnp.exp(rate * row_count)

    def starts_of(m):
        found = []
        total = jnp.int32(0)
        for j in range(spans.shape[1]):
            found.append(total)
            total = total + spans[m, j]
        return found

    def segment(position, starts):
        total = jnp.where(position >= starts[0], 1, 0)
        for start in starts[1:]:
            total = total + jnp.where(position >= start, 1, 0)
        return total

    def column(i):
        return base + i * RB + lax.broadcasted_iota(jnp.int32, (RB, 1), 0)

    def keep_of(position, starts):
        return jnp.where(segment(position, starts) == segment(position - 1, starts), 1.0, 0.0)

    def fill_powers(i, carry):
        place = (i * RB + lax.broadcasted_iota(jnp.int32, (RB, width), 0)).astype(F32)
        e0[pl.ds(pl.multiple_of(i * RB, RB), RB), :] = jnp.exp(-place * rate)
        e1[pl.ds(pl.multiple_of(i * RB, RB), RB), :] = jnp.exp((place - (row_count - 1.0)) * rate)
        return carry

    lax.fori_loop(0, chunks, fill_powers, 0)
    for m in range(batches):
        starts = starts_of(m)
        row_at = lax.broadcasted_iota(jnp.int32, (row_count, row_count), 0)
        column_at = lax.broadcasted_iota(jnp.int32, (row_count, row_count), 1)
        same = segment(base + row_at, starts) == segment(base + column_at, starts)
        lower = jnp.where(same & (column_at < row_at), 1.0, 0.0).astype(BF16)
        upper = jnp.where(same & (column_at > row_at), 1.0, 0.0).astype(BF16)
        low_mask[m, :, 0:row_count] = lower
        low_mask[m, :, row_count:] = lower
        up_mask[m, :, 0:row_count] = upper
        up_mask[m, :, row_count:] = upper
    vg[...] = jnp.zeros_like(vg)

    @pl.when(me == 0)
    def _():
        hx[...] = jnp.zeros_like(hx)
        hmid[...] = jnp.zeros_like(hmid)

    @pl.when(me == peers - 1)
    def _():
        de1[...] = jnp.zeros_like(de1)
        de2[...] = jnp.zeros_like(de2)

    greeted = (
        peers - 1
        + jnp.where(has_next, 1, 0)
        + jnp.where(has_prior, 1, 0)
        + jnp.where(has_next & has_right, 1, 0)
        + jnp.where(has_prior & has_left, 1, 0)
    )
    pl.semaphore_wait(barrier, greeted)

    def remote(source, target, send, receive, section, index):
        return pltpu.make_async_remote_copy(
            src_ref=source, dst_ref=target, send_sem=send, recv_sem=receive,
            device_id=at(section, index), device_id_type=MESH,
        )

    right = jnp.minimum(me + 1, peers - 1)
    left = jnp.maximum(me - 1, 0)
    above = jnp.minimum(me_s + 1, sections - 1)
    below = jnp.maximum(me_s - 1, 0)
    tail = pl.ds(row_count - 16, 16)
    tail8 = pl.ds(row_count - 8, 8)

    def start_halo(m):
        return remote(x_in.at[m, tail], hx.at[m], s_h0.at[m], r_hx.at[m], me_s, right)

    def result_copy(m):
        return remote(out.at[m], xs.at[m], s_x.at[m], r_x.at[m], above, me)

    def result_halo(m):
        return remote(out.at[m, tail], hx.at[m], s_hx.at[m], r_hx.at[m], above, right)

    def middle_halo(m):
        return remote(mid.at[m, tail8], hmid.at[m], s_mid.at[m], r_mid.at[m], me_s, right)

    def state_copy(m, k, slot):
        return remote(sum_row.at[m], states.at[m, slot], s_st.at[m, k], r_st.at[m, slot], me_s, k)

    def back_copy(m):
        return remote(back.at[m], dys.at[m], s_dy.at[m], r_dy.at[m], below, me)

    def second_copy(m):
        return remote(send_de2.at[m], de2.at[m], s_de2.at[m], r_de2.at[m], me_s, left)

    def first_copy(m):
        return remote(send_de1.at[m], de1.at[m], s_de1.at[m], r_de1.at[m], me_s, left)

    def back_state_copy(m, k, slot):
        return remote(
            sum_back.at[m], back_states.at[m, slot], s_bst.at[m, k], r_bst.at[m, slot], me_s, k
        )

    chip, core = me // 2, me % 2
    chips = peers // 2

    def gather_copy(which, m, k, slot):
        source, target, send, receive = (
            (lh, lh_all, s_lh, r_lh) if which == 0 else (dproj, dproj_all, s_dp, r_dp)
        )
        return remote(
            source.at[m], target.at[m, slot], send.at[m, k], receive.at[m, slot],
            me_s, 2 * k + core,
        )

    def own_copy(which, m):
        source, target = (lh, lh_all) if which == 0 else (dproj, dproj_all)
        return pltpu.make_async_copy(source.at[m], target.at[m, chip], own_sem.at[which, m])

    def each_chip(action):
        def turn(k, carry):
            @pl.when(k != chip)
            def _():
                action(k)

            return carry

        lax.fori_loop(0, chips, turn, 0)

    def start_gather(which, m):
        own_copy(which, m).start()
        each_chip(lambda k: gather_copy(which, m, k, chip).start())

    def end_gather(which, m):
        own_copy(which, m).wait()
        each_chip(lambda k: gather_copy(which, m, k, chip).wait_send())
        each_chip(lambda k: gather_copy(which, m, k, k).wait_recv())

    @pl.when((me_s == 0) & has_right)
    def _():
        for m in range(batches):
            start_halo(m).start()

    @pl.when(me_s == 0)
    def _():
        pltpu.make_async_copy(x_in, xs, x_sem).wait()

    def span_of(i):
        return pl.ds(pl.multiple_of(i * RB, RB), RB)

    def forward(m, carry):
        starts = starts_of(m)

        @pl.when(has_prior)
        def _():
            result_copy(m).wait_recv()

        @pl.when(has_left)
        def _():
            start_halo(m).wait_recv()

        halo_rows, _ = normalise(hx[m].astype(F32))
        halo_rows = halo_rows * gain1[...] + bias1[...]
        halo1[m] = halo_rows[8:16]

        def mix_in(i, last):
            rows = span_of(i)
            normed, _ = normalise(xs[m, rows, :].astype(F32))
            normed = normed * gain1[...] + bias1[...]
            earlier = moved_down(normed, last) * keep_of(column(i), starts)
            gap = normed - earlier
            lk[m, rows, :] = (earlier + gap * mix_k[...]).astype(BF16)
            lv[m, rows, :] = (earlier + gap * mix_v[...]).astype(BF16)
            lg[m, rows, :] = (earlier + gap * mix_g[...]).astype(BF16)
            return normed[RB - 1 : RB]

        lax.fori_loop(0, chunks, mix_in, halo_rows[15:16])

        @pl.when(m == 0)
        def _():
            for copy in weight_copies[0:2]:
                copy.wait()

        kk[m] = dot_nn(lk[m], wk[...])
        vv[m] = dot_nn(lv[m], wv[...])
        end_segment = segment(base + row_count - 1, starts)

        def spread_in(i, totals):
            rows = span_of(i)
            weight = jnp.exp(kk[m, rows, :]) * e1[rows, :]
            weighted = weight * vv[m, rows, :]
            high_a = weighted.astype(BF16)
            high_b = weight.astype(BF16)
            split[rows, 0:width] = high_a
            split[rows, width:] = high_b
            low = pl.ds(pl.multiple_of(row_count + i * RB, RB), RB)
            split[low, 0:width] = (weighted - high_a.astype(F32)).astype(BF16)
            split[low, width:] = (weight - high_b.astype(F32)).astype(BF16)
            chosen = segment(column(i), starts) == end_segment
            return (
                totals[0] + fold(jnp.where(chosen, weighted, 0.0)),
                totals[1] + fold(jnp.where(chosen, weight, 0.0)),
            )

        nothing = jnp.zeros((8, width), F32)
        total_a, total_b = lax.fori_loop(0, chunks, spread_in, (nothing, nothing))
        sum_row[m, 0:1] = jnp.sum(total_a, axis=0, keepdims=True)
        sum_row[m, 1:2] = jnp.sum(total_b, axis=0, keepdims=True)

        def send_state(k, carry):
            state_copy(m, k, me).start()
            return carry

        lax.fori_loop(me + 1, peers, send_state, 0)

        @pl.when(m == 0)
        def _():
            weight_copies[2].wait()

        sg[m] = dot_nn(lg[m], wg[...])
        acc[...] = dot_nn(low_mask[m], split[...])

        def receive_state(k, held):
            state_copy(m, k, k).wait_recv()
            unbroken = segment(k * row_count - 1, starts) == segment(
                (k + 1) * row_count - 1, starts
            )
            passing = jnp.where(unbroken, 1.0, 0.0) * decay_block
            return (
                passing * held[0] + states[m, k, 0:1],
                passing * held[1] + states[m, k, 1:2],
            )

        none = jnp.zeros((1, width), F32)
        enter_a, enter_b = lax.fori_loop(0, me, receive_state, (none, none))
        prior_segment = segment(base - 1, starts)

        def mix_states(i, carry):
            rows = span_of(i)
            falling = e0[rows, :]
            chosen = jnp.where(segment(column(i), starts) == prior_segment, 1.0, 0.0)
            grown = falling * grow_block
            held = falling * chosen
            state_a = grown * acc[rows, 0:width] + held * enter_a
            state_b = grown * acc[rows, width:] + held * enter_b
            sa[m, rows, :] = state_a
            sb[m, rows, :] = state_b
            present = jnp.exp(extra[...] + kk[m, rows, :])
            gate = sigmoid(sg[m, rows, :])
            sg[m, rows, :] = gate
            found = (state_a + present * vv[m, rows, :]) / (state_b + present)
            lgt[m, rows, :] = (gate * found).astype(BF16)
            return carry

        lax.fori_loop(0, chunks, mix_states, 0)

        @pl.when(m == 0)
        def _():
            weight_copies[3].wait()

        mid[m] = xs[m].astype(F32) + dot_nn(lgt[m], wo[...])

        @pl.when(has_right)
        def _():
            middle_halo(m).start()

        def mix_second(i, last):
            rows = span_of(i)
            normed, _ = normalise(mid[m, rows, :])
            normed = normed * gain2[...] + bias2[...]
            earlier = moved_down(normed, last) * keep_of(column(i), starts)
            gap = normed - earlier
            lh[m, rows, :] = (earlier + gap * mix_h[...]).astype(BF16)
            lf[m, rows, :] = (earlier + gap * mix_f[...]).astype(BF16)
            return normed[RB - 1 : RB]

        lax.fori_loop(0, chunks, mix_second, none)

        @pl.when(has_left)
        def _():
            middle_halo(m).wait_recv()

        halo_rows, _ = normalise(hmid[m])
        halo_rows = halo_rows * gain2[...] + bias2[...]
        halo2[m] = halo_rows
        mix_second(0, halo_rows[7:8])
        start_gather(0, m)

        @pl.when(m == 0)
        def _():
            for copy in weight_copies[4:7]:
                copy.wait()

        sv[m] = dot_nn(lf[m], wf[...])

        def widen(j, carry):
            columns = pl.ds(pl.multiple_of(j * width, width), width)
            active = jnp.maximum(dot_nn(lh[m], wh[:, columns]), 0.0)
            act[m, :, columns] = active.astype(BF16)
            sq[m, :, columns] = (active * active).astype(BF16)
            return carry

        lax.fori_loop(0, hidden // width, widen, 0)
        proj[m] = dot_nn(sq[m], wp[...])

        def finish(i, carry):
            rows = span_of(i)
            sieve = sigmoid(sv[m, rows, :])
            sv[m, rows, :] = sieve
            out[m, rows, :] = (mid[m, rows, :] + sieve * proj[m, rows, :]).astype(BF16)
            return carry

        lax.fori_loop(0, chunks, finish, 0)

        @pl.when(has_next)
        def _():
            result_copy(m).start()

        @pl.when(has_next & has_right)
        def _():
            result_halo(m).start()

        return carry

    lax.fori_loop(0, batches, forward, 0)

    def add_vector(index, value):
        vg[index] += fold(value)

    @pl.when(me_s == sections - 1)
    def _():
        pltpu.make_async_copy(top_in, dys, top_sem).wait()

    def backward(m, carry):
        starts = starts_of(m)
        none = jnp.zeros((1, width), F32)

        @pl.when(has_next)
        def _():
            back_copy(m).wait_recv()

        def open_back(i, carry):
            rows = span_of(i)
            incoming = dys[m, rows, :].astype(F32)
            sieve = sv[m, rows, :]
            gained = incoming * sieve
            dproj[m, rows, :] = gained.astype(BF16)
            dsv[m, rows, :] = (gained * proj[m, rows, :] * (1.0 - sieve)).astype(BF16)
            return carry

        lax.fori_loop(0, chunks, open_back, 0)
        start_gather(1, m)
        t1[...] = jnp.zeros_like(t1)

        def narrow(j, carry):
            columns = pl.ds(pl.multiple_of(j * width, width), width)
            grown = dot_nt(dproj[m], wp[columns, :])
            dh[m, :, columns] = (grown * 2.0 * act[m, :, columns].astype(F32)).astype(BF16)
            t1[...] += dot_nt(dh[m, :, columns], wh[:, columns])
            return carry

        lax.fori_loop(0, hidden // width, narrow, 0)
        t2[...] = dot_nt(dsv[m], wf[...])

        def second_earlier(rows, position):
            whole = t1[rows, :] * (1.0 - mix_h[...]) + t2[rows, :] * (1.0 - mix_f[...])
            return whole * keep_of(position, starts)

        eight = lax.broadcasted_iota(jnp.int32, (8, 1), 0)
        send_de2[m] = second_earlier(pl.ds(0, 8), base + eight)

        @pl.when(has_left)
        def _():
            second_copy(m).start()

        def back_second(i, last, following):
            rows = span_of(i)
            spare, spread = normalise(mid[m, rows, :])
            normed = spare * gain2[...] + bias2[...]
            kept = keep_of(column(i), starts)
            gap = normed - moved_down(normed, last) * kept
            from_h = t1[rows, :]
            from_f = t2[rows, :]
            add_vector(9, from_h * gap)
            add_vector(10, from_f * gap)
            straight = from_h * mix_h[...] + from_f * mix_f[...]
            earlier = (from_h + from_f - straight) * kept
            d_normed = straight + moved_up(earlier, following)
            add_vector(7, d_normed * spare)
            add_vector(8, d_normed)
            scaled = d_normed * gain2[...]
            mean_one = jnp.mean(scaled, axis=-1, keepdims=True)
            mean_two = jnp.mean(scaled * spare, axis=-1, keepdims=True)
            d_mid = dys[m, rows, :].astype(F32) + spread * (scaled - mean_one - spare * mean_two)
            t3[rows, :] = d_mid
            datt[m, rows, :] = d_mid.astype(BF16)
            return normed[RB - 1 : RB]

        def following_second(i):
            start = pl.multiple_of((i + 1) * RB, RB)
            return second_earlier(pl.ds(start, 8), base + start + eight)[0:1]

        last = lax.fori_loop(
            0, chunks - 1,
            lambda i, last: back_second(i, last, following_second(i)),
            halo2[m, 7:8],
        )

        @pl.when(has_right)
        def _():
            second_copy(m).wait_recv()

        back_second(chunks - 1, last, de2[m, 0:1])
        t1[...] = dot_nt(datt[m], wo[...])
        open_segment = segment(base, starts)

        def back_states_in(i, totals):
            rows = span_of(i)
            d_gated = t1[rows, :]
            gate = sg[m, rows, :]
            keys = kk[m, rows, :]
            values = vv[m, rows, :]
            present = jnp.exp(extra[...] + keys)
            inverse = 1.0 / (sb[m, rows, :] + present)
            found = (sa[m, rows, :] + present * values) * inverse
            d_found = d_gated * gate
            dg[m, rows, :] = (d_found * found * (1.0 - gate)).astype(BF16)
            d_a = d_found * inverse
            d_b = -d_a * found
            d_key = (d_a * values + d_b) * present
            add_vector(6, d_key)
            t1[rows, :] = d_key
            t2[rows, :] = d_a * present
            falling = e0[rows, :]
            scaled_a = d_a * falling
            scaled_b = d_b * falling
            high_a = scaled_a.astype(BF16)
            high_b = scaled_b.astype(BF16)
            split[rows, 0:width] = high_a
            split[rows, width:] = high_b
            low = pl.ds(pl.multiple_of(row_count + i * RB, RB), RB)
            split[low, 0:width] = (scaled_a - high_a.astype(F32)).astype(BF16)
            split[low, width:] = (scaled_b - high_b.astype(F32)).astype(BF16)
            chosen = segment(column(i), starts) == open_segment
            return (
                totals[0] + fold(jnp.where(chosen, scaled_a, 0.0)),
                totals[1] + fold(jnp.where(chosen, scaled_b, 0.0)),
            )

        nothing = jnp.zeros((8, width), F32)
        total_a, total_b = lax.fori_loop(0, chunks, back_states_in, (nothing, nothing))
        sum_back[m, 0:1] = jnp.sum(total_a, axis=0, keepdims=True)
        sum_back[m, 1:2] = jnp.sum(total_b, axis=0, keepdims=True)

        def send_state(k, carry):
            back_state_copy(m, k, me).start()
            return carry

        lax.fori_loop(0, me, send_state, 0)
        acc[...] = dot_nn(up_mask[m], split[...])

        def receive_state(turn, held):
            k = peers - 1 - turn
            back_state_copy(m, k, k).wait_recv()
            first = segment(k * row_count, starts)
            unbroken = first == segment((k + 1) * row_count - 1, starts)
            joined = jnp.where(first == segment(k * row_count - 1, starts), 1.0, 0.0)
            passing = jnp.where(unbroken, 1.0, 0.0) * decay_block
            return (
                joined * (passing * held[0] + back_states[m, k, 0:1]),
                joined * (passing * held[1] + back_states[m, k, 1:2]),
            )

        enter_a, enter_b = lax.fori_loop(0, peers - 1 - me, receive_state, (none, none))
        end_segment = segment(base + row_count - 1, starts)

        def back_keys(i, carry):
            rows = span_of(i)
            rising = e1[rows, :]
            chosen = jnp.where(segment(column(i), starts) == end_segment, 1.0, 0.0)
            grown = rising * grow_block
            held = rising * chosen
            d_a = grown * acc[rows, 0:width] + held * enter_a
            d_b = grown * acc[rows, width:] + held * enter_b
            add_vector(5, d_a * sa[m, rows, :] + d_b * sb[m, rows, :])
            weight = jnp.exp(kk[m, rows, :])
            dv[m, rows, :] = (t2[rows, :] + d_a * weight).astype(BF16)
            dk[m, rows, :] = (t1[rows, :] + (d_a * vv[m, rows, :] + d_b) * weight).astype(BF16)
            return carry

        lax.fori_loop(0, chunks, back_keys, 0)
        t1[...] = dot_nt(dk[m], wk[...])
        t2[...] = dot_nt(dv[m], wv[...])
        acc[:, 0:width] = dot_nt(dg[m], wg[...])

        def first_earlier(rows, position):
            whole = (
                t1[rows, :] * (1.0 - mix_k[...])
                + t2[rows, :] * (1.0 - mix_v[...])
                + acc[rows, 0:width] * (1.0 - mix_g[...])
            )
            return whole * keep_of(position, starts)

        send_de1[m] = first_earlier(pl.ds(0, 8), base + eight)

        @pl.when(has_left)
        def _():
            first_copy(m).start()

        def back_first(i, last, following):
            rows = span_of(i)
            spare, spread = normalise(xs[m, rows, :].astype(F32))
            normed = spare * gain1[...] + bias1[...]
            kept = keep_of(column(i), starts)
            gap = normed - moved_down(normed, last) * kept
            from_k = t1[rows, :]
            from_v = t2[rows, :]
            from_g = acc[rows, 0:width]
            add_vector(2, from_k * gap)
            add_vector(3, from_v * gap)
            add_vector(4, from_g * gap)
            straight = from_k * mix_k[...] + from_v * mix_v[...] + from_g * mix_g[...]
            earlier = (from_k + from_v + from_g - straight) * kept
            d_normed = straight + moved_up(earlier, following)
            add_vector(0, d_normed * spare)
            add_vector(1, d_normed)
            scaled = d_normed * gain1[...]
            mean_one = jnp.mean(scaled, axis=-1, keepdims=True)
            mean_two = jnp.mean(scaled * spare, axis=-1, keepdims=True)
            found = t3[rows, :] + spread * (scaled - mean_one - spare * mean_two)
            back[m, rows, :] = found.astype(BF16)
            return normed[RB - 1 : RB]

        def following_first(i):
            start = pl.multiple_of((i + 1) * RB, RB)
            return first_earlier(pl.ds(start, 8), base + start + eight)[0:1]

        last = lax.fori_loop(
            0, chunks - 1,
            lambda i, last: back_first(i, last, following_first(i)),
            halo1[m, 7:8],
        )

        @pl.when(has_right)
        def _():
            first_copy(m).wait_recv()

        back_first(chunks - 1, last, de1[m, 0:1])

        @pl.when(has_prior)
        def _():
            back_copy(m).start()

        return carry

    lax.fori_loop(0, batches, backward, 0)

    vgs[...] = jnp.sum(vg[...], axis=1)
    vgs[5:6] = vgs[5:6] * (-rate * jnp.exp(-rate))
    share = vgr.shape[2]

    def part(k):
        if split_vectors:
            return vgs.at[:, pl.ds(pl.multiple_of(k * share, share), share)]
        return vgs

    def vector_copy(k, slot):
        return remote(part(k), vgr.at[slot], s_vg.at[k], r_vg.at[slot], me_s, k)

    def each_peer(action):
        def turn(k, carry):
            @pl.when(k != me)
            def _():
                action(k)

            return carry

        lax.fori_loop(0, peers, turn, 0)

    each_peer(lambda k: vector_copy(k, me).start())
    if split_vectors:
        vec_out[...] = vgs[:, pl.ds(pl.multiple_of(me * share, share), share)]
    else:
        vec_out[...] = vgs[...]

    def collect(k):
        vector_copy(k, k).wait_recv()
        vec_out[...] += vgr[k]

    each_peer(collect)

    each_peer(lambda k: vector_copy(k, me).wait_send())

    def close(m, carry):
        @pl.when((me_s == 0) & has_right)
        def _():
            start_halo(m).wait_send()

        @pl.when(has_next)
        def _():
            result_copy(m).wait_send()

        @pl.when(has_next & has_right)
        def _():
            result_halo(m).wait_send()

        @pl.when(has_right)
        def _():
            middle_halo(m).wait_send()

        @pl.when(has_left)
        def _():
            second_copy(m).wait_send()
            first_copy(m).wait_send()

        @pl.when(has_prior)
        def _():
            back_copy(m).wait_send()

        def ended(k, carry):
            state_copy(m, k, me).wait_send()
            return carry

        lax.fori_loop(me + 1, peers, ended, 0)
        end_gather(0, m)
        end_gather(1, m)

        def ended_back(k, carry):
            back_state_copy(m, k, me).wait_send()
            return carry

        lax.fori_loop(0, me, ended_back, 0)
        return carry

    lax.fori_loop(0, batches, close, 0)


def relay(sections, peers, x, top, spans, vectors, matrices):
    batches, rows, width = x.shape
    hidden = matrices[4].shape[1]
    share = width // peers
    split_vectors = share % 128 == 0
    if not split_vectors:
        share = width
    shape = jax.ShapeDtypeStruct
    low = shape((batches, rows, width), BF16)
    vmem = pl.BlockSpec(memory_space=pltpu.VMEM)
    anywhere = pl.BlockSpec(memory_space=pl.ANY)
    dma = pltpu.SemaphoreType.DMA

    def narrow(kind):
        return pltpu.VMEM((batches, rows, width), kind)

    return pl.pallas_call(
        partial(relay_kernel, sections, peers, split_vectors),
        out_shape=(
            low, low, shape((VECTORS, share), F32),
            low, low, low, low, low,
            low, low, low, low, low,
            shape((batches, peers // 2, rows, width), BF16),
            shape((batches, peers // 2, rows, width), BF16),
        ),
        in_specs=[pl.BlockSpec(memory_space=pltpu.SMEM), anywhere, anywhere]
        + [vmem] * 11
        + [anywhere] * 7,
        out_specs=[vmem] * 13 + [anywhere] * 2,
        scratch_shapes=[
            narrow(BF16), pltpu.VMEM((batches, rows, hidden), BF16),
            narrow(BF16), pltpu.VMEM((batches, rows, hidden), BF16),
        ]
        + [pltpu.VMEM(matrix.shape, BF16) for matrix in matrices_order(matrices)]
        + [
            narrow(BF16), pltpu.VMEM((batches, 16, width), BF16), narrow(BF16),
            narrow(F32), narrow(F32), narrow(F32), narrow(F32), narrow(F32), narrow(F32),
            pltpu.VMEM((batches, 8, width), F32), narrow(F32), narrow(F32),
            pltpu.VMEM((batches, rows, hidden), BF16),
            pltpu.VMEM((batches, 8, width), F32), pltpu.VMEM((batches, 8, width), F32),
            pltpu.VMEM((rows, width), F32), pltpu.VMEM((rows, width), F32),
            pltpu.VMEM((batches, rows, 2 * rows), BF16), pltpu.VMEM((batches, rows, 2 * rows), BF16),
            pltpu.VMEM((2 * rows, 2 * width), BF16), pltpu.VMEM((rows, 2 * width), F32),
            pltpu.VMEM((rows, width), F32), pltpu.VMEM((rows, width), F32), pltpu.VMEM((rows, width), F32),
            pltpu.VMEM((batches, peers, 2, width), F32), pltpu.VMEM((batches, peers, 2, width), F32),
            pltpu.VMEM((batches, 8, width), F32), pltpu.VMEM((batches, 8, width), F32),
            pltpu.VMEM((batches, 2, width), F32), pltpu.VMEM((batches, 2, width), F32),
            pltpu.VMEM((batches, 8, width), F32), pltpu.VMEM((batches, 8, width), F32),
            pltpu.VMEM((VECTORS, 8, width), F32), pltpu.VMEM((VECTORS, width), F32),
            pltpu.VMEM((peers, VECTORS, share), F32),
            dma((7,)), dma, dma,
            dma((batches,)), dma((batches,)), dma((batches,)), dma((batches, peers)), dma((batches,)),
            dma((batches,)), dma((batches,)), dma((batches, peers)), dma((batches,)), dma((peers,)),
            dma((batches,)), dma((batches,)), dma((batches, peers)), dma((batches,)),
            dma((batches,)), dma((batches,)), dma((batches, peers)), dma((batches,)), dma((peers,)),
            dma((batches, peers // 2)), dma((batches, peers // 2)),
            dma((batches, peers // 2)), dma((batches, peers // 2)), dma((2, batches)),
        ],
        compiler_params=pltpu.CompilerParams(
            collective_id=0, has_side_effects=True, vmem_limit_bytes=63 * 2**20
        ),
        name="relay",
    )(spans, x, top, *vectors, *matrices_order(matrices))


def matrices_order(matrices):
    wk, wv, wg, wo, wh, wp, wf = matrices
    return (wk, wv, wg, wo, wh, wp, wf)


def sum_kernel(peers, *refs):
    left_in, right_in = refs[0:5], refs[5:10]
    lh_in, dp_in, wh_in, wp_in = refs[10:14]
    outs, wh_out, wp_out = refs[14:19], refs[19], refs[20]
    (
        lefts, rights, whole, own, pair_out, going_right, going_left,
        lh, dp, wh, wp, act, wide, hid_out, hid_in, proj_out, proj_in,
        left_sem, right_sem, lh_sem, dp_sem, wh_sem, wp_sem,
        s_pair, r_pair, s_right, r_right, s_left, r_left, s_hid, r_hid, s_proj, r_proj,
    ) = refs[21:]
    count = len(left_in)
    me_s = lax.axis_index("section")
    me = lax.axis_index("dp")
    chips = peers // 2
    chip, core = me // 2, me % 2
    sibling = me + 1 - 2 * core
    blocks, share = chips, own.shape[2]
    columns = wh.shape[2]
    has_right = chip + 1 < chips
    has_left = chip > 0
    after = jnp.minimum(me + 2, peers - 1)
    before = jnp.maximum(me - 2, 0)

    barrier = pltpu.get_barrier_semaphore()

    def greet(index):
        pl.semaphore_signal(barrier, inc=1, device_id=(me_s, index), device_id_type=MESH)

    greet(sibling)

    @pl.when(has_right)
    def _():
        greet(after)

    @pl.when(has_left)
    def _():
        greet(before)

    for w in range(count):
        pltpu.make_async_copy(left_in[w], lefts.at[w], left_sem.at[w]).start()
        pltpu.make_async_copy(right_in[w], rights.at[w], right_sem.at[w]).start()
    lh_copy = pltpu.make_async_copy(lh_in, lh, lh_sem)
    dp_copy = pltpu.make_async_copy(dp_in, dp, dp_sem)
    lh_copy.start()
    dp_copy.start()

    def wh_copy(j, slot):
        return pltpu.make_async_copy(
            wh_in.at[:, pl.ds(pl.multiple_of(j * columns, columns), columns)],
            wh.at[slot], wh_sem.at[slot],
        )

    def wp_copy(j, slot):
        return pltpu.make_async_copy(
            wp_in.at[pl.ds(pl.multiple_of(j * columns, columns), columns)],
            wp.at[slot], wp_sem.at[slot],
        )

    wh_copy(0, 0).start()
    wp_copy(0, 0).start()
    pl.semaphore_wait(
        barrier, 1 + jnp.where(has_right, 1, 0) + jnp.where(has_left, 1, 0)
    )

    def remote(source, target, send, receive, index):
        return pltpu.make_async_remote_copy(
            src_ref=source, dst_ref=target, send_sem=send, recv_sem=receive,
            device_id=(me_s, index), device_id_type=MESH,
        )

    def pair_copy(w):
        return remote(pair_out.at[w], own.at[w], s_pair.at[w], r_pair.at[w], sibling)

    def rows_of(block, parity):
        return pl.ds(pl.multiple_of((2 * block + parity) * share, share), share)

    def prepare(w):
        pltpu.make_async_copy(lefts.at[w], lefts.at[w], left_sem.at[w]).wait()
        pltpu.make_async_copy(rights.at[w], rights.at[w], right_sem.at[w]).wait()
        slot = w % 2
        whole[slot] = dot_tn(lefts[w], rights[w])

        def divide(q, carry):
            pair_out[w, q] = whole[slot, rows_of(q, 1 - core), :].astype(BF16)
            return carry

        lax.fori_loop(0, blocks, divide, 0)
        pair_copy(w).start()

    def combine(w):
        slot = w % 2
        pair_copy(w).wait_recv()

        def add(q, carry):
            own[w, q] = (
                whole[slot, rows_of(q, core), :] + own[w, q].astype(F32)
            ).astype(BF16)
            return carry

        lax.fori_loop(0, blocks, add, 0)

    def right_copy(source, w, r):
        return remote(source, going_right.at[w, r], s_right.at[w, r], r_right.at[w, r], after)

    def left_copy(source, w, r):
        return remote(source, going_left.at[w, r], s_left.at[w, r], r_left.at[w, r], before)

    from_end = chips - 1 - chip

    def travel(w, r):
        prior = jnp.maximum(r - 1, 0)

        @pl.when(has_right & (chip == 0))
        def _():
            right_copy(own.at[w, chips - 1 - r], w, r).start()

        @pl.when(has_left & (from_end == 0))
        def _():
            left_copy(own.at[w, r], w, r).start()

        @pl.when(has_right & (chip > 0) & (chip <= r))
        def _():
            slot = going_right.at[w, prior]
            right_copy(slot, w, prior).wait_recv()
            slot[...] = (
                slot[...].astype(F32) + own[w, chips - 1 - r + chip].astype(F32)
            ).astype(BF16)
            right_copy(slot, w, r).start()

        @pl.when(has_left & (from_end > 0) & (from_end <= r))
        def _():
            slot = going_left.at[w, prior]
            left_copy(slot, w, prior).wait_recv()
            slot[...] = (
                slot[...].astype(F32) + own[w, r - from_end].astype(F32)
            ).astype(BF16)
            left_copy(slot, w, r).start()

    def hid_copy(j):
        place = pl.ds(pl.multiple_of(j * columns, columns), columns)
        return remote(
            hid_out.at[:, place], hid_in.at[:, place], s_hid.at[j], r_hid.at[j], sibling
        )

    proj_copy = remote(proj_out, proj_in, s_proj, r_proj, sibling)
    group = wide.shape[0]
    first = chip * 2 * share
    start = pl.multiple_of(first // group * group, group)
    inside = first - first // group * group

    def feed(j):
        slot = j % 2
        place = pl.ds(pl.multiple_of(j * columns, columns), columns)

        @pl.when(j == 0)
        def _():
            lh_copy.wait()
            dp_copy.wait()

        wh_copy(j, slot).wait()
        wp_copy(j, slot).wait()

        @pl.when(j + 1 < peers)
        def _():
            wh_copy(j + 1, 1 - slot).start()
            wp_copy(j + 1, 1 - slot).start()

        active = jnp.maximum(dot_nn(lh[...], wh[slot]), 0.0)
        act[...] = active
        grown = (dot_nt(dp[...], wp[slot]) * 2.0 * act[...]).astype(BF16)
        wide[...] = dot_tn(lh[:, pl.ds(start, group)], grown)
        mine = pl.ds(pl.multiple_of(inside + core * share, 16), share)
        other = pl.ds(pl.multiple_of(inside + (1 - core) * share, 16), share)
        wh_out[:, place] = wide[mine, :]
        hid_out[:, place] = wide[other, :].astype(BF16)
        hid_copy(j).start()

        @pl.when(j == 2 * chip + core)
        def _():
            squared = (act[...] * act[...]).astype(BF16)
            wp_out[...] = dot_tn(squared, dp[...])

        @pl.when(j == 2 * chip + 1 - core)
        def _():
            squared = (act[...] * act[...]).astype(BF16)
            proj_out[...] = dot_tn(squared, dp[...]).astype(BF16)
            proj_copy.start()

    prepare(0)
    prepare(1)
    combine(0)
    rounds = chips - 1

    def step(t, carry):
        w, r = t // rounds, t % rounds
        travel(w, r)

        @pl.when((r == 1) & (w + 2 < count))
        def _():
            prepare(w + 2)

        @pl.when((r == 1) & (w + 1 < count))
        def _():
            combine(w + 1)

        @pl.when((t % 2 == 0) & (t // 2 < peers))
        def _():
            feed(t // 2)

        return carry

    lax.fori_loop(0, count * rounds, step, 0)

    for w in range(count):
        outs[w][...] = own[w, chip].astype(F32)

        @pl.when(has_left)
        def _():
            right_copy(own.at[w, 0], w, rounds - 1).wait_recv()
            outs[w][...] += going_right[w, rounds - 1].astype(F32)

        @pl.when(has_right)
        def _():
            left_copy(own.at[w, 0], w, rounds - 1).wait_recv()
            outs[w][...] += going_left[w, rounds - 1].astype(F32)

    def gather_hidden(j, carry):
        hid_copy(j).wait_recv()
        place = pl.ds(pl.multiple_of(j * columns, columns), columns)
        wh_out[:, place] += hid_in[:, place].astype(F32)
        return carry

    lax.fori_loop(0, peers, gather_hidden, 0)
    proj_copy.wait_recv()
    wp_out[...] += proj_in[...].astype(F32)

    def sent_hidden(j, carry):
        hid_copy(j).wait_send()
        return carry

    lax.fori_loop(0, peers, sent_hidden, 0)
    proj_copy.wait_send()

    def sent(w, carry):
        pair_copy(w).wait_send()

        def sent_round(r, inner):
            @pl.when(has_right & (chip <= r))
            def _():
                right_copy(own.at[w, 0], w, r).wait_send()

            @pl.when(has_left & (from_end <= r))
            def _():
                left_copy(own.at[w, 0], w, r).wait_send()

            return inner

        lax.fori_loop(0, rounds, sent_round, 0)
        return carry

    lax.fori_loop(0, count, sent, 0)


def gradient_sums(peers, lefts, rights, lh, dp, wh, wp):
    count = len(lefts)
    rows, width = lefts[0].shape
    hidden = wh.shape[1]
    tokens = lh.shape[0]
    chips = peers // 2
    share = width // peers
    columns = hidden // peers
    group = max(128, 2 * share)
    shape = jax.ShapeDtypeStruct
    vmem = pl.BlockSpec(memory_space=pltpu.VMEM)
    anywhere = pl.BlockSpec(memory_space=pl.ANY)
    dma = pltpu.SemaphoreType.DMA
    blocks = pltpu.VMEM((count, chips, share, width), BF16)
    slots = pltpu.VMEM((count, chips - 1, share, width), BF16)
    return pl.pallas_call(
        partial(sum_kernel, peers),
        out_shape=(shape((share, width), F32),) * count
        + (shape((share, hidden), F32), shape((columns, width), F32)),
        in_specs=[anywhere] * (2 * count + 4),
        out_specs=[vmem] * (count + 2),
        scratch_shapes=[
            pltpu.VMEM((count, rows, width), BF16), pltpu.VMEM((count, rows, width), BF16),
            pltpu.VMEM((2, width, width), F32),
            blocks, blocks, slots, slots,
            pltpu.VMEM((tokens, width), BF16), pltpu.VMEM((tokens, width), BF16),
            pltpu.VMEM((2, width, columns), BF16), pltpu.VMEM((2, columns, width), BF16),
            pltpu.VMEM((tokens, columns), F32), pltpu.VMEM((group, columns), F32),
            pltpu.VMEM((share, hidden), BF16), pltpu.VMEM((share, hidden), BF16),
            pltpu.VMEM((columns, width), BF16), pltpu.VMEM((columns, width), BF16),
            dma((count,)), dma((count,)), dma, dma, dma((2,)), dma((2,)),
            dma((count,)), dma((count,)),
            dma((count, chips - 1)), dma((count, chips - 1)),
            dma((count, chips - 1)), dma((count, chips - 1)),
            dma((peers,)), dma((peers,)), dma, dma,
        ],
        compiler_params=pltpu.CompilerParams(
            collective_id=1, has_side_effects=True, vmem_limit_bytes=63 * 2**20
        ),
        name="gradient_sums",
    )(*lefts, *rights, lh, dp, wh, wp)


def per_device(x, top, spans, *parameters):
    sections = lax.axis_size("section")
    peers = lax.axis_size("dp")
    gain1, bias1, mix_k, mix_v, mix_g, log_rate, extra = parameters[0:7]
    wk, wv, wg, wo = parameters[7:11]
    gain2, bias2, mix_h, mix_f = parameters[11:15]
    wh, wp, wf = parameters[15:18]
    vectors = (gain1, bias1, mix_k, mix_v, mix_g, log_rate, extra, gain2, bias2, mix_h, mix_f)
    matrices = tuple(w[0] for w in (wk, wv, wg, wo, wh, wp, wf))
    found = relay(sections, peers, x, top, spans, vectors, matrices)
    out, back, vec = found[0:3]
    flat = (x.shape[0] * x.shape[1], x.shape[2])
    lk, lv, lg, lgt, lf, dk, dv, dg, datt, dsv = (part.reshape(flat) for part in found[3:13])
    lh, dproj = (part.reshape(-1, x.shape[2]) for part in found[13:15])
    share = x.shape[2] // peers
    if vec.shape[1] != share:
        vec = lax.dynamic_slice_in_dim(vec, lax.axis_index("dp") * share, share, 1)
    summed = gradient_sums(
        peers, (lf, lgt, lg, lk, lv), (dsv, datt, dg, dk, dv), lh, dproj, matrices[4], matrices[5]
    )
    d_wf, d_wo, d_wg, d_wk, d_wv, d_wh, d_wp = (part[None] for part in summed)

    def row(index):
        return vec[index : index + 1]

    return (
        out[None], back[None],
        row(0), row(1), row(2), row(3), row(4), row(5), row(6),
        d_wk, d_wv, d_wg, d_wo,
        row(7), row(8), row(9), row(10),
        d_wh, d_wp, d_wf,
    )


def solution(mesh):
    tokens = P(None, "dp", None)
    vector = P("section", None)
    matrix = P("section", None, None)
    result = P("section", None, "dp", None)
    vector_grad = P("section", "dp")
    matrix_grad = P("section", "dp", None)
    return jax.shard_map(
        per_device,
        mesh=mesh,
        in_specs=(tokens, tokens, P())
        + (vector,) * 7 + (matrix,) * 4 + (vector,) * 4 + (matrix,) * 3,
        out_specs=(result, result)
        + (vector_grad,) * 7 + (matrix_grad,) * 4 + (vector_grad,) * 4 + (matrix_grad,) * 3,
        check_vma=False,
    )
```

```python
from functools import partial

import jax
import jax.numpy as jnp
from jax import lax
from jax.experimental import pallas as pl
from jax.experimental.pallas import tpu as pltpu
from jax.sharding import PartitionSpec as P

EPS = 1e-05
MESH = pl.DeviceIdType.MESH
RB = 64
VECTORS = 16
F32 = jnp.float32
BF16 = jnp.bfloat16


def dot_nn(left, right):
    return jnp.dot(left, right, preferred_element_type=F32)


def dot_nt(left, right):
    return lax.dot_general(left, right, (((1,), (1,)), ((), ())), preferred_element_type=F32)


def dot_tn(left, right):
    return lax.dot_general(left, right, (((0,), (0,)), ((), ())), preferred_element_type=F32)


def sigmoid(v):
    return 1.0 / (1.0 + jnp.exp(-v))


def normalise(source):
    centred = source - jnp.mean(source, axis=-1, keepdims=True)
    spread = lax.rsqrt(jnp.mean(centred * centred, axis=-1, keepdims=True) + EPS)
    return centred * spread, spread


def moved_down(rows, first):
    place = lax.broadcasted_iota(jnp.int32, rows.shape, 0)
    return jnp.where(place == 0, first, pltpu.roll(rows, 1, 0))


def moved_up(rows, last):
    count = rows.shape[0]
    place = lax.broadcasted_iota(jnp.int32, rows.shape, 0)
    return jnp.where(place == count - 1, last, pltpu.roll(rows, count - 1, 0))


def fold(rows):
    total = rows[0:8]
    for at in range(8, rows.shape[0], 8):
        total = total + rows[at : at + 8]
    return total


def relay_kernel(sections, peers, split_vectors, *refs):
    (
        spans, x_in, top_in,
        gain1, bias1, mix_k, mix_v, mix_g, log_rate, extra, gain2, bias2, mix_h, mix_f,
        wk_in, wv_in, wg_in, wo_in, wh_in, wp_in, wf_in,
        out, back, vec_out, lk, lv, lg, lgt, lf, dk, dv, dg, datt, dsv, dproj, lh_all,
        lh, sq, dh,
        wk, wv, wg, wo, wh, wp, wf,
        xs, hx, dys, kk, vv, sg, sa, sb, mid, hmid, proj, sv, act, halo1, halo2,
        e0, e1, low_mask, up_mask, split, acc, t1, t2, t3,
        states, back_states, de2, de1, sum_row, sum_back, send_de2, send_de1, vg, vgs, vgr,
        w_sem, x_sem, top_sem, s_h0, s_x, s_hx, s_st, s_mid, s_dy, s_de2, s_bst, s_de1, s_vg,
        r_x, r_hx, r_st, r_mid, r_dy, r_de2, r_bst, r_de1, r_vg,
        s_lh, r_lh, own_sem,
    ) = refs
    me_s = lax.axis_index("section")
    me = lax.axis_index("dp")
    batches, row_count, width = x_in.shape
    hidden = wh.shape[1]
    chunks = row_count // RB
    base = me * row_count

    def at(section, index):
        return (section, index)

    barrier = pltpu.get_barrier_semaphore()

    def greet(section, index):
        pl.semaphore_signal(barrier, inc=1, device_id=at(section, index), device_id_type=MESH)

    def greet_peer(k, carry):
        @pl.when(k != me)
        def _():
            greet(me_s, k)

        return carry

    lax.fori_loop(0, peers, greet_peer, 0)
    has_next = me_s + 1 < sections
    has_prior = me_s > 0
    has_right = me + 1 < peers
    has_left = me > 0

    @pl.when(has_next)
    def _():
        greet(me_s + 1, me)

    @pl.when(has_prior)
    def _():
        greet(me_s - 1, me)

    @pl.when(has_next & has_right)
    def _():
        greet(me_s + 1, me + 1)

    @pl.when(has_prior & has_left)
    def _():
        greet(me_s - 1, me - 1)

    weight_copies = [
        pltpu.make_async_copy(source, target, w_sem.at[index])
        for index, (source, target) in enumerate(
            ((wk_in, wk), (wv_in, wv), (wg_in, wg), (wo_in, wo), (wf_in, wf), (wh_in, wh), (wp_in, wp))
        )
    ]

    @pl.when(me_s == 0)
    def _():
        pltpu.make_async_copy(x_in, xs, x_sem).start()

    for copy in weight_copies:
        copy.start()

    @pl.when(me_s == sections - 1)
    def _():
        pltpu.make_async_copy(top_in, dys, top_sem).start()

    rate = jnp.exp(log_rate[...])
    decay_block = jnp.exp(-rate * row_count)
    grow_block = jnp.exp(rate * row_count)

    def starts_of(m):
        found = []
        total = jnp.int32(0)
        for j in range(spans.shape[1]):
            found.append(total)
            total = total + spans[m, j]
        return found

    def segment(position, starts):
        total = jnp.where(position >= starts[0], 1, 0)
        for start in starts[1:]:
            total = total + jnp.where(position >= start, 1, 0)
        return total

    def column(i):
        return base + i * RB + lax.broadcasted_iota(jnp.int32, (RB, 1), 0)

    def keep_of(position, starts):
        return jnp.where(segment(position, starts) == segment(position - 1, starts), 1.0, 0.0)

    def fill_powers(i, carry):
        place = (i * RB + lax.broadcasted_iota(jnp.int32, (RB, width), 0)).astype(F32)
        e0[pl.ds(pl.multiple_of(i * RB, RB), RB), :] = jnp.exp(-place * rate)
        e1[pl.ds(pl.multiple_of(i * RB, RB), RB), :] = jnp.exp((place - (row_count - 1.0)) * rate)
        return carry

    lax.fori_loop(0, chunks, fill_powers, 0)
    for m in range(batches):
        starts = starts_of(m)
        row_at = lax.broadcasted_iota(jnp.int32, (row_count, row_count), 0)
        column_at = lax.broadcasted_iota(jnp.int32, (row_count, row_count), 1)
        same = segment(base + row_at, starts) == segment(base + column_at, starts)
        lower = jnp.where(same & (column_at < row_at), 1.0, 0.0).astype(BF16)
        upper = jnp.where(same & (column_at > row_at), 1.0, 0.0).astype(BF16)
        low_mask[m, :, 0:row_count] = lower
        low_mask[m, :, row_count:] = lower
        up_mask[m, :, 0:row_count] = upper
        up_mask[m, :, row_count:] = upper
    vg[...] = jnp.zeros_like(vg)

    @pl.when(me == 0)
    def _():
        hx[...] = jnp.zeros_like(hx)
        hmid[...] = jnp.zeros_like(hmid)

    @pl.when(me == peers - 1)
    def _():
        de1[...] = jnp.zeros_like(de1)
        de2[...] = jnp.zeros_like(de2)

    greeted = (
        peers - 1
        + jnp.where(has_next, 1, 0)
        + jnp.where(has_prior, 1, 0)
        + jnp.where(has_next & has_right, 1, 0)
        + jnp.where(has_prior & has_left, 1, 0)
    )
    pl.semaphore_wait(barrier, greeted)

    def remote(source, target, send, receive, section, index):
        return pltpu.make_async_remote_copy(
            src_ref=source, dst_ref=target, send_sem=send, recv_sem=receive,
            device_id=at(section, index), device_id_type=MESH,
        )

    right = jnp.minimum(me + 1, peers - 1)
    left = jnp.maximum(me - 1, 0)
    above = jnp.minimum(me_s + 1, sections - 1)
    below = jnp.maximum(me_s - 1, 0)
    tail = pl.ds(row_count - 16, 16)
    tail8 = pl.ds(row_count - 8, 8)

    def start_halo(m):
        return remote(x_in.at[m, tail], hx.at[m], s_h0.at[m], r_hx.at[m], me_s, right)

    def result_copy(m):
        return remote(out.at[m], xs.at[m], s_x.at[m], r_x.at[m], above, me)

    def result_halo(m):
        return remote(out.at[m, tail], hx.at[m], s_hx.at[m], r_hx.at[m], above, right)

    def middle_halo(m):
        return remote(mid.at[m, tail8], hmid.at[m], s_mid.at[m], r_mid.at[m], me_s, right)

    def state_copy(m, k, slot):
        return remote(sum_row.at[m], states.at[m, slot], s_st.at[m, k], r_st.at[m, slot], me_s, k)

    def back_copy(m):
        return remote(back.at[m], dys.at[m], s_dy.at[m], r_dy.at[m], below, me)

    def second_copy(m):
        return remote(send_de2.at[m], de2.at[m], s_de2.at[m], r_de2.at[m], me_s, left)

    def first_copy(m):
        return remote(send_de1.at[m], de1.at[m], s_de1.at[m], r_de1.at[m], me_s, left)

    def back_state_copy(m, k, slot):
        return remote(
            sum_back.at[m], back_states.at[m, slot], s_bst.at[m, k], r_bst.at[m, slot], me_s, k
        )

    chip, core = me // 2, me % 2
    chips = peers // 2

    def gather_copy(m, k, slot):
        return remote(
            lh.at[m], lh_all.at[slot, m], s_lh.at[m, k], r_lh.at[m, slot], me_s, 2 * k + core
        )

    def own_copy(m):
        return pltpu.make_async_copy(lh.at[m], lh_all.at[chip, m], own_sem.at[m])

    def each_chip(action):
        def turn(k, carry):
            @pl.when(k != chip)
            def _():
                action(k)

            return carry

        lax.fori_loop(0, chips, turn, 0)

    def start_gather(m):
        own_copy(m).start()
        each_chip(lambda k: gather_copy(m, k, chip).start())

    def start_gathers(early):
        for m in range(batches):
            in_gap = me_s + 1 + m < sections

            @pl.when(in_gap if early else jnp.logical_not(in_gap))
            def _(m=m):
                start_gather(m)

    def end_gather(m):
        own_copy(m).wait()
        each_chip(lambda k: gather_copy(m, k, chip).wait_send())
        each_chip(lambda k: gather_copy(m, k, k).wait_recv())

    @pl.when((me_s == 0) & has_right)
    def _():
        for m in range(batches):
            start_halo(m).start()

    @pl.when(me_s == 0)
    def _():
        pltpu.make_async_copy(x_in, xs, x_sem).wait()

    def span_of(i):
        return pl.ds(pl.multiple_of(i * RB, RB), RB)

    def forward(m, carry):
        starts = starts_of(m)

        @pl.when(has_prior)
        def _():
            result_copy(m).wait_recv()

        @pl.when(has_left)
        def _():
            start_halo(m).wait_recv()

        halo_rows, _ = normalise(hx[m].astype(F32))
        halo_rows = halo_rows * gain1[...] + bias1[...]
        halo1[m] = halo_rows[8:16]

        def mix_in(i, last):
            rows = span_of(i)
            normed, _ = normalise(xs[m, rows, :].astype(F32))
            normed = normed * gain1[...] + bias1[...]
            earlier = moved_down(normed, last) * keep_of(column(i), starts)
            gap = normed - earlier
            lk[m, rows, :] = (earlier + gap * mix_k[...]).astype(BF16)
            lv[m, rows, :] = (earlier + gap * mix_v[...]).astype(BF16)
            lg[m, rows, :] = (earlier + gap * mix_g[...]).astype(BF16)
            return normed[RB - 1 : RB]

        lax.fori_loop(0, chunks, mix_in, halo_rows[15:16])

        @pl.when(m == 0)
        def _():
            for copy in weight_copies[0:2]:
                copy.wait()

        kk[m] = dot_nn(lk[m], wk[...])
        vv[m] = dot_nn(lv[m], wv[...])
        end_segment = segment(base + row_count - 1, starts)

        def spread_in(i, totals):
            rows = span_of(i)
            weight = jnp.exp(kk[m, rows, :]) * e1[rows, :]
            weighted = weight * vv[m, rows, :]
            high_a = weighted.astype(BF16)
            high_b = weight.astype(BF16)
            split[rows, 0:width] = high_a
            split[rows, width:] = high_b
            low = pl.ds(pl.multiple_of(row_count + i * RB, RB), RB)
            split[low, 0:width] = (weighted - high_a.astype(F32)).astype(BF16)
            split[low, width:] = (weight - high_b.astype(F32)).astype(BF16)
            chosen = segment(column(i), starts) == end_segment
            return (
                totals[0] + fold(jnp.where(chosen, weighted, 0.0)),
                totals[1] + fold(jnp.where(chosen, weight, 0.0)),
            )

        nothing = jnp.zeros((8, width), F32)
        total_a, total_b = lax.fori_loop(0, chunks, spread_in, (nothing, nothing))
        sum_row[m, 0:1] = jnp.sum(total_a, axis=0, keepdims=True)
        sum_row[m, 1:2] = jnp.sum(total_b, axis=0, keepdims=True)

        def send_state(k, carry):
            state_copy(m, k, me).start()
            return carry

        lax.fori_loop(me + 1, peers, send_state, 0)

        @pl.when(m == 0)
        def _():
            weight_copies[2].wait()

        sg[m] = dot_nn(lg[m], wg[...])
        acc[...] = dot_nn(low_mask[m], split[...])

        def receive_state(k, held):
            state_copy(m, k, k).wait_recv()
            unbroken = segment(k * row_count - 1, starts) == segment(
                (k + 1) * row_count - 1, starts
            )
            passing = jnp.where(unbroken, 1.0, 0.0) * decay_block
            return (
                passing * held[0] + states[m, k, 0:1],
                passing * held[1] + states[m, k, 1:2],
            )

        none = jnp.zeros((1, width), F32)
        enter_a, enter_b = lax.fori_loop(0, me, receive_state, (none, none))
        prior_segment = segment(base - 1, starts)

        def mix_states(i, carry):
            rows = span_of(i)
            falling = e0[rows, :]
            chosen = jnp.where(segment(column(i), starts) == prior_segment, 1.0, 0.0)
            grown = falling * grow_block
            held = falling * chosen
            state_a = grown * acc[rows, 0:width] + held * enter_a
            state_b = grown * acc[rows, width:] + held * enter_b
            sa[m, rows, :] = state_a
            sb[m, rows, :] = state_b
            present = jnp.exp(extra[...] + kk[m, rows, :])
            gate = sigmoid(sg[m, rows, :])
            sg[m, rows, :] = gate
            found = (state_a + present * vv[m, rows, :]) / (state_b + present)
            lgt[m, rows, :] = (gate * found).astype(BF16)
            return carry

        lax.fori_loop(0, chunks, mix_states, 0)

        @pl.when(m == 0)
        def _():
            weight_copies[3].wait()

        mid[m] = xs[m].astype(F32) + dot_nn(lgt[m], wo[...])

        @pl.when(has_right)
        def _():
            middle_halo(m).start()

        def mix_second(i, last):
            rows = span_of(i)
            normed, _ = normalise(mid[m, rows, :])
            normed = normed * gain2[...] + bias2[...]
            earlier = moved_down(normed, last) * keep_of(column(i), starts)
            gap = normed - earlier
            lh[m, rows, :] = (earlier + gap * mix_h[...]).astype(BF16)
            lf[m, rows, :] = (earlier + gap * mix_f[...]).astype(BF16)
            return normed[RB - 1 : RB]

        lax.fori_loop(0, chunks, mix_second, none)

        @pl.when(has_left)
        def _():
            middle_halo(m).wait_recv()

        halo_rows, _ = normalise(hmid[m])
        halo_rows = halo_rows * gain2[...] + bias2[...]
        halo2[m] = halo_rows
        mix_second(0, halo_rows[7:8])

        @pl.when(m == 0)
        def _():
            for copy in weight_copies[4:7]:
                copy.wait()

        sv[m] = dot_nn(lf[m], wf[...])

        def widen(j, carry):
            columns = pl.ds(pl.multiple_of(j * width, width), width)
            active = jnp.maximum(dot_nn(lh[m], wh[:, columns]), 0.0)
            act[m, :, columns] = active.astype(BF16)
            sq[m, :, columns] = (active * active).astype(BF16)
            return carry

        lax.fori_loop(0, hidden // width, widen, 0)
        proj[m] = dot_nn(sq[m], wp[...])

        def finish(i, carry):
            rows = span_of(i)
            sieve = sigmoid(sv[m, rows, :])
            sv[m, rows, :] = sieve
            out[m, rows, :] = (mid[m, rows, :] + sieve * proj[m, rows, :]).astype(BF16)
            return carry

        lax.fori_loop(0, chunks, finish, 0)

        @pl.when(has_next)
        def _():
            result_copy(m).start()

        @pl.when(has_next & has_right)
        def _():
            result_halo(m).start()

        return carry

    lax.fori_loop(0, batches, forward, 0)
    start_gathers(True)

    def add_vector(index, value):
        vg[index] += fold(value)

    @pl.when(me_s == sections - 1)
    def _():
        pltpu.make_async_copy(top_in, dys, top_sem).wait()

    def backward(m, carry):
        starts = starts_of(m)
        none = jnp.zeros((1, width), F32)

        @pl.when(has_next)
        def _():
            back_copy(m).wait_recv()

        def open_back(i, carry):
            rows = span_of(i)
            incoming = dys[m, rows, :].astype(F32)
            sieve = sv[m, rows, :]
            gained = incoming * sieve
            dproj[m, rows, :] = gained.astype(BF16)
            dsv[m, rows, :] = (gained * proj[m, rows, :] * (1.0 - sieve)).astype(BF16)
            return carry

        lax.fori_loop(0, chunks, open_back, 0)
        t1[...] = jnp.zeros_like(t1)

        def narrow(j, carry):
            columns = pl.ds(pl.multiple_of(j * width, width), width)
            grown = dot_nt(dproj[m], wp[columns, :])
            dh[m, :, columns] = (grown * 2.0 * act[m, :, columns].astype(F32)).astype(BF16)
            t1[...] += dot_nt(dh[m, :, columns], wh[:, columns])
            return carry

        lax.fori_loop(0, hidden // width, narrow, 0)
        t2[...] = dot_nt(dsv[m], wf[...])

        def second_earlier(rows, position):
            whole = t1[rows, :] * (1.0 - mix_h[...]) + t2[rows, :] * (1.0 - mix_f[...])
            return whole * keep_of(position, starts)

        eight = lax.broadcasted_iota(jnp.int32, (8, 1), 0)
        send_de2[m] = second_earlier(pl.ds(0, 8), base + eight)

        @pl.when(has_left)
        def _():
            second_copy(m).start()

        def back_second(i, last, following):
            rows = span_of(i)
            spare, spread = normalise(mid[m, rows, :])
            normed = spare * gain2[...] + bias2[...]
            kept = keep_of(column(i), starts)
            gap = normed - moved_down(normed, last) * kept
            from_h = t1[rows, :]
            from_f = t2[rows, :]
            add_vector(9, from_h * gap)
            add_vector(10, from_f * gap)
            straight = from_h * mix_h[...] + from_f * mix_f[...]
            earlier = (from_h + from_f - straight) * kept
            d_normed = straight + moved_up(earlier, following)
            add_vector(7, d_normed * spare)
            add_vector(8, d_normed)
            scaled = d_normed * gain2[...]
            mean_one = jnp.mean(scaled, axis=-1, keepdims=True)
            mean_two = jnp.mean(scaled * spare, axis=-1, keepdims=True)
            d_mid = dys[m, rows, :].astype(F32) + spread * (scaled - mean_one - spare * mean_two)
            t3[rows, :] = d_mid
            datt[m, rows, :] = d_mid.astype(BF16)
            return normed[RB - 1 : RB]

        def following_second(i):
            start = pl.multiple_of((i + 1) * RB, RB)
            return second_earlier(pl.ds(start, 8), base + start + eight)[0:1]

        last = lax.fori_loop(
            0, chunks - 1,
            lambda i, last: back_second(i, last, following_second(i)),
            halo2[m, 7:8],
        )

        @pl.when(has_right)
        def _():
            second_copy(m).wait_recv()

        back_second(chunks - 1, last, de2[m, 0:1])
        t1[...] = dot_nt(datt[m], wo[...])
        open_segment = segment(base, starts)

        def back_states_in(i, totals):
            rows = span_of(i)
            d_gated = t1[rows, :]
            gate = sg[m, rows, :]
            keys = kk[m, rows, :]
            values = vv[m, rows, :]
            present = jnp.exp(extra[...] + keys)
            inverse = 1.0 / (sb[m, rows, :] + present)
            found = (sa[m, rows, :] + present * values) * inverse
            d_found = d_gated * gate
            dg[m, rows, :] = (d_found * found * (1.0 - gate)).astype(BF16)
            d_a = d_found * inverse
            d_b = -d_a * found
            d_key = (d_a * values + d_b) * present
            add_vector(6, d_key)
            t1[rows, :] = d_key
            t2[rows, :] = d_a * present
            falling = e0[rows, :]
            scaled_a = d_a * falling
            scaled_b = d_b * falling
            high_a = scaled_a.astype(BF16)
            high_b = scaled_b.astype(BF16)
            split[rows, 0:width] = high_a
            split[rows, width:] = high_b
            low = pl.ds(pl.multiple_of(row_count + i * RB, RB), RB)
            split[low, 0:width] = (scaled_a - high_a.astype(F32)).astype(BF16)
            split[low, width:] = (scaled_b - high_b.astype(F32)).astype(BF16)
            chosen = segment(column(i), starts) == open_segment
            return (
                totals[0] + fold(jnp.where(chosen, scaled_a, 0.0)),
                totals[1] + fold(jnp.where(chosen, scaled_b, 0.0)),
            )

        nothing = jnp.zeros((8, width), F32)
        total_a, total_b = lax.fori_loop(0, chunks, back_states_in, (nothing, nothing))
        sum_back[m, 0:1] = jnp.sum(total_a, axis=0, keepdims=True)
        sum_back[m, 1:2] = jnp.sum(total_b, axis=0, keepdims=True)

        def send_state(k, carry):
            back_state_copy(m, k, me).start()
            return carry

        lax.fori_loop(0, me, send_state, 0)
        acc[...] = dot_nn(up_mask[m], split[...])

        def receive_state(turn, held):
            k = peers - 1 - turn
            back_state_copy(m, k, k).wait_recv()
            first = segment(k * row_count, starts)
            unbroken = first == segment((k + 1) * row_count - 1, starts)
            joined = jnp.where(first == segment(k * row_count - 1, starts), 1.0, 0.0)
            passing = jnp.where(unbroken, 1.0, 0.0) * decay_block
            return (
                joined * (passing * held[0] + back_states[m, k, 0:1]),
                joined * (passing * held[1] + back_states[m, k, 1:2]),
            )

        enter_a, enter_b = lax.fori_loop(0, peers - 1 - me, receive_state, (none, none))
        end_segment = segment(base + row_count - 1, starts)

        def back_keys(i, carry):
            rows = span_of(i)
            rising = e1[rows, :]
            chosen = jnp.where(segment(column(i), starts) == end_segment, 1.0, 0.0)
            grown = rising * grow_block
            held = rising * chosen
            d_a = grown * acc[rows, 0:width] + held * enter_a
            d_b = grown * acc[rows, width:] + held * enter_b
            add_vector(5, d_a * sa[m, rows, :] + d_b * sb[m, rows, :])
            weight = jnp.exp(kk[m, rows, :])
            dv[m, rows, :] = (t2[rows, :] + d_a * weight).astype(BF16)
            dk[m, rows, :] = (t1[rows, :] + (d_a * vv[m, rows, :] + d_b) * weight).astype(BF16)
            return carry

        lax.fori_loop(0, chunks, back_keys, 0)
        t1[...] = dot_nt(dk[m], wk[...])
        t2[...] = dot_nt(dv[m], wv[...])
        acc[:, 0:width] = dot_nt(dg[m], wg[...])

        def first_earlier(rows, position):
            whole = (
                t1[rows, :] * (1.0 - mix_k[...])
                + t2[rows, :] * (1.0 - mix_v[...])
                + acc[rows, 0:width] * (1.0 - mix_g[...])
            )
            return whole * keep_of(position, starts)

        send_de1[m] = first_earlier(pl.ds(0, 8), base + eight)

        @pl.when(has_left)
        def _():
            first_copy(m).start()

        def back_first(i, last, following):
            rows = span_of(i)
            spare, spread = normalise(xs[m, rows, :].astype(F32))
            normed = spare * gain1[...] + bias1[...]
            kept = keep_of(column(i), starts)
            gap = normed - moved_down(normed, last) * kept
            from_k = t1[rows, :]
            from_v = t2[rows, :]
            from_g = acc[rows, 0:width]
            add_vector(2, from_k * gap)
            add_vector(3, from_v * gap)
            add_vector(4, from_g * gap)
            straight = from_k * mix_k[...] + from_v * mix_v[...] + from_g * mix_g[...]
            earlier = (from_k + from_v + from_g - straight) * kept
            d_normed = straight + moved_up(earlier, following)
            add_vector(0, d_normed * spare)
            add_vector(1, d_normed)
            scaled = d_normed * gain1[...]
            mean_one = jnp.mean(scaled, axis=-1, keepdims=True)
            mean_two = jnp.mean(scaled * spare, axis=-1, keepdims=True)
            found = t3[rows, :] + spread * (scaled - mean_one - spare * mean_two)
            back[m, rows, :] = found.astype(BF16)
            return normed[RB - 1 : RB]

        def following_first(i):
            start = pl.multiple_of((i + 1) * RB, RB)
            return first_earlier(pl.ds(start, 8), base + start + eight)[0:1]

        last = lax.fori_loop(
            0, chunks - 1,
            lambda i, last: back_first(i, last, following_first(i)),
            halo1[m, 7:8],
        )

        @pl.when(has_right)
        def _():
            first_copy(m).wait_recv()

        back_first(chunks - 1, last, de1[m, 0:1])

        @pl.when(has_prior)
        def _():
            back_copy(m).start()

        return carry

    lax.fori_loop(0, batches, backward, 0)
    start_gathers(False)

    vgs[...] = jnp.sum(vg[...], axis=1)
    vgs[5:6] = vgs[5:6] * (-rate * jnp.exp(-rate))
    share = vgr.shape[2]

    def part(k):
        if split_vectors:
            return vgs.at[:, pl.ds(pl.multiple_of(k * share, share), share)]
        return vgs

    def vector_copy(k, slot):
        return remote(part(k), vgr.at[slot], s_vg.at[k], r_vg.at[slot], me_s, k)

    def each_peer(action):
        def turn(k, carry):
            @pl.when(k != me)
            def _():
                action(k)

            return carry

        lax.fori_loop(0, peers, turn, 0)

    each_peer(lambda k: vector_copy(k, me).start())
    if split_vectors:
        vec_out[...] = vgs[:, pl.ds(pl.multiple_of(me * share, share), share)]
    else:
        vec_out[...] = vgs[...]

    def collect(k):
        vector_copy(k, k).wait_recv()
        vec_out[...] += vgr[k]

    each_peer(collect)

    each_peer(lambda k: vector_copy(k, me).wait_send())

    def close(m, carry):
        @pl.when((me_s == 0) & has_right)
        def _():
            start_halo(m).wait_send()

        @pl.when(has_next)
        def _():
            result_copy(m).wait_send()

        @pl.when(has_next & has_right)
        def _():
            result_halo(m).wait_send()

        @pl.when(has_right)
        def _():
            middle_halo(m).wait_send()

        @pl.when(has_left)
        def _():
            second_copy(m).wait_send()
            first_copy(m).wait_send()

        @pl.when(has_prior)
        def _():
            back_copy(m).wait_send()

        def ended(k, carry):
            state_copy(m, k, me).wait_send()
            return carry

        lax.fori_loop(me + 1, peers, ended, 0)
        end_gather(m)

        def ended_back(k, carry):
            back_state_copy(m, k, me).wait_send()
            return carry

        lax.fori_loop(0, me, ended_back, 0)
        return carry

    lax.fori_loop(0, batches, close, 0)


def relay(sections, peers, x, top, spans, vectors, matrices):
    batches, rows, width = x.shape
    hidden = matrices[4].shape[1]
    share = width // peers
    split_vectors = share % 128 == 0
    if not split_vectors:
        share = width
    shape = jax.ShapeDtypeStruct
    low = shape((batches, rows, width), BF16)
    vmem = pl.BlockSpec(memory_space=pltpu.VMEM)
    anywhere = pl.BlockSpec(memory_space=pl.ANY)
    dma = pltpu.SemaphoreType.DMA

    def narrow(kind):
        return pltpu.VMEM((batches, rows, width), kind)

    return pl.pallas_call(
        partial(relay_kernel, sections, peers, split_vectors),
        out_shape=(
            low, low, shape((VECTORS, share), F32),
            low, low, low, low, low,
            low, low, low, low, low, low,
            shape((peers // 2, batches, rows, width), BF16),
        ),
        in_specs=[pl.BlockSpec(memory_space=pltpu.SMEM), anywhere, anywhere]
        + [vmem] * 11
        + [anywhere] * 7,
        out_specs=[vmem] * 14 + [anywhere],
        scratch_shapes=[
            narrow(BF16), pltpu.VMEM((batches, rows, hidden), BF16),
            pltpu.VMEM((batches, rows, hidden), BF16),
        ]
        + [pltpu.VMEM(matrix.shape, BF16) for matrix in matrices_order(matrices)]
        + [
            narrow(BF16), pltpu.VMEM((batches, 16, width), BF16), narrow(BF16),
            narrow(F32), narrow(F32), narrow(F32), narrow(F32), narrow(F32), narrow(F32),
            pltpu.VMEM((batches, 8, width), F32), narrow(F32), narrow(F32),
            pltpu.VMEM((batches, rows, hidden), BF16),
            pltpu.VMEM((batches, 8, width), F32), pltpu.VMEM((batches, 8, width), F32),
            pltpu.VMEM((rows, width), F32), pltpu.VMEM((rows, width), F32),
            pltpu.VMEM((batches, rows, 2 * rows), BF16), pltpu.VMEM((batches, rows, 2 * rows), BF16),
            pltpu.VMEM((2 * rows, 2 * width), BF16), pltpu.VMEM((rows, 2 * width), F32),
            pltpu.VMEM((rows, width), F32), pltpu.VMEM((rows, width), F32), pltpu.VMEM((rows, width), F32),
            pltpu.VMEM((batches, peers, 2, width), F32), pltpu.VMEM((batches, peers, 2, width), F32),
            pltpu.VMEM((batches, 8, width), F32), pltpu.VMEM((batches, 8, width), F32),
            pltpu.VMEM((batches, 2, width), F32), pltpu.VMEM((batches, 2, width), F32),
            pltpu.VMEM((batches, 8, width), F32), pltpu.VMEM((batches, 8, width), F32),
            pltpu.VMEM((VECTORS, 8, width), F32), pltpu.VMEM((VECTORS, width), F32),
            pltpu.VMEM((peers, VECTORS, share), F32),
            dma((7,)), dma, dma,
            dma((batches,)), dma((batches,)), dma((batches,)), dma((batches, peers)), dma((batches,)),
            dma((batches,)), dma((batches,)), dma((batches, peers)), dma((batches,)), dma((peers,)),
            dma((batches,)), dma((batches,)), dma((batches, peers)), dma((batches,)),
            dma((batches,)), dma((batches,)), dma((batches, peers)), dma((batches,)), dma((peers,)),
            dma((batches, peers // 2)), dma((batches, peers // 2)), dma((batches,)),
        ],
        compiler_params=pltpu.CompilerParams(
            collective_id=0, has_side_effects=True, vmem_limit_bytes=63 * 2**20
        ),
        name="relay",
    )(spans, x, top, *vectors, *matrices_order(matrices))


def matrices_order(matrices):
    wk, wv, wg, wo, wh, wp, wf = matrices
    return (wk, wv, wg, wo, wh, wp, wf)


def sum_kernel(peers, *refs):
    left_in, right_in = refs[0:5], refs[5:10]
    lh_in, dp_in, wh_in, wp_in = refs[10:14]
    outs, wh_out, wp_out = refs[14:19], refs[19], refs[20]
    (
        lefts, rights, whole, own, pair_out, going_right, going_left,
        lh, dp, wh, wp, act, wide, hid_out, hid_in, proj_out, proj_in,
        left_sem, right_sem, lh_sem, dp_sem, wh_sem, wp_sem,
        s_pair, r_pair, s_right, r_right, s_left, r_left, s_hid, r_hid, s_proj, r_proj,
        s_ahead, s_behind, r_rows,
    ) = refs[21:]
    count = len(left_in)
    me_s = lax.axis_index("section")
    me = lax.axis_index("dp")
    chips = peers // 2
    chip, core = me // 2, me % 2
    sibling = me + 1 - 2 * core
    blocks, share = chips, own.shape[2]
    columns = wh.shape[2]
    has_right = chip + 1 < chips
    has_left = chip > 0
    after = jnp.minimum(me + 2, peers - 1)
    before = jnp.maximum(me - 2, 0)

    barrier = pltpu.get_barrier_semaphore()

    def greet(index):
        pl.semaphore_signal(barrier, inc=1, device_id=(me_s, index), device_id_type=MESH)

    greet(sibling)

    @pl.when(has_right)
    def _():
        greet(after)

    @pl.when(has_left)
    def _():
        greet(before)

    for w in range(count):
        pltpu.make_async_copy(left_in[w], lefts.at[w], left_sem.at[w]).start()
        pltpu.make_async_copy(right_in[w], rights.at[w], right_sem.at[w]).start()
    lh_copy = pltpu.make_async_copy(lh_in, lh, lh_sem)
    rows = dp_in.shape[0]
    own_rows = pl.ds(pl.multiple_of(chip * rows, rows), rows)
    dp_copy = pltpu.make_async_copy(dp_in, dp.at[own_rows], dp_sem)
    dp_copy.start()
    lh_copy.start()

    def wh_copy(j, slot):
        return pltpu.make_async_copy(
            wh_in.at[:, pl.ds(pl.multiple_of(j * columns, columns), columns)],
            wh.at[slot], wh_sem.at[slot],
        )

    def wp_copy(j, slot):
        return pltpu.make_async_copy(
            wp_in.at[pl.ds(pl.multiple_of(j * columns, columns), columns)],
            wp.at[slot], wp_sem.at[slot],
        )

    wh_copy(0, 0).start()
    wp_copy(0, 0).start()
    pl.semaphore_wait(
        barrier, 1 + jnp.where(has_right, 1, 0) + jnp.where(has_left, 1, 0)
    )

    def remote(source, target, send, receive, index):
        return pltpu.make_async_remote_copy(
            src_ref=source, dst_ref=target, send_sem=send, recv_sem=receive,
            device_id=(me_s, index), device_id_type=MESH,
        )

    def pair_copy(w):
        return remote(pair_out.at[w], own.at[w], s_pair.at[w], r_pair.at[w], sibling)

    def rows_of(block, parity):
        return pl.ds(pl.multiple_of((2 * block + parity) * share, share), share)

    def prepare(w):
        pltpu.make_async_copy(lefts.at[w], lefts.at[w], left_sem.at[w]).wait()
        pltpu.make_async_copy(rights.at[w], rights.at[w], right_sem.at[w]).wait()
        slot = w % 2
        whole[slot] = dot_tn(lefts[w], rights[w])

        def divide(q, carry):
            pair_out[w, q] = whole[slot, rows_of(q, 1 - core), :].astype(BF16)
            return carry

        lax.fori_loop(0, blocks, divide, 0)
        pair_copy(w).start()

    def combine(w):
        slot = w % 2
        pair_copy(w).wait_recv()

        def add(q, carry):
            own[w, q] = (
                whole[slot, rows_of(q, core), :] + own[w, q].astype(F32)
            ).astype(BF16)
            return carry

        lax.fori_loop(0, blocks, add, 0)

    def right_copy(source, w, r):
        return remote(source, going_right.at[w, r], s_right.at[w, r], r_right.at[w, r], after)

    def left_copy(source, w, r):
        return remote(source, going_left.at[w, r], s_left.at[w, r], r_left.at[w, r], before)

    from_end = chips - 1 - chip

    def travel(w, r):
        prior = jnp.maximum(r - 1, 0)

        @pl.when(has_right & (chip == 0))
        def _():
            right_copy(own.at[w, chips - 1 - r], w, r).start()

        @pl.when(has_left & (from_end == 0))
        def _():
            left_copy(own.at[w, r], w, r).start()

        @pl.when(has_right & (chip > 0) & (chip <= r))
        def _():
            slot = going_right.at[w, prior]
            right_copy(slot, w, prior).wait_recv()
            slot[...] = (
                slot[...].astype(F32) + own[w, chips - 1 - r + chip].astype(F32)
            ).astype(BF16)
            right_copy(slot, w, r).start()

        @pl.when(has_left & (from_end > 0) & (from_end <= r))
        def _():
            slot = going_left.at[w, prior]
            left_copy(slot, w, prior).wait_recv()
            slot[...] = (
                slot[...].astype(F32) + own[w, r - from_end].astype(F32)
            ).astype(BF16)
            left_copy(slot, w, r).start()

    def rows_copy(origin, send, index):
        block = dp.at[pl.ds(pl.multiple_of(origin * rows, rows), rows)]
        return remote(block, block, send.at[origin], r_rows.at[origin], index)

    def each_origin(low, high):
        def turn(origin, carry):
            rows_copy(origin, s_ahead, after).wait_recv()
            return carry

        lax.fori_loop(low, high, turn, 0)

    def spread(r):
        @pl.when(has_right & (chip >= r))
        def _():
            pl.when(r > 0)(lambda: rows_copy(chip - r, s_ahead, after).wait_recv())
            rows_copy(chip - r, s_ahead, after).start()

        @pl.when(has_left & (from_end >= r))
        def _():
            pl.when(r > 0)(lambda: rows_copy(chip + r, s_behind, before).wait_recv())
            rows_copy(chip + r, s_behind, before).start()

    def hid_copy(j):
        place = pl.ds(pl.multiple_of(j * columns, columns), columns)
        return remote(
            hid_out.at[:, place], hid_in.at[:, place], s_hid.at[j], r_hid.at[j], sibling
        )

    proj_copy = remote(proj_out, proj_in, s_proj, r_proj, sibling)
    group = wide.shape[0]
    first = chip * 2 * share
    start = pl.multiple_of(first // group * group, group)
    inside = first - first // group * group

    def feed(j):
        slot = j % 2
        place = pl.ds(pl.multiple_of(j * columns, columns), columns)

        @pl.when(j == 0)
        def _():
            lh_copy.wait()
            pl.when(chip == 0)(lambda: each_origin(1, chips))
            pl.when(from_end == 0)(lambda: each_origin(0, chips - 1))

        wh_copy(j, slot).wait()
        wp_copy(j, slot).wait()

        @pl.when(j + 1 < peers)
        def _():
            wh_copy(j + 1, 1 - slot).start()
            wp_copy(j + 1, 1 - slot).start()

        active = jnp.maximum(dot_nn(lh[...], wh[slot]), 0.0)
        act[...] = active
        grown = (dot_nt(dp[...], wp[slot]) * 2.0 * act[...]).astype(BF16)
        wide[...] = dot_tn(lh[:, pl.ds(start, group)], grown)
        mine = pl.ds(pl.multiple_of(inside + core * share, 16), share)
        other = pl.ds(pl.multiple_of(inside + (1 - core) * share, 16), share)
        wh_out[:, place] = wide[mine, :]
        hid_out[:, place] = wide[other, :].astype(BF16)
        hid_copy(j).start()

        @pl.when(j == 2 * chip + core)
        def _():
            squared = (act[...] * act[...]).astype(BF16)
            wp_out[...] = dot_tn(squared, dp[...])

        @pl.when(j == 2 * chip + 1 - core)
        def _():
            squared = (act[...] * act[...]).astype(BF16)
            proj_out[...] = dot_tn(squared, dp[...]).astype(BF16)
            proj_copy.start()

    rounds = chips - 1
    dp_copy.wait()
    spread(0)
    prepare(0)
    prepare(1)
    combine(0)
    opening = count * rounds - peers

    def step(t, carry):
        w, r = t // rounds, t % rounds
        travel(w, r)

        @pl.when((r == 1) & (w + 2 < count))
        def _():
            prepare(w + 2)

        @pl.when((r == 1) & (w + 1 < count))
        def _():
            combine(w + 1)

        @pl.when(t + 1 < rounds)
        def _():
            spread(t + 1)

        @pl.when(t >= opening)
        def _():
            feed(t - opening)

        return carry

    lax.fori_loop(0, count * rounds, step, 0)

    for w in range(count):
        outs[w][...] = own[w, chip].astype(F32)

        @pl.when(has_left)
        def _():
            right_copy(own.at[w, 0], w, rounds - 1).wait_recv()
            outs[w][...] += going_right[w, rounds - 1].astype(F32)

        @pl.when(has_right)
        def _():
            left_copy(own.at[w, 0], w, rounds - 1).wait_recv()
            outs[w][...] += going_left[w, rounds - 1].astype(F32)

    def gather_hidden(j, carry):
        hid_copy(j).wait_recv()
        place = pl.ds(pl.multiple_of(j * columns, columns), columns)
        wh_out[:, place] += hid_in[:, place].astype(F32)
        return carry

    lax.fori_loop(0, peers, gather_hidden, 0)
    proj_copy.wait_recv()
    wp_out[...] += proj_in[...].astype(F32)

    def sent_hidden(j, carry):
        hid_copy(j).wait_send()
        return carry

    lax.fori_loop(0, peers, sent_hidden, 0)
    proj_copy.wait_send()

    def sent_rows(origin, carry):
        @pl.when(has_right & (origin <= chip))
        def _():
            rows_copy(origin, s_ahead, after).wait_send()

        @pl.when(has_left & (origin >= chip))
        def _():
            rows_copy(origin, s_behind, before).wait_send()

        return carry

    lax.fori_loop(0, chips, sent_rows, 0)

    def sent(w, carry):
        pair_copy(w).wait_send()

        def sent_round(r, inner):
            @pl.when(has_right & (chip <= r))
            def _():
                right_copy(own.at[w, 0], w, r).wait_send()

            @pl.when(has_left & (from_end <= r))
            def _():
                left_copy(own.at[w, 0], w, r).wait_send()

            return inner

        lax.fori_loop(0, rounds, sent_round, 0)
        return carry

    lax.fori_loop(0, count, sent, 0)


def gradient_sums(peers, lefts, rights, lh, dp, wh, wp):
    count = len(lefts)
    rows, width = lefts[0].shape
    hidden = wh.shape[1]
    tokens = lh.shape[0]
    chips = peers // 2
    share = width // peers
    columns = hidden // peers
    group = max(128, 2 * share)
    shape = jax.ShapeDtypeStruct
    vmem = pl.BlockSpec(memory_space=pltpu.VMEM)
    anywhere = pl.BlockSpec(memory_space=pl.ANY)
    dma = pltpu.SemaphoreType.DMA
    blocks = pltpu.VMEM((count, chips, share, width), BF16)
    slots = pltpu.VMEM((count, chips - 1, share, width), BF16)
    return pl.pallas_call(
        partial(sum_kernel, peers),
        out_shape=(shape((share, width), F32),) * count
        + (shape((share, hidden), F32), shape((columns, width), F32)),
        in_specs=[anywhere] * (2 * count + 4),
        out_specs=[vmem] * (count + 2),
        scratch_shapes=[
            pltpu.VMEM((count, rows, width), BF16), pltpu.VMEM((count, rows, width), BF16),
            pltpu.VMEM((2, width, width), F32),
            blocks, blocks, slots, slots,
            pltpu.VMEM((tokens, width), BF16), pltpu.VMEM((tokens, width), BF16),
            pltpu.VMEM((2, width, columns), BF16), pltpu.VMEM((2, columns, width), BF16),
            pltpu.VMEM((tokens, columns), F32), pltpu.VMEM((group, columns), F32),
            pltpu.VMEM((share, hidden), BF16), pltpu.VMEM((share, hidden), BF16),
            pltpu.VMEM((columns, width), BF16), pltpu.VMEM((columns, width), BF16),
            dma((count,)), dma((count,)), dma, dma, dma((2,)), dma((2,)),
            dma((count,)), dma((count,)),
            dma((count, chips - 1)), dma((count, chips - 1)),
            dma((count, chips - 1)), dma((count, chips - 1)),
            dma((peers,)), dma((peers,)), dma, dma,
            dma((chips,)), dma((chips,)), dma((chips,)),
        ],
        compiler_params=pltpu.CompilerParams(
            collective_id=1, has_side_effects=True, vmem_limit_bytes=63 * 2**20
        ),
        name="gradient_sums",
    )(*lefts, *rights, lh, dp, wh, wp)


def per_device(x, top, spans, *parameters):
    sections = lax.axis_size("section")
    peers = lax.axis_size("dp")
    gain1, bias1, mix_k, mix_v, mix_g, log_rate, extra = parameters[0:7]
    wk, wv, wg, wo = parameters[7:11]
    gain2, bias2, mix_h, mix_f = parameters[11:15]
    wh, wp, wf = parameters[15:18]
    vectors = (gain1, bias1, mix_k, mix_v, mix_g, log_rate, extra, gain2, bias2, mix_h, mix_f)
    matrices = tuple(w[0] for w in (wk, wv, wg, wo, wh, wp, wf))
    found = relay(sections, peers, x, top, spans, vectors, matrices)
    out, back, vec = found[0:3]
    flat = (x.shape[0] * x.shape[1], x.shape[2])
    lk, lv, lg, lgt, lf, dk, dv, dg, datt, dsv, dproj = (
        part.reshape(flat) for part in found[3:14]
    )
    lh = found[14].reshape(-1, x.shape[2])
    share = x.shape[2] // peers
    if vec.shape[1] != share:
        vec = lax.dynamic_slice_in_dim(vec, lax.axis_index("dp") * share, share, 1)
    summed = gradient_sums(
        peers, (lf, lgt, lg, lk, lv), (dsv, datt, dg, dk, dv), lh, dproj, matrices[4], matrices[5]
    )
    d_wf, d_wo, d_wg, d_wk, d_wv, d_wh, d_wp = (part[None] for part in summed)

    def row(index):
        return vec[index : index + 1]

    return (
        out[None], back[None],
        row(0), row(1), row(2), row(3), row(4), row(5), row(6),
        d_wk, d_wv, d_wg, d_wo,
        row(7), row(8), row(9), row(10),
        d_wh, d_wp, d_wf,
    )


def solution(mesh):
    tokens = P(None, "dp", None)
    vector = P("section", None)
    matrix = P("section", None, None)
    result = P("section", None, "dp", None)
    vector_grad = P("section", "dp")
    matrix_grad = P("section", "dp", None)
    return jax.shard_map(
        per_device,
        mesh=mesh,
        in_specs=(tokens, tokens, P())
        + (vector,) * 7 + (matrix,) * 4 + (vector,) * 4 + (matrix,) * 3,
        out_specs=(result, result)
        + (vector_grad,) * 7 + (matrix_grad,) * 4 + (vector_grad,) * 4 + (matrix_grad,) * 3,
        check_vma=False,
    )
```

```python
from functools import partial

import jax
import jax.numpy as jnp
from jax import lax
from jax.experimental import pallas as pl
from jax.experimental.pallas import tpu as pltpu
from jax.sharding import PartitionSpec as P

EPS = 1e-05
MESH = pl.DeviceIdType.MESH
RB = 64
PARTS = 1
VECTORS = 16
F32 = jnp.float32
BF16 = jnp.bfloat16


def dot_nn(left, right):
    return jnp.dot(left, right, preferred_element_type=F32)


def dot_nt(left, right):
    return lax.dot_general(left, right, (((1,), (1,)), ((), ())), preferred_element_type=F32)


def dot_tn(left, right):
    return lax.dot_general(left, right, (((0,), (0,)), ((), ())), preferred_element_type=F32)


def sigmoid(v):
    return 1.0 / (1.0 + jnp.exp(-v))


def normalise(source):
    centred = source - jnp.mean(source, axis=-1, keepdims=True)
    spread = lax.rsqrt(jnp.mean(centred * centred, axis=-1, keepdims=True) + EPS)
    return centred * spread, spread


def moved_down(rows, first):
    place = lax.broadcasted_iota(jnp.int32, rows.shape, 0)
    return jnp.where(place == 0, first, pltpu.roll(rows, 1, 0))


def moved_up(rows, last):
    count = rows.shape[0]
    place = lax.broadcasted_iota(jnp.int32, rows.shape, 0)
    return jnp.where(place == count - 1, last, pltpu.roll(rows, count - 1, 0))


def fold(rows):
    total = rows[0:8]
    for at in range(8, rows.shape[0], 8):
        total = total + rows[at : at + 8]
    return total


def relay_kernel(sections, peers, split_vectors, *refs):
    (
        spans, x_in, top_in,
        gain1, bias1, mix_k, mix_v, mix_g, log_rate, extra, gain2, bias2, mix_h, mix_f,
        wk_in, wv_in, wg_in, wo_in, wh_in, wp_in, wf_in,
        out, back, vec_out, lk, lv, lg, lgt, lf, dk, dv, dg, datt, dsv, dproj, lh_all,
        wk_t, wv_t, wg_t, wo_t, wf_t, wp_t, wh_t,
        lh, sq, dh, turned,
        wk, wv, wg, wo, wh, wp, wf,
        xs, hx, dys, kk, vv, sg, sa, sb, mid, hmid, proj, sv, act, halo1, halo2,
        e0, e1, low_mask, up_mask, split, acc, t1, t2, t3,
        states, back_states, de2, de1, sum_row, sum_back, send_de2, send_de1, vg, vgs, vgr,
        w_sem, x_sem, top_sem, s_h0, s_x, s_hx, s_st, s_mid, s_dy, s_de2, s_bst, s_de1, s_vg,
        r_x, r_hx, r_st, r_mid, r_dy, r_de2, r_bst, r_de1, r_vg,
        s_lh, r_lh, own_sem, turn_sem, back_sem,
    ) = refs
    me_s = lax.axis_index("section")
    me = lax.axis_index("dp")
    batches, row_count, width = x_in.shape
    hidden = wh.shape[1]
    chunks = row_count // RB
    base = me * row_count

    def at(section, index):
        return (section, index)

    barrier = pltpu.get_barrier_semaphore()

    def greet(section, index):
        pl.semaphore_signal(barrier, inc=1, device_id=at(section, index), device_id_type=MESH)

    def greet_peer(k, carry):
        @pl.when(k != me)
        def _():
            greet(me_s, k)

        return carry

    lax.fori_loop(0, peers, greet_peer, 0)
    has_next = me_s + 1 < sections
    has_prior = me_s > 0
    has_right = me + 1 < peers
    has_left = me > 0

    @pl.when(has_next)
    def _():
        greet(me_s + 1, me)

    @pl.when(has_prior)
    def _():
        greet(me_s - 1, me)

    @pl.when(has_next & has_right)
    def _():
        greet(me_s + 1, me + 1)

    @pl.when(has_prior & has_left)
    def _():
        greet(me_s - 1, me - 1)

    weight_copies = [
        pltpu.make_async_copy(source, target, w_sem.at[index])
        for index, (source, target) in enumerate(
            ((wk_in, wk), (wv_in, wv), (wg_in, wg), (wo_in, wo), (wf_in, wf), (wh_in, wh), (wp_in, wp))
        )
    ]

    @pl.when(me_s == 0)
    def _():
        pltpu.make_async_copy(x_in, xs, x_sem).start()

    for copy in weight_copies:
        copy.start()

    @pl.when(me_s == sections - 1)
    def _():
        pltpu.make_async_copy(top_in, dys, top_sem).start()

    rate = jnp.exp(log_rate[...])
    decay_block = jnp.exp(-rate * row_count)
    grow_block = jnp.exp(rate * row_count)

    def starts_of(m):
        found = []
        total = jnp.int32(0)
        for j in range(spans.shape[1]):
            found.append(total)
            total = total + spans[m, j]
        return found

    def segment(position, starts):
        total = jnp.where(position >= starts[0], 1, 0)
        for start in starts[1:]:
            total = total + jnp.where(position >= start, 1, 0)
        return total

    def column(i):
        return base + i * RB + lax.broadcasted_iota(jnp.int32, (RB, 1), 0)

    def keep_of(position, starts):
        return jnp.where(segment(position, starts) == segment(position - 1, starts), 1.0, 0.0)

    def fill_powers(i, carry):
        place = (i * RB + lax.broadcasted_iota(jnp.int32, (RB, width), 0)).astype(F32)
        e0[pl.ds(pl.multiple_of(i * RB, RB), RB), :] = jnp.exp(-place * rate)
        e1[pl.ds(pl.multiple_of(i * RB, RB), RB), :] = jnp.exp((place - (row_count - 1.0)) * rate)
        return carry

    lax.fori_loop(0, chunks, fill_powers, 0)
    for m in range(batches):
        starts = starts_of(m)
        row_at = lax.broadcasted_iota(jnp.int32, (row_count, row_count), 0)
        column_at = lax.broadcasted_iota(jnp.int32, (row_count, row_count), 1)
        same = segment(base + row_at, starts) == segment(base + column_at, starts)
        lower = jnp.where(same & (column_at < row_at), 1.0, 0.0).astype(BF16)
        upper = jnp.where(same & (column_at > row_at), 1.0, 0.0).astype(BF16)
        low_mask[m, :, 0:row_count] = lower
        low_mask[m, :, row_count:] = lower
        up_mask[m, :, 0:row_count] = upper
        up_mask[m, :, row_count:] = upper
    vg[...] = jnp.zeros_like(vg)

    @pl.when(me == 0)
    def _():
        hx[...] = jnp.zeros_like(hx)
        hmid[...] = jnp.zeros_like(hmid)

    @pl.when(me == peers - 1)
    def _():
        de1[...] = jnp.zeros_like(de1)
        de2[...] = jnp.zeros_like(de2)

    greeted = (
        peers - 1
        + jnp.where(has_next, 1, 0)
        + jnp.where(has_prior, 1, 0)
        + jnp.where(has_next & has_right, 1, 0)
        + jnp.where(has_prior & has_left, 1, 0)
    )
    pl.semaphore_wait(barrier, greeted)

    def remote(source, target, send, receive, section, index):
        return pltpu.make_async_remote_copy(
            src_ref=source, dst_ref=target, send_sem=send, recv_sem=receive,
            device_id=at(section, index), device_id_type=MESH,
        )

    right = jnp.minimum(me + 1, peers - 1)
    left = jnp.maximum(me - 1, 0)
    above = jnp.minimum(me_s + 1, sections - 1)
    below = jnp.maximum(me_s - 1, 0)
    tail = pl.ds(row_count - 16, 16)
    tail8 = pl.ds(row_count - 8, 8)

    def start_halo(m):
        return remote(x_in.at[m, tail], hx.at[m], s_h0.at[m], r_hx.at[m], me_s, right)

    def part_of(j):
        return pl.ds(pl.multiple_of(j * (width // PARTS), width // PARTS), width // PARTS)

    def result_copy(m, j):
        return remote(
            out.at[m, :, part_of(j)], xs.at[m, :, part_of(j)],
            s_x.at[m, j], r_x.at[m, j], above, me,
        )

    def each_part(action):
        def turn(j, carry):
            action(j)
            return carry

        lax.fori_loop(0, PARTS, turn, 0)

    def result_halo(m):
        return remote(out.at[m, tail], hx.at[m], s_hx.at[m], r_hx.at[m], above, right)

    def middle_halo(m):
        return remote(mid.at[m, tail8], hmid.at[m], s_mid.at[m], r_mid.at[m], me_s, right)

    def state_copy(m, k, slot):
        return remote(sum_row.at[m], states.at[m, slot], s_st.at[m, k], r_st.at[m, slot], me_s, k)

    def back_copy(m, i):
        rows = pl.ds(pl.multiple_of(i * RB, RB), RB)
        return remote(
            back.at[m, rows], dys.at[m, rows], s_dy.at[m, i], r_dy.at[m, i], below, me
        )

    def each_chunk(action):
        def turn(i, carry):
            action(i)
            return carry

        lax.fori_loop(0, chunks, turn, 0)

    def second_copy(m):
        return remote(send_de2.at[m], de2.at[m], s_de2.at[m], r_de2.at[m], me_s, left)

    def first_copy(m):
        return remote(send_de1.at[m], de1.at[m], s_de1.at[m], r_de1.at[m], me_s, left)

    def back_state_copy(m, k, slot):
        return remote(
            sum_back.at[m], back_states.at[m, slot], s_bst.at[m, k], r_bst.at[m, slot], me_s, k
        )

    chip, core = me // 2, me % 2
    chips = peers // 2

    def gather_copy(m, k, slot):
        return remote(
            lh.at[m], lh_all.at[slot, m], s_lh.at[m, k], r_lh.at[m, slot], me_s, 2 * k + core
        )

    def own_copy(m):
        return pltpu.make_async_copy(lh.at[m], lh_all.at[chip, m], own_sem.at[m])

    def each_chip(action):
        def turn(k, carry):
            @pl.when(k != chip)
            def _():
                action(k)

            return carry

        lax.fori_loop(0, chips, turn, 0)

    def start_gather(m):
        own_copy(m).start()
        each_chip(lambda k: gather_copy(m, k, chip).start())

    def start_gathers(early):
        for m in range(batches):
            in_gap = me_s + 1 + m < sections

            @pl.when(in_gap if early else jnp.logical_not(in_gap))
            def _(m=m):
                start_gather(m)

    def end_gather(m):
        own_copy(m).wait()
        each_chip(lambda k: gather_copy(m, k, chip).wait_send())
        each_chip(lambda k: gather_copy(m, k, k).wait_recv())

    @pl.when((me_s == 0) & has_right)
    def _():
        for m in range(batches):
            start_halo(m).start()

    @pl.when(me_s == 0)
    def _():
        pltpu.make_async_copy(x_in, xs, x_sem).wait()

    turns = (
        (wk, wk_t), (wv, wv_t), (wg, wg_t), (wo, wo_t), (wf, wf_t), (wh, wh_t), (wp, wp_t)
    )
    returns = (
        (wk_t, wk), (wv_t, wv), (wg_t, wg), (wo_t, wo), (wf_t, wf), (wp_t, wh), (wh_t, wp)
    )
    edge = turned.shape[1]

    def transpose_all(fresh):
        for index, (source, target) in enumerate(turns):
            if fresh:
                weight_copies[index].wait()
            tall = source.shape[0] // edge
            blocks = tall * (source.shape[1] // edge)

            def place(n, source=source, target=target, tall=tall):
                down = pl.ds(pl.multiple_of(n % tall * edge, edge), edge)
                along = pl.ds(pl.multiple_of(n // tall * edge, edge), edge)
                slot = n % 2
                return (
                    source.at[down, along],
                    turned.at[slot],
                    pltpu.make_async_copy(turned.at[slot], target.at[along, down], turn_sem.at[slot]),
                )

            def turn(n, carry, place=place):
                piece, buffer, copy = place(n)
                pl.when(n >= 2)(copy.wait)
                buffer[...] = piece[...].T
                copy.start()
                return carry

            lax.fori_loop(0, blocks, turn, 0)
            for n in range(blocks - 2, blocks):
                place(n)[2].wait()

    def return_copy(index):
        source, target = returns[index]
        return pltpu.make_async_copy(source, target, back_sem.at[index])

    is_late = 2 * me_s >= sections

    def release(m, index):
        @pl.when(is_late & (m == batches - 1))
        def _():
            return_copy(index).start()

    def weight_ready(m, index, fresh=True):
        @pl.when((m == 0) & jnp.logical_not(is_late))
        def _():
            weight_copies[index].wait()

    def span_of(i):
        return pl.ds(pl.multiple_of(i * RB, RB), RB)

    def forward(m, carry):
        starts = starts_of(m)

        @pl.when(has_prior)
        def _():
            each_part(lambda j: result_copy(m, j).wait_recv())

        @pl.when(has_left)
        def _():
            start_halo(m).wait_recv()

        halo_rows, _ = normalise(hx[m].astype(F32))
        halo_rows = halo_rows * gain1[...] + bias1[...]
        halo1[m] = halo_rows[8:16]

        def mix_in(i, last):
            rows = span_of(i)
            normed, _ = normalise(xs[m, rows, :].astype(F32))
            normed = normed * gain1[...] + bias1[...]
            earlier = moved_down(normed, last) * keep_of(column(i), starts)
            gap = normed - earlier
            lk[m, rows, :] = (earlier + gap * mix_k[...]).astype(BF16)
            lv[m, rows, :] = (earlier + gap * mix_v[...]).astype(BF16)
            lg[m, rows, :] = (earlier + gap * mix_g[...]).astype(BF16)
            return normed[RB - 1 : RB]

        lax.fori_loop(0, chunks, mix_in, halo_rows[15:16])

        weight_ready(m, 0)
        weight_ready(m, 1)
        kk[m] = dot_nn(lk[m], wk[...])
        release(m, 0)
        vv[m] = dot_nn(lv[m], wv[...])
        release(m, 1)
        end_segment = segment(base + row_count - 1, starts)

        def spread_in(i, totals):
            rows = span_of(i)
            weight = jnp.exp(kk[m, rows, :]) * e1[rows, :]
            weighted = weight * vv[m, rows, :]
            high_a = weighted.astype(BF16)
            high_b = weight.astype(BF16)
            split[rows, 0:width] = high_a
            split[rows, width:] = high_b
            low = pl.ds(pl.multiple_of(row_count + i * RB, RB), RB)
            split[low, 0:width] = (weighted - high_a.astype(F32)).astype(BF16)
            split[low, width:] = (weight - high_b.astype(F32)).astype(BF16)
            chosen = segment(column(i), starts) == end_segment
            return (
                totals[0] + fold(jnp.where(chosen, weighted, 0.0)),
                totals[1] + fold(jnp.where(chosen, weight, 0.0)),
            )

        nothing = jnp.zeros((8, width), F32)
        total_a, total_b = lax.fori_loop(0, chunks, spread_in, (nothing, nothing))
        sum_row[m, 0:1] = jnp.sum(total_a, axis=0, keepdims=True)
        sum_row[m, 1:2] = jnp.sum(total_b, axis=0, keepdims=True)

        def send_state(k, carry):
            state_copy(m, k, me).start()
            return carry

        lax.fori_loop(me + 1, peers, send_state, 0)

        weight_ready(m, 2)
        sg[m] = dot_nn(lg[m], wg[...])
        release(m, 2)
        acc[...] = dot_nn(low_mask[m], split[...])

        def receive_state(k, held):
            state_copy(m, k, k).wait_recv()
            unbroken = segment(k * row_count - 1, starts) == segment(
                (k + 1) * row_count - 1, starts
            )
            passing = jnp.where(unbroken, 1.0, 0.0) * decay_block
            return (
                passing * held[0] + states[m, k, 0:1],
                passing * held[1] + states[m, k, 1:2],
            )

        none = jnp.zeros((1, width), F32)
        enter_a, enter_b = lax.fori_loop(0, me, receive_state, (none, none))
        prior_segment = segment(base - 1, starts)

        def mix_states(i, carry):
            rows = span_of(i)
            falling = e0[rows, :]
            chosen = jnp.where(segment(column(i), starts) == prior_segment, 1.0, 0.0)
            grown = falling * grow_block
            held = falling * chosen
            state_a = grown * acc[rows, 0:width] + held * enter_a
            state_b = grown * acc[rows, width:] + held * enter_b
            sa[m, rows, :] = state_a
            sb[m, rows, :] = state_b
            present = jnp.exp(extra[...] + kk[m, rows, :])
            gate = sigmoid(sg[m, rows, :])
            sg[m, rows, :] = gate
            found = (state_a + present * vv[m, rows, :]) / (state_b + present)
            lgt[m, rows, :] = (gate * found).astype(BF16)
            return carry

        lax.fori_loop(0, chunks, mix_states, 0)

        weight_ready(m, 3)
        mid[m] = xs[m].astype(F32) + dot_nn(lgt[m], wo[...])
        release(m, 3)

        @pl.when(has_right)
        def _():
            middle_halo(m).start()

        def mix_second(i, last):
            rows = span_of(i)
            normed, _ = normalise(mid[m, rows, :])
            normed = normed * gain2[...] + bias2[...]
            earlier = moved_down(normed, last) * keep_of(column(i), starts)
            gap = normed - earlier
            lh[m, rows, :] = (earlier + gap * mix_h[...]).astype(BF16)
            lf[m, rows, :] = (earlier + gap * mix_f[...]).astype(BF16)
            return normed[RB - 1 : RB]

        lax.fori_loop(0, chunks, mix_second, none)

        @pl.when(has_left)
        def _():
            middle_halo(m).wait_recv()

        halo_rows, _ = normalise(hmid[m])
        halo_rows = halo_rows * gain2[...] + bias2[...]
        halo2[m] = halo_rows
        mix_second(0, halo_rows[7:8])

        for index in range(4, 7):
            weight_ready(m, index)
        sv[m] = dot_nn(lf[m], wf[...])
        release(m, 4)

        def widen(j, carry):
            columns = pl.ds(pl.multiple_of(j * width, width), width)
            active = jnp.maximum(dot_nn(lh[m], wh[:, columns]), 0.0)
            act[m, :, columns] = active.astype(BF16)
            sq[m, :, columns] = (active * active).astype(BF16)
            return carry

        lax.fori_loop(0, hidden // width, widen, 0)
        release(m, 5)

        def finish(j, carry):
            columns = part_of(j)
            found = dot_nn(sq[m], wp[:, columns])
            proj[m, :, columns] = found
            sieve = sigmoid(sv[m, :, columns])
            sv[m, :, columns] = sieve
            out[m, :, columns] = (mid[m, :, columns] + sieve * found).astype(BF16)

            @pl.when(has_next)
            def _():
                result_copy(m, j).start()

            return carry

        lax.fori_loop(0, PARTS, finish, 0)
        release(m, 6)

        @pl.when(has_next & has_right)
        def _():
            result_halo(m).start()

        return carry

    pl.when(is_late)(lambda: transpose_all(True))
    lax.fori_loop(0, batches, forward, 0)

    @pl.when(jnp.logical_not(is_late))
    def _():
        transpose_all(False)
        for index in range(7):
            return_copy(index).start()

    start_gathers(True)

    def add_vector(index, value):
        vg[index] += fold(value)

    @pl.when(me_s == sections - 1)
    def _():
        pltpu.make_async_copy(top_in, dys, top_sem).wait()

    def turned_ready(m, index):
        @pl.when(m == 0)
        def _():
            return_copy(index).wait()

    def backward(m, carry):
        starts = starts_of(m)
        none = jnp.zeros((1, width), F32)

        @pl.when(has_next)
        def _():
            each_chunk(lambda i: back_copy(m, i).wait_recv())

        def open_back(i, carry):
            rows = span_of(i)
            incoming = dys[m, rows, :].astype(F32)
            sieve = sv[m, rows, :]
            gained = incoming * sieve
            dproj[m, rows, :] = gained.astype(BF16)
            dsv[m, rows, :] = (gained * proj[m, rows, :] * (1.0 - sieve)).astype(BF16)
            return carry

        lax.fori_loop(0, chunks, open_back, 0)
        t1[...] = jnp.zeros_like(t1)
        turned_ready(m, 5)
        turned_ready(m, 6)

        def narrow(j, carry):
            columns = pl.ds(pl.multiple_of(j * width, width), width)
            grown = dot_nn(dproj[m], wh[:, columns])
            dh[m, :, columns] = (grown * 2.0 * act[m, :, columns].astype(F32)).astype(BF16)
            t1[...] += dot_nn(dh[m, :, columns], wp[columns, :])
            return carry

        lax.fori_loop(0, hidden // width, narrow, 0)
        turned_ready(m, 4)
        t2[...] = dot_nn(dsv[m], wf[...])

        def second_earlier(rows, position):
            whole = t1[rows, :] * (1.0 - mix_h[...]) + t2[rows, :] * (1.0 - mix_f[...])
            return whole * keep_of(position, starts)

        eight = lax.broadcasted_iota(jnp.int32, (8, 1), 0)
        send_de2[m] = second_earlier(pl.ds(0, 8), base + eight)

        @pl.when(has_left)
        def _():
            second_copy(m).start()

        def back_second(i, last, following):
            rows = span_of(i)
            spare, spread = normalise(mid[m, rows, :])
            normed = spare * gain2[...] + bias2[...]
            kept = keep_of(column(i), starts)
            gap = normed - moved_down(normed, last) * kept
            from_h = t1[rows, :]
            from_f = t2[rows, :]
            add_vector(9, from_h * gap)
            add_vector(10, from_f * gap)
            straight = from_h * mix_h[...] + from_f * mix_f[...]
            earlier = (from_h + from_f - straight) * kept
            d_normed = straight + moved_up(earlier, following)
            add_vector(7, d_normed * spare)
            add_vector(8, d_normed)
            scaled = d_normed * gain2[...]
            mean_one = jnp.mean(scaled, axis=-1, keepdims=True)
            mean_two = jnp.mean(scaled * spare, axis=-1, keepdims=True)
            d_mid = dys[m, rows, :].astype(F32) + spread * (scaled - mean_one - spare * mean_two)
            t3[rows, :] = d_mid
            datt[m, rows, :] = d_mid.astype(BF16)
            return normed[RB - 1 : RB]

        def following_second(i):
            start = pl.multiple_of((i + 1) * RB, RB)
            return second_earlier(pl.ds(start, 8), base + start + eight)[0:1]

        last = lax.fori_loop(
            0, chunks - 1,
            lambda i, last: back_second(i, last, following_second(i)),
            halo2[m, 7:8],
        )

        @pl.when(has_right)
        def _():
            second_copy(m).wait_recv()

        back_second(chunks - 1, last, de2[m, 0:1])
        turned_ready(m, 3)
        t1[...] = dot_nn(datt[m], wo[...])
        open_segment = segment(base, starts)

        def back_states_in(i, totals):
            rows = span_of(i)
            d_gated = t1[rows, :]
            gate = sg[m, rows, :]
            keys = kk[m, rows, :]
            values = vv[m, rows, :]
            present = jnp.exp(extra[...] + keys)
            inverse = 1.0 / (sb[m, rows, :] + present)
            found = (sa[m, rows, :] + present * values) * inverse
            d_found = d_gated * gate
            dg[m, rows, :] = (d_found * found * (1.0 - gate)).astype(BF16)
            d_a = d_found * inverse
            d_b = -d_a * found
            d_key = (d_a * values + d_b) * present
            add_vector(6, d_key)
            t1[rows, :] = d_key
            t2[rows, :] = d_a * present
            falling = e0[rows, :]
            scaled_a = d_a * falling
            scaled_b = d_b * falling
            high_a = scaled_a.astype(BF16)
            high_b = scaled_b.astype(BF16)
            split[rows, 0:width] = high_a
            split[rows, width:] = high_b
            low = pl.ds(pl.multiple_of(row_count + i * RB, RB), RB)
            split[low, 0:width] = (scaled_a - high_a.astype(F32)).astype(BF16)
            split[low, width:] = (scaled_b - high_b.astype(F32)).astype(BF16)
            chosen = segment(column(i), starts) == open_segment
            return (
                totals[0] + fold(jnp.where(chosen, scaled_a, 0.0)),
                totals[1] + fold(jnp.where(chosen, scaled_b, 0.0)),
            )

        nothing = jnp.zeros((8, width), F32)
        total_a, total_b = lax.fori_loop(0, chunks, back_states_in, (nothing, nothing))
        sum_back[m, 0:1] = jnp.sum(total_a, axis=0, keepdims=True)
        sum_back[m, 1:2] = jnp.sum(total_b, axis=0, keepdims=True)

        def send_state(k, carry):
            back_state_copy(m, k, me).start()
            return carry

        lax.fori_loop(0, me, send_state, 0)
        acc[...] = dot_nn(up_mask[m], split[...])

        def receive_state(turn, held):
            k = peers - 1 - turn
            back_state_copy(m, k, k).wait_recv()
            first = segment(k * row_count, starts)
            unbroken = first == segment((k + 1) * row_count - 1, starts)
            joined = jnp.where(first == segment(k * row_count - 1, starts), 1.0, 0.0)
            passing = jnp.where(unbroken, 1.0, 0.0) * decay_block
            return (
                joined * (passing * held[0] + back_states[m, k, 0:1]),
                joined * (passing * held[1] + back_states[m, k, 1:2]),
            )

        enter_a, enter_b = lax.fori_loop(0, peers - 1 - me, receive_state, (none, none))
        end_segment = segment(base + row_count - 1, starts)

        def back_keys(i, carry):
            rows = span_of(i)
            rising = e1[rows, :]
            chosen = jnp.where(segment(column(i), starts) == end_segment, 1.0, 0.0)
            grown = rising * grow_block
            held = rising * chosen
            d_a = grown * acc[rows, 0:width] + held * enter_a
            d_b = grown * acc[rows, width:] + held * enter_b
            add_vector(5, d_a * sa[m, rows, :] + d_b * sb[m, rows, :])
            weight = jnp.exp(kk[m, rows, :])
            dv[m, rows, :] = (t2[rows, :] + d_a * weight).astype(BF16)
            dk[m, rows, :] = (t1[rows, :] + (d_a * vv[m, rows, :] + d_b) * weight).astype(BF16)
            return carry

        lax.fori_loop(0, chunks, back_keys, 0)
        for index in range(3):
            turned_ready(m, index)
        t1[...] = dot_nn(dk[m], wk[...])
        t2[...] = dot_nn(dv[m], wv[...])
        acc[:, 0:width] = dot_nn(dg[m], wg[...])

        def first_earlier(rows, position):
            whole = (
                t1[rows, :] * (1.0 - mix_k[...])
                + t2[rows, :] * (1.0 - mix_v[...])
                + acc[rows, 0:width] * (1.0 - mix_g[...])
            )
            return whole * keep_of(position, starts)

        send_de1[m] = first_earlier(pl.ds(0, 8), base + eight)

        @pl.when(has_left)
        def _():
            first_copy(m).start()

        def back_first(i, last, following):
            rows = span_of(i)
            spare, spread = normalise(xs[m, rows, :].astype(F32))
            normed = spare * gain1[...] + bias1[...]
            kept = keep_of(column(i), starts)
            gap = normed - moved_down(normed, last) * kept
            from_k = t1[rows, :]
            from_v = t2[rows, :]
            from_g = acc[rows, 0:width]
            add_vector(2, from_k * gap)
            add_vector(3, from_v * gap)
            add_vector(4, from_g * gap)
            straight = from_k * mix_k[...] + from_v * mix_v[...] + from_g * mix_g[...]
            earlier = (from_k + from_v + from_g - straight) * kept
            d_normed = straight + moved_up(earlier, following)
            add_vector(0, d_normed * spare)
            add_vector(1, d_normed)
            scaled = d_normed * gain1[...]
            mean_one = jnp.mean(scaled, axis=-1, keepdims=True)
            mean_two = jnp.mean(scaled * spare, axis=-1, keepdims=True)
            found = t3[rows, :] + spread * (scaled - mean_one - spare * mean_two)
            back[m, rows, :] = found.astype(BF16)

            @pl.when(has_prior)
            def _():
                back_copy(m, i).start()

            return normed[RB - 1 : RB]

        def following_first(i):
            start = pl.multiple_of((i + 1) * RB, RB)
            return first_earlier(pl.ds(start, 8), base + start + eight)[0:1]

        last = lax.fori_loop(
            0, chunks - 1,
            lambda i, last: back_first(i, last, following_first(i)),
            halo1[m, 7:8],
        )

        @pl.when(has_right)
        def _():
            first_copy(m).wait_recv()

        back_first(chunks - 1, last, de1[m, 0:1])

        return carry

    lax.fori_loop(0, batches, backward, 0)
    pl.when(has_prior)(lambda: each_chunk(lambda i: back_copy(batches - 1, i).wait_send()))
    start_gathers(False)

    vgs[...] = jnp.sum(vg[...], axis=1)
    vgs[5:6] = vgs[5:6] * (-rate * jnp.exp(-rate))
    share = vgr.shape[2]

    def part(k):
        if split_vectors:
            return vgs.at[:, pl.ds(pl.multiple_of(k * share, share), share)]
        return vgs

    def vector_copy(k, slot):
        return remote(part(k), vgr.at[slot], s_vg.at[k], r_vg.at[slot], me_s, k)

    def each_peer(action):
        def turn(k, carry):
            @pl.when(k != me)
            def _():
                action(k)

            return carry

        lax.fori_loop(0, peers, turn, 0)

    each_peer(lambda k: vector_copy(k, me).start())
    if split_vectors:
        vec_out[...] = vgs[:, pl.ds(pl.multiple_of(me * share, share), share)]
    else:
        vec_out[...] = vgs[...]

    def collect(k):
        vector_copy(k, k).wait_recv()
        vec_out[...] += vgr[k]

    each_peer(collect)

    each_peer(lambda k: vector_copy(k, me).wait_send())

    def close(m, carry):
        @pl.when((me_s == 0) & has_right)
        def _():
            start_halo(m).wait_send()

        @pl.when(has_next)
        def _():
            each_part(lambda j: result_copy(m, j).wait_send())

        @pl.when(has_next & has_right)
        def _():
            result_halo(m).wait_send()

        @pl.when(has_right)
        def _():
            middle_halo(m).wait_send()

        @pl.when(has_left)
        def _():
            second_copy(m).wait_send()
            first_copy(m).wait_send()

        @pl.when(has_prior)
        def _():
            pl.when(m + 1 < batches)(lambda: each_chunk(lambda i: back_copy(m, i).wait_send()))

        def ended(k, carry):
            state_copy(m, k, me).wait_send()
            return carry

        lax.fori_loop(me + 1, peers, ended, 0)
        end_gather(m)

        def ended_back(k, carry):
            back_state_copy(m, k, me).wait_send()
            return carry

        lax.fori_loop(0, me, ended_back, 0)
        return carry

    lax.fori_loop(0, batches, close, 0)


def relay(sections, peers, x, top, spans, vectors, matrices):
    batches, rows, width = x.shape
    hidden = matrices[4].shape[1]
    share = width // peers
    split_vectors = share % 128 == 0
    if not split_vectors:
        share = width
    shape = jax.ShapeDtypeStruct
    low = shape((batches, rows, width), BF16)
    square = shape((width, width), BF16)
    vmem = pl.BlockSpec(memory_space=pltpu.VMEM)
    anywhere = pl.BlockSpec(memory_space=pl.ANY)
    dma = pltpu.SemaphoreType.DMA

    def narrow(kind):
        return pltpu.VMEM((batches, rows, width), kind)

    return pl.pallas_call(
        partial(relay_kernel, sections, peers, split_vectors),
        out_shape=(
            low, low, shape((VECTORS, share), F32),
            low, low, low, low, low,
            low, low, low, low, low, low,
            shape((peers // 2, batches, rows, width), BF16),
            square, square, square, square, square,
            shape((width, hidden), BF16), shape((hidden, width), BF16),
        ),
        in_specs=[pl.BlockSpec(memory_space=pltpu.SMEM), anywhere, anywhere]
        + [vmem] * 11
        + [anywhere] * 7,
        out_specs=[vmem] * 14 + [anywhere] * 8,
        scratch_shapes=[
            narrow(BF16), pltpu.VMEM((batches, rows, hidden), BF16),
            pltpu.VMEM((batches, rows, hidden), BF16), pltpu.VMEM((2, 512, 512), BF16),
        ]
        + [pltpu.VMEM(matrix.shape, BF16) for matrix in matrices_order(matrices)]
        + [
            narrow(BF16), pltpu.VMEM((batches, 16, width), BF16), narrow(BF16),
            narrow(F32), narrow(F32), narrow(F32), narrow(F32), narrow(F32), narrow(F32),
            pltpu.VMEM((batches, 8, width), F32), narrow(F32), narrow(F32),
            pltpu.VMEM((batches, rows, hidden), BF16),
            pltpu.VMEM((batches, 8, width), F32), pltpu.VMEM((batches, 8, width), F32),
            pltpu.VMEM((rows, width), F32), pltpu.VMEM((rows, width), F32),
            pltpu.VMEM((batches, rows, 2 * rows), BF16), pltpu.VMEM((batches, rows, 2 * rows), BF16),
            pltpu.VMEM((2 * rows, 2 * width), BF16), pltpu.VMEM((rows, 2 * width), F32),
            pltpu.VMEM((rows, width), F32), pltpu.VMEM((rows, width), F32), pltpu.VMEM((rows, width), F32),
            pltpu.VMEM((batches, peers, 2, width), F32), pltpu.VMEM((batches, peers, 2, width), F32),
            pltpu.VMEM((batches, 8, width), F32), pltpu.VMEM((batches, 8, width), F32),
            pltpu.VMEM((batches, 2, width), F32), pltpu.VMEM((batches, 2, width), F32),
            pltpu.VMEM((batches, 8, width), F32), pltpu.VMEM((batches, 8, width), F32),
            pltpu.VMEM((VECTORS, 8, width), F32), pltpu.VMEM((VECTORS, width), F32),
            pltpu.VMEM((peers, VECTORS, share), F32),
            dma((7,)), dma, dma,
            dma((batches,)), dma((batches, PARTS)), dma((batches,)), dma((batches, peers)),
            dma((batches,)), dma((batches, rows // RB)), dma((batches,)), dma((batches, peers)),
            dma((batches,)), dma((peers,)),
            dma((batches, PARTS)), dma((batches,)), dma((batches, peers)), dma((batches,)),
            dma((batches, rows // RB)), dma((batches,)), dma((batches, peers)), dma((batches,)),
            dma((peers,)),
            dma((batches, peers // 2)), dma((batches, peers // 2)), dma((batches,)),
            dma((2,)), dma((7,)),
        ],
        compiler_params=pltpu.CompilerParams(
            collective_id=0, has_side_effects=True, vmem_limit_bytes=63 * 2**20
        ),
        name="relay",
    )(spans, x, top, *vectors, *matrices_order(matrices))


def matrices_order(matrices):
    wk, wv, wg, wo, wh, wp, wf = matrices
    return (wk, wv, wg, wo, wh, wp, wf)


def sum_kernel(peers, *refs):
    left_in, right_in = refs[0:5], refs[5:10]
    lh_in, dp_in, wh_in, wp_in = refs[10:14]
    outs, wh_out, wp_out = refs[14:19], refs[19], refs[20]
    (
        lefts, rights, whole, own, pair_out, going_right, going_left,
        lh, dp, wh, wp, act, wide, hid_out, hid_in, proj_out, proj_in,
        left_sem, right_sem, lh_sem, dp_sem, wh_sem, wp_sem,
        s_pair, r_pair, s_right, r_right, s_left, r_left, s_hid, r_hid, s_proj, r_proj,
        s_ahead, s_behind, r_rows,
    ) = refs[21:]
    count = len(left_in)
    me_s = lax.axis_index("section")
    me = lax.axis_index("dp")
    chips = peers // 2
    chip, core = me // 2, me % 2
    sibling = me + 1 - 2 * core
    blocks, share = chips, own.shape[2]
    columns = wh.shape[2]
    has_right = chip + 1 < chips
    has_left = chip > 0
    after = jnp.minimum(me + 2, peers - 1)
    before = jnp.maximum(me - 2, 0)

    barrier = pltpu.get_barrier_semaphore()

    def greet(index):
        pl.semaphore_signal(barrier, inc=1, device_id=(me_s, index), device_id_type=MESH)

    greet(sibling)

    @pl.when(has_right)
    def _():
        greet(after)

    @pl.when(has_left)
    def _():
        greet(before)

    for w in range(count):
        pltpu.make_async_copy(left_in[w], lefts.at[w], left_sem.at[w]).start()
        pltpu.make_async_copy(right_in[w], rights.at[w], right_sem.at[w]).start()
    lh_copy = pltpu.make_async_copy(lh_in, lh, lh_sem)
    rows = dp_in.shape[0]
    own_rows = pl.ds(pl.multiple_of(chip * rows, rows), rows)
    dp_copy = pltpu.make_async_copy(dp_in, dp.at[own_rows], dp_sem)
    dp_copy.start()
    lh_copy.start()

    def wh_copy(j, slot):
        return pltpu.make_async_copy(
            wh_in.at[:, pl.ds(pl.multiple_of(j * columns, columns), columns)],
            wh.at[slot], wh_sem.at[slot],
        )

    def wp_copy(j, slot):
        return pltpu.make_async_copy(
            wp_in.at[pl.ds(pl.multiple_of(j * columns, columns), columns)],
            wp.at[slot], wp_sem.at[slot],
        )

    wh_copy(0, 0).start()
    wp_copy(0, 0).start()
    pl.semaphore_wait(
        barrier, 1 + jnp.where(has_right, 1, 0) + jnp.where(has_left, 1, 0)
    )

    def remote(source, target, send, receive, index):
        return pltpu.make_async_remote_copy(
            src_ref=source, dst_ref=target, send_sem=send, recv_sem=receive,
            device_id=(me_s, index), device_id_type=MESH,
        )

    def pair_copy(w):
        return remote(pair_out.at[w], own.at[w], s_pair.at[w], r_pair.at[w], sibling)

    def rows_of(block, parity):
        return pl.ds(pl.multiple_of((2 * block + parity) * share, share), share)

    def prepare(w):
        pltpu.make_async_copy(lefts.at[w], lefts.at[w], left_sem.at[w]).wait()
        pltpu.make_async_copy(rights.at[w], rights.at[w], right_sem.at[w]).wait()
        slot = w % 2
        whole[slot] = dot_tn(lefts[w], rights[w])

        def divide(q, carry):
            pair_out[w, q] = whole[slot, rows_of(q, 1 - core), :].astype(BF16)
            return carry

        lax.fori_loop(0, blocks, divide, 0)
        pair_copy(w).start()

    def combine(w):
        slot = w % 2
        pair_copy(w).wait_recv()

        def add(q, carry):
            own[w, q] = (
                whole[slot, rows_of(q, core), :] + own[w, q].astype(F32)
            ).astype(BF16)
            return carry

        lax.fori_loop(0, blocks, add, 0)

    def right_copy(source, w, r):
        return remote(source, going_right.at[w, r], s_right.at[w, r], r_right.at[w, r], after)

    def left_copy(source, w, r):
        return remote(source, going_left.at[w, r], s_left.at[w, r], r_left.at[w, r], before)

    from_end = chips - 1 - chip

    def travel(w, r):
        prior = jnp.maximum(r - 1, 0)

        @pl.when(has_right & (chip == 0))
        def _():
            right_copy(own.at[w, chips - 1 - r], w, r).start()

        @pl.when(has_left & (from_end == 0))
        def _():
            left_copy(own.at[w, r], w, r).start()

        @pl.when(has_right & (chip > 0) & (chip <= r))
        def _():
            slot = going_right.at[w, prior]
            right_copy(slot, w, prior).wait_recv()
            slot[...] = (
                slot[...].astype(F32) + own[w, chips - 1 - r + chip].astype(F32)
            ).astype(BF16)
            right_copy(slot, w, r).start()

        @pl.when(has_left & (from_end > 0) & (from_end <= r))
        def _():
            slot = going_left.at[w, prior]
            left_copy(slot, w, prior).wait_recv()
            slot[...] = (
                slot[...].astype(F32) + own[w, r - from_end].astype(F32)
            ).astype(BF16)
            left_copy(slot, w, r).start()

    def rows_copy(origin, send, index):
        block = dp.at[pl.ds(pl.multiple_of(origin * rows, rows), rows)]
        return remote(block, block, send.at[origin], r_rows.at[origin], index)

    def each_origin(low, high):
        def turn(origin, carry):
            rows_copy(origin, s_ahead, after).wait_recv()
            return carry

        lax.fori_loop(low, high, turn, 0)

    def spread(r):
        @pl.when(has_right & (chip >= r))
        def _():
            pl.when(r > 0)(lambda: rows_copy(chip - r, s_ahead, after).wait_recv())
            rows_copy(chip - r, s_ahead, after).start()

        @pl.when(has_left & (from_end >= r))
        def _():
            pl.when(r > 0)(lambda: rows_copy(chip + r, s_behind, before).wait_recv())
            rows_copy(chip + r, s_behind, before).start()

    def hid_copy(j):
        place = pl.ds(pl.multiple_of(j * columns, columns), columns)
        return remote(
            hid_out.at[:, place], hid_in.at[:, place], s_hid.at[j], r_hid.at[j], sibling
        )

    proj_copy = remote(proj_out, proj_in, s_proj, r_proj, sibling)
    group = wide.shape[0]
    first = chip * 2 * share
    start = pl.multiple_of(first // group * group, group)
    inside = first - first // group * group

    def feed(j):
        slot = j % 2
        place = pl.ds(pl.multiple_of(j * columns, columns), columns)

        @pl.when(j == 0)
        def _():
            lh_copy.wait()
            pl.when(chip == 0)(lambda: each_origin(1, chips))
            pl.when(from_end == 0)(lambda: each_origin(0, chips - 1))

        wh_copy(j, slot).wait()
        wp_copy(j, slot).wait()

        @pl.when(j + 1 < peers)
        def _():
            wh_copy(j + 1, 1 - slot).start()
            wp_copy(j + 1, 1 - slot).start()

        active = jnp.maximum(dot_nn(lh[...], wh[slot]), 0.0)
        act[...] = active
        grown = (dot_nt(dp[...], wp[slot]) * 2.0 * act[...]).astype(BF16)
        wide[...] = dot_tn(lh[:, pl.ds(start, group)], grown)
        mine = pl.ds(pl.multiple_of(inside + core * share, 16), share)
        other = pl.ds(pl.multiple_of(inside + (1 - core) * share, 16), share)
        wh_out[:, place] = wide[mine, :]
        hid_out[:, place] = wide[other, :].astype(BF16)
        hid_copy(j).start()

        @pl.when(j == 2 * chip + core)
        def _():
            squared = (act[...] * act[...]).astype(BF16)
            wp_out[...] = dot_tn(squared, dp[...])

        @pl.when(j == 2 * chip + 1 - core)
        def _():
            squared = (act[...] * act[...]).astype(BF16)
            proj_out[...] = dot_tn(squared, dp[...]).astype(BF16)
            proj_copy.start()

    rounds = chips - 1
    dp_copy.wait()
    spread(0)
    prepare(0)
    prepare(1)
    combine(0)
    opening = count * rounds - peers

    def step(t, carry):
        w, r = t // rounds, t % rounds
        travel(w, r)

        @pl.when((r == 1) & (w + 2 < count))
        def _():
            prepare(w + 2)

        @pl.when((r == 1) & (w + 1 < count))
        def _():
            combine(w + 1)

        @pl.when(t + 1 < rounds)
        def _():
            spread(t + 1)

        @pl.when(t >= opening)
        def _():
            feed(t - opening)

        return carry

    lax.fori_loop(0, count * rounds, step, 0)

    for w in range(count):
        outs[w][...] = own[w, chip].astype(F32)

        @pl.when(has_left)
        def _():
            right_copy(own.at[w, 0], w, rounds - 1).wait_recv()
            outs[w][...] += going_right[w, rounds - 1].astype(F32)

        @pl.when(has_right)
        def _():
            left_copy(own.at[w, 0], w, rounds - 1).wait_recv()
            outs[w][...] += going_left[w, rounds - 1].astype(F32)

    def gather_hidden(j, carry):
        hid_copy(j).wait_recv()
        place = pl.ds(pl.multiple_of(j * columns, columns), columns)
        wh_out[:, place] += hid_in[:, place].astype(F32)
        return carry

    lax.fori_loop(0, peers, gather_hidden, 0)
    proj_copy.wait_recv()
    wp_out[...] += proj_in[...].astype(F32)

    def sent_hidden(j, carry):
        hid_copy(j).wait_send()
        return carry

    lax.fori_loop(0, peers, sent_hidden, 0)
    proj_copy.wait_send()

    def sent_rows(origin, carry):
        @pl.when(has_right & (origin <= chip))
        def _():
            rows_copy(origin, s_ahead, after).wait_send()

        @pl.when(has_left & (origin >= chip))
        def _():
            rows_copy(origin, s_behind, before).wait_send()

        return carry

    lax.fori_loop(0, chips, sent_rows, 0)

    def sent(w, carry):
        pair_copy(w).wait_send()

        def sent_round(r, inner):
            @pl.when(has_right & (chip <= r))
            def _():
                right_copy(own.at[w, 0], w, r).wait_send()

            @pl.when(has_left & (from_end <= r))
            def _():
                left_copy(own.at[w, 0], w, r).wait_send()

            return inner

        lax.fori_loop(0, rounds, sent_round, 0)
        return carry

    lax.fori_loop(0, count, sent, 0)


def gradient_sums(peers, lefts, rights, lh, dp, wh, wp):
    count = len(lefts)
    rows, width = lefts[0].shape
    hidden = wh.shape[1]
    tokens = lh.shape[0]
    chips = peers // 2
    share = width // peers
    columns = hidden // peers
    group = max(128, 2 * share)
    shape = jax.ShapeDtypeStruct
    vmem = pl.BlockSpec(memory_space=pltpu.VMEM)
    anywhere = pl.BlockSpec(memory_space=pl.ANY)
    dma = pltpu.SemaphoreType.DMA
    blocks = pltpu.VMEM((count, chips, share, width), BF16)
    slots = pltpu.VMEM((count, chips - 1, share, width), BF16)
    return pl.pallas_call(
        partial(sum_kernel, peers),
        out_shape=(shape((share, width), F32),) * count
        + (shape((share, hidden), F32), shape((columns, width), F32)),
        in_specs=[anywhere] * (2 * count + 4),
        out_specs=[vmem] * (count + 2),
        scratch_shapes=[
            pltpu.VMEM((count, rows, width), BF16), pltpu.VMEM((count, rows, width), BF16),
            pltpu.VMEM((2, width, width), F32),
            blocks, blocks, slots, slots,
            pltpu.VMEM((tokens, width), BF16), pltpu.VMEM((tokens, width), BF16),
            pltpu.VMEM((2, width, columns), BF16), pltpu.VMEM((2, columns, width), BF16),
            pltpu.VMEM((tokens, columns), F32), pltpu.VMEM((group, columns), F32),
            pltpu.VMEM((share, hidden), BF16), pltpu.VMEM((share, hidden), BF16),
            pltpu.VMEM((columns, width), BF16), pltpu.VMEM((columns, width), BF16),
            dma((count,)), dma((count,)), dma, dma, dma((2,)), dma((2,)),
            dma((count,)), dma((count,)),
            dma((count, chips - 1)), dma((count, chips - 1)),
            dma((count, chips - 1)), dma((count, chips - 1)),
            dma((peers,)), dma((peers,)), dma, dma,
            dma((chips,)), dma((chips,)), dma((chips,)),
        ],
        compiler_params=pltpu.CompilerParams(
            collective_id=1, has_side_effects=True, vmem_limit_bytes=63 * 2**20
        ),
        name="gradient_sums",
    )(*lefts, *rights, lh, dp, wh, wp)


def per_device(x, top, spans, *parameters):
    sections = lax.axis_size("section")
    peers = lax.axis_size("dp")
    gain1, bias1, mix_k, mix_v, mix_g, log_rate, extra = parameters[0:7]
    wk, wv, wg, wo = parameters[7:11]
    gain2, bias2, mix_h, mix_f = parameters[11:15]
    wh, wp, wf = parameters[15:18]
    vectors = (gain1, bias1, mix_k, mix_v, mix_g, log_rate, extra, gain2, bias2, mix_h, mix_f)
    matrices = tuple(w[0] for w in (wk, wv, wg, wo, wh, wp, wf))
    found = relay(sections, peers, x, top, spans, vectors, matrices)
    out, back, vec = found[0:3]
    flat = (x.shape[0] * x.shape[1], x.shape[2])
    lk, lv, lg, lgt, lf, dk, dv, dg, datt, dsv, dproj = (
        part.reshape(flat) for part in found[3:14]
    )
    lh = found[14].reshape(-1, x.shape[2])
    share = x.shape[2] // peers
    if vec.shape[1] != share:
        vec = lax.dynamic_slice_in_dim(vec, lax.axis_index("dp") * share, share, 1)
    summed = gradient_sums(
        peers, (lf, lgt, lg, lk, lv), (dsv, datt, dg, dk, dv), lh, dproj, matrices[4], matrices[5]
    )
    d_wf, d_wo, d_wg, d_wk, d_wv, d_wh, d_wp = (part[None] for part in summed)

    def row(index):
        return vec[index : index + 1]

    return (
        out[None], back[None],
        row(0), row(1), row(2), row(3), row(4), row(5), row(6),
        d_wk, d_wv, d_wg, d_wo,
        row(7), row(8), row(9), row(10),
        d_wh, d_wp, d_wf,
    )


def solution(mesh):
    tokens = P(None, "dp", None)
    vector = P("section", None)
    matrix = P("section", None, None)
    result = P("section", None, "dp", None)
    vector_grad = P("section", "dp")
    matrix_grad = P("section", "dp", None)
    return jax.shard_map(
        per_device,
        mesh=mesh,
        in_specs=(tokens, tokens, P())
        + (vector,) * 7 + (matrix,) * 4 + (vector,) * 4 + (matrix,) * 3,
        out_specs=(result, result)
        + (vector_grad,) * 7 + (matrix_grad,) * 4 + (vector_grad,) * 4 + (matrix_grad,) * 3,
        check_vma=False,
    )
```

```python
from functools import partial

import jax
import jax.numpy as jnp
from jax import lax
from jax.experimental import pallas as pl
from jax.experimental.pallas import tpu as pltpu
from jax.sharding import PartitionSpec as P

EPS = 1e-05
MESH = pl.DeviceIdType.MESH
RB = 64
PARTS = 1
VECTORS = 16
F32 = jnp.float32
BF16 = jnp.bfloat16


def dot_nn(left, right):
    return jnp.dot(left, right, preferred_element_type=F32)


def dot_nt(left, right):
    return lax.dot_general(left, right, (((1,), (1,)), ((), ())), preferred_element_type=F32)


def dot_tn(left, right):
    return lax.dot_general(left, right, (((0,), (0,)), ((), ())), preferred_element_type=F32)


def sigmoid(v):
    return 1.0 / (1.0 + jnp.exp(-v))


def normalise(source):
    centred = source - jnp.mean(source, axis=-1, keepdims=True)
    spread = lax.rsqrt(jnp.mean(centred * centred, axis=-1, keepdims=True) + EPS)
    return centred * spread, spread


def moved_down(rows, first):
    place = lax.broadcasted_iota(jnp.int32, rows.shape, 0)
    return jnp.where(place == 0, first, pltpu.roll(rows, 1, 0))


def moved_up(rows, last):
    count = rows.shape[0]
    place = lax.broadcasted_iota(jnp.int32, rows.shape, 0)
    return jnp.where(place == count - 1, last, pltpu.roll(rows, count - 1, 0))


def fold(rows):
    total = rows[0:8]
    for at in range(8, rows.shape[0], 8):
        total = total + rows[at : at + 8]
    return total


def relay_kernel(sections, peers, *refs):
    (
        spans, x_in, top_in,
        gain1, bias1, mix_k, mix_v, mix_g, log_rate, extra, gain2, bias2, mix_h, mix_f,
        wk_in, wv_in, wg_in, wo_in, wh_in, wp_in, wf_in,
        out_hbm, back_hbm, lk_hbm, lv_hbm, lg_hbm, lgt_hbm, lf_hbm,
        dk_hbm, dv_hbm, dg_hbm, datt_hbm, dsv_hbm, dproj_hbm, vgs, lh_all,
        wk_t, wv_t, wg_t, wo_t, wf_t, wp_t, wh_t,
        out, back, lk, lv, lg, lgt, lf, dk, dv, dg, datt, dsv, dproj,
        lh, sq, dh, turned,
        wk, wv, wg, wo, wh, wp, wf,
        xs, hx, dys, kk, vv, sg, sa, sb, mid, hmid, proj, sv, act, halo1, halo2,
        e0, e1, low_mask, up_mask, split, acc, t1, t2, t3,
        states, back_states, de2, de1, sum_row, sum_back, send_de2, send_de1, vg,
        w_sem, x_sem, top_sem, s_h0, s_x, s_hx, s_st, s_mid, s_dy, s_de2, s_bst, s_de1,
        r_x, r_hx, r_st, r_mid, r_dy, r_de2, r_bst, r_de1, store_sem,
        s_lh, r_lh, own_sem, turn_sem, back_sem,
    ) = refs
    me_s = lax.axis_index("section")
    me = lax.axis_index("dp")
    batches, row_count, width = x_in.shape
    hidden = wh.shape[1]
    chunks = row_count // RB
    base = me * row_count

    def at(section, index):
        return (section, index)

    barrier = pltpu.get_barrier_semaphore()

    def greet(section, index):
        pl.semaphore_signal(barrier, inc=1, device_id=at(section, index), device_id_type=MESH)

    def greet_peer(k, carry):
        @pl.when(k != me)
        def _():
            greet(me_s, k)

        return carry

    lax.fori_loop(0, peers, greet_peer, 0)
    has_next = me_s + 1 < sections
    has_prior = me_s > 0
    has_right = me + 1 < peers
    has_left = me > 0

    @pl.when(has_next)
    def _():
        greet(me_s + 1, me)

    @pl.when(has_prior)
    def _():
        greet(me_s - 1, me)

    @pl.when(has_next & has_right)
    def _():
        greet(me_s + 1, me + 1)

    @pl.when(has_prior & has_left)
    def _():
        greet(me_s - 1, me - 1)

    weight_copies = [
        pltpu.make_async_copy(source, target, w_sem.at[index])
        for index, (source, target) in enumerate(
            ((wk_in, wk), (wv_in, wv), (wg_in, wg), (wo_in, wo), (wf_in, wf), (wh_in, wh), (wp_in, wp))
        )
    ]

    @pl.when(me_s == 0)
    def _():
        pltpu.make_async_copy(x_in, xs, x_sem).start()

    for copy in weight_copies[0:2]:
        copy.start()

    @pl.when(me_s == sections - 1)
    def _():
        pltpu.make_async_copy(top_in, dys, top_sem).start()

    rate = jnp.exp(log_rate[...])
    decay_block = jnp.exp(-rate * row_count)
    grow_block = jnp.exp(rate * row_count)

    half = width // 128

    def packed(row_a, row_b):
        return jnp.concatenate(
            [row[:, j * 128 : (j + 1) * 128] for row in (row_a, row_b) for j in range(half)], axis=0
        )

    def unpacked(tile, part):
        return jnp.concatenate(
            [tile[part * half + j : part * half + j + 1] for j in range(half)], axis=1
        )

    decay_tile = packed(decay_block, decay_block)

    def starts_of(m):
        found = []
        total = jnp.int32(0)
        for j in range(spans.shape[1]):
            found.append(total)
            total = total + spans[m, j]
        return found

    def segment(position, starts):
        total = jnp.where(position >= starts[0], 1, 0)
        for start in starts[1:]:
            total = total + jnp.where(position >= start, 1, 0)
        return total

    def column(i):
        return base + i * RB + lax.broadcasted_iota(jnp.int32, (RB, 1), 0)

    def keep_of(position, starts):
        return jnp.where(segment(position, starts) == segment(position - 1, starts), 1.0, 0.0)

    def fill_powers(i, carry):
        place = (i * RB + lax.broadcasted_iota(jnp.int32, (RB, width), 0)).astype(F32)
        e0[pl.ds(pl.multiple_of(i * RB, RB), RB), :] = jnp.exp(-place * rate)
        e1[pl.ds(pl.multiple_of(i * RB, RB), RB), :] = jnp.exp((place - (row_count - 1.0)) * rate)
        return carry

    lax.fori_loop(0, chunks, fill_powers, 0)
    for m in range(batches):
        starts = starts_of(m)
        row_at = lax.broadcasted_iota(jnp.int32, (row_count, row_count), 0)
        column_at = lax.broadcasted_iota(jnp.int32, (row_count, row_count), 1)
        same = segment(base + row_at, starts) == segment(base + column_at, starts)
        lower = jnp.where(same & (column_at < row_at), 1.0, 0.0).astype(BF16)
        upper = jnp.where(same & (column_at > row_at), 1.0, 0.0).astype(BF16)
        low_mask[m, :, 0:row_count] = lower
        low_mask[m, :, row_count:] = lower
        up_mask[m, :, 0:row_count] = upper
        up_mask[m, :, row_count:] = upper
    vg[...] = jnp.zeros_like(vg)

    @pl.when(me == 0)
    def _():
        hx[...] = jnp.zeros_like(hx)
        hmid[...] = jnp.zeros_like(hmid)

    @pl.when(me == peers - 1)
    def _():
        de1[...] = jnp.zeros_like(de1)
        de2[...] = jnp.zeros_like(de2)

    greeted = (
        peers - 1
        + jnp.where(has_next, 1, 0)
        + jnp.where(has_prior, 1, 0)
        + jnp.where(has_next & has_right, 1, 0)
        + jnp.where(has_prior & has_left, 1, 0)
    )
    pl.semaphore_wait(barrier, greeted)
    for copy in weight_copies[2:7]:
        copy.start()

    def remote(source, target, send, receive, section, index):
        return pltpu.make_async_remote_copy(
            src_ref=source, dst_ref=target, send_sem=send, recv_sem=receive,
            device_id=at(section, index), device_id_type=MESH,
        )

    right = jnp.minimum(me + 1, peers - 1)
    left = jnp.maximum(me - 1, 0)
    above = jnp.minimum(me_s + 1, sections - 1)
    below = jnp.maximum(me_s - 1, 0)
    tail = pl.ds(row_count - 16, 16)
    final = pl.ds(row_count - 1, 1)

    stored = (
        (out, out_hbm), (lk, lk_hbm), (lv, lv_hbm), (lg, lg_hbm), (lgt, lgt_hbm), (lf, lf_hbm),
        (dproj, dproj_hbm), (dsv, dsv_hbm), (datt, datt_hbm), (dg, dg_hbm), (dk, dk_hbm),
        (dv, dv_hbm), (back, back_hbm),
    )

    def store_copy(index, m):
        source, target = stored[index]
        return pltpu.make_async_copy(source.at[m], target.at[m], store_sem.at[index, m])

    def start_halo(m):
        return remote(x_in.at[m, tail], hx.at[m], s_h0.at[m], r_hx.at[m], me_s, right)

    def part_of(j):
        return pl.ds(pl.multiple_of(j * (width // PARTS), width // PARTS), width // PARTS)

    def result_copy(m, j):
        return remote(
            out.at[m, :, part_of(j)], xs.at[m, :, part_of(j)],
            s_x.at[m, j], r_x.at[m, j], above, me,
        )

    def each_part(action):
        def turn(j, carry):
            action(j)
            return carry

        lax.fori_loop(0, PARTS, turn, 0)

    def result_halo(m):
        return remote(out.at[m, tail], hx.at[m], s_hx.at[m], r_hx.at[m], above, right)

    def middle_halo(m):
        return remote(mid.at[m, final], hmid.at[m], s_mid.at[m], r_mid.at[m], me_s, right)

    def state_copy(m, k, slot):
        return remote(sum_row.at[m], states.at[m, slot], s_st.at[m, k], r_st.at[m, slot], me_s, k)

    def back_copy(m, i):
        rows = pl.ds(pl.multiple_of(i * RB, RB), RB)
        return remote(
            back.at[m, rows], dys.at[m, rows], s_dy.at[m, i], r_dy.at[m, i], below, me
        )

    def each_chunk(action):
        def turn(i, carry):
            action(i)
            return carry

        lax.fori_loop(0, chunks, turn, 0)

    def second_copy(m):
        return remote(send_de2.at[m], de2.at[m], s_de2.at[m], r_de2.at[m], me_s, left)

    def first_copy(m):
        return remote(send_de1.at[m], de1.at[m], s_de1.at[m], r_de1.at[m], me_s, left)

    def back_state_copy(m, k, slot):
        return remote(
            sum_back.at[m], back_states.at[m, slot], s_bst.at[m, k], r_bst.at[m, slot], me_s, k
        )

    chip, core = me // 2, me % 2
    chips = peers // 2

    def gather_copy(m, k, slot):
        return remote(
            lh.at[m], lh_all.at[slot, m], s_lh.at[m, k], r_lh.at[m, slot], me_s, 2 * k + core
        )

    def own_copy(m):
        return pltpu.make_async_copy(lh.at[m], lh_all.at[chip, m], own_sem.at[m])

    def each_chip(action):
        def turn(k, carry):
            @pl.when(k != chip)
            def _():
                action(k)

            return carry

        lax.fori_loop(0, chips, turn, 0)

    def start_gather(m):
        own_copy(m).start()
        each_chip(lambda k: gather_copy(m, k, chip).start())

    def start_gathers(early):
        for m in range(batches):
            in_gap = me_s + 1 + m < sections

            @pl.when(in_gap if early else jnp.logical_not(in_gap))
            def _(m=m):
                start_gather(m)

    def end_gather(m):
        own_copy(m).wait()
        each_chip(lambda k: gather_copy(m, k, chip).wait_send())
        each_chip(lambda k: gather_copy(m, k, k).wait_recv())

    @pl.when((me_s == 0) & has_right)
    def _():
        for m in range(batches):
            start_halo(m).start()

    @pl.when(me_s == 0)
    def _():
        pltpu.make_async_copy(x_in, xs, x_sem).wait()

    turns = (
        (wk, wk_t), (wv, wv_t), (wg, wg_t), (wo, wo_t), (wf, wf_t), (wh, wh_t), (wp, wp_t)
    )
    returns = (
        (wk_t, wk), (wv_t, wv), (wg_t, wg), (wo_t, wo), (wf_t, wf), (wp_t, wh), (wh_t, wp)
    )
    edge = turned.shape[1]

    def transpose_all(fresh):
        for index, (source, target) in enumerate(turns):
            if fresh:
                weight_copies[index].wait()
            tall = source.shape[0] // edge
            blocks = tall * (source.shape[1] // edge)

            def place(n, source=source, target=target, tall=tall):
                down = pl.ds(pl.multiple_of(n % tall * edge, edge), edge)
                along = pl.ds(pl.multiple_of(n // tall * edge, edge), edge)
                slot = n % 2
                return (
                    source.at[down, along],
                    turned.at[slot],
                    pltpu.make_async_copy(turned.at[slot], target.at[along, down], turn_sem.at[slot]),
                )

            def turn(n, carry, place=place):
                piece, buffer, copy = place(n)
                pl.when(n >= 2)(copy.wait)
                buffer[...] = piece[...].T
                copy.start()
                return carry

            lax.fori_loop(0, blocks, turn, 0)
            for n in range(blocks - 2, blocks):
                place(n)[2].wait()

    def return_copy(index):
        source, target = returns[index]
        return pltpu.make_async_copy(source, target, back_sem.at[index])

    is_late = 2 * me_s >= sections

    def release(m, index):
        @pl.when(is_late & (m == batches - 1))
        def _():
            return_copy(index).start()

    def weight_ready(m, index, fresh=True):
        @pl.when((m == 0) & jnp.logical_not(is_late))
        def _():
            weight_copies[index].wait()

    def span_of(i):
        return pl.ds(pl.multiple_of(i * RB, RB), RB)

    def forward(m, carry):
        starts = starts_of(m)

        @pl.when(has_prior)
        def _():
            each_part(lambda j: result_copy(m, j).wait_recv())

        @pl.when(has_left)
        def _():
            start_halo(m).wait_recv()

        halo_rows, _ = normalise(hx[m].astype(F32))
        halo_rows = halo_rows * gain1[...] + bias1[...]
        halo1[m] = halo_rows[8:16]

        def mix_in(i, last):
            rows = span_of(i)
            normed, _ = normalise(xs[m, rows, :].astype(F32))
            normed = normed * gain1[...] + bias1[...]
            earlier = moved_down(normed, last) * keep_of(column(i), starts)
            gap = normed - earlier
            lk[m, rows, :] = (earlier + gap * mix_k[...]).astype(BF16)
            lv[m, rows, :] = (earlier + gap * mix_v[...]).astype(BF16)
            lg[m, rows, :] = (earlier + gap * mix_g[...]).astype(BF16)
            return normed[RB - 1 : RB]

        lax.fori_loop(0, chunks, mix_in, halo_rows[15:16], unroll=True)

        weight_ready(m, 0)
        weight_ready(m, 1)
        kk[m] = dot_nn(lk[m], wk[...])
        vv[m] = dot_nn(lv[m], wv[...])
        release(m, 0)
        release(m, 1)
        end_segment = segment(base + row_count - 1, starts)

        def spread_in(i, totals):
            rows = span_of(i)
            weight = jnp.exp(kk[m, rows, :]) * e1[rows, :]
            weighted = weight * vv[m, rows, :]
            high_a = weighted.astype(BF16)
            high_b = weight.astype(BF16)
            split[rows, 0:width] = high_a
            split[rows, width:] = high_b
            low = pl.ds(pl.multiple_of(row_count + i * RB, RB), RB)
            split[low, 0:width] = (weighted - high_a.astype(F32)).astype(BF16)
            split[low, width:] = (weight - high_b.astype(F32)).astype(BF16)
            chosen = segment(column(i), starts) == end_segment
            return (
                totals[0] + fold(jnp.where(chosen, weighted, 0.0)),
                totals[1] + fold(jnp.where(chosen, weight, 0.0)),
            )

        nothing = jnp.zeros((8, width), F32)
        total_a, total_b = lax.fori_loop(0, chunks, spread_in, (nothing, nothing), unroll=True)
        sum_row[m] = packed(
            jnp.sum(total_a, axis=0, keepdims=True), jnp.sum(total_b, axis=0, keepdims=True)
        )

        def send_state(k, carry):
            state_copy(m, k, me).start()
            return carry

        lax.fori_loop(me + 1, peers, send_state, 0)

        weight_ready(m, 2)
        sg[m] = dot_nn(lg[m], wg[...])
        acc[...] = dot_nn(low_mask[m], split[...])
        release(m, 2)

        def receive_state(k, held):
            state_copy(m, k, k).wait_recv()
            unbroken = segment(k * row_count - 1, starts) == segment(
                (k + 1) * row_count - 1, starts
            )
            passing = jnp.where(unbroken, 1.0, 0.0) * decay_tile
            return passing * held + states[m, k]

        none = jnp.zeros((1, width), F32)
        entered = lax.fori_loop(0, me, receive_state, jnp.zeros_like(decay_tile))
        enter_a, enter_b = unpacked(entered, 0), unpacked(entered, 1)
        prior_segment = segment(base - 1, starts)

        def mix_states(i, carry):
            rows = span_of(i)
            falling = e0[rows, :]
            chosen = jnp.where(segment(column(i), starts) == prior_segment, 1.0, 0.0)
            grown = falling * grow_block
            held = falling * chosen
            state_a = grown * acc[rows, 0:width] + held * enter_a
            state_b = grown * acc[rows, width:] + held * enter_b
            sa[m, rows, :] = state_a
            sb[m, rows, :] = state_b
            present = jnp.exp(extra[...] + kk[m, rows, :])
            gate = sigmoid(sg[m, rows, :])
            sg[m, rows, :] = gate
            found = (state_a + present * vv[m, rows, :]) / (state_b + present)
            lgt[m, rows, :] = (gate * found).astype(BF16)
            return carry

        lax.fori_loop(0, chunks, mix_states, 0, unroll=True)

        weight_ready(m, 3)
        mid[m] = xs[m].astype(F32) + dot_nn(lgt[m], wo[...])
        release(m, 3)

        @pl.when(has_right)
        def _():
            middle_halo(m).start()

        def mix_second(i, last):
            rows = span_of(i)
            normed, _ = normalise(mid[m, rows, :])
            normed = normed * gain2[...] + bias2[...]
            earlier = moved_down(normed, last) * keep_of(column(i), starts)
            gap = normed - earlier
            lh[m, rows, :] = (earlier + gap * mix_h[...]).astype(BF16)
            lf[m, rows, :] = (earlier + gap * mix_f[...]).astype(BF16)
            return normed[RB - 1 : RB]

        lax.fori_loop(0, chunks, mix_second, none, unroll=True)

        @pl.when(has_left)
        def _():
            middle_halo(m).wait_recv()

        halo_rows, _ = normalise(hmid[m])
        halo_rows = halo_rows * gain2[...] + bias2[...]
        halo2[m] = halo_rows
        mix_second(0, halo_rows)

        for index in range(4, 7):
            weight_ready(m, index)
        sv[m] = dot_nn(lf[m], wf[...])

        def widen(j, carry):
            columns = pl.ds(pl.multiple_of(j * width, width), width)
            active = jnp.maximum(dot_nn(lh[m], wh[:, columns]), 0.0)
            act[m, :, columns] = active.astype(BF16)
            sq[m, :, columns] = (active * active).astype(BF16)
            return carry

        lax.fori_loop(0, hidden // width, widen, 0, unroll=True)
        release(m, 4)
        release(m, 5)

        def finish(j, carry):
            columns = part_of(j)
            found = dot_nn(sq[m], wp[:, columns])
            proj[m, :, columns] = found
            sieve = sigmoid(sv[m, :, columns])
            sv[m, :, columns] = sieve
            out[m, :, columns] = (mid[m, :, columns] + sieve * found).astype(BF16)

            @pl.when(has_next)
            def _():
                result_copy(m, j).start()

            return carry

        lax.fori_loop(0, PARTS, finish, 0)
        release(m, 6)

        @pl.when(has_next & has_right)
        def _():
            result_halo(m).start()

        for index in range(6):
            store_copy(index, m).start()

        return carry

    pl.when(is_late)(lambda: transpose_all(True))
    lax.fori_loop(0, batches, forward, 0)

    @pl.when(jnp.logical_not(is_late))
    def _():
        transpose_all(False)
        for index in range(7):
            return_copy(index).start()

    start_gathers(True)

    def add_vector(index, value):
        vg[index] += fold(value)

    @pl.when(me_s == sections - 1)
    def _():
        pltpu.make_async_copy(top_in, dys, top_sem).wait()

    def turned_ready(m, index):
        @pl.when(m == 0)
        def _():
            return_copy(index).wait()

    def backward(m, carry):
        starts = starts_of(m)
        none = jnp.zeros((1, width), F32)

        @pl.when(has_next)
        def _():
            each_chunk(lambda i: back_copy(m, i).wait_recv())

        def open_back(i, carry):
            rows = span_of(i)
            incoming = dys[m, rows, :].astype(F32)
            sieve = sv[m, rows, :]
            gained = incoming * sieve
            dproj[m, rows, :] = gained.astype(BF16)
            dsv[m, rows, :] = (gained * proj[m, rows, :] * (1.0 - sieve)).astype(BF16)
            return carry

        lax.fori_loop(0, chunks, open_back, 0, unroll=True)
        t1[...] = jnp.zeros_like(t1)
        turned_ready(m, 5)
        turned_ready(m, 6)

        def narrow(j, carry):
            columns = pl.ds(pl.multiple_of(j * width, width), width)
            grown = dot_nn(dproj[m], wh[:, columns])
            dh[m, :, columns] = (grown * 2.0 * act[m, :, columns].astype(F32)).astype(BF16)
            t1[...] += dot_nn(dh[m, :, columns], wp[columns, :])
            return carry

        lax.fori_loop(0, hidden // width, narrow, 0, unroll=True)
        turned_ready(m, 4)
        t2[...] = dot_nn(dsv[m], wf[...])

        def second_earlier(rows, position):
            whole = t1[rows, :] * (1.0 - mix_h[...]) + t2[rows, :] * (1.0 - mix_f[...])
            return whole * keep_of(position, starts)

        eight = lax.broadcasted_iota(jnp.int32, (8, 1), 0)
        send_de2[m] = second_earlier(pl.ds(0, 8), base + eight)[0:1]

        @pl.when(has_left)
        def _():
            second_copy(m).start()

        def back_second(i, last, following):
            rows = span_of(i)
            spare, spread = normalise(mid[m, rows, :])
            normed = spare * gain2[...] + bias2[...]
            kept = keep_of(column(i), starts)
            gap = normed - moved_down(normed, last) * kept
            from_h = t1[rows, :]
            from_f = t2[rows, :]
            add_vector(9, from_h * gap)
            add_vector(10, from_f * gap)
            straight = from_h * mix_h[...] + from_f * mix_f[...]
            earlier = (from_h + from_f - straight) * kept
            d_normed = straight + moved_up(earlier, following)
            add_vector(7, d_normed * spare)
            add_vector(8, d_normed)
            scaled = d_normed * gain2[...]
            mean_one = jnp.mean(scaled, axis=-1, keepdims=True)
            mean_two = jnp.mean(scaled * spare, axis=-1, keepdims=True)
            d_mid = dys[m, rows, :].astype(F32) + spread * (scaled - mean_one - spare * mean_two)
            t3[rows, :] = d_mid
            datt[m, rows, :] = d_mid.astype(BF16)
            return normed[RB - 1 : RB]

        def following_second(i):
            start = pl.multiple_of((i + 1) * RB, RB)
            return second_earlier(pl.ds(start, 8), base + start + eight)[0:1]

        last = halo2[m]
        for i in range(chunks - 1):
            last = back_second(i, last, following_second(i))

        @pl.when(has_right)
        def _():
            second_copy(m).wait_recv()

        back_second(chunks - 1, last, de2[m])
        turned_ready(m, 3)
        t1[...] = dot_nn(datt[m], wo[...])
        open_segment = segment(base, starts)

        def back_states_in(i, totals):
            rows = span_of(i)
            d_gated = t1[rows, :]
            gate = sg[m, rows, :]
            keys = kk[m, rows, :]
            values = vv[m, rows, :]
            present = jnp.exp(extra[...] + keys)
            inverse = 1.0 / (sb[m, rows, :] + present)
            found = (sa[m, rows, :] + present * values) * inverse
            d_found = d_gated * gate
            dg[m, rows, :] = (d_found * found * (1.0 - gate)).astype(BF16)
            d_a = d_found * inverse
            d_b = -d_a * found
            d_key = (d_a * values + d_b) * present
            add_vector(6, d_key)
            t1[rows, :] = d_key
            t2[rows, :] = d_a * present
            falling = e0[rows, :]
            scaled_a = d_a * falling
            scaled_b = d_b * falling
            high_a = scaled_a.astype(BF16)
            high_b = scaled_b.astype(BF16)
            split[rows, 0:width] = high_a
            split[rows, width:] = high_b
            low = pl.ds(pl.multiple_of(row_count + i * RB, RB), RB)
            split[low, 0:width] = (scaled_a - high_a.astype(F32)).astype(BF16)
            split[low, width:] = (scaled_b - high_b.astype(F32)).astype(BF16)
            chosen = segment(column(i), starts) == open_segment
            return (
                totals[0] + fold(jnp.where(chosen, scaled_a, 0.0)),
                totals[1] + fold(jnp.where(chosen, scaled_b, 0.0)),
            )

        nothing = jnp.zeros((8, width), F32)
        total_a, total_b = lax.fori_loop(0, chunks, back_states_in, (nothing, nothing), unroll=True)
        sum_back[m] = packed(
            jnp.sum(total_a, axis=0, keepdims=True), jnp.sum(total_b, axis=0, keepdims=True)
        )

        def send_state(k, carry):
            back_state_copy(m, k, me).start()
            return carry

        lax.fori_loop(0, me, send_state, 0)
        acc[...] = dot_nn(up_mask[m], split[...])

        def receive_state(turn, held):
            k = peers - 1 - turn
            back_state_copy(m, k, k).wait_recv()
            first = segment(k * row_count, starts)
            unbroken = first == segment((k + 1) * row_count - 1, starts)
            joined = jnp.where(first == segment(k * row_count - 1, starts), 1.0, 0.0)
            passing = jnp.where(unbroken, 1.0, 0.0) * decay_tile
            return joined * (passing * held + back_states[m, k])

        entered = lax.fori_loop(0, peers - 1 - me, receive_state, jnp.zeros_like(decay_tile))
        enter_a, enter_b = unpacked(entered, 0), unpacked(entered, 1)
        end_segment = segment(base + row_count - 1, starts)

        def back_keys(i, carry):
            rows = span_of(i)
            rising = e1[rows, :]
            chosen = jnp.where(segment(column(i), starts) == end_segment, 1.0, 0.0)
            grown = rising * grow_block
            held = rising * chosen
            d_a = grown * acc[rows, 0:width] + held * enter_a
            d_b = grown * acc[rows, width:] + held * enter_b
            add_vector(5, d_a * sa[m, rows, :] + d_b * sb[m, rows, :])
            weight = jnp.exp(kk[m, rows, :])
            dv[m, rows, :] = (t2[rows, :] + d_a * weight).astype(BF16)
            dk[m, rows, :] = (t1[rows, :] + (d_a * vv[m, rows, :] + d_b) * weight).astype(BF16)
            return carry

        lax.fori_loop(0, chunks, back_keys, 0, unroll=True)
        for index in range(3):
            turned_ready(m, index)
        t1[...] = dot_nn(dk[m], wk[...])
        t2[...] = dot_nn(dv[m], wv[...])
        acc[:, 0:width] = dot_nn(dg[m], wg[...])

        def first_earlier(rows, position):
            whole = (
                t1[rows, :] * (1.0 - mix_k[...])
                + t2[rows, :] * (1.0 - mix_v[...])
                + acc[rows, 0:width] * (1.0 - mix_g[...])
            )
            return whole * keep_of(position, starts)

        send_de1[m] = first_earlier(pl.ds(0, 8), base + eight)[0:1]

        @pl.when(has_left)
        def _():
            first_copy(m).start()

        for index in range(6, 12):
            store_copy(index, m).start()

        def back_first(i, last, following):
            rows = span_of(i)
            spare, spread = normalise(xs[m, rows, :].astype(F32))
            normed = spare * gain1[...] + bias1[...]
            kept = keep_of(column(i), starts)
            gap = normed - moved_down(normed, last) * kept
            from_k = t1[rows, :]
            from_v = t2[rows, :]
            from_g = acc[rows, 0:width]
            add_vector(2, from_k * gap)
            add_vector(3, from_v * gap)
            add_vector(4, from_g * gap)
            straight = from_k * mix_k[...] + from_v * mix_v[...] + from_g * mix_g[...]
            earlier = (from_k + from_v + from_g - straight) * kept
            d_normed = straight + moved_up(earlier, following)
            add_vector(0, d_normed * spare)
            add_vector(1, d_normed)
            scaled = d_normed * gain1[...]
            mean_one = jnp.mean(scaled, axis=-1, keepdims=True)
            mean_two = jnp.mean(scaled * spare, axis=-1, keepdims=True)
            found = t3[rows, :] + spread * (scaled - mean_one - spare * mean_two)
            back[m, rows, :] = found.astype(BF16)

            @pl.when(has_prior)
            def _():
                back_copy(m, i).start()

            return normed[RB - 1 : RB]

        def following_first(i):
            start = pl.multiple_of((i + 1) * RB, RB)
            return first_earlier(pl.ds(start, 8), base + start + eight)[0:1]

        last = halo1[m, 7:8]
        for i in range(chunks - 1):
            last = back_first(i, last, following_first(i))

        @pl.when(has_right)
        def _():
            first_copy(m).wait_recv()

        back_first(chunks - 1, last, de1[m])
        store_copy(12, m).start()

        return carry

    lax.fori_loop(0, batches, backward, 0)
    pl.when(has_prior)(lambda: each_chunk(lambda i: back_copy(batches - 1, i).wait_send()))
    start_gathers(False)

    vgs[...] = jnp.sum(vg[...], axis=1)
    vgs[5:6] = vgs[5:6] * (-rate * jnp.exp(-rate))
    def close(m, carry):
        @pl.when((me_s == 0) & has_right)
        def _():
            start_halo(m).wait_send()

        @pl.when(has_next)
        def _():
            each_part(lambda j: result_copy(m, j).wait_send())

        @pl.when(has_next & has_right)
        def _():
            result_halo(m).wait_send()

        @pl.when(has_right)
        def _():
            middle_halo(m).wait_send()

        @pl.when(has_left)
        def _():
            second_copy(m).wait_send()
            first_copy(m).wait_send()

        @pl.when(has_prior)
        def _():
            pl.when(m + 1 < batches)(lambda: each_chunk(lambda i: back_copy(m, i).wait_send()))

        for index in range(13):
            store_copy(index, m).wait()

        def ended(k, carry):
            state_copy(m, k, me).wait_send()
            return carry

        lax.fori_loop(me + 1, peers, ended, 0)
        end_gather(m)

        def ended_back(k, carry):
            back_state_copy(m, k, me).wait_send()
            return carry

        lax.fori_loop(0, me, ended_back, 0)
        return carry

    lax.fori_loop(0, batches, close, 0)


def relay(sections, peers, x, top, spans, vectors, matrices):
    batches, rows, width = x.shape
    hidden = matrices[4].shape[1]
    shape = jax.ShapeDtypeStruct
    low = shape((batches, rows, width), BF16)
    square = shape((width, width), BF16)
    vmem = pl.BlockSpec(memory_space=pltpu.VMEM)
    anywhere = pl.BlockSpec(memory_space=pl.ANY)
    dma = pltpu.SemaphoreType.DMA

    def narrow(kind):
        return pltpu.VMEM((batches, rows, width), kind)

    return pl.pallas_call(
        partial(relay_kernel, sections, peers),
        out_shape=(
            low, low, low, low, low, low, low,
            low, low, low, low, low, low, shape((VECTORS, width), F32),
            shape((peers // 2, batches, rows, width), BF16),
            square, square, square, square, square,
            shape((width, hidden), BF16), shape((hidden, width), BF16),
        ),
        in_specs=[pl.BlockSpec(memory_space=pltpu.SMEM), anywhere, anywhere]
        + [vmem] * 11
        + [anywhere] * 7,
        out_specs=[anywhere] * 13 + [vmem] + [anywhere] * 8,
        scratch_shapes=[narrow(BF16)] * 13 + [
            narrow(BF16), pltpu.VMEM((batches, rows, hidden), BF16),
            pltpu.VMEM((batches, rows, hidden), BF16), pltpu.VMEM((2, 512, 512), BF16),
        ]
        + [pltpu.VMEM(matrix.shape, BF16) for matrix in matrices_order(matrices)]
        + [
            narrow(BF16), pltpu.VMEM((batches, 16, width), BF16), narrow(BF16),
            narrow(F32), narrow(F32), narrow(F32), narrow(F32), narrow(F32), narrow(F32),
            pltpu.VMEM((batches, 1, width), F32), narrow(F32), narrow(F32),
            pltpu.VMEM((batches, rows, hidden), BF16),
            pltpu.VMEM((batches, 8, width), F32), pltpu.VMEM((batches, 1, width), F32),
            pltpu.VMEM((rows, width), F32), pltpu.VMEM((rows, width), F32),
            pltpu.VMEM((batches, rows, 2 * rows), BF16), pltpu.VMEM((batches, rows, 2 * rows), BF16),
            pltpu.VMEM((2 * rows, 2 * width), BF16), pltpu.VMEM((rows, 2 * width), F32),
            pltpu.VMEM((rows, width), F32), pltpu.VMEM((rows, width), F32), pltpu.VMEM((rows, width), F32),
            pltpu.VMEM((batches, peers, width // 64, 128), F32),
            pltpu.VMEM((batches, peers, width // 64, 128), F32),
            pltpu.VMEM((batches, 1, width), F32), pltpu.VMEM((batches, 1, width), F32),
            pltpu.VMEM((batches, width // 64, 128), F32),
            pltpu.VMEM((batches, width // 64, 128), F32),
            pltpu.VMEM((batches, 1, width), F32), pltpu.VMEM((batches, 1, width), F32),
            pltpu.VMEM((VECTORS, 8, width), F32),
            dma((7,)), dma, dma,
            dma((batches,)), dma((batches, PARTS)), dma((batches,)), dma((batches, peers)),
            dma((batches,)), dma((batches, rows // RB)), dma((batches,)), dma((batches, peers)),
            dma((batches,)),
            dma((batches, PARTS)), dma((batches,)), dma((batches, peers)), dma((batches,)),
            dma((batches, rows // RB)), dma((batches,)), dma((batches, peers)), dma((batches,)),
            dma((13, batches)),
            dma((batches, peers // 2)), dma((batches, peers // 2)), dma((batches,)),
            dma((2,)), dma((7,)),
        ],
        compiler_params=pltpu.CompilerParams(
            collective_id=0, has_side_effects=True, vmem_limit_bytes=63 * 2**20
        ),
        name="relay",
    )(spans, x, top, *vectors, *matrices_order(matrices))


def matrices_order(matrices):
    wk, wv, wg, wo, wh, wp, wf = matrices
    return (wk, wv, wg, wo, wh, wp, wf)


def sum_kernel(peers, split_vectors, *refs):
    left_in, right_in = refs[0:5], refs[5:10]
    lh_in, dp_in, wh_in, wp_in, vgs = refs[10:15]
    outs_hbm, wh_hbm, wp_hbm, vec_out = refs[15:19]
    (
        lefts, rights, whole, own, pair_out, going_right, going_left,
        lh, dp, wh, wp, act, wide, hid_out, hid_in, proj_out, proj_in,
        left_sem, right_sem, lh_sem, dp_sem, wh_sem, wp_sem,
        s_pair, r_pair, s_right, r_right, s_left, r_left, s_hid, r_hid, s_proj, r_proj,
        s_ahead, s_behind, r_rows,
        outs, wh_out, wp_out, vgr, s_vg, r_vg, outs_sem, wh_out_sem, wp_out_sem,
    ) = refs[19:]
    count = len(left_in)
    me_s = lax.axis_index("section")
    me = lax.axis_index("dp")
    chips = peers // 2
    chip, core = me // 2, me % 2
    sibling = me + 1 - 2 * core
    blocks, share = chips, own.shape[2]
    columns = wh.shape[2]
    has_right = chip + 1 < chips
    has_left = chip > 0
    after = jnp.minimum(me + 2, peers - 1)
    before = jnp.maximum(me - 2, 0)

    barrier = pltpu.get_barrier_semaphore()

    def greet(index):
        pl.semaphore_signal(barrier, inc=1, device_id=(me_s, index), device_id_type=MESH)

    def each_peer(action):
        def turn(k, carry):
            @pl.when(k != me)
            def _():
                action(k)

            return carry

        lax.fori_loop(0, peers, turn, 0)

    each_peer(greet)
    for w in range(count):
        pltpu.make_async_copy(left_in[w], lefts.at[w], left_sem.at[w]).start()
        pltpu.make_async_copy(right_in[w], rights.at[w], right_sem.at[w]).start()
    lh_copy = pltpu.make_async_copy(lh_in, lh, lh_sem)
    rows = dp_in.shape[0]
    own_rows = pl.ds(pl.multiple_of(chip * rows, rows), rows)
    dp_copy = pltpu.make_async_copy(dp_in, dp.at[own_rows], dp_sem)
    dp_copy.start()
    lh_copy.start()

    def wh_copy(j, slot):
        return pltpu.make_async_copy(
            wh_in.at[:, pl.ds(pl.multiple_of(j * columns, columns), columns)],
            wh.at[slot], wh_sem.at[slot],
        )

    def wp_copy(j, slot):
        return pltpu.make_async_copy(
            wp_in.at[pl.ds(pl.multiple_of(j * columns, columns), columns)],
            wp.at[slot], wp_sem.at[slot],
        )

    wh_copy(0, 0).start()
    wp_copy(0, 0).start()
    def remote(source, target, send, receive, index):
        return pltpu.make_async_remote_copy(
            src_ref=source, dst_ref=target, send_sem=send, recv_sem=receive,
            device_id=(me_s, index), device_id_type=MESH,
        )

    def pair_copy(w):
        return remote(pair_out.at[w], own.at[w], s_pair.at[w], r_pair.at[w], sibling)

    cut = vgr.shape[2]

    def vector_copy(k, slot):
        part = vgs.at[:, pl.ds(pl.multiple_of(k * cut, cut), cut)] if split_vectors else vgs
        return remote(part, vgr.at[slot], s_vg.at[k], r_vg.at[slot], k)

    def rows_of(block, parity):
        return pl.ds(pl.multiple_of((2 * block + parity) * share, share), share)

    def prepare(w):
        pltpu.make_async_copy(lefts.at[w], lefts.at[w], left_sem.at[w]).wait()
        pltpu.make_async_copy(rights.at[w], rights.at[w], right_sem.at[w]).wait()
        slot = w % 2
        whole[slot] = dot_tn(lefts[w], rights[w])

        def divide(q, carry):
            pair_out[w, q] = whole[slot, rows_of(q, 1 - core), :].astype(BF16)
            return carry

        lax.fori_loop(0, blocks, divide, 0)

    def combine(w):
        slot = w % 2
        pair_copy(w).wait_recv()

        def add(q, carry):
            own[w, q] = (
                whole[slot, rows_of(q, core), :] + own[w, q].astype(F32)
            ).astype(BF16)
            return carry

        lax.fori_loop(0, blocks, add, 0)

    def right_copy(source, w, r):
        return remote(source, going_right.at[w, r], s_right.at[w, r], r_right.at[w, r], after)

    def left_copy(source, w, r):
        return remote(source, going_left.at[w, r], s_left.at[w, r], r_left.at[w, r], before)

    from_end = chips - 1 - chip

    def travel(w, r):
        prior = jnp.maximum(r - 1, 0)

        @pl.when(has_right & (chip == 0))
        def _():
            right_copy(own.at[w, chips - 1 - r], w, r).start()

        @pl.when(has_left & (from_end == 0))
        def _():
            left_copy(own.at[w, r], w, r).start()

        @pl.when(has_right & (chip > 0) & (chip <= r))
        def _():
            slot = going_right.at[w, prior]
            right_copy(slot, w, prior).wait_recv()
            slot[...] = (
                slot[...].astype(F32) + own[w, chips - 1 - r + chip].astype(F32)
            ).astype(BF16)
            right_copy(slot, w, r).start()

        @pl.when(has_left & (from_end > 0) & (from_end <= r))
        def _():
            slot = going_left.at[w, prior]
            left_copy(slot, w, prior).wait_recv()
            slot[...] = (
                slot[...].astype(F32) + own[w, r - from_end].astype(F32)
            ).astype(BF16)
            left_copy(slot, w, r).start()

    def rows_copy(origin, send, index):
        block = dp.at[pl.ds(pl.multiple_of(origin * rows, rows), rows)]
        return remote(block, block, send.at[origin], r_rows.at[origin], index)

    def each_origin(low, high):
        def turn(origin, carry):
            rows_copy(origin, s_ahead, after).wait_recv()
            return carry

        lax.fori_loop(low, high, turn, 0)

    def spread(r):
        @pl.when(has_right & (chip >= r))
        def _():
            pl.when(r > 0)(lambda: rows_copy(chip - r, s_ahead, after).wait_recv())
            rows_copy(chip - r, s_ahead, after).start()

        @pl.when(has_left & (from_end >= r))
        def _():
            pl.when(r > 0)(lambda: rows_copy(chip + r, s_behind, before).wait_recv())
            rows_copy(chip + r, s_behind, before).start()

    def hid_copy(j):
        place = pl.ds(pl.multiple_of(j * columns, columns), columns)
        return remote(
            hid_out.at[:, place], hid_in.at[:, place], s_hid.at[j], r_hid.at[j], sibling
        )

    proj_copy = remote(proj_out, proj_in, s_proj, r_proj, sibling)
    group = wide.shape[0]
    first = chip * 2 * share
    start = pl.multiple_of(first // group * group, group)
    inside = first - first // group * group

    def hidden_store(j):
        place = pl.ds(pl.multiple_of(j * columns, columns), columns)
        return pltpu.make_async_copy(wh_out.at[:, place], wh_hbm.at[:, place], wh_out_sem.at[j])

    def close_hidden(j):
        hid_copy(j).wait_recv()
        place = pl.ds(pl.multiple_of(j * columns, columns), columns)
        wh_out[:, place] += hid_in[:, place].astype(F32)
        hidden_store(j).start()

    def sum_store(w):
        return pltpu.make_async_copy(outs.at[w], outs_hbm.at[w], outs_sem.at[w])

    proj_store = pltpu.make_async_copy(wp_out, wp_hbm, wp_out_sem)

    def close_sum(w):
        outs[w] = own[w, chip].astype(F32)

        @pl.when(has_left)
        def _():
            right_copy(own.at[w, 0], w, rounds - 1).wait_recv()
            outs[w] += going_right[w, rounds - 1].astype(F32)

        @pl.when(has_right)
        def _():
            left_copy(own.at[w, 0], w, rounds - 1).wait_recv()
            outs[w] += going_left[w, rounds - 1].astype(F32)

        sum_store(w).start()

    def feed(j):
        slot = j % 2
        place = pl.ds(pl.multiple_of(j * columns, columns), columns)

        @pl.when(j == 0)
        def _():
            lh_copy.wait()
            pl.when(chip == 0)(lambda: each_origin(1, chips))
            pl.when(from_end == 0)(lambda: each_origin(0, chips - 1))

        wh_copy(j, slot).wait()
        wp_copy(j, slot).wait()

        @pl.when(j + 1 < peers)
        def _():
            wh_copy(j + 1, 1 - slot).start()
            wp_copy(j + 1, 1 - slot).start()

        active = jnp.maximum(dot_nn(lh[...], wh[slot]), 0.0)
        act[...] = active
        grown = (dot_nt(dp[...], wp[slot]) * 2.0 * act[...]).astype(BF16)
        wide[...] = dot_tn(lh[:, pl.ds(start, group)], grown)
        mine = pl.ds(pl.multiple_of(inside + core * share, 16), share)
        other = pl.ds(pl.multiple_of(inside + (1 - core) * share, 16), share)
        wh_out[:, place] = wide[mine, :]
        hid_out[:, place] = wide[other, :].astype(BF16)
        hid_copy(j).start()
        pl.when(j > 0)(lambda: close_hidden(j - 1))

        @pl.when(j == 2 * chip + core)
        def _():
            squared = (act[...] * act[...]).astype(BF16)
            wp_out[...] = dot_tn(squared, dp[...])

        @pl.when(j == 2 * chip + 1 - core)
        def _():
            squared = (act[...] * act[...]).astype(BF16)
            proj_out[...] = dot_tn(squared, dp[...]).astype(BF16)
            proj_copy.start()

    rounds = chips - 1
    prepare(0)
    pl.semaphore_wait(barrier, peers - 1)
    pair_copy(0).start()
    dp_copy.wait()
    spread(0)
    each_peer(lambda k: vector_copy(k, me).start())
    prepare(1)
    pair_copy(1).start()
    combine(0)
    if split_vectors:
        vec_out[...] = vgs[:, pl.ds(pl.multiple_of(me * cut, cut), cut)]
    else:
        vec_out[...] = vgs[...]
    opening = count * rounds - peers

    def step(t, carry):
        w, r = t // rounds, t % rounds
        travel(w, r)

        @pl.when((r == 1) & (w + 2 < count))
        def _():
            prepare(w + 2)
            pair_copy(w + 2).start()

        @pl.when((r == 1) & (w + 1 < count))
        def _():
            combine(w + 1)

        @pl.when(t + 1 < rounds)
        def _():
            spread(t + 1)

        @pl.when(t >= opening)
        def _():
            feed(t - opening)

        @pl.when((r == rounds - 1) & (w > 0))
        def _():
            close_sum(w - 1)

        return carry

    lax.fori_loop(0, count * rounds, step, 0)

    close_hidden(peers - 1)
    proj_copy.wait_recv()
    wp_out[...] += proj_in[...].astype(F32)
    proj_store.start()

    def collect(k):
        vector_copy(k, k).wait_recv()
        vec_out[...] += vgr[k]

    each_peer(collect)
    close_sum(count - 1)
    each_peer(lambda k: vector_copy(k, me).wait_send())

    def sent_hidden(j, carry):
        hid_copy(j).wait_send()
        hidden_store(j).wait()
        return carry

    lax.fori_loop(0, peers, sent_hidden, 0)
    proj_copy.wait_send()
    proj_store.wait()

    def sent_rows(origin, carry):
        @pl.when(has_right & (origin <= chip))
        def _():
            rows_copy(origin, s_ahead, after).wait_send()

        @pl.when(has_left & (origin >= chip))
        def _():
            rows_copy(origin, s_behind, before).wait_send()

        return carry

    lax.fori_loop(0, chips, sent_rows, 0)

    def sent(w, carry):
        pair_copy(w).wait_send()
        sum_store(w).wait()

        def sent_round(r, inner):
            @pl.when(has_right & (chip <= r))
            def _():
                right_copy(own.at[w, 0], w, r).wait_send()

            @pl.when(has_left & (from_end <= r))
            def _():
                left_copy(own.at[w, 0], w, r).wait_send()

            return inner

        lax.fori_loop(0, rounds, sent_round, 0)
        return carry

    lax.fori_loop(0, count, sent, 0)


def gradient_sums(peers, lefts, rights, lh, dp, wh, wp, vgs):
    count = len(lefts)
    rows, width = lefts[0].shape
    hidden = wh.shape[1]
    tokens = lh.shape[0]
    chips = peers // 2
    share = width // peers
    columns = hidden // peers
    group = max(128, 2 * share)
    shape = jax.ShapeDtypeStruct
    vmem = pl.BlockSpec(memory_space=pltpu.VMEM)
    anywhere = pl.BlockSpec(memory_space=pl.ANY)
    dma = pltpu.SemaphoreType.DMA
    blocks = pltpu.VMEM((count, chips, share, width), BF16)
    slots = pltpu.VMEM((count, chips - 1, share, width), BF16)
    split_vectors = share % 128 == 0
    cut = share if split_vectors else width
    return pl.pallas_call(
        partial(sum_kernel, peers, split_vectors),
        out_shape=(
            shape((count, share, width), F32), shape((share, hidden), F32),
            shape((columns, width), F32), shape((VECTORS, cut), F32),
        ),
        in_specs=[anywhere] * (2 * count + 4) + [vmem],
        out_specs=[anywhere] * 3 + [vmem],
        scratch_shapes=[
            pltpu.VMEM((count, rows, width), BF16), pltpu.VMEM((count, rows, width), BF16),
            pltpu.VMEM((2, width, width), F32),
            blocks, blocks, slots, slots,
            pltpu.VMEM((tokens, width), BF16), pltpu.VMEM((tokens, width), BF16),
            pltpu.VMEM((2, width, columns), BF16), pltpu.VMEM((2, columns, width), BF16),
            pltpu.VMEM((tokens, columns), F32), pltpu.VMEM((group, columns), F32),
            pltpu.VMEM((share, hidden), BF16), pltpu.VMEM((share, hidden), BF16),
            pltpu.VMEM((columns, width), BF16), pltpu.VMEM((columns, width), BF16),
            dma((count,)), dma((count,)), dma, dma, dma((2,)), dma((2,)),
            dma((count,)), dma((count,)),
            dma((count, chips - 1)), dma((count, chips - 1)),
            dma((count, chips - 1)), dma((count, chips - 1)),
            dma((peers,)), dma((peers,)), dma, dma,
            dma((chips,)), dma((chips,)), dma((chips,)),
            pltpu.VMEM((count, share, width), F32), pltpu.VMEM((share, hidden), F32),
            pltpu.VMEM((columns, width), F32), pltpu.VMEM((peers, VECTORS, cut), F32),
            dma((peers,)), dma((peers,)), dma((count,)), dma((peers,)), dma,
        ],
        compiler_params=pltpu.CompilerParams(
            collective_id=1, has_side_effects=True, vmem_limit_bytes=63 * 2**20
        ),
        name="gradient_sums",
    )(*lefts, *rights, lh, dp, wh, wp, vgs)


def deliver_kernel(count, vectors, *refs):
    vec, sources = refs[0], refs[1:6]
    targets = refs[6 : 6 + count]
    rows = refs[6 + count : 6 + count + vectors]
    buffers = refs[6 + count + vectors : -2]
    in_sem, out_sem = refs[-2:]
    pieces = list(sources[:-1]) + [sources[-1].at[w] for w in range(count - 4)]
    enter = [
        pltpu.make_async_copy(piece, buffer, in_sem.at[index])
        for index, (piece, buffer) in enumerate(zip(pieces, buffers))
    ]
    leave = [
        pltpu.make_async_copy(buffer, target, out_sem.at[index])
        for index, (buffer, target) in enumerate(zip(buffers, targets))
    ]
    for copy in enter:
        copy.start()
    for index, row in enumerate(rows):
        row[...] = vec[index : index + 1, :]
    for first, second in zip(enter, leave):
        first.wait()
        second.start()
    for copy in leave:
        copy.wait()


def deliver(vec, hidden, project, out, back, squares, vectors):
    shapes = [(out.shape, BF16), (back.shape, BF16), (hidden.shape, F32), (project.shape, F32)]
    shapes += [(squares.shape[1:], F32)] * squares.shape[0]
    count = len(shapes)
    anywhere = pl.BlockSpec(memory_space=pl.ANY)
    vmem = pl.BlockSpec(memory_space=pltpu.VMEM)
    dma = pltpu.SemaphoreType.DMA
    found = pl.pallas_call(
        partial(deliver_kernel, count, vectors),
        out_shape=tuple(jax.ShapeDtypeStruct(*kind) for kind in shapes)
        + (jax.ShapeDtypeStruct((1, vec.shape[1]), F32),) * vectors,
        in_specs=[vmem] + [anywhere] * 5,
        out_specs=[anywhere] * count + [vmem] * vectors,
        scratch_shapes=[pltpu.VMEM(*kind) for kind in shapes] + [dma((count,)), dma((count,))],
        compiler_params=pltpu.CompilerParams(vmem_limit_bytes=40 * 2**20),
        name="deliver",
    )(vec, out, back, hidden, project, squares)
    return found[:count], found[count:]


def per_device(x, top, spans, *parameters):
    sections = lax.axis_size("section")
    peers = lax.axis_size("dp")
    gain1, bias1, mix_k, mix_v, mix_g, log_rate, extra = parameters[0:7]
    wk, wv, wg, wo = parameters[7:11]
    gain2, bias2, mix_h, mix_f = parameters[11:15]
    wh, wp, wf = parameters[15:18]
    vectors = (gain1, bias1, mix_k, mix_v, mix_g, log_rate, extra, gain2, bias2, mix_h, mix_f)
    matrices = tuple(w[0] for w in (wk, wv, wg, wo, wh, wp, wf))
    found = relay(sections, peers, x, top, spans, vectors, matrices)
    out, back, lk, lv, lg, lgt, lf, dk, dv, dg, datt, dsv, dproj = found[0:13]
    vgs, lh = found[13], found[14].reshape(-1, x.shape[2])
    flat = (x.shape[0] * x.shape[1], x.shape[2])
    squares, d_wh, d_wp, vec = gradient_sums(
        peers,
        [part.reshape(flat) for part in (lf, lgt, lg, lk, lv)],
        [part.reshape(flat) for part in (dsv, datt, dg, dk, dv)],
        lh, dproj.reshape(flat), matrices[4], matrices[5], vgs,
    )
    share = x.shape[2] // peers
    if vec.shape[1] != share:
        vec = lax.dynamic_slice_in_dim(vec, lax.axis_index("dp") * share, share, 1)
    moved, rows = deliver(vec, d_wh, d_wp, out, back, squares, 11)
    out, back, d_wh, d_wp, d_wf, d_wo, d_wg, d_wk, d_wv = (part[None] for part in moved)
    return (
        out, back,
        rows[0], rows[1], rows[2], rows[3], rows[4], rows[5], rows[6],
        d_wk, d_wv, d_wg, d_wo,
        rows[7], rows[8], rows[9], rows[10],
        d_wh, d_wp, d_wf,
    )


def solution(mesh):
    tokens = P(None, "dp", None)
    vector = P("section", None)
    matrix = P("section", None, None)
    result = P("section", None, "dp", None)
    vector_grad = P("section", "dp")
    matrix_grad = P("section", "dp", None)
    return jax.shard_map(
        per_device,
        mesh=mesh,
        in_specs=(tokens, tokens, P())
        + (vector,) * 7 + (matrix,) * 4 + (vector,) * 4 + (matrix,) * 3,
        out_specs=(result, result)
        + (vector_grad,) * 7 + (matrix_grad,) * 4 + (vector_grad,) * 4 + (matrix_grad,) * 3,
        check_vma=False,
    )
```

```python
from functools import partial

import jax
import jax.numpy as jnp
from jax import lax
from jax.experimental import pallas as pl
from jax.experimental.pallas import tpu as pltpu
from jax.sharding import PartitionSpec as P

EPS = 1e-05
MESH = pl.DeviceIdType.MESH
RB = 64
PARTS = 1
VECTORS = 16
F32 = jnp.float32
BF16 = jnp.bfloat16


def dot_nn(left, right):
    return jnp.dot(left, right, preferred_element_type=F32)


def dot_nt(left, right):
    return lax.dot_general(left, right, (((1,), (1,)), ((), ())), preferred_element_type=F32)


def dot_tn(left, right):
    return lax.dot_general(left, right, (((0,), (0,)), ((), ())), preferred_element_type=F32)


def sigmoid(v):
    return 1.0 / (1.0 + jnp.exp(-v))


def normalise(source):
    centred = source - jnp.mean(source, axis=-1, keepdims=True)
    spread = lax.rsqrt(jnp.mean(centred * centred, axis=-1, keepdims=True) + EPS)
    return centred * spread, spread


def moved_down(rows, first):
    place = lax.broadcasted_iota(jnp.int32, rows.shape, 0)
    return jnp.where(place == 0, first, pltpu.roll(rows, 1, 0))


def moved_up(rows, last):
    count = rows.shape[0]
    place = lax.broadcasted_iota(jnp.int32, rows.shape, 0)
    return jnp.where(place == count - 1, last, pltpu.roll(rows, count - 1, 0))


def fold(rows):
    total = rows[0:8]
    for at in range(8, rows.shape[0], 8):
        total = total + rows[at : at + 8]
    return total


def relay_kernel(sections, peers, *refs):
    (
        spans, x_in, top_in,
        gain1, bias1, mix_k, mix_v, mix_g, log_rate, extra, gain2, bias2, mix_h, mix_f,
        wk_in, wv_in, wg_in, wo_in, wh_in, wp_in, wf_in,
        out_hbm, back_hbm, lk_hbm, lv_hbm, lg_hbm, lgt_hbm, lf_hbm,
        dk_hbm, dv_hbm, dg_hbm, datt_hbm, dsv_hbm, dproj_hbm, vgs, lh_all, near,
        wk_t, wv_t, wg_t, wo_t, wf_t, wp_t, wh_t,
        out, back, lk, lv, lg, lgt, lf, dk, dv, dg, datt, dsv, dproj,
        lh, sq, dh, turned,
        wk, wv, wg, wo, wh, wp, wf,
        xs, hx, dys, kk, vv, sg, sa, sb, mid, hmid, proj, sv, act,
        e0, e1, low_mask, up_mask, split, acc, t1, t2, t3,
        states, back_states, de2, de1, sum_row, sum_back, send_de2, send_de1, vg,
        sp1, gp1, sd1, sp2, gp2, sd2, fo, iv,
        w_sem, x_sem, top_sem, s_h0, s_x, s_hx, s_st, s_mid, s_dy, s_de2, s_bst, s_de1,
        r_x, r_hx, r_st, r_mid, r_dy, r_de2, r_bst, r_de1, store_sem,
        s_lh, r_lh, own_sem, s_near, r_near, turn_sem, back_sem,
    ) = refs
    me_s = lax.axis_index("section")
    me = lax.axis_index("dp")
    batches, row_count, width = x_in.shape
    hidden = wh.shape[1]
    chunks = row_count // RB
    base = me * row_count

    def at(section, index):
        return (section, index)

    barrier = pltpu.get_barrier_semaphore()

    def greet(section, index):
        pl.semaphore_signal(barrier, inc=1, device_id=at(section, index), device_id_type=MESH)

    def greet_peer(k, carry):
        @pl.when(k != me)
        def _():
            greet(me_s, k)

        return carry

    lax.fori_loop(0, peers, greet_peer, 0)
    has_next = me_s + 1 < sections
    has_prior = me_s > 0
    has_right = me + 1 < peers
    has_left = me > 0

    @pl.when(has_next)
    def _():
        greet(me_s + 1, me)

    @pl.when(has_prior)
    def _():
        greet(me_s - 1, me)

    @pl.when(has_next & has_right)
    def _():
        greet(me_s + 1, me + 1)

    @pl.when(has_prior & has_left)
    def _():
        greet(me_s - 1, me - 1)

    weight_copies = [
        pltpu.make_async_copy(source, target, w_sem.at[index])
        for index, (source, target) in enumerate(
            ((wk_in, wk), (wv_in, wv), (wg_in, wg), (wo_in, wo), (wf_in, wf), (wh_in, wh), (wp_in, wp))
        )
    ]

    @pl.when(me_s == 0)
    def _():
        pltpu.make_async_copy(x_in, xs, x_sem).start()

    for copy in weight_copies[0:2]:
        copy.start()

    @pl.when(me_s == sections - 1)
    def _():
        pltpu.make_async_copy(top_in, dys, top_sem).start()

    rate = jnp.exp(log_rate[...])
    boost = jnp.exp(extra[...])
    decay_block = jnp.exp(-rate * row_count)
    grow_block = jnp.exp(rate * row_count)

    half = width // 128

    def packed(row_a, row_b):
        return jnp.concatenate(
            [row[:, j * 128 : (j + 1) * 128] for row in (row_a, row_b) for j in range(half)], axis=0
        )

    def unpacked(tile, part):
        return jnp.concatenate(
            [tile[part * half + j : part * half + j + 1] for j in range(half)], axis=1
        )

    decay_tile = packed(decay_block, decay_block)

    def starts_of(m):
        found = []
        total = jnp.int32(0)
        for j in range(spans.shape[1]):
            found.append(total)
            total = total + spans[m, j]
        return found

    def segment(position, starts):
        total = jnp.where(position >= starts[0], 1, 0)
        for start in starts[1:]:
            total = total + jnp.where(position >= start, 1, 0)
        return total

    def column(i):
        return base + i * RB + lax.broadcasted_iota(jnp.int32, (RB, 1), 0)

    def keep_of(position, starts):
        return jnp.where(segment(position, starts) == segment(position - 1, starts), 1.0, 0.0)

    def fill_powers(i, carry):
        place = (i * RB + lax.broadcasted_iota(jnp.int32, (RB, width), 0)).astype(F32)
        e0[pl.ds(pl.multiple_of(i * RB, RB), RB), :] = jnp.exp(-place * rate)
        e1[pl.ds(pl.multiple_of(i * RB, RB), RB), :] = jnp.exp((place - (row_count - 1.0)) * rate)
        return carry

    lax.fori_loop(0, chunks, fill_powers, 0)
    for m in range(batches):
        starts = starts_of(m)
        row_at = lax.broadcasted_iota(jnp.int32, (row_count, row_count), 0)
        column_at = lax.broadcasted_iota(jnp.int32, (row_count, row_count), 1)
        same = segment(base + row_at, starts) == segment(base + column_at, starts)
        lower = jnp.where(same & (column_at < row_at), 1.0, 0.0).astype(BF16)
        upper = jnp.where(same & (column_at > row_at), 1.0, 0.0).astype(BF16)
        low_mask[m, :, 0:row_count] = lower
        low_mask[m, :, row_count:] = lower
        up_mask[m, :, 0:row_count] = upper
        up_mask[m, :, row_count:] = upper
    vg[...] = jnp.zeros_like(vg)

    @pl.when(me == 0)
    def _():
        hx[...] = jnp.zeros_like(hx)
        hmid[...] = jnp.zeros_like(hmid)

    @pl.when(me == peers - 1)
    def _():
        de1[...] = jnp.zeros_like(de1)
        de2[...] = jnp.zeros_like(de2)

    greeted = (
        peers - 1
        + jnp.where(has_next, 1, 0)
        + jnp.where(has_prior, 1, 0)
        + jnp.where(has_next & has_right, 1, 0)
        + jnp.where(has_prior & has_left, 1, 0)
    )
    pl.semaphore_wait(barrier, greeted)
    for copy in weight_copies[2:7]:
        copy.start()

    def remote(source, target, send, receive, section, index):
        return pltpu.make_async_remote_copy(
            src_ref=source, dst_ref=target, send_sem=send, recv_sem=receive,
            device_id=at(section, index), device_id_type=MESH,
        )

    right = jnp.minimum(me + 1, peers - 1)
    left = jnp.maximum(me - 1, 0)
    above = jnp.minimum(me_s + 1, sections - 1)
    below = jnp.maximum(me_s - 1, 0)
    tail = pl.ds(row_count - 16, 16)
    final = pl.ds(row_count - 1, 1)

    stored = (
        (out, out_hbm), (lk, lk_hbm), (lv, lv_hbm), (lg, lg_hbm), (lgt, lgt_hbm), (lf, lf_hbm),
        (dproj, dproj_hbm), (dsv, dsv_hbm), (datt, datt_hbm), (dg, dg_hbm), (dk, dk_hbm),
        (dv, dv_hbm), (back, back_hbm),
    )

    def store_copy(index, m):
        source, target = stored[index]
        return pltpu.make_async_copy(source.at[m], target.at[m], store_sem.at[index, m])

    def start_halo(m):
        return remote(x_in.at[m, tail], hx.at[m], s_h0.at[m], r_hx.at[m], me_s, right)

    def part_of(j):
        return pl.ds(pl.multiple_of(j * (width // PARTS), width // PARTS), width // PARTS)

    def result_copy(m, j):
        return remote(
            out.at[m, :, part_of(j)], xs.at[m, :, part_of(j)],
            s_x.at[m, j], r_x.at[m, j], above, me,
        )

    def each_part(action):
        def turn(j, carry):
            action(j)
            return carry

        lax.fori_loop(0, PARTS, turn, 0)

    def result_halo(m):
        return remote(out.at[m, tail], hx.at[m], s_hx.at[m], r_hx.at[m], above, right)

    def middle_halo(m):
        return remote(mid.at[m, final], hmid.at[m], s_mid.at[m], r_mid.at[m], me_s, right)

    def state_copy(m, k, slot):
        return remote(sum_row.at[m], states.at[m, slot], s_st.at[m, k], r_st.at[m, slot], me_s, k)

    pieces = (
        (0, row_count // 2), (row_count // 2, row_count // 2 - 16), (row_count - 16, 16)
    )

    def back_copy(m, index):
        rows = pl.ds(*pieces[index])
        return remote(
            back.at[m, rows], dys.at[m, rows], s_dy.at[m, index], r_dy.at[m, index], below, me
        )

    def each_piece(action):
        for index in range(len(pieces)):
            action(index)

    def second_copy(m):
        return remote(send_de2.at[m], de2.at[m], s_de2.at[m], r_de2.at[m], me_s, left)

    def first_copy(m):
        return remote(send_de1.at[m], de1.at[m], s_de1.at[m], r_de1.at[m], me_s, left)

    def back_state_copy(m, k, slot):
        return remote(
            sum_back.at[m], back_states.at[m, slot], s_bst.at[m, k], r_bst.at[m, slot], me_s, k
        )

    chip, core = me // 2, me % 2
    chips = peers // 2

    def gather_copy(m, k, slot):
        return remote(
            lh.at[m], lh_all.at[slot, m], s_lh.at[m, k], r_lh.at[m, slot], me_s, 2 * k + core
        )

    is_late = 2 * me_s >= sections

    def own_copy(m):
        return pltpu.make_async_copy(lh.at[m], lh_all.at[chip, m], own_sem.at[m])

    def each_chip(action):
        def turn(k, carry):
            @pl.when(k != chip)
            def _():
                action(k)

            return carry

        lax.fori_loop(0, chips, turn, 0)

    ahead = jnp.minimum(me + 2, peers - 1)
    behind = jnp.maximum(me - 2, 0)
    has_ahead = chip + 1 < chips
    has_behind = chip > 0

    def near_copy(m, way):
        return remote(
            dproj.at[m], near.at[way, m], s_near.at[way, m], r_near.at[way, m],
            me_s, behind if way else ahead,
        )

    def send_near(m):
        pl.when(has_ahead)(lambda: near_copy(m, 0).start())
        pl.when(has_behind)(lambda: near_copy(m, 1).start())

    def end_near(m):
        @pl.when(has_ahead)
        def _():
            near_copy(m, 0).wait_send()
            near_copy(m, 1).wait_recv()

        @pl.when(has_behind)
        def _():
            near_copy(m, 1).wait_send()
            near_copy(m, 0).wait_recv()

    def start_gathers():
        for m in range(batches):
            own_copy(m).start()

            @pl.when(jnp.logical_not(is_late))
            def _(m=m):
                each_chip(lambda k: gather_copy(m, k, chip).start())

    def end_gather(m):
        own_copy(m).wait()

        @pl.when(jnp.logical_not(is_late))
        def _():
            each_chip(lambda k: gather_copy(m, k, chip).wait_send())
            each_chip(lambda k: gather_copy(m, k, k).wait_recv())

    @pl.when((me_s == 0) & has_right)
    def _():
        for m in range(batches):
            start_halo(m).start()

    @pl.when(me_s == 0)
    def _():
        pltpu.make_async_copy(x_in, xs, x_sem).wait()

    turns = (
        (wk, wk_t), (wv, wv_t), (wg, wg_t), (wo, wo_t), (wf, wf_t), (wh, wh_t), (wp, wp_t)
    )
    returns = (
        (wk_t, wk), (wv_t, wv), (wg_t, wg), (wo_t, wo), (wf_t, wf), (wp_t, wh), (wh_t, wp)
    )
    edge = turned.shape[1]

    def transpose_all(fresh):
        for index, (source, target) in enumerate(turns):
            if fresh:
                weight_copies[index].wait()
            tall = source.shape[0] // edge
            blocks = tall * (source.shape[1] // edge)

            def place(n, source=source, target=target, tall=tall):
                down = pl.ds(pl.multiple_of(n % tall * edge, edge), edge)
                along = pl.ds(pl.multiple_of(n // tall * edge, edge), edge)
                slot = n % 2
                return (
                    source.at[down, along],
                    turned.at[slot],
                    pltpu.make_async_copy(turned.at[slot], target.at[along, down], turn_sem.at[slot]),
                )

            def turn(n, carry, place=place):
                piece, buffer, copy = place(n)
                pl.when(n >= 2)(copy.wait)
                buffer[...] = piece[...].T
                copy.start()
                return carry

            lax.fori_loop(0, blocks, turn, 0)
            for n in range(blocks - 2, blocks):
                place(n)[2].wait()

    def return_copy(index):
        source, target = returns[index]
        return pltpu.make_async_copy(source, target, back_sem.at[index])


    def release(m, index):
        @pl.when(is_late & (m == batches - 1))
        def _():
            return_copy(index).start()

    def weight_ready(m, index, fresh=True):
        @pl.when((m == 0) & jnp.logical_not(is_late))
        def _():
            weight_copies[index].wait()

    def span_of(i):
        return pl.ds(pl.multiple_of(i * RB, RB), RB)

    def split_sums():
        def turn(i, carry):
            rows = span_of(i)
            low = pl.ds(pl.multiple_of(row_count + i * RB, RB), RB)
            for source, place in ((t1, pl.ds(0, width)), (t2, pl.ds(width, width))):
                value = source[rows, :]
                high = value.astype(BF16)
                split[rows, place] = high
                split[low, place] = (value - high.astype(F32)).astype(BF16)
            return carry

        lax.fori_loop(0, chunks, turn, 0, unroll=True)

    def forward(m, carry):
        starts = starts_of(m)

        @pl.when(has_prior)
        def _():
            each_part(lambda j: result_copy(m, j).wait_recv())

        @pl.when(has_left)
        def _():
            start_halo(m).wait_recv()

        halo_rows, _ = normalise(hx[m].astype(F32))
        halo_rows = halo_rows * gain1[...] + bias1[...]

        def mix_in(i, last):
            rows = span_of(i)
            spare, spread = normalise(xs[m, rows, :].astype(F32))
            sp1[m, rows, :] = spare
            sd1[m, rows, :] = spread
            normed = spare * gain1[...] + bias1[...]
            earlier = moved_down(normed, last) * keep_of(column(i), starts)
            gap = normed - earlier
            gp1[m, rows, :] = gap.astype(BF16)
            lk[m, rows, :] = (earlier + gap * mix_k[...]).astype(BF16)
            lv[m, rows, :] = (earlier + gap * mix_v[...]).astype(BF16)
            lg[m, rows, :] = (earlier + gap * mix_g[...]).astype(BF16)
            return normed[RB - 1 : RB]

        lax.fori_loop(0, chunks, mix_in, halo_rows[15:16], unroll=True)
        weight_ready(m, 0)
        weight_ready(m, 1)
        kk[m] = dot_nn(lk[m], wk[...])
        vv[m] = dot_nn(lv[m], wv[...])
        release(m, 0)
        release(m, 1)
        end_segment = segment(base + row_count - 1, starts)

        def spread_in(i, totals):
            rows = span_of(i)
            plain = jnp.exp(kk[m, rows, :])
            kk[m, rows, :] = plain
            weight = plain * e1[rows, :]
            weighted = weight * vv[m, rows, :]
            t1[rows, :] = weighted
            t2[rows, :] = weight
            chosen = segment(column(i), starts) == end_segment
            return (
                totals[0] + fold(jnp.where(chosen, weighted, 0.0)),
                totals[1] + fold(jnp.where(chosen, weight, 0.0)),
            )

        nothing = jnp.zeros((8, width), F32)
        total_a, total_b = lax.fori_loop(0, chunks, spread_in, (nothing, nothing), unroll=True)
        sum_row[m] = packed(
            jnp.sum(total_a, axis=0, keepdims=True), jnp.sum(total_b, axis=0, keepdims=True)
        )

        def send_state(k, carry):
            state_copy(m, k, me).start()
            return carry

        lax.fori_loop(me + 1, peers, send_state, 0)

        weight_ready(m, 2)
        sg[m] = dot_nn(lg[m], wg[...])
        split_sums()
        acc[...] = dot_nn(low_mask[m], split[...])
        sg[m] = sigmoid(sg[m])
        release(m, 2)

        def receive_state(k, held):
            state_copy(m, k, k).wait_recv()
            unbroken = segment(k * row_count - 1, starts) == segment(
                (k + 1) * row_count - 1, starts
            )
            passing = jnp.where(unbroken, 1.0, 0.0) * decay_tile
            return passing * held + states[m, k]

        none = jnp.zeros((1, width), F32)
        entered = lax.fori_loop(0, me, receive_state, jnp.zeros_like(decay_tile))
        enter_a, enter_b = unpacked(entered, 0), unpacked(entered, 1)
        prior_segment = segment(base - 1, starts)

        def mix_states(i, carry):
            rows = span_of(i)
            falling = e0[rows, :]
            chosen = jnp.where(segment(column(i), starts) == prior_segment, 1.0, 0.0)
            grown = falling * grow_block
            held = falling * chosen
            state_a = grown * acc[rows, 0:width] + held * enter_a
            state_b = grown * acc[rows, width:] + held * enter_b
            sa[m, rows, :] = state_a
            sb[m, rows, :] = state_b
            present = boost * kk[m, rows, :]
            inverse = 1.0 / (state_b + present)
            found = (state_a + present * vv[m, rows, :]) * inverse
            iv[m, rows, :] = inverse
            fo[m, rows, :] = found
            lgt[m, rows, :] = (sg[m, rows, :] * found).astype(BF16)
            return carry

        lax.fori_loop(0, chunks, mix_states, 0, unroll=True)

        weight_ready(m, 3)
        mid[m] = xs[m].astype(F32) + dot_nn(lgt[m], wo[...])
        release(m, 3)

        @pl.when(has_right)
        def _():
            middle_halo(m).start()

        def mix_second(start, size, last):
            rows = pl.ds(start, size)
            spare, spread = normalise(mid[m, rows, :])
            sp2[m, rows, :] = spare
            sd2[m, rows, :] = spread
            normed = spare * gain2[...] + bias2[...]
            position = base + start + lax.broadcasted_iota(jnp.int32, (size, 1), 0)
            earlier = moved_down(normed, last) * keep_of(position, starts)
            gap = normed - earlier
            gp2[m, rows, :] = gap.astype(BF16)
            lh[m, rows, :] = (earlier + gap * mix_h[...]).astype(BF16)
            lf[m, rows, :] = (earlier + gap * mix_f[...]).astype(BF16)
            return normed[size - 1 : size]

        last = none
        for start in range(0, row_count, RB):
            last = mix_second(start, RB, last)

        @pl.when(has_left)
        def _():
            middle_halo(m).wait_recv()

        halo_rows, _ = normalise(hmid[m])
        mix_second(0, 16, halo_rows * gain2[...] + bias2[...])

        for index in range(4, 7):
            weight_ready(m, index)
        sv[m] = dot_nn(lf[m], wf[...])

        def widen(j, carry):
            columns = pl.ds(pl.multiple_of(j * width, width), width)
            active = jnp.maximum(dot_nn(lh[m], wh[:, columns]), 0.0)
            act[m, :, columns] = active.astype(BF16)
            sq[m, :, columns] = (active * active).astype(BF16)
            return carry

        lax.fori_loop(0, hidden // width, widen, 0, unroll=True)
        release(m, 4)
        release(m, 5)

        def finish(j, carry):
            columns = part_of(j)
            found = dot_nn(sq[m], wp[:, columns])
            proj[m, :, columns] = found
            sieve = sigmoid(sv[m, :, columns])
            sv[m, :, columns] = sieve
            out[m, :, columns] = (mid[m, :, columns] + sieve * found).astype(BF16)

            @pl.when(has_next)
            def _():
                result_copy(m, j).start()

            return carry

        lax.fori_loop(0, PARTS, finish, 0)
        release(m, 6)

        @pl.when(has_next & has_right)
        def _():
            result_halo(m).start()

        for index in range(6):
            store_copy(index, m).start()

        return carry

    pl.when(is_late)(lambda: transpose_all(True))
    lax.fori_loop(0, batches, forward, 0)

    @pl.when(jnp.logical_not(is_late))
    def _():
        transpose_all(False)
        for index in range(7):
            return_copy(index).start()

    start_gathers()

    def add_vector(index, value):
        vg[index] += fold(value)

    @pl.when(me_s == sections - 1)
    def _():
        pltpu.make_async_copy(top_in, dys, top_sem).wait()

    def turned_ready(m, index):
        @pl.when(m == 0)
        def _():
            return_copy(index).wait()

    def backward(m, carry):
        starts = starts_of(m)
        none = jnp.zeros((1, width), F32)

        @pl.when(has_next)
        def _():
            each_piece(lambda i: back_copy(m, i).wait_recv())

        def open_back(i, carry):
            rows = span_of(i)
            incoming = dys[m, rows, :].astype(F32)
            sieve = sv[m, rows, :]
            gained = incoming * sieve
            dproj[m, rows, :] = gained.astype(BF16)
            dsv[m, rows, :] = (gained * proj[m, rows, :] * (1.0 - sieve)).astype(BF16)
            return carry

        lax.fori_loop(0, chunks, open_back, 0, unroll=True)
        t1[...] = jnp.zeros_like(t1)
        turned_ready(m, 5)
        turned_ready(m, 6)

        def narrow(j, carry):
            columns = pl.ds(pl.multiple_of(j * width, width), width)
            grown = dot_nn(dproj[m], wh[:, columns])
            dh[m, :, columns] = (grown * 2.0 * act[m, :, columns].astype(F32)).astype(BF16)
            t1[...] += dot_nn(dh[m, :, columns], wp[columns, :])
            return carry

        lax.fori_loop(0, hidden // width, narrow, 0, unroll=True)
        turned_ready(m, 4)
        t2[...] = dot_nn(dsv[m], wf[...])

        def second_earlier(rows, position):
            whole = t1[rows, :] * (1.0 - mix_h[...]) + t2[rows, :] * (1.0 - mix_f[...])
            return whole * keep_of(position, starts)

        eight = lax.broadcasted_iota(jnp.int32, (8, 1), 0)
        send_de2[m] = second_earlier(pl.ds(0, 8), base + eight)[0:1]

        @pl.when(has_left)
        def _():
            second_copy(m).start()

        def back_second(start, size, following):
            rows = pl.ds(start, size)
            spare, spread = sp2[m, rows, :], sd2[m, rows, :]
            gap = gp2[m, rows, :].astype(F32)
            position = base + start + lax.broadcasted_iota(jnp.int32, (size, 1), 0)
            kept = keep_of(position, starts)
            from_h = t1[rows, :]
            from_f = t2[rows, :]
            add_vector(9, from_h * gap)
            add_vector(10, from_f * gap)
            straight = from_h * mix_h[...] + from_f * mix_f[...]
            earlier = (from_h + from_f - straight) * kept
            d_normed = straight + moved_up(earlier, following)
            add_vector(7, d_normed * spare)
            add_vector(8, d_normed)
            scaled = d_normed * gain2[...]
            mean_one = jnp.mean(scaled, axis=-1, keepdims=True)
            mean_two = jnp.mean(scaled * spare, axis=-1, keepdims=True)
            d_mid = dys[m, rows, :].astype(F32) + spread * (scaled - mean_one - spare * mean_two)
            t3[rows, :] = d_mid
            datt[m, rows, :] = d_mid.astype(BF16)

        for start, size in pieces[:-1]:
            end = start + size
            back_second(start, size, second_earlier(pl.ds(end, 8), base + end + eight)[0:1])

        @pl.when(has_right)
        def _():
            second_copy(m).wait_recv()

        back_second(*pieces[-1], de2[m])
        turned_ready(m, 3)
        t1[...] = dot_nn(datt[m], wo[...])
        open_segment = segment(base, starts)

        def back_states_in(i, totals):
            rows = span_of(i)
            d_found = t1[rows, :] * sg[m, rows, :]
            d_a = d_found * iv[m, rows, :]
            d_b = -d_a * fo[m, rows, :]
            falling = e0[rows, :]
            scaled_a = d_a * falling
            scaled_b = d_b * falling
            t1[rows, :] = scaled_a
            t2[rows, :] = scaled_b
            acc[rows, 0:width] = d_found
            chosen = segment(column(i), starts) == open_segment
            return (
                totals[0] + fold(jnp.where(chosen, scaled_a, 0.0)),
                totals[1] + fold(jnp.where(chosen, scaled_b, 0.0)),
            )

        nothing = jnp.zeros((8, width), F32)
        total_a, total_b = lax.fori_loop(0, chunks, back_states_in, (nothing, nothing), unroll=True)
        sum_back[m] = packed(
            jnp.sum(total_a, axis=0, keepdims=True), jnp.sum(total_b, axis=0, keepdims=True)
        )

        def send_state(k, carry):
            back_state_copy(m, k, me).start()
            return carry

        lax.fori_loop(0, me, send_state, 0)
        split_sums()

        def back_present(i, carry):
            rows = span_of(i)
            gate, found = sg[m, rows, :], fo[m, rows, :]
            d_found = acc[rows, 0:width]
            dg[m, rows, :] = (d_found * found * (1.0 - gate)).astype(BF16)
            gained = d_found * iv[m, rows, :] * (boost * kk[m, rows, :])
            d_key = gained * (vv[m, rows, :] - found)
            add_vector(6, d_key)
            t1[rows, :] = d_key
            t2[rows, :] = gained
            return carry

        lax.fori_loop(0, chunks, back_present, 0, unroll=True)
        acc[...] = dot_nn(up_mask[m], split[...])

        def receive_state(turn, held):
            k = peers - 1 - turn
            back_state_copy(m, k, k).wait_recv()
            first = segment(k * row_count, starts)
            unbroken = first == segment((k + 1) * row_count - 1, starts)
            joined = jnp.where(first == segment(k * row_count - 1, starts), 1.0, 0.0)
            passing = jnp.where(unbroken, 1.0, 0.0) * decay_tile
            return joined * (passing * held + back_states[m, k])

        entered = lax.fori_loop(0, peers - 1 - me, receive_state, jnp.zeros_like(decay_tile))
        enter_a, enter_b = unpacked(entered, 0), unpacked(entered, 1)
        end_segment = segment(base + row_count - 1, starts)

        def back_keys(i, carry):
            rows = span_of(i)
            rising = e1[rows, :]
            chosen = jnp.where(segment(column(i), starts) == end_segment, 1.0, 0.0)
            grown = rising * grow_block
            held = rising * chosen
            d_a = grown * acc[rows, 0:width] + held * enter_a
            d_b = grown * acc[rows, width:] + held * enter_b
            add_vector(5, d_a * sa[m, rows, :] + d_b * sb[m, rows, :])
            weight = kk[m, rows, :]
            dv[m, rows, :] = (t2[rows, :] + d_a * weight).astype(BF16)
            dk[m, rows, :] = (t1[rows, :] + (d_a * vv[m, rows, :] + d_b) * weight).astype(BF16)
            return carry

        lax.fori_loop(0, chunks, back_keys, 0, unroll=True)
        for index in range(3):
            turned_ready(m, index)
        t1[...] = dot_nn(dk[m], wk[...])
        t2[...] = dot_nn(dv[m], wv[...])
        acc[:, 0:width] = dot_nn(dg[m], wg[...])

        def first_earlier(rows, position):
            whole = (
                t1[rows, :] * (1.0 - mix_k[...])
                + t2[rows, :] * (1.0 - mix_v[...])
                + acc[rows, 0:width] * (1.0 - mix_g[...])
            )
            return whole * keep_of(position, starts)

        send_de1[m] = first_earlier(pl.ds(0, 8), base + eight)[0:1]

        @pl.when(has_left)
        def _():
            first_copy(m).start()

        pl.when(me_s == 0)(lambda: send_near(m))
        for index in range(6, 12):
            store_copy(index, m).start()

        def back_first(index, following):
            start, size = pieces[index]
            rows = pl.ds(start, size)
            spare, spread = sp1[m, rows, :], sd1[m, rows, :]
            gap = gp1[m, rows, :].astype(F32)
            position = base + start + lax.broadcasted_iota(jnp.int32, (size, 1), 0)
            kept = keep_of(position, starts)
            from_k = t1[rows, :]
            from_v = t2[rows, :]
            from_g = acc[rows, 0:width]
            add_vector(2, from_k * gap)
            add_vector(3, from_v * gap)
            add_vector(4, from_g * gap)
            straight = from_k * mix_k[...] + from_v * mix_v[...] + from_g * mix_g[...]
            earlier = (from_k + from_v + from_g - straight) * kept
            d_normed = straight + moved_up(earlier, following)
            add_vector(0, d_normed * spare)
            add_vector(1, d_normed)
            scaled = d_normed * gain1[...]
            mean_one = jnp.mean(scaled, axis=-1, keepdims=True)
            mean_two = jnp.mean(scaled * spare, axis=-1, keepdims=True)
            found = t3[rows, :] + spread * (scaled - mean_one - spare * mean_two)
            back[m, rows, :] = found.astype(BF16)

            @pl.when(has_prior)
            def _():
                back_copy(m, index).start()

        for index, (start, size) in enumerate(pieces[:-1]):
            end = start + size
            back_first(index, first_earlier(pl.ds(end, 8), base + end + eight)[0:1])

        @pl.when(has_right)
        def _():
            first_copy(m).wait_recv()

        back_first(len(pieces) - 1, de1[m])
        store_copy(12, m).start()
        return carry

    lax.fori_loop(0, batches, backward, 0)
    pl.when(has_prior)(lambda: each_piece(lambda i: back_copy(batches - 1, i).wait_send()))

    @pl.when(me_s > 0)
    def _():
        for m in range(batches):
            send_near(m)


    vgs[...] = jnp.sum(vg[...], axis=1)
    vgs[5:6] = vgs[5:6] * (-rate * jnp.exp(-rate))
    def close(m, carry):
        @pl.when((me_s == 0) & has_right)
        def _():
            start_halo(m).wait_send()

        @pl.when(has_next)
        def _():
            each_part(lambda j: result_copy(m, j).wait_send())

        @pl.when(has_next & has_right)
        def _():
            result_halo(m).wait_send()

        @pl.when(has_right)
        def _():
            middle_halo(m).wait_send()

        @pl.when(has_left)
        def _():
            second_copy(m).wait_send()
            first_copy(m).wait_send()

        @pl.when(has_prior)
        def _():
            pl.when(m + 1 < batches)(lambda: each_piece(lambda i: back_copy(m, i).wait_send()))

        for index in range(13):
            store_copy(index, m).wait()

        def ended(k, carry):
            state_copy(m, k, me).wait_send()
            return carry

        lax.fori_loop(me + 1, peers, ended, 0)
        end_gather(m)
        end_near(m)

        def ended_back(k, carry):
            back_state_copy(m, k, me).wait_send()
            return carry

        lax.fori_loop(0, me, ended_back, 0)
        return carry

    lax.fori_loop(0, batches, close, 0)


def relay(sections, peers, x, top, spans, vectors, matrices):
    batches, rows, width = x.shape
    hidden = matrices[4].shape[1]
    shape = jax.ShapeDtypeStruct
    low = shape((batches, rows, width), BF16)
    square = shape((width, width), BF16)
    vmem = pl.BlockSpec(memory_space=pltpu.VMEM)
    anywhere = pl.BlockSpec(memory_space=pl.ANY)
    dma = pltpu.SemaphoreType.DMA

    def narrow(kind):
        return pltpu.VMEM((batches, rows, width), kind)

    return pl.pallas_call(
        partial(relay_kernel, sections, peers),
        out_shape=(
            low, low, low, low, low, low, low,
            low, low, low, low, low, low, shape((VECTORS, width), F32),
            shape((peers // 2, batches, rows, width), BF16),
            shape((2, batches, rows, width), BF16),
            square, square, square, square, square,
            shape((width, hidden), BF16), shape((hidden, width), BF16),
        ),
        in_specs=[pl.BlockSpec(memory_space=pltpu.SMEM), anywhere, anywhere]
        + [vmem] * 11
        + [anywhere] * 7,
        out_specs=[anywhere] * 13 + [vmem] + [anywhere] * 9,
        scratch_shapes=[narrow(BF16)] * 13 + [
            narrow(BF16), pltpu.VMEM((batches, rows, hidden), BF16),
            pltpu.VMEM((batches, rows, hidden), BF16), pltpu.VMEM((2, 512, 512), BF16),
        ]
        + [pltpu.VMEM(matrix.shape, BF16) for matrix in matrices_order(matrices)]
        + [
            narrow(BF16), pltpu.VMEM((batches, 16, width), BF16), narrow(BF16),
            narrow(F32), narrow(F32), narrow(F32), narrow(F32), narrow(F32), narrow(F32),
            pltpu.VMEM((batches, 1, width), F32), narrow(F32), narrow(F32),
            pltpu.VMEM((batches, rows, hidden), BF16),
            pltpu.VMEM((rows, width), F32), pltpu.VMEM((rows, width), F32),
            pltpu.VMEM((batches, rows, 2 * rows), BF16), pltpu.VMEM((batches, rows, 2 * rows), BF16),
            pltpu.VMEM((2 * rows, 2 * width), BF16), pltpu.VMEM((rows, 2 * width), F32),
            pltpu.VMEM((rows, width), F32), pltpu.VMEM((rows, width), F32), pltpu.VMEM((rows, width), F32),
            pltpu.VMEM((batches, peers, width // 64, 128), F32),
            pltpu.VMEM((batches, peers, width // 64, 128), F32),
            pltpu.VMEM((batches, 1, width), F32), pltpu.VMEM((batches, 1, width), F32),
            pltpu.VMEM((batches, width // 64, 128), F32),
            pltpu.VMEM((batches, width // 64, 128), F32),
            pltpu.VMEM((batches, 1, width), F32), pltpu.VMEM((batches, 1, width), F32),
            pltpu.VMEM((VECTORS, 8, width), F32),
            narrow(F32), narrow(BF16), pltpu.VMEM((batches, rows, 1), F32),
            narrow(F32), narrow(BF16), pltpu.VMEM((batches, rows, 1), F32),
            narrow(F32), narrow(F32),
            dma((7,)), dma, dma,
            dma((batches,)), dma((batches, PARTS)), dma((batches,)), dma((batches, peers)),
            dma((batches,)), dma((batches, 3)), dma((batches,)), dma((batches, peers)),
            dma((batches,)),
            dma((batches, PARTS)), dma((batches,)), dma((batches, peers)), dma((batches,)),
            dma((batches, 3)), dma((batches,)), dma((batches, peers)), dma((batches,)),
            dma((13, batches)),
            dma((batches, peers // 2)), dma((batches, peers // 2)), dma((batches,)),
            dma((2, batches)), dma((2, batches)),
            dma((2,)), dma((7,)),
        ],
        compiler_params=pltpu.CompilerParams(
            collective_id=0, has_side_effects=True, vmem_limit_bytes=63 * 2**20
        ),
        name="relay",
    )(spans, x, top, *vectors, *matrices_order(matrices))


def matrices_order(matrices):
    wk, wv, wg, wo, wh, wp, wf = matrices
    return (wk, wv, wg, wo, wh, wp, wf)


def sum_kernel(sections, peers, split_vectors, *refs):
    left_in, right_in = refs[0:5], refs[5:10]
    lh_in, dp_in, near_in, wh_in, wp_in, vgs = refs[10:16]
    outs_hbm, wh_hbm, wp_hbm, vec_out = refs[16:20]
    (
        lefts, rights, whole, own, pair_out, going_right, going_left,
        lh, dp, wh, wp, act, wide, hid_out, hid_in, proj_out, proj_in,
        left_sem, right_sem, lh_sem, dp_sem, wh_sem, wp_sem,
        s_pair, r_pair, s_right, r_right, s_left, r_left, s_hid, r_hid, s_proj, r_proj,
        s_ahead, s_behind, r_rows,
        outs, wh_out, wp_out, vgr, s_vg, r_vg, outs_sem, wh_out_sem, wp_out_sem,
        near_sem,
    ) = refs[20:]
    count = len(left_in)
    me_s = lax.axis_index("section")
    me = lax.axis_index("dp")
    chips = peers // 2
    chip, core = me // 2, me % 2
    sibling = me + 1 - 2 * core
    blocks, share = chips, own.shape[2]
    columns = wh.shape[2]
    has_right = chip + 1 < chips
    has_left = chip > 0
    after = jnp.minimum(me + 2, peers - 1)
    before = jnp.maximum(me - 2, 0)

    barrier = pltpu.get_barrier_semaphore()

    def greet(index):
        pl.semaphore_signal(barrier, inc=1, device_id=(me_s, index), device_id_type=MESH)

    def each_peer(action):
        def turn(k, carry):
            @pl.when(k != me)
            def _():
                action(k)

            return carry

        lax.fori_loop(0, peers, turn, 0)

    each_peer(greet)
    for w in range(count):
        pltpu.make_async_copy(left_in[w], lefts.at[w], left_sem.at[w]).start()
        pltpu.make_async_copy(right_in[w], rights.at[w], right_sem.at[w]).start()
    is_late = 2 * me_s >= sections
    lh_copy = pltpu.make_async_copy(lh_in, lh, lh_sem)
    rows = dp_in.shape[0]
    own_rows = pl.ds(pl.multiple_of(chip * rows, rows), rows)
    dp_copy = pltpu.make_async_copy(dp_in, dp.at[own_rows], dp_sem)
    dp_copy.start()

    def near_load(way):
        origin = jnp.minimum(chip + 1, chips - 1) if way else jnp.maximum(chip - 1, 0)
        place = pl.ds(pl.multiple_of(origin * rows, rows), rows)
        return pltpu.make_async_copy(near_in.at[way], dp.at[place], near_sem.at[way])

    pl.when(has_left)(lambda: near_load(0).start())
    pl.when(has_right)(lambda: near_load(1).start())
    lh_own = pltpu.make_async_copy(lh_in.at[own_rows], lh.at[own_rows], lh_sem)
    pl.when(is_late)(lh_own.start)
    pl.when(jnp.logical_not(is_late))(lh_copy.start)

    def wh_copy(j, slot):
        return pltpu.make_async_copy(
            wh_in.at[:, pl.ds(pl.multiple_of(j * columns, columns), columns)],
            wh.at[slot], wh_sem.at[slot],
        )

    def wp_copy(j, slot):
        return pltpu.make_async_copy(
            wp_in.at[pl.ds(pl.multiple_of(j * columns, columns), columns)],
            wp.at[slot], wp_sem.at[slot],
        )

    wh_copy(0, 0).start()
    wp_copy(0, 0).start()
    def remote(source, target, send, receive, index):
        return pltpu.make_async_remote_copy(
            src_ref=source, dst_ref=target, send_sem=send, recv_sem=receive,
            device_id=(me_s, index), device_id_type=MESH,
        )

    def pair_copy(w):
        return remote(pair_out.at[w], own.at[w], s_pair.at[w], r_pair.at[w], sibling)

    cut = vgr.shape[2]

    def vector_copy(k, slot):
        part = vgs.at[:, pl.ds(pl.multiple_of(k * cut, cut), cut)] if split_vectors else vgs
        return remote(part, vgr.at[slot], s_vg.at[k], r_vg.at[slot], k)

    def rows_of(block, parity):
        return pl.ds(pl.multiple_of((2 * block + parity) * share, share), share)

    def prepare(w):
        pltpu.make_async_copy(lefts.at[w], lefts.at[w], left_sem.at[w]).wait()
        pltpu.make_async_copy(rights.at[w], rights.at[w], right_sem.at[w]).wait()
        slot = w % 2
        whole[slot] = dot_tn(lefts[w], rights[w])

        def divide(q, carry):
            pair_out[w, q] = whole[slot, rows_of(q, 1 - core), :].astype(BF16)
            return carry

        lax.fori_loop(0, blocks, divide, 0)

    def combine(w):
        slot = w % 2
        pair_copy(w).wait_recv()

        def add(q, carry):
            own[w, q] = (
                whole[slot, rows_of(q, core), :] + own[w, q].astype(F32)
            ).astype(BF16)
            return carry

        lax.fori_loop(0, blocks, add, 0)

    def right_copy(source, w, r):
        return remote(source, going_right.at[w, r], s_right.at[w, r], r_right.at[w, r], after)

    def left_copy(source, w, r):
        return remote(source, going_left.at[w, r], s_left.at[w, r], r_left.at[w, r], before)

    from_end = chips - 1 - chip

    def launch(w):
        def turn(r, carry):
            @pl.when(has_right & (chip == 0))
            def _():
                right_copy(own.at[w, chips - 1 - r], w, r).start()

            @pl.when(has_left & (from_end == 0))
            def _():
                left_copy(own.at[w, r], w, r).start()

            return carry

        lax.fori_loop(0, rounds, turn, 0)

    def travel(w, r):
        prior = jnp.maximum(r - 1, 0)

        @pl.when(has_right & (chip > 0) & (chip <= r))
        def _():
            slot = going_right.at[w, prior]
            right_copy(slot, w, prior).wait_recv()
            slot[...] = (
                slot[...].astype(F32) + own[w, chips - 1 - r + chip].astype(F32)
            ).astype(BF16)
            right_copy(slot, w, r).start()

        @pl.when(has_left & (from_end > 0) & (from_end <= r))
        def _():
            slot = going_left.at[w, prior]
            left_copy(slot, w, prior).wait_recv()
            slot[...] = (
                slot[...].astype(F32) + own[w, r - from_end].astype(F32)
            ).astype(BF16)
            left_copy(slot, w, r).start()

    def rows_copy(kind, origin, send, index):
        block = (lh if kind else dp).at[pl.ds(pl.multiple_of(origin * rows, rows), rows)]
        return remote(block, block, send.at[kind, origin], r_rows.at[kind, origin], index)

    def each_origin(kind, low, high):
        def turn(origin, carry):
            rows_copy(kind, origin, s_ahead, after).wait_recv()
            return carry

        lax.fori_loop(low, high, turn, 0)

    def spread(kind, r):
        held = 0 if kind else 1

        @pl.when(has_right & (chip >= r))
        def _():
            pl.when(r > held)(lambda: rows_copy(kind, chip - r, s_ahead, after).wait_recv())
            rows_copy(kind, chip - r, s_ahead, after).start()

        @pl.when(has_left & (from_end >= r))
        def _():
            pl.when(r > held)(lambda: rows_copy(kind, chip + r, s_behind, before).wait_recv())
            rows_copy(kind, chip + r, s_behind, before).start()

    def hid_copy(j):
        place = pl.ds(pl.multiple_of(j * columns, columns), columns)
        return remote(
            hid_out.at[:, place], hid_in.at[:, place], s_hid.at[j], r_hid.at[j], sibling
        )

    proj_copy = remote(proj_out, proj_in, s_proj, r_proj, sibling)
    group = wide.shape[0]
    first = chip * 2 * share
    start = pl.multiple_of(first // group * group, group)
    inside = first - first // group * group

    def hidden_store(j):
        place = pl.ds(pl.multiple_of(j * columns, columns), columns)
        return pltpu.make_async_copy(wh_out.at[:, place], wh_hbm.at[:, place], wh_out_sem.at[j])

    def close_hidden(j):
        hid_copy(j).wait_recv()
        place = pl.ds(pl.multiple_of(j * columns, columns), columns)
        wh_out[:, place] += hid_in[:, place].astype(F32)
        hidden_store(j).start()

    def sum_store(w):
        return pltpu.make_async_copy(outs.at[w], outs_hbm.at[w], outs_sem.at[w])

    proj_store = pltpu.make_async_copy(wp_out, wp_hbm, wp_out_sem)

    def close_sum(w):
        outs[w] = own[w, chip].astype(F32)

        @pl.when(has_left)
        def _():
            right_copy(own.at[w, 0], w, rounds - 1).wait_recv()
            outs[w] += going_right[w, rounds - 1].astype(F32)

        @pl.when(has_right)
        def _():
            left_copy(own.at[w, 0], w, rounds - 1).wait_recv()
            outs[w] += going_left[w, rounds - 1].astype(F32)

        sum_store(w).start()

    def feed(j):
        slot = j % 2
        place = pl.ds(pl.multiple_of(j * columns, columns), columns)

        @pl.when(j == 0)
        def _():
            dp_copy.wait()
            pl.when(chip == 0)(lambda: each_origin(0, 2, chips))
            pl.when(from_end == 0)(lambda: each_origin(0, 0, chips - 2))
            pl.when(jnp.logical_not(is_late))(lh_copy.wait)
            pl.when(is_late & (chip == 0))(lambda: each_origin(1, 1, chips))
            pl.when(is_late & (from_end == 0))(lambda: each_origin(1, 0, chips - 1))

        wh_copy(j, slot).wait()
        wp_copy(j, slot).wait()

        @pl.when(j + 1 < peers)
        def _():
            wh_copy(j + 1, 1 - slot).start()
            wp_copy(j + 1, 1 - slot).start()

        active = jnp.maximum(dot_nn(lh[...], wh[slot]), 0.0)
        act[...] = active
        grown = (dot_nt(dp[...], wp[slot]) * 2.0 * act[...]).astype(BF16)
        wide[...] = dot_tn(lh[:, pl.ds(start, group)], grown)
        mine = pl.ds(pl.multiple_of(inside + core * share, 16), share)
        other = pl.ds(pl.multiple_of(inside + (1 - core) * share, 16), share)
        wh_out[:, place] = wide[mine, :]
        hid_out[:, place] = wide[other, :].astype(BF16)
        hid_copy(j).start()
        pl.when(j > 0)(lambda: close_hidden(j - 1))

        @pl.when(j == 2 * chip + core)
        def _():
            squared = (act[...] * act[...]).astype(BF16)
            wp_out[...] = dot_tn(squared, dp[...])

        @pl.when(j == 2 * chip + 1 - core)
        def _():
            squared = (act[...] * act[...]).astype(BF16)
            proj_out[...] = dot_tn(squared, dp[...]).astype(BF16)
            proj_copy.start()

    rounds = chips - 1
    prepare(0)
    pl.semaphore_wait(barrier, peers - 1)
    pair_copy(0).start()
    pl.when(has_left)(lambda: near_load(0).wait())
    pl.when(has_right)(lambda: near_load(1).wait())
    spread(0, 1)

    @pl.when(is_late)
    def _():
        lh_own.wait()
        spread(1, 0)

    each_peer(lambda k: vector_copy(k, me).start())
    prepare(1)
    pair_copy(1).start()
    combine(0)
    launch(0)
    if split_vectors:
        vec_out[...] = vgs[:, pl.ds(pl.multiple_of(me * cut, cut), cut)]
    else:
        vec_out[...] = vgs[...]
    opening = count * rounds - peers

    def step(t, carry):
        w, r = t // rounds, t % rounds
        travel(w, r)

        @pl.when((r == 1) & (w + 2 < count))
        def _():
            prepare(w + 2)
            pair_copy(w + 2).start()

        @pl.when((r == 1) & (w + 1 < count))
        def _():
            combine(w + 1)
            launch(w + 1)

        @pl.when(t + 2 < rounds)
        def _():
            spread(0, t + 2)

        @pl.when(is_late & (t + 1 < rounds))
        def _():
            spread(1, t + 1)

        @pl.when(t >= opening)
        def _():
            feed(t - opening)

        @pl.when((r == rounds - 1) & (w > 0))
        def _():
            close_sum(w - 1)

        return carry

    lax.fori_loop(0, count * rounds, step, 0)

    close_hidden(peers - 1)
    proj_copy.wait_recv()
    wp_out[...] += proj_in[...].astype(F32)
    proj_store.start()

    def collect(k):
        vector_copy(k, k).wait_recv()
        vec_out[...] += vgr[k]

    each_peer(collect)
    close_sum(count - 1)
    each_peer(lambda k: vector_copy(k, me).wait_send())

    def sent_hidden(j, carry):
        hid_copy(j).wait_send()
        hidden_store(j).wait()
        return carry

    lax.fori_loop(0, peers, sent_hidden, 0)
    proj_copy.wait_send()
    proj_store.wait()

    def sent_rows(origin, carry):
        @pl.when(has_right & (origin < chip))
        def _():
            rows_copy(0, origin, s_ahead, after).wait_send()

        @pl.when(has_left & (origin > chip))
        def _():
            rows_copy(0, origin, s_behind, before).wait_send()

        @pl.when(is_late & has_right & (origin <= chip))
        def _():
            rows_copy(1, origin, s_ahead, after).wait_send()

        @pl.when(is_late & has_left & (origin >= chip))
        def _():
            rows_copy(1, origin, s_behind, before).wait_send()

        return carry

    lax.fori_loop(0, chips, sent_rows, 0)

    def sent(w, carry):
        pair_copy(w).wait_send()
        sum_store(w).wait()

        def sent_round(r, inner):
            @pl.when(has_right & (chip <= r))
            def _():
                right_copy(own.at[w, 0], w, r).wait_send()

            @pl.when(has_left & (from_end <= r))
            def _():
                left_copy(own.at[w, 0], w, r).wait_send()

            return inner

        lax.fori_loop(0, rounds, sent_round, 0)
        return carry

    lax.fori_loop(0, count, sent, 0)


def gradient_sums(sections, peers, lefts, rights, lh, dp, near, wh, wp, vgs):
    count = len(lefts)
    rows, width = lefts[0].shape
    hidden = wh.shape[1]
    tokens = lh.shape[0]
    chips = peers // 2
    share = width // peers
    columns = hidden // peers
    group = max(128, 2 * share)
    shape = jax.ShapeDtypeStruct
    vmem = pl.BlockSpec(memory_space=pltpu.VMEM)
    anywhere = pl.BlockSpec(memory_space=pl.ANY)
    dma = pltpu.SemaphoreType.DMA
    blocks = pltpu.VMEM((count, chips, share, width), BF16)
    slots = pltpu.VMEM((count, chips - 1, share, width), BF16)
    split_vectors = share % 128 == 0
    cut = share if split_vectors else width
    return pl.pallas_call(
        partial(sum_kernel, sections, peers, split_vectors),
        out_shape=(
            shape((count, share, width), F32), shape((share, hidden), F32),
            shape((columns, width), F32), shape((VECTORS, cut), F32),
        ),
        in_specs=[anywhere] * (2 * count + 5) + [vmem],
        out_specs=[anywhere] * 3 + [vmem],
        scratch_shapes=[
            pltpu.VMEM((count, rows, width), BF16), pltpu.VMEM((count, rows, width), BF16),
            pltpu.VMEM((2, width, width), F32),
            blocks, blocks, slots, slots,
            pltpu.VMEM((tokens, width), BF16), pltpu.VMEM((tokens, width), BF16),
            pltpu.VMEM((2, width, columns), BF16), pltpu.VMEM((2, columns, width), BF16),
            pltpu.VMEM((tokens, columns), F32), pltpu.VMEM((group, columns), F32),
            pltpu.VMEM((share, hidden), BF16), pltpu.VMEM((share, hidden), BF16),
            pltpu.VMEM((columns, width), BF16), pltpu.VMEM((columns, width), BF16),
            dma((count,)), dma((count,)), dma, dma, dma((2,)), dma((2,)),
            dma((count,)), dma((count,)),
            dma((count, chips - 1)), dma((count, chips - 1)),
            dma((count, chips - 1)), dma((count, chips - 1)),
            dma((peers,)), dma((peers,)), dma, dma,
            dma((2, chips)), dma((2, chips)), dma((2, chips)),
            pltpu.VMEM((count, share, width), F32), pltpu.VMEM((share, hidden), F32),
            pltpu.VMEM((columns, width), F32), pltpu.VMEM((peers, VECTORS, cut), F32),
            dma((peers,)), dma((peers,)), dma((count,)), dma((peers,)), dma, dma((2,)),
        ],
        compiler_params=pltpu.CompilerParams(
            collective_id=1, has_side_effects=True, vmem_limit_bytes=63 * 2**20
        ),
        name="gradient_sums",
    )(*lefts, *rights, lh, dp, near, wh, wp, vgs)


def deliver_kernel(count, vectors, *refs):
    vec, sources = refs[0], refs[1:6]
    targets = refs[6 : 6 + count]
    rows = refs[6 + count : 6 + count + vectors]
    buffers = refs[6 + count + vectors : -2]
    in_sem, out_sem = refs[-2:]
    pieces = list(sources[:-1]) + [sources[-1].at[w] for w in range(count - 4)]
    enter = [
        pltpu.make_async_copy(piece, buffer, in_sem.at[index])
        for index, (piece, buffer) in enumerate(zip(pieces, buffers))
    ]
    leave = [
        pltpu.make_async_copy(buffer, target, out_sem.at[index])
        for index, (buffer, target) in enumerate(zip(buffers, targets))
    ]
    for copy in enter:
        copy.start()
    for index, row in enumerate(rows):
        row[...] = vec[index : index + 1, :]
    for first, second in zip(enter, leave):
        first.wait()
        second.start()
    for copy in leave:
        copy.wait()


def deliver(vec, hidden, project, out, back, squares, vectors):
    shapes = [(out.shape, BF16), (back.shape, BF16), (hidden.shape, F32), (project.shape, F32)]
    shapes += [(squares.shape[1:], F32)] * squares.shape[0]
    count = len(shapes)
    anywhere = pl.BlockSpec(memory_space=pl.ANY)
    vmem = pl.BlockSpec(memory_space=pltpu.VMEM)
    dma = pltpu.SemaphoreType.DMA
    found = pl.pallas_call(
        partial(deliver_kernel, count, vectors),
        out_shape=tuple(jax.ShapeDtypeStruct(*kind) for kind in shapes)
        + (jax.ShapeDtypeStruct((1, vec.shape[1]), F32),) * vectors,
        in_specs=[vmem] + [anywhere] * 5,
        out_specs=[anywhere] * count + [vmem] * vectors,
        scratch_shapes=[pltpu.VMEM(*kind) for kind in shapes] + [dma((count,)), dma((count,))],
        compiler_params=pltpu.CompilerParams(vmem_limit_bytes=63 * 2**20),
        name="deliver",
    )(vec, out, back, hidden, project, squares)
    return found[:count], found[count:]


def per_device(x, top, spans, *parameters):
    sections = lax.axis_size("section")
    peers = lax.axis_size("dp")
    gain1, bias1, mix_k, mix_v, mix_g, log_rate, extra = parameters[0:7]
    wk, wv, wg, wo = parameters[7:11]
    gain2, bias2, mix_h, mix_f = parameters[11:15]
    wh, wp, wf = parameters[15:18]
    vectors = (gain1, bias1, mix_k, mix_v, mix_g, log_rate, extra, gain2, bias2, mix_h, mix_f)
    matrices = tuple(w[0] for w in (wk, wv, wg, wo, wh, wp, wf))
    found = relay(sections, peers, x, top, spans, vectors, matrices)
    out, back, lk, lv, lg, lgt, lf, dk, dv, dg, datt, dsv, dproj = found[0:13]
    vgs, lh = found[13], found[14].reshape(-1, x.shape[2])
    flat = (x.shape[0] * x.shape[1], x.shape[2])
    squares, d_wh, d_wp, vec = gradient_sums(
        sections, peers,
        [part.reshape(flat) for part in (lf, lgt, lg, lk, lv)],
        [part.reshape(flat) for part in (dsv, datt, dg, dk, dv)],
        lh, dproj.reshape(flat), found[15].reshape(2, *flat), matrices[4], matrices[5], vgs,
    )
    share = x.shape[2] // peers
    if vec.shape[1] != share:
        vec = lax.dynamic_slice_in_dim(vec, lax.axis_index("dp") * share, share, 1)
    moved, rows = deliver(vec, d_wh, d_wp, out, back, squares, 11)
    out, back, d_wh, d_wp, d_wf, d_wo, d_wg, d_wk, d_wv = (part[None] for part in moved)
    return (
        out, back,
        rows[0], rows[1], rows[2], rows[3], rows[4], rows[5], rows[6],
        d_wk, d_wv, d_wg, d_wo,
        rows[7], rows[8], rows[9], rows[10],
        d_wh, d_wp, d_wf,
    )


def solution(mesh):
    tokens = P(None, "dp", None)
    vector = P("section", None)
    matrix = P("section", None, None)
    result = P("section", None, "dp", None)
    vector_grad = P("section", "dp")
    matrix_grad = P("section", "dp", None)
    return jax.shard_map(
        per_device,
        mesh=mesh,
        in_specs=(tokens, tokens, P())
        + (vector,) * 7 + (matrix,) * 4 + (vector,) * 4 + (matrix,) * 3,
        out_specs=(result, result)
        + (vector_grad,) * 7 + (matrix_grad,) * 4 + (vector_grad,) * 4 + (matrix_grad,) * 3,
        check_vma=False,
    )
```

```python
from functools import partial

import jax
import jax.numpy as jnp
from jax import lax
from jax.experimental import pallas as pl
from jax.experimental.pallas import tpu as pltpu
from jax.sharding import PartitionSpec as P

EPS = 1e-05
MESH = pl.DeviceIdType.MESH
RB = 64
SLOTS = 4
VECTORS = 16
F32 = jnp.float32
BF16 = jnp.bfloat16


def dot_nn(left, right):
    return jnp.dot(left, right, preferred_element_type=F32)


def dot_nt(left, right):
    return lax.dot_general(left, right, (((1,), (1,)), ((), ())), preferred_element_type=F32)


def dot_tn(left, right):
    return lax.dot_general(left, right, (((0,), (0,)), ((), ())), preferred_element_type=F32)


def sigmoid(v):
    return 1.0 / (1.0 + jnp.exp(-v))


def normalise(source):
    centred = source - jnp.mean(source, axis=-1, keepdims=True)
    spread = lax.rsqrt(jnp.mean(centred * centred, axis=-1, keepdims=True) + EPS)
    return centred * spread, spread


def moved_down(rows, first):
    place = lax.broadcasted_iota(jnp.int32, rows.shape, 0)
    return jnp.where(place == 0, first, pltpu.roll(rows, 1, 0))


def moved_up(rows, last):
    count = rows.shape[0]
    place = lax.broadcasted_iota(jnp.int32, rows.shape, 0)
    return jnp.where(place == count - 1, last, pltpu.roll(rows, count - 1, 0))


def fold(rows):
    total = rows[0:8]
    for at in range(8, rows.shape[0], 8):
        total = total + rows[at : at + 8]
    return total


def relay_kernel(sections, peers, *refs):
    (
        spans, x_in, top_in,
        gain1, bias1, mix_k, mix_v, mix_g, log_rate, extra, gain2, bias2, mix_h, mix_f,
        wk_in, wv_in, wg_in, wo_in, wh_in, wp_in, wf_in,
        out_hbm, back_hbm, lk_hbm, lv_hbm, lg_hbm, lgt_hbm, lf_hbm,
        dk_hbm, dv_hbm, dg_hbm, datt_hbm, dsv_hbm, dproj_hbm, vgs, lh_all, near,
        wk_t, wv_t, wg_t, wo_t, wf_t, wp_t, wh_t,
        out, back, lk, lv, lg, lgt, lf, dk, dv, dg, datt, dsv, dproj,
        lh, sq, dh, turned,
        wk, wv, wg, wo, wh, wp, wf,
        xs, hx, dys, kk, vv, sg, sa, sb, mid, hmid, proj, sv, act,
        e0, e1, low_mask, up_mask, split, acc, t1, t2, t3,
        states, back_states, de2, de1, sum_row, sum_back, send_de2, send_de1, vg,
        sp1, gp1, sd1, sp2, gp2, sd2, fo, iv,
        w_sem, x_sem, top_sem, s_h0, s_x, s_hx, s_st, s_mid, s_dy, s_de2, s_bst, s_de1,
        r_x, r_hx, r_st, r_mid, r_dy, r_de2, r_bst, r_de1, store_sem,
        s_lh, r_lh, own_sem, s_near, r_near, turn_sem, back_sem,
    ) = refs
    me_s = lax.axis_index("section")
    me = lax.axis_index("dp")
    batches, row_count, width = x_in.shape
    hidden = wh.shape[1]
    chunks = row_count // RB
    base = me * row_count

    def at(section, index):
        return (section, index)

    barrier = pltpu.get_barrier_semaphore()

    def greet(section, index):
        pl.semaphore_signal(barrier, inc=1, device_id=at(section, index), device_id_type=MESH)

    def greet_peer(k, carry):
        @pl.when(k != me)
        def _():
            greet(me_s, k)

        return carry

    lax.fori_loop(0, peers, greet_peer, 0)
    has_next = me_s + 1 < sections
    has_prior = me_s > 0
    has_right = me + 1 < peers
    has_left = me > 0

    @pl.when(has_next)
    def _():
        greet(me_s + 1, me)

    @pl.when(has_prior)
    def _():
        greet(me_s - 1, me)

    @pl.when(has_next & has_right)
    def _():
        greet(me_s + 1, me + 1)

    @pl.when(has_prior & has_left)
    def _():
        greet(me_s - 1, me - 1)

    weight_copies = [
        pltpu.make_async_copy(source, target, w_sem.at[index])
        for index, (source, target) in enumerate(
            ((wk_in, wk), (wv_in, wv), (wg_in, wg), (wo_in, wo), (wf_in, wf), (wh_in, wh), (wp_in, wp))
        )
    ]

    @pl.when(me_s == 0)
    def _():
        pltpu.make_async_copy(x_in, xs, x_sem).start()

    for copy in weight_copies[0:2]:
        copy.start()

    @pl.when(me_s == sections - 1)
    def _():
        pltpu.make_async_copy(top_in, dys, top_sem).start()

    rate = jnp.exp(log_rate[...])
    boost = jnp.exp(extra[...])
    decay_block = jnp.exp(-rate * row_count)
    grow_block = jnp.exp(rate * row_count)

    half = width // 128

    def packed(row_a, row_b):
        return jnp.concatenate(
            [row[:, j * 128 : (j + 1) * 128] for row in (row_a, row_b) for j in range(half)], axis=0
        )

    def unpacked(tile, part):
        return jnp.concatenate(
            [tile[part * half + j : part * half + j + 1] for j in range(half)], axis=1
        )

    decay_tile = packed(decay_block, decay_block)

    def starts_of(m):
        found = []
        total = jnp.int32(0)
        for j in range(spans.shape[1]):
            found.append(total)
            total = total + spans[m, j]
        return found

    def segment(position, starts):
        total = jnp.where(position >= starts[0], 1, 0)
        for start in starts[1:]:
            total = total + jnp.where(position >= start, 1, 0)
        return total

    def column(i):
        return base + i * RB + lax.broadcasted_iota(jnp.int32, (RB, 1), 0)

    def keep_of(position, starts):
        return jnp.where(segment(position, starts) == segment(position - 1, starts), 1.0, 0.0)

    def fill_powers(i, carry):
        place = (i * RB + lax.broadcasted_iota(jnp.int32, (RB, width), 0)).astype(F32)
        e0[pl.ds(pl.multiple_of(i * RB, RB), RB), :] = jnp.exp(-place * rate)
        e1[pl.ds(pl.multiple_of(i * RB, RB), RB), :] = jnp.exp((place - (row_count - 1.0)) * rate)
        return carry

    lax.fori_loop(0, chunks, fill_powers, 0)
    for m in range(batches):
        starts = starts_of(m)
        row_at = lax.broadcasted_iota(jnp.int32, (row_count, row_count), 0)
        column_at = lax.broadcasted_iota(jnp.int32, (row_count, row_count), 1)
        same = segment(base + row_at, starts) == segment(base + column_at, starts)
        lower = jnp.where(same & (column_at < row_at), 1.0, 0.0).astype(BF16)
        upper = jnp.where(same & (column_at > row_at), 1.0, 0.0).astype(BF16)
        low_mask[m, :, 0:row_count] = lower
        low_mask[m, :, row_count:] = lower
        up_mask[m, :, 0:row_count] = upper
        up_mask[m, :, row_count:] = upper
    vg[...] = jnp.zeros_like(vg)

    @pl.when(me == 0)
    def _():
        hx[...] = jnp.zeros_like(hx)
        hmid[...] = jnp.zeros_like(hmid)

    @pl.when(me == peers - 1)
    def _():
        de1[...] = jnp.zeros_like(de1)
        de2[...] = jnp.zeros_like(de2)

    greeted = (
        peers - 1
        + jnp.where(has_next, 1, 0)
        + jnp.where(has_prior, 1, 0)
        + jnp.where(has_next & has_right, 1, 0)
        + jnp.where(has_prior & has_left, 1, 0)
    )
    pl.semaphore_wait(barrier, greeted)
    for copy in weight_copies[2:7]:
        copy.start()

    def remote(source, target, send, receive, section, index):
        return pltpu.make_async_remote_copy(
            src_ref=source, dst_ref=target, send_sem=send, recv_sem=receive,
            device_id=at(section, index), device_id_type=MESH,
        )

    right = jnp.minimum(me + 1, peers - 1)
    left = jnp.maximum(me - 1, 0)
    above = jnp.minimum(me_s + 1, sections - 1)
    below = jnp.maximum(me_s - 1, 0)
    tail = pl.ds(row_count - 16, 16)
    final = pl.ds(row_count - 1, 1)

    stored = (
        (out, out_hbm), (lk, lk_hbm), (lv, lv_hbm), (lg, lg_hbm), (lgt, lgt_hbm), (lf, lf_hbm),
        (dproj, dproj_hbm), (dsv, dsv_hbm), (datt, datt_hbm), (dg, dg_hbm), (dk, dk_hbm),
        (dv, dv_hbm), (back, back_hbm),
    )

    def store_copy(index, m):
        source, target = stored[index]
        return pltpu.make_async_copy(source.at[m], target.at[m], store_sem.at[index, m])

    def start_halo(m):
        return remote(x_in.at[m, tail], hx.at[m], s_h0.at[m], r_hx.at[m], me_s, right)

    def result_copy(m, i):
        rows = pl.ds(i * RB, RB)
        return remote(
            out.at[m, rows], xs.at[m, rows], s_x.at[m, i], r_x.at[m, i], above, me
        )

    def result_halo(m):
        return remote(out.at[m, tail], hx.at[m], s_hx.at[m], r_hx.at[m], above, right)

    def middle_halo(m):
        return remote(mid.at[m, final], hmid.at[m], s_mid.at[m], r_mid.at[m], me_s, right)

    def state_copy(m, k, slot):
        return remote(sum_row.at[m], states.at[m, slot], s_st.at[m, k], r_st.at[m, slot], me_s, k)

    pieces = (
        (0, row_count // 2), (row_count // 2, row_count // 2 - 16), (row_count - 16, 16)
    )

    def back_copy(m, index):
        rows = pl.ds(*pieces[index])
        return remote(
            back.at[m, rows], dys.at[m, rows], s_dy.at[m, index], r_dy.at[m, index], below, me
        )

    def each_piece(action):
        for index in range(len(pieces)):
            action(index)

    def second_copy(m):
        return remote(send_de2.at[m], de2.at[m], s_de2.at[m], r_de2.at[m], me_s, left)

    def first_copy(m):
        return remote(send_de1.at[m], de1.at[m], s_de1.at[m], r_de1.at[m], me_s, left)

    def back_state_copy(m, k, slot):
        return remote(
            sum_back.at[m], back_states.at[m, slot], s_bst.at[m, k], r_bst.at[m, slot], me_s, k
        )

    chip, core = me // 2, me % 2
    chips = peers // 2

    def gather_copy(m, k, slot):
        return remote(
            lh.at[m], lh_all.at[slot, m], s_lh.at[m, k], r_lh.at[m, slot], me_s, 2 * k + core
        )

    is_late = 2 * me_s >= sections

    def own_copy(m):
        return pltpu.make_async_copy(lh.at[m], lh_all.at[chip, m], own_sem.at[m])

    def each_chip(action):
        def turn(k, carry):
            @pl.when(k != chip)
            def _():
                action(k)

            return carry

        lax.fori_loop(0, chips, turn, 0)

    ahead = jnp.minimum(me + 2, peers - 1)
    behind = jnp.maximum(me - 2, 0)
    has_ahead = chip + 1 < chips
    has_behind = chip > 0

    def near_copy(m, way):
        return remote(
            dproj.at[m], near.at[way, m], s_near.at[way, m], r_near.at[way, m],
            me_s, behind if way else ahead,
        )

    def send_near(m):
        pl.when(has_ahead)(lambda: near_copy(m, 0).start())
        pl.when(has_behind)(lambda: near_copy(m, 1).start())

    def end_near(m):
        @pl.when(has_ahead)
        def _():
            near_copy(m, 0).wait_send()
            near_copy(m, 1).wait_recv()

        @pl.when(has_behind)
        def _():
            near_copy(m, 1).wait_send()
            near_copy(m, 0).wait_recv()

    def start_gathers():
        for m in range(batches):
            own_copy(m).start()

            @pl.when(jnp.logical_not(is_late))
            def _(m=m):
                each_chip(lambda k: gather_copy(m, k, chip).start())

    def end_gather(m):
        own_copy(m).wait()

        @pl.when(jnp.logical_not(is_late))
        def _():
            each_chip(lambda k: gather_copy(m, k, chip).wait_send())
            each_chip(lambda k: gather_copy(m, k, k).wait_recv())

    @pl.when((me_s == 0) & has_right)
    def _():
        for m in range(batches):
            start_halo(m).start()

    @pl.when(me_s == 0)
    def _():
        pltpu.make_async_copy(x_in, xs, x_sem).wait()

    turns = (
        (wk, wk_t), (wv, wv_t), (wg, wg_t), (wo, wo_t), (wf, wf_t), (wh, wh_t), (wp, wp_t)
    )
    returns = (
        (wk_t, wk), (wv_t, wv), (wg_t, wg), (wo_t, wo), (wf_t, wf), (wp_t, wh), (wh_t, wp)
    )
    edge = turned.shape[1]

    def transpose_all(fresh):
        for index, (source, target) in enumerate(turns):
            if fresh:
                weight_copies[index].wait()
            tall = source.shape[0] // edge
            blocks = tall * (source.shape[1] // edge)

            def place(n, source=source, target=target, tall=tall):
                down = pl.ds(pl.multiple_of(n % tall * edge, edge), edge)
                along = pl.ds(pl.multiple_of(n // tall * edge, edge), edge)
                slot = n % SLOTS
                return (
                    source.at[down, along],
                    turned.at[slot],
                    pltpu.make_async_copy(turned.at[slot], target.at[along, down], turn_sem.at[slot]),
                )

            def turn(n, carry, place=place):
                piece, buffer, copy = place(n)
                pl.when(n >= SLOTS)(copy.wait)
                buffer[...] = piece[...].T
                copy.start()
                return carry

            lax.fori_loop(0, blocks, turn, 0)
            for n in range(blocks - SLOTS, blocks):
                place(n)[2].wait()

    def return_copy(index):
        source, target = returns[index]
        return pltpu.make_async_copy(source, target, back_sem.at[index])


    def release(m, index):
        @pl.when(is_late & (m == batches - 1))
        def _():
            return_copy(index).start()

    def weight_ready(m, index, fresh=True):
        @pl.when((m == 0) & jnp.logical_not(is_late))
        def _():
            weight_copies[index].wait()

    def span_of(i):
        return pl.ds(pl.multiple_of(i * RB, RB), RB)

    def split_sums():
        def turn(i, carry):
            rows = span_of(i)
            low = pl.ds(pl.multiple_of(row_count + i * RB, RB), RB)
            for source, place in ((t1, pl.ds(0, width)), (t2, pl.ds(width, width))):
                value = source[rows, :]
                high = value.astype(BF16)
                split[rows, place] = high
                split[low, place] = (value - high.astype(F32)).astype(BF16)
            return carry

        lax.fori_loop(0, chunks, turn, 0, unroll=True)

    def forward(m, carry):
        starts = starts_of(m)

        none = jnp.zeros((1, width), F32)

        def mix_in(start, size, last):
            rows = pl.ds(start, size)
            spare, spread = normalise(xs[m, rows, :].astype(F32))
            sp1[m, rows, :] = spare
            sd1[m, rows, :] = spread
            normed = spare * gain1[...] + bias1[...]
            position = base + start + lax.broadcasted_iota(jnp.int32, (size, 1), 0)
            earlier = moved_down(normed, last) * keep_of(position, starts)
            gap = normed - earlier
            gp1[m, rows, :] = gap.astype(BF16)
            lk[m, rows, :] = (earlier + gap * mix_k[...]).astype(BF16)
            lv[m, rows, :] = (earlier + gap * mix_v[...]).astype(BF16)
            lg[m, rows, :] = (earlier + gap * mix_g[...]).astype(BF16)
            return normed[size - 1 : size]

        last = none
        for i in range(chunks):
            pl.when(has_prior)(lambda i=i: result_copy(m, i).wait_recv())
            last = mix_in(i * RB, RB, last)

        @pl.when(has_left)
        def _():
            start_halo(m).wait_recv()

        halo_rows, _ = normalise(hx[m].astype(F32))
        mix_in(0, 16, (halo_rows * gain1[...] + bias1[...])[15:16])
        weight_ready(m, 0)
        weight_ready(m, 1)
        kk[m] = dot_nn(lk[m], wk[...])
        vv[m] = dot_nn(lv[m], wv[...])
        release(m, 0)
        release(m, 1)
        end_segment = segment(base + row_count - 1, starts)

        def spread_in(i, totals):
            rows = span_of(i)
            plain = jnp.exp(kk[m, rows, :])
            kk[m, rows, :] = plain
            weight = plain * e1[rows, :]
            weighted = weight * vv[m, rows, :]
            t1[rows, :] = weighted
            t2[rows, :] = weight
            chosen = segment(column(i), starts) == end_segment
            return (
                totals[0] + fold(jnp.where(chosen, weighted, 0.0)),
                totals[1] + fold(jnp.where(chosen, weight, 0.0)),
            )

        nothing = jnp.zeros((8, width), F32)
        total_a, total_b = lax.fori_loop(0, chunks, spread_in, (nothing, nothing), unroll=True)
        sum_row[m] = packed(
            jnp.sum(total_a, axis=0, keepdims=True), jnp.sum(total_b, axis=0, keepdims=True)
        )

        def send_state(k, carry):
            state_copy(m, k, me).start()
            return carry

        lax.fori_loop(me + 1, peers, send_state, 0)

        weight_ready(m, 2)
        sg[m] = dot_nn(lg[m], wg[...])
        split_sums()
        acc[...] = dot_nn(low_mask[m], split[...])
        sg[m] = sigmoid(sg[m])
        release(m, 2)

        def receive_state(k, held):
            state_copy(m, k, k).wait_recv()
            unbroken = segment(k * row_count - 1, starts) == segment(
                (k + 1) * row_count - 1, starts
            )
            passing = jnp.where(unbroken, 1.0, 0.0) * decay_tile
            return passing * held + states[m, k]

        entered = lax.fori_loop(0, me, receive_state, jnp.zeros_like(decay_tile))
        enter_a, enter_b = unpacked(entered, 0), unpacked(entered, 1)
        prior_segment = segment(base - 1, starts)

        def mix_states(i, carry):
            rows = span_of(i)
            falling = e0[rows, :]
            chosen = jnp.where(segment(column(i), starts) == prior_segment, 1.0, 0.0)
            grown = falling * grow_block
            held = falling * chosen
            state_a = grown * acc[rows, 0:width] + held * enter_a
            state_b = grown * acc[rows, width:] + held * enter_b
            sa[m, rows, :] = state_a
            sb[m, rows, :] = state_b
            present = boost * kk[m, rows, :]
            inverse = 1.0 / (state_b + present)
            found = (state_a + present * vv[m, rows, :]) * inverse
            iv[m, rows, :] = inverse
            fo[m, rows, :] = found
            lgt[m, rows, :] = (sg[m, rows, :] * found).astype(BF16)
            return carry

        lax.fori_loop(0, chunks, mix_states, 0, unroll=True)

        weight_ready(m, 3)
        mid[m] = xs[m].astype(F32) + dot_nn(lgt[m], wo[...])
        release(m, 3)

        @pl.when(has_right)
        def _():
            middle_halo(m).start()

        def mix_second(start, size, last):
            rows = pl.ds(start, size)
            spare, spread = normalise(mid[m, rows, :])
            sp2[m, rows, :] = spare
            sd2[m, rows, :] = spread
            normed = spare * gain2[...] + bias2[...]
            position = base + start + lax.broadcasted_iota(jnp.int32, (size, 1), 0)
            earlier = moved_down(normed, last) * keep_of(position, starts)
            gap = normed - earlier
            gp2[m, rows, :] = gap.astype(BF16)
            lh[m, rows, :] = (earlier + gap * mix_h[...]).astype(BF16)
            lf[m, rows, :] = (earlier + gap * mix_f[...]).astype(BF16)
            return normed[size - 1 : size]

        last = none
        for start in range(0, row_count, RB):
            last = mix_second(start, RB, last)

        @pl.when(has_left)
        def _():
            middle_halo(m).wait_recv()

        halo_rows, _ = normalise(hmid[m])
        mix_second(0, 16, halo_rows * gain2[...] + bias2[...])

        for index in range(4, 7):
            weight_ready(m, index)
        sv[m] = sigmoid(dot_nn(lf[m], wf[...]))

        def widen(j, carry):
            columns = pl.ds(pl.multiple_of(j * width, width), width)
            active = jnp.maximum(dot_nn(lh[m], wh[:, columns]), 0.0)
            act[m, :, columns] = active.astype(BF16)
            sq[m, :, columns] = (active * active).astype(BF16)
            return carry

        lax.fori_loop(0, hidden // width, widen, 0, unroll=True)
        release(m, 4)
        release(m, 5)

        proj[m] = dot_nn(sq[m], wp[...])
        for i in range(chunks):
            rows = pl.ds(i * RB, RB)
            out[m, rows, :] = (mid[m, rows, :] + sv[m, rows, :] * proj[m, rows, :]).astype(BF16)
            pl.when(has_next)(lambda i=i: result_copy(m, i).start())

        release(m, 6)

        @pl.when(has_next & has_right)
        def _():
            result_halo(m).start()

        for index in range(6):
            store_copy(index, m).start()

        return carry

    pl.when(is_late)(lambda: transpose_all(True))
    lax.fori_loop(0, batches, forward, 0)

    @pl.when(jnp.logical_not(is_late))
    def _():
        transpose_all(False)
        for index in range(7):
            return_copy(index).start()

    start_gathers()

    def add_vectors(n, carry):
        m, i = n // chunks, n % chunks
        rows = span_of(i)
        gap = gp2[m, rows, :].astype(F32)
        found = {
            9: mid[m, rows, :] * gap, 10: proj[m, rows, :] * gap,
            7: sv[m, rows, :] * sp2[m, rows, :], 8: sv[m, rows, :],
            5: sa[m, rows, :], 6: iv[m, rows, :],
        }
        gap = gp1[m, rows, :].astype(F32)
        found.update({
            2: kk[m, rows, :] * gap, 3: vv[m, rows, :] * gap, 4: sg[m, rows, :] * gap,
            0: fo[m, rows, :] * sp1[m, rows, :], 1: fo[m, rows, :],
        })
        for index in sorted(found):
            vg[index] += fold(found[index])
        return carry

    @pl.when(me_s == sections - 1)
    def _():
        pltpu.make_async_copy(top_in, dys, top_sem).wait()

    def turned_ready(m, index):
        @pl.when(m == 0)
        def _():
            return_copy(index).wait()

    def backward(m, carry):
        starts = starts_of(m)
        none = jnp.zeros((1, width), F32)

        for index, (start, size) in enumerate(pieces):
            pl.when(has_next)(lambda index=index: back_copy(m, index).wait_recv())
            rows = pl.ds(start, size)
            sieve = sv[m, rows, :]
            gained = dys[m, rows, :].astype(F32) * sieve
            dproj[m, rows, :] = gained.astype(BF16)
            dsv[m, rows, :] = (gained * proj[m, rows, :] * (1.0 - sieve)).astype(BF16)

        turned_ready(m, 5)
        turned_ready(m, 6)

        def narrow(j, carry):
            columns = pl.ds(pl.multiple_of(j * width, width), width)
            grown = dot_nn(dproj[m], wh[:, columns])
            dh[m, :, columns] = (grown * 2.0 * act[m, :, columns].astype(F32)).astype(BF16)
            return carry

        lax.fori_loop(0, hidden // width, narrow, 0, unroll=True)
        pl.when(has_right)(lambda: middle_halo(m).wait_send())
        mid[m] = dot_nn(dh[m], wp[...])
        turned_ready(m, 4)
        proj[m] = dot_nn(dsv[m], wf[...])

        def second_earlier(rows, position):
            whole = mid[m, rows, :] * (1.0 - mix_h[...]) + proj[m, rows, :] * (1.0 - mix_f[...])
            return whole * keep_of(position, starts)

        eight = lax.broadcasted_iota(jnp.int32, (8, 1), 0)
        send_de2[m] = second_earlier(pl.ds(0, 8), base + eight)[0:1]

        @pl.when(has_left)
        def _():
            second_copy(m).start()

        def back_second(start, size, following):
            rows = pl.ds(start, size)
            spare, spread = sp2[m, rows, :], sd2[m, rows, :]
            position = base + start + lax.broadcasted_iota(jnp.int32, (size, 1), 0)
            kept = keep_of(position, starts)
            from_h = mid[m, rows, :]
            from_f = proj[m, rows, :]
            straight = from_h * mix_h[...] + from_f * mix_f[...]
            earlier = (from_h + from_f - straight) * kept
            d_normed = straight + moved_up(earlier, following)
            sv[m, rows, :] = d_normed
            scaled = d_normed * gain2[...]
            mean_one = jnp.mean(scaled, axis=-1, keepdims=True)
            mean_two = jnp.mean(scaled * spare, axis=-1, keepdims=True)
            d_mid = dys[m, rows, :].astype(F32) + spread * (scaled - mean_one - spare * mean_two)
            t3[rows, :] = d_mid
            datt[m, rows, :] = d_mid.astype(BF16)

        for start, size in pieces[:-1]:
            end = start + size
            back_second(start, size, second_earlier(pl.ds(end, 8), base + end + eight)[0:1])

        @pl.when(has_right)
        def _():
            second_copy(m).wait_recv()

        back_second(*pieces[-1], de2[m])
        turned_ready(m, 3)
        t1[...] = dot_nn(datt[m], wo[...])
        open_segment = segment(base, starts)

        def back_states_in(i, totals):
            rows = span_of(i)
            d_found = t1[rows, :] * sg[m, rows, :]
            d_a = d_found * iv[m, rows, :]
            d_b = -d_a * fo[m, rows, :]
            falling = e0[rows, :]
            scaled_a = d_a * falling
            scaled_b = d_b * falling
            t1[rows, :] = scaled_a
            t2[rows, :] = scaled_b
            acc[rows, 0:width] = d_found
            chosen = segment(column(i), starts) == open_segment
            return (
                totals[0] + fold(jnp.where(chosen, scaled_a, 0.0)),
                totals[1] + fold(jnp.where(chosen, scaled_b, 0.0)),
            )

        nothing = jnp.zeros((8, width), F32)
        total_a, total_b = lax.fori_loop(0, chunks, back_states_in, (nothing, nothing), unroll=True)
        sum_back[m] = packed(
            jnp.sum(total_a, axis=0, keepdims=True), jnp.sum(total_b, axis=0, keepdims=True)
        )

        def send_state(k, carry):
            back_state_copy(m, k, me).start()
            return carry

        lax.fori_loop(0, me, send_state, 0)
        split_sums()

        def back_present(i, carry):
            rows = span_of(i)
            gate, found = sg[m, rows, :], fo[m, rows, :]
            d_found = acc[rows, 0:width]
            dg[m, rows, :] = (d_found * found * (1.0 - gate)).astype(BF16)
            gained = d_found * iv[m, rows, :] * (boost * kk[m, rows, :])
            d_key = gained * (vv[m, rows, :] - found)
            iv[m, rows, :] = d_key
            t2[rows, :] = gained
            return carry

        lax.fori_loop(0, chunks, back_present, 0, unroll=True)
        acc[...] = dot_nn(up_mask[m], split[...])

        def receive_state(turn, held):
            k = peers - 1 - turn
            back_state_copy(m, k, k).wait_recv()
            first = segment(k * row_count, starts)
            unbroken = first == segment((k + 1) * row_count - 1, starts)
            joined = jnp.where(first == segment(k * row_count - 1, starts), 1.0, 0.0)
            passing = jnp.where(unbroken, 1.0, 0.0) * decay_tile
            return joined * (passing * held + back_states[m, k])

        entered = lax.fori_loop(0, peers - 1 - me, receive_state, jnp.zeros_like(decay_tile))
        enter_a, enter_b = unpacked(entered, 0), unpacked(entered, 1)
        end_segment = segment(base + row_count - 1, starts)

        def back_keys(i, carry):
            rows = span_of(i)
            rising = e1[rows, :]
            chosen = jnp.where(segment(column(i), starts) == end_segment, 1.0, 0.0)
            grown = rising * grow_block
            held = rising * chosen
            d_a = grown * acc[rows, 0:width] + held * enter_a
            d_b = grown * acc[rows, width:] + held * enter_b
            sa[m, rows, :] = d_a * sa[m, rows, :] + d_b * sb[m, rows, :]
            weight = kk[m, rows, :]
            dv[m, rows, :] = (t2[rows, :] + d_a * weight).astype(BF16)
            dk[m, rows, :] = (iv[m, rows, :] + (d_a * vv[m, rows, :] + d_b) * weight).astype(BF16)
            return carry

        lax.fori_loop(0, chunks, back_keys, 0, unroll=True)
        for index in range(3):
            turned_ready(m, index)
        kk[m] = dot_nn(dk[m], wk[...])
        vv[m] = dot_nn(dv[m], wv[...])
        sg[m] = dot_nn(dg[m], wg[...])

        def first_earlier(rows, position):
            whole = (
                kk[m, rows, :] * (1.0 - mix_k[...])
                + vv[m, rows, :] * (1.0 - mix_v[...])
                + sg[m, rows, :] * (1.0 - mix_g[...])
            )
            return whole * keep_of(position, starts)

        send_de1[m] = first_earlier(pl.ds(0, 8), base + eight)[0:1]

        @pl.when(has_left)
        def _():
            first_copy(m).start()

        pl.when(me_s == 0)(lambda: send_near(m))
        for index in range(6, 12):
            store_copy(index, m).start()

        def back_first(index, following):
            start, size = pieces[index]
            rows = pl.ds(start, size)
            spare, spread = sp1[m, rows, :], sd1[m, rows, :]
            position = base + start + lax.broadcasted_iota(jnp.int32, (size, 1), 0)
            kept = keep_of(position, starts)
            from_k = kk[m, rows, :]
            from_v = vv[m, rows, :]
            from_g = sg[m, rows, :]
            straight = from_k * mix_k[...] + from_v * mix_v[...] + from_g * mix_g[...]
            earlier = (from_k + from_v + from_g - straight) * kept
            d_normed = straight + moved_up(earlier, following)
            fo[m, rows, :] = d_normed
            scaled = d_normed * gain1[...]
            mean_one = jnp.mean(scaled, axis=-1, keepdims=True)
            mean_two = jnp.mean(scaled * spare, axis=-1, keepdims=True)
            found = t3[rows, :] + spread * (scaled - mean_one - spare * mean_two)
            back[m, rows, :] = found.astype(BF16)

            @pl.when(has_prior)
            def _():
                back_copy(m, index).start()

        for index, (start, size) in enumerate(pieces[:-1]):
            end = start + size
            back_first(index, first_earlier(pl.ds(end, 8), base + end + eight)[0:1])

        @pl.when(has_right)
        def _():
            first_copy(m).wait_recv()

        back_first(len(pieces) - 1, de1[m])
        store_copy(12, m).start()
        return carry

    lax.fori_loop(0, batches, backward, 0)
    pl.when(has_prior)(lambda: each_piece(lambda i: back_copy(batches - 1, i).wait_send()))

    @pl.when(me_s > 0)
    def _():
        for m in range(batches):
            send_near(m)


    lax.fori_loop(0, batches * chunks, add_vectors, 0)
    vgs[...] = jnp.sum(vg[...], axis=1)
    vgs[5:6] = vgs[5:6] * (-rate * jnp.exp(-rate))
    def close(m, carry):
        @pl.when((me_s == 0) & has_right)
        def _():
            start_halo(m).wait_send()

        @pl.when(has_next)
        def _():
            for i in range(chunks):
                result_copy(m, i).wait_send()

        @pl.when(has_next & has_right)
        def _():
            result_halo(m).wait_send()

        @pl.when(has_left)
        def _():
            second_copy(m).wait_send()
            first_copy(m).wait_send()

        @pl.when(has_prior)
        def _():
            pl.when(m + 1 < batches)(lambda: each_piece(lambda i: back_copy(m, i).wait_send()))

        for index in range(13):
            store_copy(index, m).wait()

        def ended(k, carry):
            state_copy(m, k, me).wait_send()
            return carry

        lax.fori_loop(me + 1, peers, ended, 0)
        end_gather(m)
        end_near(m)

        def ended_back(k, carry):
            back_state_copy(m, k, me).wait_send()
            return carry

        lax.fori_loop(0, me, ended_back, 0)
        return carry

    lax.fori_loop(0, batches, close, 0)


def relay(sections, peers, x, top, spans, vectors, matrices):
    batches, rows, width = x.shape
    hidden = matrices[4].shape[1]
    shape = jax.ShapeDtypeStruct
    low = shape((batches, rows, width), BF16)
    square = shape((width, width), BF16)
    vmem = pl.BlockSpec(memory_space=pltpu.VMEM)
    anywhere = pl.BlockSpec(memory_space=pl.ANY)
    dma = pltpu.SemaphoreType.DMA

    def narrow(kind):
        return pltpu.VMEM((batches, rows, width), kind)

    return pl.pallas_call(
        partial(relay_kernel, sections, peers),
        out_shape=(
            low, low, low, low, low, low, low,
            low, low, low, low, low, low, shape((VECTORS, width), F32),
            shape((peers // 2, batches, rows, width), BF16),
            shape((2, batches, rows, width), BF16),
            square, square, square, square, square,
            shape((width, hidden), BF16), shape((hidden, width), BF16),
        ),
        in_specs=[pl.BlockSpec(memory_space=pltpu.SMEM), anywhere, anywhere]
        + [vmem] * 11
        + [anywhere] * 7,
        out_specs=[anywhere] * 13 + [vmem] + [anywhere] * 9,
        scratch_shapes=[narrow(BF16)] * 13 + [
            narrow(BF16), pltpu.VMEM((batches, rows, hidden), BF16),
            pltpu.VMEM((batches, rows, hidden), BF16), pltpu.VMEM((SLOTS, 512, 512), BF16),
        ]
        + [pltpu.VMEM(matrix.shape, BF16) for matrix in matrices_order(matrices)]
        + [
            narrow(BF16), pltpu.VMEM((batches, 16, width), BF16), narrow(BF16),
            narrow(F32), narrow(F32), narrow(F32), narrow(F32), narrow(F32), narrow(F32),
            pltpu.VMEM((batches, 1, width), F32), narrow(F32), narrow(F32),
            pltpu.VMEM((batches, rows, hidden), BF16),
            pltpu.VMEM((rows, width), F32), pltpu.VMEM((rows, width), F32),
            pltpu.VMEM((batches, rows, 2 * rows), BF16), pltpu.VMEM((batches, rows, 2 * rows), BF16),
            pltpu.VMEM((2 * rows, 2 * width), BF16), pltpu.VMEM((rows, 2 * width), F32),
            pltpu.VMEM((rows, width), F32), pltpu.VMEM((rows, width), F32), pltpu.VMEM((rows, width), F32),
            pltpu.VMEM((batches, peers, width // 64, 128), F32),
            pltpu.VMEM((batches, peers, width // 64, 128), F32),
            pltpu.VMEM((batches, 1, width), F32), pltpu.VMEM((batches, 1, width), F32),
            pltpu.VMEM((batches, width // 64, 128), F32),
            pltpu.VMEM((batches, width // 64, 128), F32),
            pltpu.VMEM((batches, 1, width), F32), pltpu.VMEM((batches, 1, width), F32),
            pltpu.VMEM((VECTORS, 8, width), F32),
            narrow(F32), narrow(BF16), pltpu.VMEM((batches, rows, 1), F32),
            narrow(F32), narrow(BF16), pltpu.VMEM((batches, rows, 1), F32),
            narrow(F32), narrow(F32),
            dma((7,)), dma, dma,
            dma((batches,)), dma((batches, rows // RB)), dma((batches,)), dma((batches, peers)),
            dma((batches,)), dma((batches, 3)), dma((batches,)), dma((batches, peers)),
            dma((batches,)),
            dma((batches, rows // RB)), dma((batches,)), dma((batches, peers)), dma((batches,)),
            dma((batches, 3)), dma((batches,)), dma((batches, peers)), dma((batches,)),
            dma((13, batches)),
            dma((batches, peers // 2)), dma((batches, peers // 2)), dma((batches,)),
            dma((2, batches)), dma((2, batches)),
            dma((SLOTS,)), dma((7,)),
        ],
        compiler_params=pltpu.CompilerParams(
            collective_id=0, has_side_effects=True, vmem_limit_bytes=63 * 2**20
        ),
        name="relay",
    )(spans, x, top, *vectors, *matrices_order(matrices))


def matrices_order(matrices):
    wk, wv, wg, wo, wh, wp, wf = matrices
    return (wk, wv, wg, wo, wh, wp, wf)


def sum_kernel(sections, peers, split_vectors, *refs):
    left_in, right_in = refs[0:5], refs[5:10]
    lh_in, dp_in, near_in, wh_in, wp_in, vgs = refs[10:16]
    outs_hbm, wh_hbm, wp_hbm, vec_out = refs[16:20]
    (
        lefts, rights, whole, own, pair_out, going_right, going_left,
        lh, dp, wh, wp, act, wide, hid_out, hid_in, proj_out, proj_in,
        left_sem, right_sem, lh_sem, dp_sem, wh_sem, wp_sem,
        s_pair, r_pair, s_right, r_right, s_left, r_left, s_hid, r_hid, s_proj, r_proj,
        s_ahead, s_behind, r_rows,
        outs, wh_out, wp_out, vgr, s_vg, r_vg, outs_sem, wh_out_sem, wp_out_sem,
        near_sem,
    ) = refs[20:]
    count = len(left_in)
    me_s = lax.axis_index("section")
    me = lax.axis_index("dp")
    chips = peers // 2
    chip, core = me // 2, me % 2
    sibling = me + 1 - 2 * core
    blocks, share = chips, own.shape[2]
    columns = wh.shape[2]
    has_right = chip + 1 < chips
    has_left = chip > 0
    after = jnp.minimum(me + 2, peers - 1)
    before = jnp.maximum(me - 2, 0)

    barrier = pltpu.get_barrier_semaphore()

    def greet(index):
        pl.semaphore_signal(barrier, inc=1, device_id=(me_s, index), device_id_type=MESH)

    def each_peer(action):
        def turn(k, carry):
            @pl.when(k != me)
            def _():
                action(k)

            return carry

        lax.fori_loop(0, peers, turn, 0)

    each_peer(greet)
    for w in range(count):
        pltpu.make_async_copy(left_in[w], lefts.at[w], left_sem.at[w]).start()
        pltpu.make_async_copy(right_in[w], rights.at[w], right_sem.at[w]).start()
    is_late = 2 * me_s >= sections
    lh_copy = pltpu.make_async_copy(lh_in, lh, lh_sem)
    rows = dp_in.shape[0]
    own_rows = pl.ds(pl.multiple_of(chip * rows, rows), rows)
    dp_copy = pltpu.make_async_copy(dp_in, dp.at[own_rows], dp_sem)
    dp_copy.start()

    def near_load(way):
        origin = jnp.minimum(chip + 1, chips - 1) if way else jnp.maximum(chip - 1, 0)
        place = pl.ds(pl.multiple_of(origin * rows, rows), rows)
        return pltpu.make_async_copy(near_in.at[way], dp.at[place], near_sem.at[way])

    pl.when(has_left)(lambda: near_load(0).start())
    pl.when(has_right)(lambda: near_load(1).start())
    lh_own = pltpu.make_async_copy(lh_in.at[own_rows], lh.at[own_rows], lh_sem)
    pl.when(is_late)(lh_own.start)
    pl.when(jnp.logical_not(is_late))(lh_copy.start)

    def wh_copy(j, slot):
        return pltpu.make_async_copy(
            wh_in.at[:, pl.ds(pl.multiple_of(j * columns, columns), columns)],
            wh.at[slot], wh_sem.at[slot],
        )

    def wp_copy(j, slot):
        return pltpu.make_async_copy(
            wp_in.at[pl.ds(pl.multiple_of(j * columns, columns), columns)],
            wp.at[slot], wp_sem.at[slot],
        )

    wh_copy(0, 0).start()
    wp_copy(0, 0).start()
    def remote(source, target, send, receive, index):
        return pltpu.make_async_remote_copy(
            src_ref=source, dst_ref=target, send_sem=send, recv_sem=receive,
            device_id=(me_s, index), device_id_type=MESH,
        )

    def pair_copy(w):
        return remote(pair_out.at[w], own.at[w], s_pair.at[w], r_pair.at[w], sibling)

    cut = vgr.shape[2]

    def vector_copy(k, slot):
        part = vgs.at[:, pl.ds(pl.multiple_of(k * cut, cut), cut)] if split_vectors else vgs
        return remote(part, vgr.at[slot], s_vg.at[k], r_vg.at[slot], k)

    def rows_of(block, parity):
        return pl.ds(pl.multiple_of((2 * block + parity) * share, share), share)

    def prepare(w):
        pltpu.make_async_copy(lefts.at[w], lefts.at[w], left_sem.at[w]).wait()
        pltpu.make_async_copy(rights.at[w], rights.at[w], right_sem.at[w]).wait()
        slot = w % 2
        whole[slot] = dot_tn(lefts[w], rights[w])

        def divide(q, carry):
            pair_out[w, q] = whole[slot, rows_of(q, 1 - core), :].astype(BF16)
            return carry

        lax.fori_loop(0, blocks, divide, 0)

    def combine(w):
        slot = w % 2
        pair_copy(w).wait_recv()

        def add(q, carry):
            own[w, q] = (
                whole[slot, rows_of(q, core), :] + own[w, q].astype(F32)
            ).astype(BF16)
            return carry

        lax.fori_loop(0, blocks, add, 0)

    def right_copy(source, w, r):
        return remote(source, going_right.at[w, r], s_right.at[w, r], r_right.at[w, r], after)

    def left_copy(source, w, r):
        return remote(source, going_left.at[w, r], s_left.at[w, r], r_left.at[w, r], before)

    from_end = chips - 1 - chip

    def launch(w):
        def turn(r, carry):
            @pl.when(has_right & (chip == 0))
            def _():
                right_copy(own.at[w, chips - 1 - r], w, r).start()

            @pl.when(has_left & (from_end == 0))
            def _():
                left_copy(own.at[w, r], w, r).start()

            return carry

        lax.fori_loop(0, rounds, turn, 0)

    def travel(w, r):
        prior = jnp.maximum(r - 1, 0)

        @pl.when(has_right & (chip > 0) & (chip <= r))
        def _():
            slot = going_right.at[w, prior]
            right_copy(slot, w, prior).wait_recv()
            slot[...] = (
                slot[...].astype(F32) + own[w, chips - 1 - r + chip].astype(F32)
            ).astype(BF16)
            right_copy(slot, w, r).start()

        @pl.when(has_left & (from_end > 0) & (from_end <= r))
        def _():
            slot = going_left.at[w, prior]
            left_copy(slot, w, prior).wait_recv()
            slot[...] = (
                slot[...].astype(F32) + own[w, r - from_end].astype(F32)
            ).astype(BF16)
            left_copy(slot, w, r).start()

    def rows_copy(kind, origin, send, index):
        block = (lh if kind else dp).at[pl.ds(pl.multiple_of(origin * rows, rows), rows)]
        return remote(block, block, send.at[kind, origin], r_rows.at[kind, origin], index)

    def each_origin(kind, low, high):
        def turn(origin, carry):
            rows_copy(kind, origin, s_ahead, after).wait_recv()
            return carry

        lax.fori_loop(low, high, turn, 0)

    def spread(kind, r):
        held = 0 if kind else 1

        @pl.when(has_right & (chip >= r))
        def _():
            pl.when(r > held)(lambda: rows_copy(kind, chip - r, s_ahead, after).wait_recv())
            rows_copy(kind, chip - r, s_ahead, after).start()

        @pl.when(has_left & (from_end >= r))
        def _():
            pl.when(r > held)(lambda: rows_copy(kind, chip + r, s_behind, before).wait_recv())
            rows_copy(kind, chip + r, s_behind, before).start()

    def hid_copy(j):
        place = pl.ds(pl.multiple_of(j * columns, columns), columns)
        return remote(
            hid_out.at[:, place], hid_in.at[:, place], s_hid.at[j], r_hid.at[j], sibling
        )

    proj_copy = remote(proj_out, proj_in, s_proj, r_proj, sibling)
    group = wide.shape[0]
    first = chip * 2 * share
    start = pl.multiple_of(first // group * group, group)
    inside = first - first // group * group

    def hidden_store(j):
        place = pl.ds(pl.multiple_of(j * columns, columns), columns)
        return pltpu.make_async_copy(wh_out.at[:, place], wh_hbm.at[:, place], wh_out_sem.at[j])

    def close_hidden(j):
        hid_copy(j).wait_recv()
        place = pl.ds(pl.multiple_of(j * columns, columns), columns)
        wh_out[:, place] += hid_in[:, place].astype(F32)
        hidden_store(j).start()

    def sum_store(w):
        return pltpu.make_async_copy(outs.at[w], outs_hbm.at[w], outs_sem.at[w])

    proj_store = pltpu.make_async_copy(wp_out, wp_hbm, wp_out_sem)

    def close_sum(w):
        outs[w] = own[w, chip].astype(F32)

        @pl.when(has_left)
        def _():
            right_copy(own.at[w, 0], w, rounds - 1).wait_recv()
            outs[w] += going_right[w, rounds - 1].astype(F32)

        @pl.when(has_right)
        def _():
            left_copy(own.at[w, 0], w, rounds - 1).wait_recv()
            outs[w] += going_left[w, rounds - 1].astype(F32)

        sum_store(w).start()

    def feed(j):
        slot = j % 2
        place = pl.ds(pl.multiple_of(j * columns, columns), columns)

        @pl.when(j == 0)
        def _():
            dp_copy.wait()
            pl.when(chip == 0)(lambda: each_origin(0, 2, chips))
            pl.when(from_end == 0)(lambda: each_origin(0, 0, chips - 2))
            pl.when(jnp.logical_not(is_late))(lh_copy.wait)
            pl.when(is_late & (chip == 0))(lambda: each_origin(1, 1, chips))
            pl.when(is_late & (from_end == 0))(lambda: each_origin(1, 0, chips - 1))

        wh_copy(j, slot).wait()
        wp_copy(j, slot).wait()

        @pl.when(j + 1 < peers)
        def _():
            wh_copy(j + 1, 1 - slot).start()
            wp_copy(j + 1, 1 - slot).start()

        active = jnp.maximum(dot_nn(lh[...], wh[slot]), 0.0)
        act[...] = active
        grown = (dot_nt(dp[...], wp[slot]) * 2.0 * act[...]).astype(BF16)
        wide[...] = dot_tn(lh[:, pl.ds(start, group)], grown)
        mine = pl.ds(pl.multiple_of(inside + core * share, 16), share)
        other = pl.ds(pl.multiple_of(inside + (1 - core) * share, 16), share)
        wh_out[:, place] = wide[mine, :]
        hid_out[:, place] = wide[other, :].astype(BF16)
        hid_copy(j).start()
        pl.when(j > 0)(lambda: close_hidden(j - 1))

        @pl.when(j == 2 * chip + core)
        def _():
            squared = (act[...] * act[...]).astype(BF16)
            wp_out[...] = dot_tn(squared, dp[...])

        @pl.when(j == 2 * chip + 1 - core)
        def _():
            squared = (act[...] * act[...]).astype(BF16)
            proj_out[...] = dot_tn(squared, dp[...]).astype(BF16)
            proj_copy.start()

    rounds = chips - 1
    prepare(0)
    pl.semaphore_wait(barrier, peers - 1)
    pair_copy(0).start()
    pl.when(has_left)(lambda: near_load(0).wait())
    pl.when(has_right)(lambda: near_load(1).wait())
    spread(0, 1)

    @pl.when(is_late)
    def _():
        lh_own.wait()
        spread(1, 0)

    each_peer(lambda k: vector_copy(k, me).start())
    prepare(1)
    pair_copy(1).start()
    combine(0)
    launch(0)
    if split_vectors:
        vec_out[...] = vgs[:, pl.ds(pl.multiple_of(me * cut, cut), cut)]
    else:
        vec_out[...] = vgs[...]
    opening = count * rounds - peers

    def step(t, carry):
        w, r = t // rounds, t % rounds
        travel(w, r)

        @pl.when((r == 1) & (w + 2 < count))
        def _():
            prepare(w + 2)
            pair_copy(w + 2).start()

        @pl.when((r == 1) & (w + 1 < count))
        def _():
            combine(w + 1)
            launch(w + 1)

        @pl.when(t + 2 < rounds)
        def _():
            spread(0, t + 2)

        @pl.when(is_late & (t + 1 < rounds))
        def _():
            spread(1, t + 1)

        @pl.when(t >= opening)
        def _():
            feed(t - opening)

        @pl.when((r == rounds - 1) & (w > 0))
        def _():
            close_sum(w - 1)

        return carry

    lax.fori_loop(0, count * rounds, step, 0)

    close_hidden(peers - 1)
    proj_copy.wait_recv()
    wp_out[...] += proj_in[...].astype(F32)
    proj_store.start()

    def collect(k):
        vector_copy(k, k).wait_recv()
        vec_out[...] += vgr[k]

    each_peer(collect)
    close_sum(count - 1)
    each_peer(lambda k: vector_copy(k, me).wait_send())

    def sent_hidden(j, carry):
        hid_copy(j).wait_send()
        hidden_store(j).wait()
        return carry

    lax.fori_loop(0, peers, sent_hidden, 0)
    proj_copy.wait_send()
    proj_store.wait()

    def sent_rows(origin, carry):
        @pl.when(has_right & (origin < chip))
        def _():
            rows_copy(0, origin, s_ahead, after).wait_send()

        @pl.when(has_left & (origin > chip))
        def _():
            rows_copy(0, origin, s_behind, before).wait_send()

        @pl.when(is_late & has_right & (origin <= chip))
        def _():
            rows_copy(1, origin, s_ahead, after).wait_send()

        @pl.when(is_late & has_left & (origin >= chip))
        def _():
            rows_copy(1, origin, s_behind, before).wait_send()

        return carry

    lax.fori_loop(0, chips, sent_rows, 0)

    def sent(w, carry):
        pair_copy(w).wait_send()
        sum_store(w).wait()

        def sent_round(r, inner):
            @pl.when(has_right & (chip <= r))
            def _():
                right_copy(own.at[w, 0], w, r).wait_send()

            @pl.when(has_left & (from_end <= r))
            def _():
                left_copy(own.at[w, 0], w, r).wait_send()

            return inner

        lax.fori_loop(0, rounds, sent_round, 0)
        return carry

    lax.fori_loop(0, count, sent, 0)


def gradient_sums(sections, peers, lefts, rights, lh, dp, near, wh, wp, vgs):
    count = len(lefts)
    rows, width = lefts[0].shape
    hidden = wh.shape[1]
    tokens = lh.shape[0]
    chips = peers // 2
    share = width // peers
    columns = hidden // peers
    group = max(128, 2 * share)
    shape = jax.ShapeDtypeStruct
    vmem = pl.BlockSpec(memory_space=pltpu.VMEM)
    anywhere = pl.BlockSpec(memory_space=pl.ANY)
    dma = pltpu.SemaphoreType.DMA
    blocks = pltpu.VMEM((count, chips, share, width), BF16)
    slots = pltpu.VMEM((count, chips - 1, share, width), BF16)
    split_vectors = share % 128 == 0
    cut = share if split_vectors else width
    return pl.pallas_call(
        partial(sum_kernel, sections, peers, split_vectors),
        out_shape=(
            shape((count, share, width), F32), shape((share, hidden), F32),
            shape((columns, width), F32), shape((VECTORS, cut), F32),
        ),
        in_specs=[anywhere] * (2 * count + 5) + [vmem],
        out_specs=[anywhere] * 3 + [vmem],
        scratch_shapes=[
            pltpu.VMEM((count, rows, width), BF16), pltpu.VMEM((count, rows, width), BF16),
            pltpu.VMEM((2, width, width), F32),
            blocks, blocks, slots, slots,
            pltpu.VMEM((tokens, width), BF16), pltpu.VMEM((tokens, width), BF16),
            pltpu.VMEM((2, width, columns), BF16), pltpu.VMEM((2, columns, width), BF16),
            pltpu.VMEM((tokens, columns), F32), pltpu.VMEM((group, columns), F32),
            pltpu.VMEM((share, hidden), BF16), pltpu.VMEM((share, hidden), BF16),
            pltpu.VMEM((columns, width), BF16), pltpu.VMEM((columns, width), BF16),
            dma((count,)), dma((count,)), dma, dma, dma((2,)), dma((2,)),
            dma((count,)), dma((count,)),
            dma((count, chips - 1)), dma((count, chips - 1)),
            dma((count, chips - 1)), dma((count, chips - 1)),
            dma((peers,)), dma((peers,)), dma, dma,
            dma((2, chips)), dma((2, chips)), dma((2, chips)),
            pltpu.VMEM((count, share, width), F32), pltpu.VMEM((share, hidden), F32),
            pltpu.VMEM((columns, width), F32), pltpu.VMEM((peers, VECTORS, cut), F32),
            dma((peers,)), dma((peers,)), dma((count,)), dma((peers,)), dma, dma((2,)),
        ],
        compiler_params=pltpu.CompilerParams(
            collective_id=1, has_side_effects=True, vmem_limit_bytes=63 * 2**20
        ),
        name="gradient_sums",
    )(*lefts, *rights, lh, dp, near, wh, wp, vgs)


def deliver_kernel(count, vectors, *refs):
    vec, sources = refs[0], refs[1:6]
    targets = refs[6 : 6 + count]
    rows = refs[6 + count : 6 + count + vectors]
    buffers = refs[6 + count + vectors : -2]
    in_sem, out_sem = refs[-2:]
    pieces = list(sources[:-1]) + [sources[-1].at[w] for w in range(count - 4)]
    enter = [
        pltpu.make_async_copy(piece, buffer, in_sem.at[index])
        for index, (piece, buffer) in enumerate(zip(pieces, buffers))
    ]
    leave = [
        pltpu.make_async_copy(buffer, target, out_sem.at[index])
        for index, (buffer, target) in enumerate(zip(buffers, targets))
    ]
    for copy in enter:
        copy.start()
    for index, row in enumerate(rows):
        row[...] = vec[index : index + 1, :]
    for first, second in zip(enter, leave):
        first.wait()
        second.start()
    for copy in leave:
        copy.wait()


def deliver(vec, hidden, project, out, back, squares, vectors):
    shapes = [(out.shape, BF16), (back.shape, BF16), (hidden.shape, F32), (project.shape, F32)]
    shapes += [(squares.shape[1:], F32)] * squares.shape[0]
    count = len(shapes)
    anywhere = pl.BlockSpec(memory_space=pl.ANY)
    vmem = pl.BlockSpec(memory_space=pltpu.VMEM)
    dma = pltpu.SemaphoreType.DMA
    found = pl.pallas_call(
        partial(deliver_kernel, count, vectors),
        out_shape=tuple(jax.ShapeDtypeStruct(*kind) for kind in shapes)
        + (jax.ShapeDtypeStruct((1, vec.shape[1]), F32),) * vectors,
        in_specs=[vmem] + [anywhere] * 5,
        out_specs=[anywhere] * count + [vmem] * vectors,
        scratch_shapes=[pltpu.VMEM(*kind) for kind in shapes] + [dma((count,)), dma((count,))],
        compiler_params=pltpu.CompilerParams(vmem_limit_bytes=63 * 2**20),
        name="deliver",
    )(vec, out, back, hidden, project, squares)
    return found[:count], found[count:]


def per_device(x, top, spans, *parameters):
    sections = lax.axis_size("section")
    peers = lax.axis_size("dp")
    gain1, bias1, mix_k, mix_v, mix_g, log_rate, extra = parameters[0:7]
    wk, wv, wg, wo = parameters[7:11]
    gain2, bias2, mix_h, mix_f = parameters[11:15]
    wh, wp, wf = parameters[15:18]
    vectors = (gain1, bias1, mix_k, mix_v, mix_g, log_rate, extra, gain2, bias2, mix_h, mix_f)
    matrices = tuple(w[0] for w in (wk, wv, wg, wo, wh, wp, wf))
    found = relay(sections, peers, x, top, spans, vectors, matrices)
    out, back, lk, lv, lg, lgt, lf, dk, dv, dg, datt, dsv, dproj = found[0:13]
    vgs, lh = found[13], found[14].reshape(-1, x.shape[2])
    flat = (x.shape[0] * x.shape[1], x.shape[2])
    squares, d_wh, d_wp, vec = gradient_sums(
        sections, peers,
        [part.reshape(flat) for part in (lf, lgt, lg, lk, lv)],
        [part.reshape(flat) for part in (dsv, datt, dg, dk, dv)],
        lh, dproj.reshape(flat), found[15].reshape(2, *flat), matrices[4], matrices[5], vgs,
    )
    share = x.shape[2] // peers
    if vec.shape[1] != share:
        vec = lax.dynamic_slice_in_dim(vec, lax.axis_index("dp") * share, share, 1)
    moved, rows = deliver(vec, d_wh, d_wp, out, back, squares, 11)
    out, back, d_wh, d_wp, d_wf, d_wo, d_wg, d_wk, d_wv = (part[None] for part in moved)
    return (
        out, back,
        rows[0], rows[1], rows[2], rows[3], rows[4], rows[5], rows[6],
        d_wk, d_wv, d_wg, d_wo,
        rows[7], rows[8], rows[9], rows[10],
        d_wh, d_wp, d_wf,
    )


def solution(mesh):
    tokens = P(None, "dp", None)
    vector = P("section", None)
    matrix = P("section", None, None)
    result = P("section", None, "dp", None)
    vector_grad = P("section", "dp")
    matrix_grad = P("section", "dp", None)
    return jax.shard_map(
        per_device,
        mesh=mesh,
        in_specs=(tokens, tokens, P())
        + (vector,) * 7 + (matrix,) * 4 + (vector,) * 4 + (matrix,) * 3,
        out_specs=(result, result)
        + (vector_grad,) * 7 + (matrix_grad,) * 4 + (vector_grad,) * 4 + (matrix_grad,) * 3,
        check_vma=False,
    )
```

```python
from functools import partial

import jax
import jax.numpy as jnp
from jax import lax
from jax.experimental import pallas as pl
from jax.experimental.pallas import tpu as pltpu
from jax.sharding import PartitionSpec as P

EPS = 1e-05
MESH = pl.DeviceIdType.MESH
RB = 64
VECTORS = 16
F32 = jnp.float32
BF16 = jnp.bfloat16


def dot_nn(left, right):
    return jnp.dot(left, right, preferred_element_type=F32)


def dot_nt(left, right):
    return lax.dot_general(left, right, (((1,), (1,)), ((), ())), preferred_element_type=F32)


def dot_tn(left, right):
    return lax.dot_general(left, right, (((0,), (0,)), ((), ())), preferred_element_type=F32)


def sigmoid(v):
    return 1.0 / (1.0 + jnp.exp(-v))


def normalise(source):
    centred = source - jnp.mean(source, axis=-1, keepdims=True)
    spread = lax.rsqrt(jnp.mean(centred * centred, axis=-1, keepdims=True) + EPS)
    return centred * spread, spread


def moved_down(rows, first):
    place = lax.broadcasted_iota(jnp.int32, rows.shape, 0)
    return jnp.where(place == 0, first, pltpu.roll(rows, 1, 0))


def moved_up(rows, last):
    count = rows.shape[0]
    place = lax.broadcasted_iota(jnp.int32, rows.shape, 0)
    return jnp.where(place == count - 1, last, pltpu.roll(rows, count - 1, 0))


def fold(rows):
    total = rows[0:8]
    for at in range(8, rows.shape[0], 8):
        total = total + rows[at : at + 8]
    return total


def relay_kernel(sections, peers, *refs):
    (
        spans, x_in, top_in,
        gain1, bias1, mix_k, mix_v, mix_g, log_rate, extra, gain2, bias2, mix_h, mix_f,
        wk_in, wv_in, wg_in, wo_in, wh_in, wp_in, wf_in,
        out_hbm, back_hbm, lk_hbm, lv_hbm, lg_hbm, lgt_hbm, lf_hbm,
        dk_hbm, dv_hbm, dg_hbm, datt_hbm, dsv_hbm, dproj_hbm, vgs, lh_all, near,
        wk_t, wv_t, wg_t, wo_t, wf_t, wp_t, wh_t,
        out, back, lk, lv, lg, lgt, lf, dk, dv, dg, datt, dsv, dproj,
        lh, sq, dh, turned,
        wk, wv, wg, wo, wh, wp, wf,
        xs, hx, dys, kk, vv, sg, sa, sb, mid, hmid, proj, sv, act,
        e0, e1, low_mask, up_mask, split, acc, t1, t2, t3,
        states, back_states, de2, de1, sum_row, sum_back, send_de2, send_de1, vg,
        sp1, gp1, sd1, sp2, gp2, sd2, fo, iv,
        w_sem, x_sem, top_sem, s_h0, s_x, s_hx, s_st, s_mid, s_dy, s_de2, s_bst, s_de1,
        r_x, r_hx, r_st, r_mid, r_dy, r_de2, r_bst, r_de1, store_sem,
        s_lh, r_lh, own_sem, s_near, r_near, turn_sem, back_sem,
    ) = refs
    me_s = lax.axis_index("section")
    me = lax.axis_index("dp")
    batches, row_count, width = x_in.shape
    hidden = wh.shape[1]
    chunks = row_count // RB
    base = me * row_count

    def at(section, index):
        return (section, index)

    barrier = pltpu.get_barrier_semaphore()

    def greet(section, index):
        pl.semaphore_signal(barrier, inc=1, device_id=at(section, index), device_id_type=MESH)

    def greet_peer(k, carry):
        @pl.when(k != me)
        def _():
            greet(me_s, k)

        return carry

    lax.fori_loop(0, peers, greet_peer, 0)
    has_next = me_s + 1 < sections
    has_prior = me_s > 0
    has_right = me + 1 < peers
    has_left = me > 0

    @pl.when(has_next)
    def _():
        greet(me_s + 1, me)

    @pl.when(has_prior)
    def _():
        greet(me_s - 1, me)

    @pl.when(has_next & has_right)
    def _():
        greet(me_s + 1, me + 1)

    @pl.when(has_prior & has_left)
    def _():
        greet(me_s - 1, me - 1)

    weight_copies = [
        pltpu.make_async_copy(source, target, w_sem.at[index])
        for index, (source, target) in enumerate(
            ((wk_in, wk), (wv_in, wv), (wg_in, wg), (wo_in, wo), (wf_in, wf), (wh_in, wh), (wp_in, wp))
        )
    ]

    @pl.when(me_s == 0)
    def _():
        pltpu.make_async_copy(x_in, xs, x_sem).start()

    for copy in weight_copies[0:2]:
        copy.start()

    @pl.when(me_s == sections - 1)
    def _():
        pltpu.make_async_copy(top_in, dys, top_sem).start()

    rate = jnp.exp(log_rate[...])
    boost = jnp.exp(extra[...])
    decay_block = jnp.exp(-rate * row_count)
    grow_block = jnp.exp(rate * row_count)

    half = width // 128

    def packed(row_a, row_b):
        return jnp.concatenate(
            [row[:, j * 128 : (j + 1) * 128] for row in (row_a, row_b) for j in range(half)], axis=0
        )

    def unpacked(tile, part):
        return jnp.concatenate(
            [tile[part * half + j : part * half + j + 1] for j in range(half)], axis=1
        )

    decay_tile = packed(decay_block, decay_block)

    def starts_of(m):
        found = []
        total = jnp.int32(0)
        for j in range(spans.shape[1]):
            found.append(total)
            total = total + spans[m, j]
        return found

    def segment(position, starts):
        total = jnp.where(position >= starts[0], 1, 0)
        for start in starts[1:]:
            total = total + jnp.where(position >= start, 1, 0)
        return total

    def column(i):
        return base + i * RB + lax.broadcasted_iota(jnp.int32, (RB, 1), 0)

    def keep_of(position, starts):
        return jnp.where(segment(position, starts) == segment(position - 1, starts), 1.0, 0.0)

    def fill_powers(i, carry):
        place = (i * RB + lax.broadcasted_iota(jnp.int32, (RB, width), 0)).astype(F32)
        e0[pl.ds(pl.multiple_of(i * RB, RB), RB), :] = jnp.exp(-place * rate)
        e1[pl.ds(pl.multiple_of(i * RB, RB), RB), :] = jnp.exp((place - (row_count - 1.0)) * rate)
        return carry

    lax.fori_loop(0, chunks, fill_powers, 0)
    for m in range(batches):
        starts = starts_of(m)
        row_at = lax.broadcasted_iota(jnp.int32, (row_count, row_count), 0)
        column_at = lax.broadcasted_iota(jnp.int32, (row_count, row_count), 1)
        same = segment(base + row_at, starts) == segment(base + column_at, starts)
        lower = jnp.where(same & (column_at < row_at), 1.0, 0.0).astype(BF16)
        upper = jnp.where(same & (column_at > row_at), 1.0, 0.0).astype(BF16)
        low_mask[m, :, 0:row_count] = lower
        low_mask[m, :, row_count:] = lower
        up_mask[m, :, 0:row_count] = upper
        up_mask[m, :, row_count:] = upper
    vg[...] = jnp.zeros_like(vg)

    @pl.when(me == 0)
    def _():
        hx[...] = jnp.zeros_like(hx)
        hmid[...] = jnp.zeros_like(hmid)

    @pl.when(me == peers - 1)
    def _():
        de1[...] = jnp.zeros_like(de1)
        de2[...] = jnp.zeros_like(de2)

    greeted = (
        peers - 1
        + jnp.where(has_next, 1, 0)
        + jnp.where(has_prior, 1, 0)
        + jnp.where(has_next & has_right, 1, 0)
        + jnp.where(has_prior & has_left, 1, 0)
    )
    for copy in weight_copies[2:7]:
        copy.start()

    def remote(source, target, send, receive, section, index):
        return pltpu.make_async_remote_copy(
            src_ref=source, dst_ref=target, send_sem=send, recv_sem=receive,
            device_id=at(section, index), device_id_type=MESH,
        )

    right = jnp.minimum(me + 1, peers - 1)
    left = jnp.maximum(me - 1, 0)
    above = jnp.minimum(me_s + 1, sections - 1)
    below = jnp.maximum(me_s - 1, 0)
    tail = pl.ds(row_count - 16, 16)
    final = pl.ds(row_count - 1, 1)

    stored = (
        (out, out_hbm), (lk, lk_hbm), (lv, lv_hbm), (lg, lg_hbm), (lgt, lgt_hbm), (lf, lf_hbm),
        (dproj, dproj_hbm), (dsv, dsv_hbm), (datt, datt_hbm), (dg, dg_hbm), (dk, dk_hbm),
        (dv, dv_hbm), (back, back_hbm),
    )

    def store_copy(index, m):
        source, target = stored[index]
        return pltpu.make_async_copy(source.at[m], target.at[m], store_sem.at[index, m])

    def start_halo(m):
        return remote(x_in.at[m, tail], hx.at[m], s_h0.at[m], r_hx.at[m], me_s, right)

    def result_copy(m, i):
        rows = pl.ds(i * RB, RB)
        return remote(
            out.at[m, rows], xs.at[m, rows], s_x.at[m, i], r_x.at[m, i], above, me
        )

    def result_halo(m):
        return remote(out.at[m, tail], hx.at[m], s_hx.at[m], r_hx.at[m], above, right)

    def middle_halo(m):
        return remote(mid.at[m, final], hmid.at[m], s_mid.at[m], r_mid.at[m], me_s, right)

    def state_copy(m, k, slot):
        return remote(sum_row.at[m], states.at[m, slot], s_st.at[m, k], r_st.at[m, slot], me_s, k)

    pieces = (
        (0, row_count // 2), (row_count // 2, row_count // 2 - 16), (row_count - 16, 16)
    )

    def back_copy(m, index):
        rows = pl.ds(*pieces[index])
        return remote(
            back.at[m, rows], dys.at[m, rows], s_dy.at[m, index], r_dy.at[m, index], below, me
        )

    def each_piece(action):
        for index in range(len(pieces)):
            action(index)

    def second_copy(m):
        return remote(send_de2.at[m], de2.at[m], s_de2.at[m], r_de2.at[m], me_s, left)

    def first_copy(m):
        return remote(send_de1.at[m], de1.at[m], s_de1.at[m], r_de1.at[m], me_s, left)

    def back_state_copy(m, k, slot):
        return remote(
            sum_back.at[m], back_states.at[m, slot], s_bst.at[m, k], r_bst.at[m, slot], me_s, k
        )

    chip, core = me // 2, me % 2
    chips = peers // 2

    def gather_copy(m, k, slot):
        return remote(
            lh.at[m], lh_all.at[slot, m], s_lh.at[m, k], r_lh.at[m, slot], me_s, 2 * k + core
        )

    is_late = 2 * me_s >= sections

    def own_copy(m):
        return pltpu.make_async_copy(lh.at[m], lh_all.at[chip, m], own_sem.at[m])

    def each_chip(action):
        def turn(k, carry):
            @pl.when(k != chip)
            def _():
                action(k)

            return carry

        lax.fori_loop(0, chips, turn, 0)

    ahead = jnp.minimum(me + 2, peers - 1)
    behind = jnp.maximum(me - 2, 0)
    has_ahead = chip + 1 < chips
    has_behind = chip > 0

    def near_copy(m, way):
        return remote(
            dproj.at[m], near.at[way, m], s_near.at[way, m], r_near.at[way, m],
            me_s, behind if way else ahead,
        )

    def send_near(m):
        pl.when(has_ahead)(lambda: near_copy(m, 0).start())
        pl.when(has_behind)(lambda: near_copy(m, 1).start())

    def end_near(m):
        @pl.when(has_ahead)
        def _():
            near_copy(m, 0).wait_send()
            near_copy(m, 1).wait_recv()

        @pl.when(has_behind)
        def _():
            near_copy(m, 1).wait_send()
            near_copy(m, 0).wait_recv()

    def start_gathers():
        for m in range(batches):
            own_copy(m).start()

            @pl.when(jnp.logical_not(is_late))
            def _(m=m):
                each_chip(lambda k: gather_copy(m, k, chip).start())

    def end_gather(m):
        own_copy(m).wait()

        @pl.when(jnp.logical_not(is_late))
        def _():
            each_chip(lambda k: gather_copy(m, k, chip).wait_send())
            each_chip(lambda k: gather_copy(m, k, k).wait_recv())

    @pl.when(me_s == 0)
    def _():
        pltpu.make_async_copy(x_in, xs, x_sem).wait()

    turns = (
        (wk, wk_t), (wv, wv_t), (wg, wg_t), (wo, wo_t), (wf, wf_t), (wh, wh_t), (wp, wp_t)
    )
    returns = (
        (wk_t, wk), (wv_t, wv), (wg_t, wg), (wo_t, wo), (wf_t, wf), (wp_t, wh), (wh_t, wp)
    )
    slots, edge = turned.shape[0], turned.shape[1]

    def transpose_all(fresh):
        for index, (source, target) in enumerate(turns):
            if fresh:
                weight_copies[index].wait()
            tall = source.shape[0] // edge
            blocks = tall * (source.shape[1] // edge)

            def place(n, source=source, target=target, tall=tall):
                down = pl.ds(pl.multiple_of(n % tall * edge, edge), edge)
                along = pl.ds(pl.multiple_of(n // tall * edge, edge), edge)
                slot = n % slots
                return (
                    source.at[down, along],
                    turned.at[slot],
                    pltpu.make_async_copy(turned.at[slot], target.at[along, down], turn_sem.at[slot]),
                )

            def turn(n, carry, place=place):
                piece, buffer, copy = place(n)
                pl.when(n >= slots)(copy.wait)
                buffer[...] = piece[...].T
                copy.start()
                return carry

            lax.fori_loop(0, blocks, turn, 0)
            for n in range(blocks - slots, blocks):
                place(n)[2].wait()

    def return_copy(index):
        source, target = returns[index]
        return pltpu.make_async_copy(source, target, back_sem.at[index])


    def release(m, index):
        if m == batches - 1:
            pl.when(is_late)(lambda: return_copy(index).start())

    def weight_ready(m, index, fresh=True):
        if m == 0:
            pl.when(jnp.logical_not(is_late))(lambda: weight_copies[index].wait())

    def span_of(i):
        return pl.ds(pl.multiple_of(i * RB, RB), RB)

    def split_sums():
        def turn(i, carry):
            rows = span_of(i)
            low = pl.ds(pl.multiple_of(row_count + i * RB, RB), RB)
            for source, place in ((t1, pl.ds(0, width)), (t2, pl.ds(width, width))):
                value = source[rows, :]
                high = value.astype(BF16)
                split[rows, place] = high
                split[low, place] = (value - high.astype(F32)).astype(BF16)
            return carry

        lax.fori_loop(0, chunks, turn, 0, unroll=True)

    def forward(m, carry):
        starts = starts_of(m)

        none = jnp.zeros((1, width), F32)

        def mix_in(start, size, last):
            rows = pl.ds(start, size)
            spare, spread = normalise(xs[m, rows, :].astype(F32))
            sp1[m, rows, :] = spare
            sd1[m, rows, :] = spread
            normed = spare * gain1[...] + bias1[...]
            position = base + start + lax.broadcasted_iota(jnp.int32, (size, 1), 0)
            earlier = moved_down(normed, last) * keep_of(position, starts)
            gap = normed - earlier
            gp1[m, rows, :] = gap.astype(BF16)
            lk[m, rows, :] = (earlier + gap * mix_k[...]).astype(BF16)
            lv[m, rows, :] = (earlier + gap * mix_v[...]).astype(BF16)
            lg[m, rows, :] = (earlier + gap * mix_g[...]).astype(BF16)
            return normed[size - 1 : size]

        last = none
        for i in range(chunks):
            pl.when(has_prior)(lambda i=i: result_copy(m, i).wait_recv())
            last = mix_in(i * RB, RB, last)

        if m == 0:
            pl.semaphore_wait(barrier, greeted)

            @pl.when((me_s == 0) & has_right)
            def _():
                for n in range(batches):
                    start_halo(n).start()

        @pl.when(has_left)
        def _():
            start_halo(m).wait_recv()

        halo_rows, _ = normalise(hx[m].astype(F32))
        mix_in(0, 16, (halo_rows * gain1[...] + bias1[...])[15:16])
        weight_ready(m, 0)
        weight_ready(m, 1)
        kk[m] = dot_nn(lk[m], wk[...])
        vv[m] = dot_nn(lv[m], wv[...])
        release(m, 0)
        release(m, 1)
        end_segment = segment(base + row_count - 1, starts)

        def spread_in(i, totals):
            rows = span_of(i)
            plain = jnp.exp(kk[m, rows, :])
            kk[m, rows, :] = plain
            weight = plain * e1[rows, :]
            weighted = weight * vv[m, rows, :]
            t1[rows, :] = weighted
            t2[rows, :] = weight
            chosen = segment(column(i), starts) == end_segment
            return (
                totals[0] + fold(jnp.where(chosen, weighted, 0.0)),
                totals[1] + fold(jnp.where(chosen, weight, 0.0)),
            )

        nothing = jnp.zeros((8, width), F32)
        total_a, total_b = lax.fori_loop(0, chunks, spread_in, (nothing, nothing), unroll=True)
        sum_row[m] = packed(
            jnp.sum(total_a, axis=0, keepdims=True), jnp.sum(total_b, axis=0, keepdims=True)
        )

        def send_state(k, carry):
            state_copy(m, k, me).start()
            return carry

        lax.fori_loop(me + 1, peers, send_state, 0)

        weight_ready(m, 2)
        sg[m] = dot_nn(lg[m], wg[...])
        split_sums()
        acc[...] = dot_nn(low_mask[m], split[...])
        sg[m] = sigmoid(sg[m])
        release(m, 2)

        def receive_state(k, held):
            state_copy(m, k, k).wait_recv()
            unbroken = segment(k * row_count - 1, starts) == segment(
                (k + 1) * row_count - 1, starts
            )
            passing = jnp.where(unbroken, 1.0, 0.0) * decay_tile
            return passing * held + states[m, k]

        entered = lax.fori_loop(0, me, receive_state, jnp.zeros_like(decay_tile))
        enter_a, enter_b = unpacked(entered, 0), unpacked(entered, 1)
        prior_segment = segment(base - 1, starts)

        def mix_states(i, carry):
            rows = span_of(i)
            falling = e0[rows, :]
            chosen = jnp.where(segment(column(i), starts) == prior_segment, 1.0, 0.0)
            grown = falling * grow_block
            held = falling * chosen
            state_a = grown * acc[rows, 0:width] + held * enter_a
            state_b = grown * acc[rows, width:] + held * enter_b
            sa[m, rows, :] = state_a
            sb[m, rows, :] = state_b
            present = boost * kk[m, rows, :]
            inverse = 1.0 / (state_b + present)
            found = (state_a + present * vv[m, rows, :]) * inverse
            iv[m, rows, :] = inverse
            fo[m, rows, :] = found
            lgt[m, rows, :] = (sg[m, rows, :] * found).astype(BF16)
            return carry

        lax.fori_loop(0, chunks, mix_states, 0, unroll=True)

        weight_ready(m, 3)
        mid[m] = xs[m].astype(F32) + dot_nn(lgt[m], wo[...])
        release(m, 3)

        @pl.when(has_right)
        def _():
            middle_halo(m).start()

        def mix_second(start, size, last):
            rows = pl.ds(start, size)
            spare, spread = normalise(mid[m, rows, :])
            sp2[m, rows, :] = spare
            sd2[m, rows, :] = spread
            normed = spare * gain2[...] + bias2[...]
            position = base + start + lax.broadcasted_iota(jnp.int32, (size, 1), 0)
            earlier = moved_down(normed, last) * keep_of(position, starts)
            gap = normed - earlier
            gp2[m, rows, :] = gap.astype(BF16)
            lh[m, rows, :] = (earlier + gap * mix_h[...]).astype(BF16)
            lf[m, rows, :] = (earlier + gap * mix_f[...]).astype(BF16)
            return normed[size - 1 : size]

        last = none
        for start in range(0, row_count, RB):
            last = mix_second(start, RB, last)

        @pl.when(has_left)
        def _():
            middle_halo(m).wait_recv()

        halo_rows, _ = normalise(hmid[m])
        mix_second(0, 16, halo_rows * gain2[...] + bias2[...])

        for index in range(4, 7):
            weight_ready(m, index)
        sv[m] = sigmoid(dot_nn(lf[m], wf[...]))

        def widen(j, carry):
            columns = pl.ds(pl.multiple_of(j * width, width), width)
            active = jnp.maximum(dot_nn(lh[m], wh[:, columns]), 0.0)
            act[m, :, columns] = active.astype(BF16)
            sq[m, :, columns] = (active * active).astype(BF16)
            return carry

        lax.fori_loop(0, hidden // width, widen, 0, unroll=True)
        release(m, 4)
        release(m, 5)

        proj[m] = dot_nn(sq[m], wp[...])
        for i in range(chunks):
            rows = pl.ds(i * RB, RB)
            out[m, rows, :] = (mid[m, rows, :] + sv[m, rows, :] * proj[m, rows, :]).astype(BF16)
            pl.when(has_next)(lambda i=i: result_copy(m, i).start())

        release(m, 6)

        @pl.when(has_next & has_right)
        def _():
            result_halo(m).start()

        for index in range(6):
            store_copy(index, m).start()

        return carry

    pl.when(is_late)(lambda: transpose_all(True))
    for m in range(batches):
        forward(m, 0)

    @pl.when(jnp.logical_not(is_late))
    def _():
        transpose_all(False)
        for index in range(7):
            return_copy(index).start()

    start_gathers()

    def add_vectors(n, carry):
        m, i = n // chunks, n % chunks
        rows = span_of(i)
        gap = gp2[m, rows, :].astype(F32)
        found = {
            9: mid[m, rows, :] * gap, 10: proj[m, rows, :] * gap,
            7: sv[m, rows, :] * sp2[m, rows, :], 8: sv[m, rows, :],
            5: sa[m, rows, :], 6: iv[m, rows, :],
        }
        gap = gp1[m, rows, :].astype(F32)
        found.update({
            2: kk[m, rows, :] * gap, 3: vv[m, rows, :] * gap, 4: sg[m, rows, :] * gap,
            0: fo[m, rows, :] * sp1[m, rows, :], 1: fo[m, rows, :],
        })
        for index in sorted(found):
            vg[index] += fold(found[index])
        return carry

    @pl.when(me_s == sections - 1)
    def _():
        pltpu.make_async_copy(top_in, dys, top_sem).wait()

    def turned_ready(m, index):
        if m == 0:
            return_copy(index).wait()

    def backward(m, carry):
        starts = starts_of(m)
        none = jnp.zeros((1, width), F32)

        for index, (start, size) in enumerate(pieces):
            pl.when(has_next)(lambda index=index: back_copy(m, index).wait_recv())
            rows = pl.ds(start, size)
            sieve = sv[m, rows, :]
            gained = dys[m, rows, :].astype(F32) * sieve
            dproj[m, rows, :] = gained.astype(BF16)
            dsv[m, rows, :] = (gained * proj[m, rows, :] * (1.0 - sieve)).astype(BF16)

        turned_ready(m, 5)
        turned_ready(m, 6)

        def narrow(j, carry):
            columns = pl.ds(pl.multiple_of(j * width, width), width)
            grown = dot_nn(dproj[m], wh[:, columns])
            dh[m, :, columns] = (grown * 2.0 * act[m, :, columns].astype(F32)).astype(BF16)
            return carry

        lax.fori_loop(0, hidden // width, narrow, 0, unroll=True)
        pl.when(has_right)(lambda: middle_halo(m).wait_send())
        mid[m] = dot_nn(dh[m], wp[...])
        turned_ready(m, 4)
        proj[m] = dot_nn(dsv[m], wf[...])

        def second_earlier(rows, position):
            whole = mid[m, rows, :] * (1.0 - mix_h[...]) + proj[m, rows, :] * (1.0 - mix_f[...])
            return whole * keep_of(position, starts)

        eight = lax.broadcasted_iota(jnp.int32, (8, 1), 0)
        send_de2[m] = second_earlier(pl.ds(0, 8), base + eight)[0:1]

        @pl.when(has_left)
        def _():
            second_copy(m).start()

        def back_second(start, size, following):
            rows = pl.ds(start, size)
            spare, spread = sp2[m, rows, :], sd2[m, rows, :]
            position = base + start + lax.broadcasted_iota(jnp.int32, (size, 1), 0)
            kept = keep_of(position, starts)
            from_h = mid[m, rows, :]
            from_f = proj[m, rows, :]
            straight = from_h * mix_h[...] + from_f * mix_f[...]
            earlier = (from_h + from_f - straight) * kept
            d_normed = straight + moved_up(earlier, following)
            sv[m, rows, :] = d_normed
            scaled = d_normed * gain2[...]
            mean_one = jnp.mean(scaled, axis=-1, keepdims=True)
            mean_two = jnp.mean(scaled * spare, axis=-1, keepdims=True)
            d_mid = dys[m, rows, :].astype(F32) + spread * (scaled - mean_one - spare * mean_two)
            t3[rows, :] = d_mid
            datt[m, rows, :] = d_mid.astype(BF16)

        for start, size in pieces[:-1]:
            end = start + size
            back_second(start, size, second_earlier(pl.ds(end, 8), base + end + eight)[0:1])

        @pl.when(has_right)
        def _():
            second_copy(m).wait_recv()

        back_second(*pieces[-1], de2[m])
        turned_ready(m, 3)
        t1[...] = dot_nn(datt[m], wo[...])
        open_segment = segment(base, starts)

        def back_states_in(i, totals):
            rows = span_of(i)
            d_found = t1[rows, :] * sg[m, rows, :]
            d_a = d_found * iv[m, rows, :]
            d_b = -d_a * fo[m, rows, :]
            falling = e0[rows, :]
            scaled_a = d_a * falling
            scaled_b = d_b * falling
            t1[rows, :] = scaled_a
            t2[rows, :] = scaled_b
            acc[rows, 0:width] = d_found
            chosen = segment(column(i), starts) == open_segment
            return (
                totals[0] + fold(jnp.where(chosen, scaled_a, 0.0)),
                totals[1] + fold(jnp.where(chosen, scaled_b, 0.0)),
            )

        nothing = jnp.zeros((8, width), F32)
        total_a, total_b = lax.fori_loop(0, chunks, back_states_in, (nothing, nothing), unroll=True)
        sum_back[m] = packed(
            jnp.sum(total_a, axis=0, keepdims=True), jnp.sum(total_b, axis=0, keepdims=True)
        )

        def send_state(k, carry):
            back_state_copy(m, k, me).start()
            return carry

        lax.fori_loop(0, me, send_state, 0)
        split_sums()

        def back_present(i, carry):
            rows = span_of(i)
            gate, found = sg[m, rows, :], fo[m, rows, :]
            d_found = acc[rows, 0:width]
            dg[m, rows, :] = (d_found * found * (1.0 - gate)).astype(BF16)
            gained = d_found * iv[m, rows, :] * (boost * kk[m, rows, :])
            d_key = gained * (vv[m, rows, :] - found)
            iv[m, rows, :] = d_key
            t2[rows, :] = gained
            return carry

        lax.fori_loop(0, chunks, back_present, 0, unroll=True)
        acc[...] = dot_nn(up_mask[m], split[...])

        def receive_state(turn, held):
            k = peers - 1 - turn
            back_state_copy(m, k, k).wait_recv()
            first = segment(k * row_count, starts)
            unbroken = first == segment((k + 1) * row_count - 1, starts)
            joined = jnp.where(first == segment(k * row_count - 1, starts), 1.0, 0.0)
            passing = jnp.where(unbroken, 1.0, 0.0) * decay_tile
            return joined * (passing * held + back_states[m, k])

        entered = lax.fori_loop(0, peers - 1 - me, receive_state, jnp.zeros_like(decay_tile))
        enter_a, enter_b = unpacked(entered, 0), unpacked(entered, 1)
        end_segment = segment(base + row_count - 1, starts)

        def back_keys(i, carry):
            rows = span_of(i)
            rising = e1[rows, :]
            chosen = jnp.where(segment(column(i), starts) == end_segment, 1.0, 0.0)
            grown = rising * grow_block
            held = rising * chosen
            d_a = grown * acc[rows, 0:width] + held * enter_a
            d_b = grown * acc[rows, width:] + held * enter_b
            sa[m, rows, :] = d_a * sa[m, rows, :] + d_b * sb[m, rows, :]
            weight = kk[m, rows, :]
            dv[m, rows, :] = (t2[rows, :] + d_a * weight).astype(BF16)
            dk[m, rows, :] = (iv[m, rows, :] + (d_a * vv[m, rows, :] + d_b) * weight).astype(BF16)
            return carry

        lax.fori_loop(0, chunks, back_keys, 0, unroll=True)
        for index in range(3):
            turned_ready(m, index)
        kk[m] = dot_nn(dk[m], wk[...])
        vv[m] = dot_nn(dv[m], wv[...])
        sg[m] = dot_nn(dg[m], wg[...])

        def first_earlier(rows, position):
            whole = (
                kk[m, rows, :] * (1.0 - mix_k[...])
                + vv[m, rows, :] * (1.0 - mix_v[...])
                + sg[m, rows, :] * (1.0 - mix_g[...])
            )
            return whole * keep_of(position, starts)

        send_de1[m] = first_earlier(pl.ds(0, 8), base + eight)[0:1]

        @pl.when(has_left)
        def _():
            first_copy(m).start()

        pl.when(me_s == 0)(lambda: send_near(m))
        for index in range(6, 12):
            store_copy(index, m).start()

        def back_first(index, following):
            start, size = pieces[index]
            rows = pl.ds(start, size)
            spare, spread = sp1[m, rows, :], sd1[m, rows, :]
            position = base + start + lax.broadcasted_iota(jnp.int32, (size, 1), 0)
            kept = keep_of(position, starts)
            from_k = kk[m, rows, :]
            from_v = vv[m, rows, :]
            from_g = sg[m, rows, :]
            straight = from_k * mix_k[...] + from_v * mix_v[...] + from_g * mix_g[...]
            earlier = (from_k + from_v + from_g - straight) * kept
            d_normed = straight + moved_up(earlier, following)
            fo[m, rows, :] = d_normed
            scaled = d_normed * gain1[...]
            mean_one = jnp.mean(scaled, axis=-1, keepdims=True)
            mean_two = jnp.mean(scaled * spare, axis=-1, keepdims=True)
            found = t3[rows, :] + spread * (scaled - mean_one - spare * mean_two)
            back[m, rows, :] = found.astype(BF16)

            @pl.when(has_prior)
            def _():
                back_copy(m, index).start()

        for index, (start, size) in enumerate(pieces[:-1]):
            end = start + size
            back_first(index, first_earlier(pl.ds(end, 8), base + end + eight)[0:1])

        @pl.when(has_right)
        def _():
            first_copy(m).wait_recv()

        back_first(len(pieces) - 1, de1[m])
        store_copy(12, m).start()
        return carry

    for m in range(batches):
        backward(m, 0)
    pl.when(has_prior)(lambda: each_piece(lambda i: back_copy(batches - 1, i).wait_send()))

    @pl.when(me_s > 0)
    def _():
        for m in range(batches):
            send_near(m)


    lax.fori_loop(0, batches * chunks, add_vectors, 0)
    vgs[...] = jnp.sum(vg[...], axis=1)
    vgs[5:6] = vgs[5:6] * (-rate * jnp.exp(-rate))
    def close(m, carry):
        @pl.when((me_s == 0) & has_right)
        def _():
            start_halo(m).wait_send()

        @pl.when(has_next)
        def _():
            for i in range(chunks):
                result_copy(m, i).wait_send()

        @pl.when(has_next & has_right)
        def _():
            result_halo(m).wait_send()

        @pl.when(has_left)
        def _():
            second_copy(m).wait_send()
            first_copy(m).wait_send()

        @pl.when(has_prior)
        def _():
            pl.when(m + 1 < batches)(lambda: each_piece(lambda i: back_copy(m, i).wait_send()))

        for index in range(13):
            store_copy(index, m).wait()

        def ended(k, carry):
            state_copy(m, k, me).wait_send()
            return carry

        lax.fori_loop(me + 1, peers, ended, 0)
        end_gather(m)
        end_near(m)

        def ended_back(k, carry):
            back_state_copy(m, k, me).wait_send()
            return carry

        lax.fori_loop(0, me, ended_back, 0)
        return carry

    lax.fori_loop(0, batches, close, 0)


def relay(sections, peers, x, top, spans, vectors, matrices):
    batches, rows, width = x.shape
    hidden = matrices[4].shape[1]
    slots = 4 if peers <= 8 else 2
    shape = jax.ShapeDtypeStruct
    low = shape((batches, rows, width), BF16)
    square = shape((width, width), BF16)
    vmem = pl.BlockSpec(memory_space=pltpu.VMEM)
    anywhere = pl.BlockSpec(memory_space=pl.ANY)
    dma = pltpu.SemaphoreType.DMA

    def narrow(kind):
        return pltpu.VMEM((batches, rows, width), kind)

    return pl.pallas_call(
        partial(relay_kernel, sections, peers),
        out_shape=(
            low, low, low, low, low, low, low,
            low, low, low, low, low, low, shape((VECTORS, width), F32),
            shape((peers // 2, batches, rows, width), BF16),
            shape((2, batches, rows, width), BF16),
            square, square, square, square, square,
            shape((width, hidden), BF16), shape((hidden, width), BF16),
        ),
        in_specs=[pl.BlockSpec(memory_space=pltpu.SMEM), anywhere, anywhere]
        + [vmem] * 11
        + [anywhere] * 7,
        out_specs=[anywhere] * 13 + [vmem] + [anywhere] * 9,
        scratch_shapes=[narrow(BF16)] * 13 + [
            narrow(BF16), pltpu.VMEM((batches, rows, hidden), BF16),
            pltpu.VMEM((batches, rows, hidden), BF16), pltpu.VMEM((slots, 512, 512), BF16),
        ]
        + [pltpu.VMEM(matrix.shape, BF16) for matrix in matrices_order(matrices)]
        + [
            narrow(BF16), pltpu.VMEM((batches, 16, width), BF16), narrow(BF16),
            narrow(F32), narrow(F32), narrow(F32), narrow(F32), narrow(F32), narrow(F32),
            pltpu.VMEM((batches, 1, width), F32), narrow(F32), narrow(F32),
            pltpu.VMEM((batches, rows, hidden), BF16),
            pltpu.VMEM((rows, width), F32), pltpu.VMEM((rows, width), F32),
            pltpu.VMEM((batches, rows, 2 * rows), BF16), pltpu.VMEM((batches, rows, 2 * rows), BF16),
            pltpu.VMEM((2 * rows, 2 * width), BF16), pltpu.VMEM((rows, 2 * width), F32),
            pltpu.VMEM((rows, width), F32), pltpu.VMEM((rows, width), F32), pltpu.VMEM((rows, width), F32),
            pltpu.VMEM((batches, peers, width // 64, 128), F32),
            pltpu.VMEM((batches, peers, width // 64, 128), F32),
            pltpu.VMEM((batches, 1, width), F32), pltpu.VMEM((batches, 1, width), F32),
            pltpu.VMEM((batches, width // 64, 128), F32),
            pltpu.VMEM((batches, width // 64, 128), F32),
            pltpu.VMEM((batches, 1, width), F32), pltpu.VMEM((batches, 1, width), F32),
            pltpu.VMEM((VECTORS, 8, width), F32),
            narrow(F32), narrow(BF16), pltpu.VMEM((batches, rows, 1), F32),
            narrow(F32), narrow(BF16), pltpu.VMEM((batches, rows, 1), F32),
            narrow(F32), narrow(F32),
            dma((7,)), dma, dma,
            dma((batches,)), dma((batches, rows // RB)), dma((batches,)), dma((batches, peers)),
            dma((batches,)), dma((batches, 3)), dma((batches,)), dma((batches, peers)),
            dma((batches,)),
            dma((batches, rows // RB)), dma((batches,)), dma((batches, peers)), dma((batches,)),
            dma((batches, 3)), dma((batches,)), dma((batches, peers)), dma((batches,)),
            dma((13, batches)),
            dma((batches, peers // 2)), dma((batches, peers // 2)), dma((batches,)),
            dma((2, batches)), dma((2, batches)),
            dma((slots,)), dma((7,)),
        ],
        compiler_params=pltpu.CompilerParams(
            collective_id=0, has_side_effects=True, vmem_limit_bytes=63 * 2**20
        ),
        name="relay",
    )(spans, x, top, *vectors, *matrices_order(matrices))


def matrices_order(matrices):
    wk, wv, wg, wo, wh, wp, wf = matrices
    return (wk, wv, wg, wo, wh, wp, wf)


def sum_kernel(sections, peers, split_vectors, *refs):
    left_in, right_in = refs[0:5], refs[5:10]
    lh_in, dp_in, near_in, wh_in, wp_in, vgs = refs[10:16]
    outs_hbm, wh_hbm, wp_hbm, vec_out = refs[16:20]
    (
        lefts, rights, whole, own, pair_out, going_right, going_left,
        lh, dp, wh, wp, act, wide, hid_out, hid_in, proj_out, proj_in,
        left_sem, right_sem, lh_sem, dp_sem, wh_sem, wp_sem,
        s_pair, r_pair, s_right, r_right, s_left, r_left, s_hid, r_hid, s_proj, r_proj,
        s_ahead, s_behind, r_rows,
        total, wh_out, wp_out, vgr, s_vg, r_vg, outs_sem, wh_out_sem, wp_out_sem,
        near_sem,
    ) = refs[20:]
    count = len(left_in)
    me_s = lax.axis_index("section")
    me = lax.axis_index("dp")
    chips = peers // 2
    chip, core = me // 2, me % 2
    sibling = me + 1 - 2 * core
    blocks, share = chips, own.shape[2]
    columns = wh.shape[2]
    has_right = chip + 1 < chips
    has_left = chip > 0
    after = jnp.minimum(me + 2, peers - 1)
    before = jnp.maximum(me - 2, 0)

    barrier = pltpu.get_barrier_semaphore()

    def greet(index):
        pl.semaphore_signal(barrier, inc=1, device_id=(me_s, index), device_id_type=MESH)

    def each_peer(action):
        def turn(k, carry):
            @pl.when(k != me)
            def _():
                action(k)

            return carry

        lax.fori_loop(0, peers, turn, 0)

    each_peer(greet)
    for w in range(count):
        pltpu.make_async_copy(left_in[w], lefts.at[w], left_sem.at[w]).start()
        pltpu.make_async_copy(right_in[w], rights.at[w], right_sem.at[w]).start()
    is_late = 2 * me_s >= sections
    lh_copy = pltpu.make_async_copy(lh_in, lh, lh_sem)
    rows = dp_in.shape[0]
    own_rows = pl.ds(pl.multiple_of(chip * rows, rows), rows)
    dp_copy = pltpu.make_async_copy(dp_in, dp.at[own_rows], dp_sem)
    dp_copy.start()

    def near_load(way):
        origin = jnp.minimum(chip + 1, chips - 1) if way else jnp.maximum(chip - 1, 0)
        place = pl.ds(pl.multiple_of(origin * rows, rows), rows)
        return pltpu.make_async_copy(near_in.at[way], dp.at[place], near_sem.at[way])

    pl.when(has_left)(lambda: near_load(0).start())
    pl.when(has_right)(lambda: near_load(1).start())
    lh_own = pltpu.make_async_copy(lh_in.at[own_rows], lh.at[own_rows], lh_sem)
    pl.when(is_late)(lh_own.start)
    pl.when(jnp.logical_not(is_late))(lh_copy.start)

    def wh_copy(j, slot):
        return pltpu.make_async_copy(
            wh_in.at[:, pl.ds(pl.multiple_of(j * columns, columns), columns)],
            wh.at[slot], wh_sem.at[slot],
        )

    def wp_copy(j, slot):
        return pltpu.make_async_copy(
            wp_in.at[pl.ds(pl.multiple_of(j * columns, columns), columns)],
            wp.at[slot], wp_sem.at[slot],
        )

    wh_copy(0, 0).start()
    wp_copy(0, 0).start()
    def remote(source, target, send, receive, index):
        return pltpu.make_async_remote_copy(
            src_ref=source, dst_ref=target, send_sem=send, recv_sem=receive,
            device_id=(me_s, index), device_id_type=MESH,
        )

    def pair_copy(w):
        return remote(pair_out.at[w], own.at[w], s_pair.at[w], r_pair.at[w], sibling)

    cut = vgr.shape[2]

    def vector_copy(k, slot):
        part = vgs.at[:, pl.ds(pl.multiple_of(k * cut, cut), cut)] if split_vectors else vgs
        return remote(part, vgr.at[slot], s_vg.at[k], r_vg.at[slot], k)

    def rows_of(block, parity):
        return pl.ds(pl.multiple_of((2 * block + parity) * share, share), share)

    def prepare(w):
        pltpu.make_async_copy(lefts.at[w], lefts.at[w], left_sem.at[w]).wait()
        pltpu.make_async_copy(rights.at[w], rights.at[w], right_sem.at[w]).wait()
        slot = w % 2
        whole[slot] = dot_tn(lefts[w], rights[w])

        def divide(q, carry):
            pair_out[w, q] = whole[slot, rows_of(q, 1 - core), :].astype(BF16)
            return carry

        lax.fori_loop(0, blocks, divide, 0)

    def combine(w):
        slot = w % 2
        pair_copy(w).wait_recv()

        def add(q, carry):
            own[w, q] = (
                whole[slot, rows_of(q, core), :] + own[w, q].astype(F32)
            ).astype(BF16)
            return carry

        lax.fori_loop(0, blocks, add, 0)

    def right_copy(source, w, r):
        return remote(source, going_right.at[w, r], s_right.at[w, r], r_right.at[w, r], after)

    def left_copy(source, w, r):
        return remote(source, going_left.at[w, r], s_left.at[w, r], r_left.at[w, r], before)

    from_end = chips - 1 - chip

    def launch(w):
        def turn(r, carry):
            @pl.when(has_right & (chip == 0))
            def _():
                right_copy(own.at[w, chips - 1 - r], w, r).start()

            @pl.when(has_left & (from_end == 0))
            def _():
                left_copy(own.at[w, r], w, r).start()

            return carry

        lax.fori_loop(0, rounds, turn, 0)

    def travel(w, r):
        prior = jnp.maximum(r - 1, 0)

        @pl.when(has_right & (chip > 0) & (chip <= r))
        def _():
            slot = going_right.at[w, prior]
            right_copy(slot, w, prior).wait_recv()
            slot[...] = (
                slot[...].astype(F32) + own[w, chips - 1 - r + chip].astype(F32)
            ).astype(BF16)
            right_copy(slot, w, r).start()

        @pl.when(has_left & (from_end > 0) & (from_end <= r))
        def _():
            slot = going_left.at[w, prior]
            left_copy(slot, w, prior).wait_recv()
            slot[...] = (
                slot[...].astype(F32) + own[w, r - from_end].astype(F32)
            ).astype(BF16)
            left_copy(slot, w, r).start()

    def rows_copy(kind, origin, send, index):
        block = (lh if kind else dp).at[pl.ds(pl.multiple_of(origin * rows, rows), rows)]
        return remote(block, block, send.at[kind, origin], r_rows.at[kind, origin], index)

    def each_origin(kind, low, high):
        def turn(origin, carry):
            rows_copy(kind, origin, s_ahead, after).wait_recv()
            return carry

        lax.fori_loop(low, high, turn, 0)

    def spread(kind, r):
        held = 0 if kind else 1

        @pl.when(has_right & (chip >= r))
        def _():
            pl.when(r > held)(lambda: rows_copy(kind, chip - r, s_ahead, after).wait_recv())
            rows_copy(kind, chip - r, s_ahead, after).start()

        @pl.when(has_left & (from_end >= r))
        def _():
            pl.when(r > held)(lambda: rows_copy(kind, chip + r, s_behind, before).wait_recv())
            rows_copy(kind, chip + r, s_behind, before).start()

    def hid_copy(j):
        place = pl.ds(pl.multiple_of(j * columns, columns), columns)
        return remote(
            hid_out.at[:, place], hid_in.at[:, place], s_hid.at[j], r_hid.at[j], sibling
        )

    proj_copy = remote(proj_out, proj_in, s_proj, r_proj, sibling)
    group = wide.shape[0]
    first = chip * 2 * share
    start = pl.multiple_of(first // group * group, group)
    inside = first - first // group * group

    def hidden_store(j):
        place = pl.ds(pl.multiple_of(j * columns, columns), columns)
        return pltpu.make_async_copy(hid_in.at[:, place], wh_hbm.at[:, place], wh_out_sem.at[j])

    def close_hidden(j):
        hid_copy(j).wait_recv()
        place = pl.ds(pl.multiple_of(j * columns, columns), columns)
        hid_in[:, place] = (wh_out[:, place] + hid_in[:, place].astype(F32)).astype(BF16)
        hidden_store(j).start()

    def sum_store(w):
        return pltpu.make_async_copy(own.at[w, chip], outs_hbm.at[w], outs_sem.at[w])

    proj_store = pltpu.make_async_copy(proj_in, wp_hbm, wp_out_sem)

    def close_sum(w):
        total[...] = own[w, chip].astype(F32)

        @pl.when(has_left)
        def _():
            right_copy(own.at[w, 0], w, rounds - 1).wait_recv()
            total[...] += going_right[w, rounds - 1].astype(F32)

        @pl.when(has_right)
        def _():
            left_copy(own.at[w, 0], w, rounds - 1).wait_recv()
            total[...] += going_left[w, rounds - 1].astype(F32)

        own[w, chip] = total[...].astype(BF16)
        sum_store(w).start()

    def feed(j):
        slot = j % 2
        place = pl.ds(pl.multiple_of(j * columns, columns), columns)

        @pl.when(j == 0)
        def _():
            dp_copy.wait()
            pl.when(chip == 0)(lambda: each_origin(0, 2, chips))
            pl.when(from_end == 0)(lambda: each_origin(0, 0, chips - 2))
            pl.when(jnp.logical_not(is_late))(lh_copy.wait)
            pl.when(is_late & (chip == 0))(lambda: each_origin(1, 1, chips))
            pl.when(is_late & (from_end == 0))(lambda: each_origin(1, 0, chips - 1))

        wh_copy(j, slot).wait()
        wp_copy(j, slot).wait()

        @pl.when(j + 1 < peers)
        def _():
            wh_copy(j + 1, 1 - slot).start()
            wp_copy(j + 1, 1 - slot).start()

        active = jnp.maximum(dot_nn(lh[...], wh[slot]), 0.0)
        act[...] = active
        grown = (dot_nt(dp[...], wp[slot]) * 2.0 * act[...]).astype(BF16)
        wide[...] = dot_tn(lh[:, pl.ds(start, group)], grown)
        mine = pl.ds(pl.multiple_of(inside + core * share, 16), share)
        other = pl.ds(pl.multiple_of(inside + (1 - core) * share, 16), share)
        wh_out[:, place] = wide[mine, :]
        hid_out[:, place] = wide[other, :].astype(BF16)
        hid_copy(j).start()
        pl.when(j > 0)(lambda: close_hidden(j - 1))

        @pl.when(j == 2 * chip + core)
        def _():
            squared = (act[...] * act[...]).astype(BF16)
            wp_out[...] = dot_tn(squared, dp[...])

        @pl.when(j == 2 * chip + 1 - core)
        def _():
            squared = (act[...] * act[...]).astype(BF16)
            proj_out[...] = dot_tn(squared, dp[...]).astype(BF16)
            proj_copy.start()

    rounds = chips - 1
    prepare(0)
    pl.semaphore_wait(barrier, peers - 1)
    pair_copy(0).start()
    pl.when(has_left)(lambda: near_load(0).wait())
    pl.when(has_right)(lambda: near_load(1).wait())
    spread(0, 1)

    @pl.when(is_late)
    def _():
        lh_own.wait()
        spread(1, 0)

    each_peer(lambda k: vector_copy(k, me).start())
    prepare(1)
    pair_copy(1).start()
    combine(0)
    launch(0)
    if split_vectors:
        vec_out[...] = vgs[:, pl.ds(pl.multiple_of(me * cut, cut), cut)]
    else:
        vec_out[...] = vgs[...]
    opening = count * rounds - peers

    def step(t, carry):
        w, r = t // rounds, t % rounds
        travel(w, r)

        @pl.when((r == 1) & (w + 2 < count))
        def _():
            prepare(w + 2)
            pair_copy(w + 2).start()

        @pl.when((r == 1) & (w + 1 < count))
        def _():
            combine(w + 1)
            launch(w + 1)

        @pl.when(t + 2 < rounds)
        def _():
            spread(0, t + 2)

        @pl.when(is_late & (t + 1 < rounds))
        def _():
            spread(1, t + 1)

        @pl.when(t >= opening)
        def _():
            feed(t - opening)

        @pl.when((r == rounds - 1) & (w > 0))
        def _():
            close_sum(w - 1)

        return carry

    lax.fori_loop(0, count * rounds, step, 0)

    close_hidden(peers - 1)
    proj_copy.wait_recv()
    proj_in[...] = (wp_out[...] + proj_in[...].astype(F32)).astype(BF16)
    proj_store.start()

    def collect(k):
        vector_copy(k, k).wait_recv()
        vec_out[...] += vgr[k]

    each_peer(collect)
    close_sum(count - 1)
    each_peer(lambda k: vector_copy(k, me).wait_send())

    def sent_hidden(j, carry):
        hid_copy(j).wait_send()
        hidden_store(j).wait()
        return carry

    lax.fori_loop(0, peers, sent_hidden, 0)
    proj_copy.wait_send()
    proj_store.wait()

    def sent_rows(origin, carry):
        @pl.when(has_right & (origin < chip))
        def _():
            rows_copy(0, origin, s_ahead, after).wait_send()

        @pl.when(has_left & (origin > chip))
        def _():
            rows_copy(0, origin, s_behind, before).wait_send()

        @pl.when(is_late & has_right & (origin <= chip))
        def _():
            rows_copy(1, origin, s_ahead, after).wait_send()

        @pl.when(is_late & has_left & (origin >= chip))
        def _():
            rows_copy(1, origin, s_behind, before).wait_send()

        return carry

    lax.fori_loop(0, chips, sent_rows, 0)

    def sent(w, carry):
        pair_copy(w).wait_send()
        sum_store(w).wait()

        def sent_round(r, inner):
            @pl.when(has_right & (chip <= r))
            def _():
                right_copy(own.at[w, 0], w, r).wait_send()

            @pl.when(has_left & (from_end <= r))
            def _():
                left_copy(own.at[w, 0], w, r).wait_send()

            return inner

        lax.fori_loop(0, rounds, sent_round, 0)
        return carry

    lax.fori_loop(0, count, sent, 0)


def gradient_sums(sections, peers, lefts, rights, lh, dp, near, wh, wp, vgs):
    count = len(lefts)
    rows, width = lefts[0].shape
    hidden = wh.shape[1]
    tokens = lh.shape[0]
    chips = peers // 2
    share = width // peers
    columns = hidden // peers
    group = max(128, 2 * share)
    shape = jax.ShapeDtypeStruct
    vmem = pl.BlockSpec(memory_space=pltpu.VMEM)
    anywhere = pl.BlockSpec(memory_space=pl.ANY)
    dma = pltpu.SemaphoreType.DMA
    blocks = pltpu.VMEM((count, chips, share, width), BF16)
    slots = pltpu.VMEM((count, chips - 1, share, width), BF16)
    split_vectors = share % 128 == 0
    cut = share if split_vectors else width
    return pl.pallas_call(
        partial(sum_kernel, sections, peers, split_vectors),
        out_shape=(
            shape((count, share, width), BF16), shape((share, hidden), BF16),
            shape((columns, width), BF16), shape((VECTORS, cut), F32),
        ),
        in_specs=[anywhere] * (2 * count + 5) + [vmem],
        out_specs=[anywhere] * 3 + [vmem],
        scratch_shapes=[
            pltpu.VMEM((count, rows, width), BF16), pltpu.VMEM((count, rows, width), BF16),
            pltpu.VMEM((2, width, width), F32),
            blocks, blocks, slots, slots,
            pltpu.VMEM((tokens, width), BF16), pltpu.VMEM((tokens, width), BF16),
            pltpu.VMEM((2, width, columns), BF16), pltpu.VMEM((2, columns, width), BF16),
            pltpu.VMEM((tokens, columns), F32), pltpu.VMEM((group, columns), F32),
            pltpu.VMEM((share, hidden), BF16), pltpu.VMEM((share, hidden), BF16),
            pltpu.VMEM((columns, width), BF16), pltpu.VMEM((columns, width), BF16),
            dma((count,)), dma((count,)), dma, dma, dma((2,)), dma((2,)),
            dma((count,)), dma((count,)),
            dma((count, chips - 1)), dma((count, chips - 1)),
            dma((count, chips - 1)), dma((count, chips - 1)),
            dma((peers,)), dma((peers,)), dma, dma,
            dma((2, chips)), dma((2, chips)), dma((2, chips)),
            pltpu.VMEM((share, width), F32), pltpu.VMEM((share, hidden), F32),
            pltpu.VMEM((columns, width), F32), pltpu.VMEM((peers, VECTORS, cut), F32),
            dma((peers,)), dma((peers,)), dma((count,)), dma((peers,)), dma, dma((2,)),
        ],
        compiler_params=pltpu.CompilerParams(
            collective_id=1, has_side_effects=True, vmem_limit_bytes=63 * 2**20
        ),
        name="gradient_sums",
    )(*lefts, *rights, lh, dp, near, wh, wp, vgs)


def deliver_kernel(count, vectors, *refs):
    vec, sources = refs[0], refs[1:6]
    targets = refs[6 : 6 + count]
    rows = refs[6 + count : 6 + count + vectors]
    buffers = refs[6 + count + vectors : 6 + 2 * count + vectors]
    wide = refs[6 + 2 * count + vectors : -2]
    in_sem, out_sem = refs[-2:]
    pieces = list(sources[:-1]) + [sources[-1].at[w] for w in range(count - 4)]
    enter = [
        pltpu.make_async_copy(piece, buffer, in_sem.at[index])
        for index, (piece, buffer) in enumerate(zip(pieces, buffers))
    ]
    leave = [
        pltpu.make_async_copy(buffer, target, out_sem.at[index])
        for index, (buffer, target) in enumerate(zip(buffers[:2] + wide, targets))
    ]
    for copy in enter:
        copy.start()
    for index, row in enumerate(rows):
        row[...] = vec[index : index + 1, :]
    for index, (first, second) in enumerate(zip(enter, leave)):
        first.wait()
        if index >= 2:
            wide[index - 2][...] = buffers[index][...].astype(F32)
        second.start()
    for copy in leave:
        copy.wait()


def deliver(vec, hidden, project, out, back, squares, vectors):
    shapes = [(out.shape, BF16), (back.shape, BF16), (hidden.shape, F32), (project.shape, F32)]
    shapes += [(squares.shape[1:], F32)] * squares.shape[0]
    count = len(shapes)
    anywhere = pl.BlockSpec(memory_space=pl.ANY)
    vmem = pl.BlockSpec(memory_space=pltpu.VMEM)
    dma = pltpu.SemaphoreType.DMA
    found = pl.pallas_call(
        partial(deliver_kernel, count, vectors),
        out_shape=tuple(jax.ShapeDtypeStruct(*kind) for kind in shapes)
        + (jax.ShapeDtypeStruct((1, vec.shape[1]), F32),) * vectors,
        in_specs=[vmem] + [anywhere] * 5,
        out_specs=[anywhere] * count + [vmem] * vectors,
        scratch_shapes=[pltpu.VMEM(kind[0], BF16) for kind in shapes]
        + [pltpu.VMEM(*kind) for kind in shapes[2:]]
        + [dma((count,)), dma((count,))],
        compiler_params=pltpu.CompilerParams(vmem_limit_bytes=63 * 2**20),
        name="deliver",
    )(vec, out, back, hidden, project, squares)
    return found[:count], found[count:]


def per_device(x, top, spans, *parameters):
    sections = lax.axis_size("section")
    peers = lax.axis_size("dp")
    gain1, bias1, mix_k, mix_v, mix_g, log_rate, extra = parameters[0:7]
    wk, wv, wg, wo = parameters[7:11]
    gain2, bias2, mix_h, mix_f = parameters[11:15]
    wh, wp, wf = parameters[15:18]
    vectors = (gain1, bias1, mix_k, mix_v, mix_g, log_rate, extra, gain2, bias2, mix_h, mix_f)
    matrices = tuple(w[0] for w in (wk, wv, wg, wo, wh, wp, wf))
    found = relay(sections, peers, x, top, spans, vectors, matrices)
    out, back, lk, lv, lg, lgt, lf, dk, dv, dg, datt, dsv, dproj = found[0:13]
    vgs, lh = found[13], found[14].reshape(-1, x.shape[2])
    flat = (x.shape[0] * x.shape[1], x.shape[2])
    squares, d_wh, d_wp, vec = gradient_sums(
        sections, peers,
        [part.reshape(flat) for part in (lf, lgt, lg, lk, lv)],
        [part.reshape(flat) for part in (dsv, datt, dg, dk, dv)],
        lh, dproj.reshape(flat), found[15].reshape(2, *flat), matrices[4], matrices[5], vgs,
    )
    share = x.shape[2] // peers
    if vec.shape[1] != share:
        vec = lax.dynamic_slice_in_dim(vec, lax.axis_index("dp") * share, share, 1)
    moved, rows = deliver(vec, d_wh, d_wp, out, back, squares, 11)
    out, back, d_wh, d_wp, d_wf, d_wo, d_wg, d_wk, d_wv = (part[None] for part in moved)
    return (
        out, back,
        rows[0], rows[1], rows[2], rows[3], rows[4], rows[5], rows[6],
        d_wk, d_wv, d_wg, d_wo,
        rows[7], rows[8], rows[9], rows[10],
        d_wh, d_wp, d_wf,
    )


def solution(mesh):
    tokens = P(None, "dp", None)
    vector = P("section", None)
    matrix = P("section", None, None)
    result = P("section", None, "dp", None)
    vector_grad = P("section", "dp")
    matrix_grad = P("section", "dp", None)
    return jax.shard_map(
        per_device,
        mesh=mesh,
        in_specs=(tokens, tokens, P())
        + (vector,) * 7 + (matrix,) * 4 + (vector,) * 4 + (matrix,) * 3,
        out_specs=(result, result)
        + (vector_grad,) * 7 + (matrix_grad,) * 4 + (vector_grad,) * 4 + (matrix_grad,) * 3,
        check_vma=False,
    )
```
